32 devices in a mesh: dp: 4 (over y, core), label: 8 (over z, x).
Axes of the slice: x: 2, y: 2, z: 4, core: 2. Of those that a mesh axis runs over, the one named last changes fastest.
Arguments:
- feats: bfloat16 [2048, 1024], P('dp'), may hold values from -2 to 2
- weights: bfloat16 [128, 256, 1024], P(('dp', 'label')), may hold values from -5 to 5
- shortlist: int32 [16, 16], replicated, may hold values from 0 to 127, as said below
- slot_of: int32 [128], replicated, may hold values from 0 to 127, as said below
- positives: int32 [2048, 8], P('dp'), may hold values from 0 to 32767, as said below
Outputs:
- loss: float32 [2048], P('dp')
- grad_feats: bfloat16 [2048, 1024], P('dp', 'label')
The draws below stay inside these ranges and needn't reach their ends.
Inputs may be any that keep to these rules, and one draw needn't show every extreme that they name: `slot_of`: A permutation of the cluster ids: the slot of each cluster. For each index d of dp, its blocks d * 4 to d * 4 + 3: the first 2 of them together shortlist one cluster stored on each device (the device of slot s being s // 4 in the order of the weights' placement), each once, and the last 2 shortlist the same clusters, each once; so every such cluster is shortlisted by exactly two blocks of d. `positives`: an instance's 8 labels are different, and each lies in a cluster that the instance's block shortlists.
All inputs are finite; a program needn't handle non-finite values.
Results may differ from the reference program's by a relative error of at most 0.0034.
Values may be sent and summed in bfloat16 or wider, within the bound.
No kernel may reach another device: no remote copies, remote signals or barrier semaphores. Data moves between devices by JAX's collectives and lax.ppermute only.
A program may use at most 64 MiB of HBM per device.

```python
import math
import jax
import jax.numpy as jnp
from jax import lax

D = 1024
CS = 256
BLK = 128
POS = 8
CL_DEV = 4
NB = 4
KB = 16
INST = 2048
NBT = 16
NCL = 128
N_DP = 4
N_LABEL = 8


def cluster_rows(key, slot):
    sub_key = jax.random.fold_in(jax.random.fold_in(key, 13), slot)
    values = jnp.clip(jax.random.normal(sub_key, (CS, D), jnp.float32), -5.0, 5.0)
    return values


def slot_table(key):
    return jax.random.permutation(jax.random.fold_in(key, 11), NCL).astype(jnp.int32)


def shortlist_table(key):
    slot_of = slot_table(key)
    cluster_at = jnp.zeros((NCL,), jnp.int32).at[slot_of].set(jnp.arange(NCL, dtype=jnp.int32))
    dev_total = N_DP * N_LABEL
    local_key, first_key, second_key = jax.random.split(jax.random.fold_in(key, 12), 3)
    local_ids = jax.random.randint(local_key, (N_DP, dev_total), 0, CL_DEV)
    chosen = cluster_at[jnp.arange(dev_total, dtype=jnp.int32)[None, :] * CL_DEV + local_ids]
    first_order = jax.vmap(lambda sub_key: jax.random.permutation(sub_key, dev_total))(jax.random.split(first_key, N_DP))
    second_order = jax.vmap(lambda sub_key: jax.random.permutation(sub_key, dev_total))(jax.random.split(second_key, N_DP))
    low_half = jnp.take_along_axis(chosen, first_order, axis=1).reshape(N_DP, NB // 2, KB)
    high_half = jnp.take_along_axis(chosen, second_order, axis=1).reshape(N_DP, NB // 2, KB)
    return jnp.concatenate([low_half, high_half], axis=1).reshape(NBT, KB).astype(jnp.int32)


def draw_slot_of(key, part):
    return slot_table(key)


def draw_shortlist(key, part):
    return shortlist_table(key)


def draw_weights(key, part):
    values = jax.vmap(lambda slot: cluster_rows(key, slot))(jnp.arange(NCL, dtype=jnp.int32))
    return values.astype(jnp.bfloat16)


def draw_positives(key, part):
    shortlist = shortlist_table(key)
    pick_key, offset_key = jax.random.split(jax.random.fold_in(key, 14))
    picks = jax.random.randint(pick_key, (INST, POS), 0, KB)
    stride = CS // POS
    offsets = jnp.arange(POS, dtype=jnp.int32)[None, :] * stride + jax.random.randint(offset_key, (INST, POS), 0, stride)
    block_ids = jnp.arange(INST, dtype=jnp.int32) // BLK
    clusters = shortlist[block_ids[:, None], picks]
    return (clusters * CS + offsets).astype(jnp.int32)


def draw_feats(key, part):
    base_key = jax.random.fold_in(key, 15)
    value_key = jax.random.fold_in(base_key, 1)
    spread = 3.0 / math.sqrt(D)
    values = jnp.clip(jax.random.normal(value_key, (INST, D), jnp.float32), -6.0, 6.0) * spread
    return values.astype(jnp.bfloat16)


def setup_inputs(seed: int = 0) -> dict:
    keys = jax.random.split(jax.random.key(seed), 6)
    return {
        "feats": draw_feats(jax.random.fold_in(keys[5], 71), 0),
        "weights": draw_weights(jax.random.fold_in(keys[5], 71), 0),
        "shortlist": draw_shortlist(jax.random.fold_in(keys[5], 71), 0),
        "slot_of": draw_slot_of(jax.random.fold_in(keys[5], 71), 0),
        "positives": draw_positives(jax.random.fold_in(keys[5], 71), 0),
    }


def block_terms(feat_block, clusters, pos_block, weights, slot_of):
    slots = slot_of[clusters]
    table = weights[slots].reshape(KB * CS, D)
    logits = jnp.dot(feat_block, table.T, preferred_element_type=jnp.float32)
    highest = jnp.max(logits, axis=1)
    total = jnp.sum(jnp.exp(logits - highest[:, None]), axis=1)
    log_sum = highest + jnp.log(total)
    pos_cluster = pos_block // CS
    pos_offset = pos_block % CS
    cluster_match = (pos_cluster[:, :, None] == clusters[None, None, :]).astype(jnp.float32)
    offset_hot = (pos_offset[:, :, None] == jnp.arange(CS, dtype=jnp.int32)[None, None, :]).astype(jnp.float32)
    target = jnp.einsum("ipk,ipo->iko", cluster_match, offset_hot).reshape(BLK, KB * CS)
    pos_total = jnp.sum(target * logits, axis=1)
    loss_rows = log_sum - pos_total / POS
    dlogit = (jnp.exp(logits - log_sum[:, None]) - target / POS).astype(jnp.bfloat16)
    grads = jnp.dot(dlogit, table, preferred_element_type=jnp.float32).astype(jnp.bfloat16)
    return loss_rows, grads


def reference(feats, weights, shortlist, slot_of, positives):
    blocks = feats.shape[0] // BLK

    def one_block(items):
        feat_block, clusters, pos_block = items
        return block_terms(feat_block, clusters, pos_block, weights, slot_of)

    loss_rows, grads = lax.map(one_block, (feats.reshape(blocks, BLK, D), shortlist, positives.reshape(blocks, BLK, POS)))
    return loss_rows.reshape(-1), grads.reshape(-1, D)
```

```python
import functools

import jax
import jax.numpy as jnp
from jax import lax
from jax.experimental import pallas as pl
from jax.experimental.pallas import tpu as pltpu
from jax.sharding import PartitionSpec as P

BLK = 128
NEG_FILL = -1e30
VMEM_BYTES = 56 * 1024 * 1024


def pick_kernel(sizes, place_ref, lists_ref, slot_ref, weights_ref, table_ref, *rest):
    dp_count, lab_count, stored, block_count, short_count = sizes
    outs, sems = rest[:-1], rest[-1]
    dp_index, lab_index = place_ref[0], place_ref[1]
    mine = dp_index * lab_count + lab_index
    half = block_count // 2
    unroll = half * short_count if half * short_count <= 32 else 8
    copies = []
    for k in range(1, dp_count):
        base = (dp_index ^ k) * block_count

        def look(e, found, base=base):
            slot = slot_ref[lists_ref[base + lax.div(e, short_count), lax.rem(e, short_count)]]
            return jnp.where(lax.div(slot, stored) == mine, lax.rem(slot, stored), found)

        found = lax.fori_loop(0, half * short_count, look, jnp.int32(0), unroll=unroll)
        copy = pltpu.make_async_copy(weights_ref.at[found], outs[k - 1], sems.at[k - 1])
        copy.start()
        copies.append(copy)

    for side in range(2):

        def note(e, carry, side=side):
            block = side * half + lax.div(e, short_count)
            cluster = lists_ref[dp_index * block_count + block, lax.rem(e, short_count)]
            slot = slot_ref[cluster]
            device = lax.div(slot, stored)

            @pl.when(lax.rem(device, lab_count) == lab_index)
            def _():
                entry = lax.div(device, lab_count) ^ dp_index
                table_ref[entry, 0] = cluster
                table_ref[entry, 1 + side] = block
                table_ref[entry, 3] = lax.rem(slot, stored)

            return carry

        lax.fori_loop(0, half * short_count, note, 0)
    for copy in copies:
        copy.wait()


def target_of(pos_ref, block, first, cluster_size):
    labels = lax.broadcasted_iota(jnp.int32, (cluster_size, BLK), 0) + first
    pos = pos_ref[block]
    hit = pos[0:1, :] == labels
    for p in range(1, pos.shape[0]):
        hit = hit | (pos[p : p + 1, :] == labels)
    return hit


def start_rows(weights_ref, arrived, table_ref, held, sems):
    copies = [pltpu.make_async_copy(weights_ref.at[table_ref[0, 3]], held.at[0], sems.at[0])]
    for k, ref in enumerate(arrived):
        copies.append(pltpu.make_async_copy(ref, held.at[k + 1], sems.at[k + 1]))
    for copy in copies:
        copy.start()
    return copies


def logit_kernel(dp_count, table_ref, feats_ref, pos_ref, weights_ref, *rest):
    arrived = rest[: dp_count - 1]
    logits_ref, stats_ref, held, sems = rest[dp_count - 1 :]
    cluster_size = held.shape[1]
    copies = start_rows(weights_ref, arrived, table_ref, held, sems)
    stats_ref[0] = jnp.full(stats_ref.shape[1:], NEG_FILL, jnp.float32)
    stats_ref[1] = jnp.zeros(stats_ref.shape[1:], jnp.float32)
    stats_ref[2] = jnp.zeros(stats_ref.shape[1:], jnp.float32)
    for s in range(dp_count):
        copies[s].wait()
        first = table_ref[s, 0] * cluster_size
        for side in range(2):
            block = table_ref[s, 1 + side]
            logits = lax.dot_general(
                held[s],
                feats_ref[block],
                (((1,), (1,)), ((), ())),
                preferred_element_type=jnp.float32,
            )
            logits_ref[s, :, side * BLK : (side + 1) * BLK] = logits
            hit = target_of(pos_ref, block, first, cluster_size)
            highest = jnp.max(logits, axis=0, keepdims=True)
            total = jnp.sum(jnp.exp(logits - highest), axis=0, keepdims=True)
            positive = jnp.sum(jnp.where(hit, logits, 0.0), axis=0, keepdims=True)
            row = pl.ds(block, 1)
            before = stats_ref[0, row, :]
            after = jnp.maximum(before, highest)
            stats_ref[0, row, :] = after
            stats_ref[1, row, :] = stats_ref[1, row, :] * jnp.exp(before - after) + total * jnp.exp(
                highest - after
            )
            stats_ref[2, row, :] = stats_ref[2, row, :] + positive


def grad_kernel(dp_count, lab_count, table_ref, pos_ref, logits_ref, weights_ref, *rest):
    arrived = rest[: dp_count - 1]
    stats = rest[dp_count - 1 : dp_count - 1 + lab_count]
    loss_ref, out_ref, held, lse_ref, total_ref, sems = rest[dp_count - 1 + lab_count :]
    cluster_size = held.shape[1]
    pos_count = pos_ref.shape[1]
    copies = start_rows(weights_ref, arrived, table_ref, held, sems)
    highest = stats[0][0]
    for ref in stats[1:]:
        highest = jnp.maximum(highest, ref[0])
    summed = jnp.zeros_like(highest)
    positive = jnp.zeros_like(highest)
    for ref in stats:
        summed = summed + ref[1] * jnp.exp(ref[0] - highest)
        positive = positive + ref[2]
    lse = highest + jnp.log(summed)
    lse_ref[...] = lse
    loss_ref[...] = lse - positive / pos_count
    total_ref[...] = jnp.zeros_like(total_ref)
    for s in range(dp_count):
        copies[s].wait()
        first = table_ref[s, 0] * cluster_size
        for side in range(2):
            block = table_ref[s, 1 + side]
            logits = logits_ref[s, :, side * BLK : (side + 1) * BLK]
            hit = target_of(pos_ref, block, first, cluster_size)
            dlogit = jnp.exp(logits - lse_ref[pl.ds(block, 1), :]) - jnp.where(
                hit, 1.0 / pos_count, 0.0
            )
            total_ref[block] += lax.dot_general(
                dlogit.T.astype(jnp.bfloat16),
                held[s],
                (((1,), (0,)), ((), ())),
                preferred_element_type=jnp.float32,
            )
    part = out_ref.shape[2]
    for j in range(lab_count):
        for b in range(total_ref.shape[0]):
            out_ref[j, b * BLK : (b + 1) * BLK, :] = total_ref[
                b, :, j * part : (j + 1) * part
            ].astype(jnp.bfloat16)


def smem():
    return pl.BlockSpec(memory_space=pltpu.SMEM)


def vmem():
    return pl.BlockSpec(memory_space=pltpu.VMEM)


def anywhere():
    return pl.BlockSpec(memory_space=pl.ANY)


def shards(feats, weights, shortlist, slot_of, positives):
    dp_count = lax.axis_size("dp")
    lab_count = lax.axis_size("label")
    place = jnp.stack([lax.axis_index("dp"), lax.axis_index("label")]).astype(jnp.int32)
    stored, cluster_size, width = weights.shape
    inst_count = feats.shape[0]
    pos_count = positives.shape[1]
    block_count = inst_count // BLK
    short_count = shortlist.shape[1]
    params = pltpu.CompilerParams(vmem_limit_bytes=VMEM_BYTES)
    rows = jax.ShapeDtypeStruct((cluster_size, width), weights.dtype)

    table, *wanted = pl.pallas_call(
        functools.partial(
            pick_kernel, (dp_count, lab_count, stored, block_count, short_count)
        ),
        out_shape=[jax.ShapeDtypeStruct((dp_count, 4), jnp.int32)] + [rows] * (dp_count - 1),
        in_specs=[smem(), smem(), smem(), anywhere()],
        out_specs=[smem()] + [anywhere()] * (dp_count - 1),
        scratch_shapes=[pltpu.SemaphoreType.DMA((dp_count - 1,))],
        compiler_params=params,
        name="pick",
    )(place, shortlist, slot_of, weights)
    arrived = [
        lax.ppermute(wanted[k - 1], "dp", [(i, i ^ k) for i in range(dp_count)])
        for k in range(1, dp_count)
    ]

    feat_blocks = feats.reshape(block_count, BLK, width)
    pos_blocks = positives.reshape(block_count, BLK, pos_count).transpose(0, 2, 1)
    held = pltpu.VMEM((dp_count, cluster_size, width), weights.dtype)
    logits, stats = pl.pallas_call(
        functools.partial(logit_kernel, dp_count),
        out_shape=[
            jax.ShapeDtypeStruct((dp_count, cluster_size, 2 * BLK), jnp.float32),
            jax.ShapeDtypeStruct((3, block_count, BLK), jnp.float32),
        ],
        in_specs=[smem(), vmem(), vmem(), anywhere()] + [anywhere()] * (dp_count - 1),
        out_specs=[vmem(), vmem()],
        scratch_shapes=[held, pltpu.SemaphoreType.DMA((dp_count,))],
        compiler_params=params,
        name="logits",
    )(table, feat_blocks, pos_blocks, weights, *arrived)

    all_stats = [stats] + [
        lax.ppermute(stats, "label", [(i, i ^ k) for i in range(lab_count)])
        for k in range(1, lab_count)
    ]
    loss, parts = pl.pallas_call(
        functools.partial(grad_kernel, dp_count, lab_count),
        out_shape=[
            jax.ShapeDtypeStruct((block_count, BLK), jnp.float32),
            jax.ShapeDtypeStruct((lab_count, inst_count, width // lab_count), jnp.bfloat16),
        ],
        in_specs=[smem(), vmem(), vmem(), anywhere()]
        + [anywhere()] * (dp_count - 1)
        + [vmem()] * lab_count,
        out_specs=[vmem(), vmem()],
        scratch_shapes=[
            held,
            pltpu.VMEM((block_count, BLK), jnp.float32),
            pltpu.VMEM((block_count, BLK, width), jnp.float32),
            pltpu.SemaphoreType.DMA((dp_count,)),
        ],
        compiler_params=params,
        name="grads",
    )(table, pos_blocks, logits, weights, *arrived, *all_stats)

    gathered = lax.all_to_all(parts, "label", split_axis=0, concat_axis=0, tiled=True)
    grads = jnp.sum(gathered.astype(jnp.float32), axis=0).astype(jnp.bfloat16)
    return loss.reshape(inst_count), grads


def solution(mesh):
    in_specs = (P("dp", None), P(("dp", "label"), None, None), P(), P(), P("dp", None))
    out_specs = (P("dp"), P("dp", "label"))
    return jax.shard_map(shards, mesh=mesh, in_specs=in_specs, out_specs=out_specs, check_vma=False)
```

```python
import functools

import jax
import jax.numpy as jnp
from jax import lax
from jax.experimental import pallas as pl
from jax.experimental.pallas import tpu as pltpu
from jax.sharding import PartitionSpec as P

BLK = 128
NEG_FILL = -1e30
VMEM_BYTES = 32 * 1024 * 1024


def divide(value, by):
    if by & (by - 1) == 0:
        return lax.shift_right_logical(value, jnp.int32(by.bit_length() - 1))
    return lax.div(value, jnp.int32(by))


def remainder(value, by):
    if by & (by - 1) == 0:
        return value & jnp.int32(by - 1)
    return lax.rem(value, jnp.int32(by))


def each_entry(count, short_count, body, carry):
    if count <= 64:
        for e in range(count):
            carry = body(e // short_count, e % short_count, carry)
        return carry
    step = lambda e, c: body(divide(e, short_count), remainder(e, short_count), c)
    return lax.fori_loop(0, count, step, carry)


def pick_kernel(sizes, place_ref, lists_ref, slot_ref, weights_ref, table_ref, *rest):
    dp_count, lab_count, stored, block_count, short_count = sizes
    outs, sems = rest[:-1], rest[-1]
    dp_index, lab_index = place_ref[0], place_ref[1]
    mine = dp_index * lab_count + lab_index
    half = block_count // 2
    copies = []
    for k in range(dp_count):
        base = (dp_index ^ k) * block_count

        def look(row, column, found, base=base):
            slot = slot_ref[lists_ref[base + row, column]]
            return jnp.where(divide(slot, stored) == mine, remainder(slot, stored), found)

        found = each_entry(half * short_count, short_count, look, jnp.int32(0))
        copy = pltpu.make_async_copy(weights_ref.at[found], outs[k], sems.at[k])
        copy.start()
        copies.append(copy)

    for side in range(2):

        def note(row, column, carry, side=side):
            block = side * half + row
            cluster = lists_ref[dp_index * block_count + block, column]
            device = divide(slot_ref[cluster], stored)

            @pl.when(remainder(device, lab_count) == lab_index)
            def _():
                entry = divide(device, lab_count) ^ dp_index
                table_ref[entry, 0] = cluster
                table_ref[entry, 1 + side] = jnp.int32(block)

            return carry

        each_entry(half * short_count, short_count, note, jnp.int32(0))
    for copy in copies:
        copy.wait()


def target_of(pos_ref, block, first, cluster_size):
    labels = lax.broadcasted_iota(jnp.int32, (cluster_size, BLK), 0) + first
    pos = pos_ref[block]
    hit = pos[0:1, :] == labels
    for p in range(1, pos.shape[0]):
        hit = hit | (pos[p : p + 1, :] == labels)
    return hit


def logit_kernel(slots, copies, table_ref, feats_ref, pos_ref, *rest):
    count = len(slots)
    rows = rest[:count]
    stats_in = rest[count] if slots[0] else None
    logits_ref, out_ref, stats_ref = rest[-3:]
    cluster_size = rows[0].shape[0]
    if stats_in is None:
        stats_ref[0] = jnp.full(stats_ref.shape[1:], NEG_FILL, jnp.float32)
        stats_ref[1] = jnp.zeros(stats_ref.shape[1:], jnp.float32)
        stats_ref[2] = jnp.zeros(stats_ref.shape[1:], jnp.float32)
    else:
        stats_ref[...] = stats_in[0]
    for s, ref in zip(slots, rows):
        first = table_ref[s, 0] * cluster_size
        for side in range(2):
            block = table_ref[s, 1 + side]
            logits = lax.dot_general(
                ref[...],
                feats_ref[block],
                (((1,), (1,)), ((), ())),
                preferred_element_type=jnp.float32,
            )
            logits_ref[s - slots[0], :, side * BLK : (side + 1) * BLK] = logits
            hit = target_of(pos_ref, block, first, cluster_size)
            highest = jnp.max(logits, axis=0, keepdims=True)
            total = jnp.sum(jnp.exp(logits - highest), axis=0, keepdims=True)
            positive = jnp.sum(jnp.where(hit, logits, 0.0), axis=0, keepdims=True)
            row = pl.ds(block, 1)
            before = stats_ref[0, row, :]
            after = jnp.maximum(before, highest)
            stats_ref[0, row, :] = after
            stats_ref[1, row, :] = stats_ref[1, row, :] * jnp.exp(before - after) + total * jnp.exp(
                highest - after
            )
            stats_ref[2, row, :] = stats_ref[2, row, :] + positive
    for i in range(copies):
        out_ref[i] = stats_ref[...]


def grad_kernel(groups, lab_count, table_ref, pos_ref, stats_ref, *rest):
    dp_count = groups[-1][-1] + 1
    logits_refs = rest[: len(groups)]
    rows = rest[len(groups) : len(groups) + dp_count]
    loss_ref, out_ref, lse_ref, total_ref = rest[len(groups) + dp_count :]
    cluster_size = rows[0].shape[0]
    pos_count = pos_ref.shape[1]
    highest = stats_ref[0, 0]
    for i in range(1, lab_count):
        highest = jnp.maximum(highest, stats_ref[i, 0])
    summed = jnp.zeros_like(highest)
    positive = jnp.zeros_like(highest)
    for i in range(lab_count):
        summed = summed + stats_ref[i, 1] * jnp.exp(stats_ref[i, 0] - highest)
        positive = positive + stats_ref[i, 2]
    lse = highest + jnp.log(summed)
    lse_ref[...] = lse
    loss_ref[...] = lse - positive / pos_count
    total_ref[...] = jnp.zeros_like(total_ref)

    def add_slot(s, logits):
        first = table_ref[s, 0] * cluster_size
        for side in range(2):
            block = table_ref[s, 1 + side]
            hit = target_of(pos_ref, block, first, cluster_size)
            dlogit = jnp.exp(
                logits[:, side * BLK : (side + 1) * BLK] - lse_ref[pl.ds(block, 1), :]
            ) - jnp.where(hit, 1.0 / pos_count, 0.0)
            total_ref[block] += lax.dot_general(
                dlogit.T.astype(jnp.bfloat16),
                rows[s][...],
                (((1,), (0,)), ((), ())),
                preferred_element_type=jnp.float32,
            )

    for slots, logits_ref in zip(groups, logits_refs):
        for s in slots:
            body = functools.partial(add_slot, s, logits_ref.at[s - slots[0]])
            if dp_count <= 4:
                body()
            else:
                pl.when(table_ref[s, 0] >= 0)(body)
    part = out_ref.shape[2]
    for j in range(lab_count):
        for b in range(total_ref.shape[0]):
            out_ref[j, b * BLK : (b + 1) * BLK, :] = total_ref[
                b, :, j * part : (j + 1) * part
            ].astype(jnp.bfloat16)


def smem():
    return pl.BlockSpec(memory_space=pltpu.SMEM)


def vmem():
    return pl.BlockSpec(memory_space=pltpu.VMEM)


def anywhere():
    return pl.BlockSpec(memory_space=pl.ANY)


def shards(feats, weights, shortlist, slot_of, positives):
    dp_count = lax.axis_size("dp")
    lab_count = lax.axis_size("label")
    place = jnp.stack([lax.axis_index("dp"), lax.axis_index("label")]).astype(jnp.int32)
    stored, cluster_size, width = weights.shape
    inst_count = feats.shape[0]
    pos_count = positives.shape[1]
    block_count = inst_count // BLK
    short_count = shortlist.shape[1]
    params = pltpu.CompilerParams(vmem_limit_bytes=VMEM_BYTES)
    row_type = jax.ShapeDtypeStruct((cluster_size, width), weights.dtype)
    stat_shape = (3, block_count, BLK)

    table, *rows = pl.pallas_call(
        functools.partial(
            pick_kernel, (dp_count, lab_count, stored, block_count, short_count)
        ),
        out_shape=[jax.ShapeDtypeStruct((dp_count, 4), jnp.int32)] + [row_type] * dp_count,
        in_specs=[smem(), smem(), smem(), anywhere()],
        out_specs=[smem()] + [vmem()] * dp_count,
        scratch_shapes=[pltpu.SemaphoreType.DMA((dp_count,))],
        compiler_params=params,
        name="pick",
    )(place, shortlist, slot_of, weights)
    for k in range(1, dp_count):
        rows[k] = lax.ppermute(rows[k], "dp", [(i, i ^ k) for i in range(dp_count)])

    feat_blocks = feats.reshape(block_count, BLK, width)
    pos_blocks = positives.reshape(block_count, BLK, pos_count).transpose(0, 2, 1)
    cuts = (0, dp_count // 2, dp_count * 3 // 4, dp_count)
    groups = [tuple(range(a, b)) for a, b in zip(cuts[:-1], cuts[1:])]
    kept = []
    stats = []
    for slots in groups:
        count = len(slots)
        copies = lab_count if slots is groups[-1] else 1
        logits, stats_out = pl.pallas_call(
            functools.partial(logit_kernel, slots, copies),
            out_shape=[
                jax.ShapeDtypeStruct((count, cluster_size, 2 * BLK), jnp.float32),
                jax.ShapeDtypeStruct((copies,) + stat_shape, jnp.float32),
            ],
            in_specs=[smem()] + [vmem()] * (2 + count + len(stats)),
            out_specs=[vmem(), vmem()],
            scratch_shapes=[pltpu.VMEM(stat_shape, jnp.float32)],
            compiler_params=params,
            cost_estimate=pl.CostEstimate(
                flops=count * 4 * BLK * cluster_size * width,
                bytes_accessed=count * cluster_size * width * 2,
                transcendentals=0,
            ),
            name="logits",
        )(table, feat_blocks, pos_blocks, *[rows[s] for s in slots], *stats)
        kept.append(logits)
        stats = [stats_out]

    all_stats = lax.all_to_all(stats[0], "label", split_axis=0, concat_axis=0, tiled=True)
    loss, parts = pl.pallas_call(
        functools.partial(grad_kernel, groups, lab_count),
        out_shape=[
            jax.ShapeDtypeStruct((block_count, BLK), jnp.float32),
            jax.ShapeDtypeStruct((lab_count, inst_count, width // lab_count), jnp.bfloat16),
        ],
        in_specs=[smem()] + [vmem()] * (2 + len(groups) + dp_count),
        out_specs=[vmem(), vmem()],
        scratch_shapes=[
            pltpu.VMEM((block_count, BLK), jnp.float32),
            pltpu.VMEM((block_count, BLK, width), jnp.float32),
        ],
        compiler_params=params,
        name="grads",
    )(table, pos_blocks, all_stats, *kept, *rows)

    gathered = lax.all_to_all(parts, "label", split_axis=0, concat_axis=0, tiled=True)
    grads = jnp.sum(gathered.astype(jnp.float32), axis=0).astype(jnp.bfloat16)
    return loss.reshape(inst_count), grads


def solution(mesh):
    in_specs = (P("dp", None), P(("dp", "label"), None, None), P(), P(), P("dp", None))
    out_specs = (P("dp"), P("dp", "label"))
    return jax.shard_map(shards, mesh=mesh, in_specs=in_specs, out_specs=out_specs, check_vma=False)
```

```python
import functools

import jax
import jax.numpy as jnp
from jax import lax
from jax.experimental import pallas as pl
from jax.experimental.pallas import tpu as pltpu
from jax.sharding import PartitionSpec as P

BLK = 128
NEG_FILL = -1e30
VMEM_BYTES = 32 * 1024 * 1024
VMEM_PICK = 56 * 1024 * 1024


def divide(value, by):
    if by & (by - 1) == 0:
        return lax.shift_right_logical(value, jnp.int32(by.bit_length() - 1))
    return lax.div(value, jnp.int32(by))


def remainder(value, by):
    if by & (by - 1) == 0:
        return value & jnp.int32(by - 1)
    return lax.rem(value, jnp.int32(by))


def each_entry(count, short_count, body, carry):
    if count <= 64:
        for e in range(count):
            carry = body(e // short_count, e % short_count, carry)
        return carry
    step = lambda e, c: body(divide(e, short_count), remainder(e, short_count), c)
    return lax.fori_loop(0, count, step, carry)


def pick_kernel(sizes, lists_ref, slot_ref, weights_ref, table_ref, *rest):
    dp_count, lab_count, stored, block_count, short_count = sizes
    outs, held, sems = rest[:-2], rest[-2], rest[-1]
    dp_index, lab_index = lax.axis_index("dp"), lax.axis_index("label")
    mine = dp_index * lab_count + lab_index
    half = block_count // 2
    stage = pltpu.make_async_copy(weights_ref, held, sems.at[dp_count])
    stage.start()
    wanted = []
    for k in range(dp_count):
        base = (dp_index ^ k) * block_count

        def look(row, column, found, base=base):
            slot = slot_ref[lists_ref[base + row, column]]
            return jnp.where(divide(slot, stored) == mine, remainder(slot, stored), found)

        wanted.append(each_entry(half * short_count, short_count, look, jnp.int32(0)))
    stage.wait()
    copies = []
    for k, found in enumerate(wanted):
        copies.append(pltpu.make_async_copy(held.at[found], outs[k], sems.at[k]))
        copies[-1].start()

    for side in range(2):

        def note(row, column, carry, side=side):
            block = side * half + row
            cluster = lists_ref[dp_index * block_count + block, column]
            device = divide(slot_ref[cluster], stored)

            @pl.when(remainder(device, lab_count) == lab_index)
            def _():
                entry = divide(device, lab_count) ^ dp_index
                table_ref[entry, 0] = cluster
                table_ref[entry, 1 + side] = jnp.int32(block)

            return carry

        each_entry(half * short_count, short_count, note, jnp.int32(0))
    for copy in copies:
        copy.wait()


def target_of(pos_ref, block, first, cluster_size):
    labels = lax.broadcasted_iota(jnp.int32, (cluster_size, BLK), 0) + first
    pos = pos_ref[block]
    hit = pos[0:1, :] == labels
    for p in range(1, pos.shape[0]):
        hit = hit | (pos[p : p + 1, :] == labels)
    return hit


def logit_kernel(slots, copies, table_ref, feats_ref, pos_ref, *rest):
    count = len(slots)
    rows = rest[:count]
    stats_in = rest[count] if slots[0] else None
    logits_ref, out_ref, stats_ref = rest[-3:]
    cluster_size = rows[0].shape[0]
    if stats_in is None:
        stats_ref[0] = jnp.full(stats_ref.shape[1:], NEG_FILL, jnp.float32)
        stats_ref[1] = jnp.zeros(stats_ref.shape[1:], jnp.float32)
        stats_ref[2] = jnp.zeros(stats_ref.shape[1:], jnp.float32)
    else:
        stats_ref[...] = stats_in[0]
    for s, ref in zip(slots, rows):
        first = table_ref[s, 0] * cluster_size
        for side in range(2):
            block = table_ref[s, 1 + side]
            logits = lax.dot_general(
                ref[...],
                feats_ref[block],
                (((1,), (1,)), ((), ())),
                preferred_element_type=jnp.float32,
            )
            logits_ref[s - slots[0], :, side * BLK : (side + 1) * BLK] = logits
            hit = target_of(pos_ref, block, first, cluster_size)
            highest = jnp.max(logits, axis=0, keepdims=True)
            total = jnp.sum(jnp.exp(logits - highest), axis=0, keepdims=True)
            positive = jnp.sum(jnp.where(hit, logits, 0.0), axis=0, keepdims=True)
            row = pl.ds(block, 1)
            before = stats_ref[0, row, :]
            after = jnp.maximum(before, highest)
            stats_ref[0, row, :] = after
            stats_ref[1, row, :] = stats_ref[1, row, :] * jnp.exp(before - after) + total * jnp.exp(
                highest - after
            )
            stats_ref[2, row, :] = stats_ref[2, row, :] + positive
    for i in range(copies):
        out_ref[i] = stats_ref[...]


def row_sums(stats_ref, lab_count):
    highest = stats_ref[0, 0]
    for i in range(1, lab_count):
        highest = jnp.maximum(highest, stats_ref[i, 0])
    summed = jnp.zeros_like(highest)
    positive = jnp.zeros_like(highest)
    for i in range(lab_count):
        summed = summed + stats_ref[i, 1] * jnp.exp(stats_ref[i, 0] - highest)
        positive = positive + stats_ref[i, 2]
    return highest + jnp.log(summed), positive


def add_slot(side, s, table_ref, pos_ref, logits_ref, rows_ref, lse_ref, total_ref, first_block):
    cluster_size = rows_ref.shape[0]
    pos_count = pos_ref.shape[1]
    block = table_ref[s, 1 + side]
    hit = target_of(pos_ref, block, table_ref[s, 0] * cluster_size, cluster_size)
    dlogit = jnp.exp(
        logits_ref[:, side * BLK : (side + 1) * BLK] - lse_ref[pl.ds(block, 1), :]
    ) - jnp.where(hit, 1.0 / pos_count, 0.0)
    total_ref[block - first_block] += lax.dot_general(
        dlogit.T.astype(jnp.bfloat16),
        rows_ref[...],
        (((1,), (0,)), ((), ())),
        preferred_element_type=jnp.float32,
    )


def half_kernel(side, groups, lab_count, table_ref, pos_ref, stats_ref, *rest):
    dp_count = groups[-1][-1] + 1
    logits_refs = rest[: len(groups)]
    rows = rest[len(groups) : len(groups) + dp_count]
    loss_ref, keep_ref, send_ref, lse_ref, total_ref = rest[len(groups) + dp_count :]
    lse, positive = row_sums(stats_ref, lab_count)
    lse_ref[...] = lse
    loss_ref[...] = lse - positive / pos_ref.shape[1]
    total_ref[...] = jnp.zeros_like(total_ref)
    half = total_ref.shape[0]
    for slots, logits_ref in zip(groups, logits_refs):
        for s in slots:
            add_slot(
                side,
                s,
                table_ref,
                pos_ref,
                logits_ref.at[s - slots[0]],
                rows[s],
                lse_ref,
                total_ref,
                side * half,
            )
    part = keep_ref.shape[2]
    lab_index = lax.axis_index("label")
    for j in range(lab_count // 2):
        mine = pl.ds(pl.multiple_of((lab_index ^ (2 * j)) * part, part), part)
        other = pl.ds(pl.multiple_of((lab_index ^ (2 * j + 1)) * part, part), part)
        for b in range(half):
            here = pl.ds(b * BLK, BLK)
            keep_ref[j, here, :] = total_ref[b, :, mine]
            send_ref[j, here, :] = total_ref[b, :, other].astype(jnp.bfloat16)


def pair_kernel(keep_ref, got_ref, *outs):
    outs[0][...] = keep_ref[0] + got_ref[0].astype(jnp.float32)
    for j in range(1, len(outs)):
        outs[j][...] = (keep_ref[j] + got_ref[j].astype(jnp.float32)).astype(jnp.bfloat16)


def last_kernel(count, *refs):
    out_ref = refs[-1]
    for h in range(len(refs[:-1]) // count):
        total = refs[h * count][...]
        for ref in refs[h * count + 1 : (h + 1) * count]:
            total = total + ref[...].astype(jnp.float32)
        rows = total.shape[0]
        out_ref[h * rows : (h + 1) * rows, :] = total.astype(jnp.bfloat16)


def grad_kernel(groups, lab_count, table_ref, pos_ref, stats_ref, *rest):
    dp_count = groups[-1][-1] + 1
    logits_refs = rest[: len(groups)]
    rows = rest[len(groups) : len(groups) + dp_count]
    loss_ref, out_ref, lse_ref, total_ref = rest[len(groups) + dp_count :]
    lse, positive = row_sums(stats_ref, lab_count)
    lse_ref[...] = lse
    loss_ref[...] = lse - positive / pos_ref.shape[1]
    total_ref[...] = jnp.zeros_like(total_ref)
    for slots, logits_ref in zip(groups, logits_refs):
        for s in slots:

            @pl.when(table_ref[s, 0] >= 0)
            def _(s=s, logits_ref=logits_ref.at[s - slots[0]]):
                for side in range(2):
                    add_slot(
                        side, s, table_ref, pos_ref, logits_ref, rows[s], lse_ref, total_ref, 0
                    )

    part = out_ref.shape[2]
    for j in range(lab_count):
        for b in range(total_ref.shape[0]):
            out_ref[j, b * BLK : (b + 1) * BLK, :] = total_ref[
                b, :, j * part : (j + 1) * part
            ].astype(jnp.bfloat16)


def smem():
    return pl.BlockSpec(memory_space=pltpu.SMEM)


def vmem():
    return pl.BlockSpec(memory_space=pltpu.VMEM)


def anywhere():
    return pl.BlockSpec(memory_space=pl.ANY)


def shards(feats, weights, shortlist, slot_of, positives):
    dp_count = lax.axis_size("dp")
    lab_count = lax.axis_size("label")
    stored, cluster_size, width = weights.shape
    inst_count = feats.shape[0]
    pos_count = positives.shape[1]
    block_count = inst_count // BLK
    short_count = shortlist.shape[1]
    params = pltpu.CompilerParams(vmem_limit_bytes=VMEM_BYTES)
    row_type = jax.ShapeDtypeStruct((cluster_size, width), weights.dtype)
    stat_shape = (3, block_count, BLK)

    table, *rows = pl.pallas_call(
        functools.partial(
            pick_kernel, (dp_count, lab_count, stored, block_count, short_count)
        ),
        out_shape=[jax.ShapeDtypeStruct((dp_count, 4), jnp.int32)] + [row_type] * dp_count,
        in_specs=[smem(), smem(), anywhere()],
        out_specs=[smem()] + [anywhere()] * dp_count,
        scratch_shapes=[
            pltpu.VMEM(weights.shape, weights.dtype),
            pltpu.SemaphoreType.DMA((dp_count + 1,)),
        ],
        compiler_params=pltpu.CompilerParams(vmem_limit_bytes=VMEM_PICK),
        name="pick",
    )(shortlist, slot_of, weights)
    for k in range(1, dp_count):
        rows[k] = lax.ppermute(rows[k], "dp", [(i, i ^ k) for i in range(dp_count)])

    feat_blocks = feats.reshape(block_count, BLK, width)
    pos_blocks = positives.reshape(block_count, BLK, pos_count).transpose(0, 2, 1)
    cuts = (0, dp_count // 2, dp_count * 3 // 4, dp_count)
    groups = [tuple(range(a, b)) for a, b in zip(cuts[:-1], cuts[1:])]
    kept = []
    stats = []
    for slots in groups:
        count = len(slots)
        copies = lab_count if slots is groups[-1] else 1
        logits, stats_out = pl.pallas_call(
            functools.partial(logit_kernel, slots, copies),
            out_shape=[
                jax.ShapeDtypeStruct((count, cluster_size, 2 * BLK), jnp.float32),
                jax.ShapeDtypeStruct((copies,) + stat_shape, jnp.float32),
            ],
            in_specs=[smem()] + [vmem()] * (2 + count + len(stats)),
            out_specs=[vmem(), vmem()],
            scratch_shapes=[pltpu.VMEM(stat_shape, jnp.float32)],
            compiler_params=params,
            cost_estimate=pl.CostEstimate(
                flops=count * 4 * BLK * cluster_size * width,
                bytes_accessed=count * cluster_size * width * 2,
                transcendentals=0,
            ),
            name="logits",
        )(table, feat_blocks, pos_blocks, *[rows[s] for s in slots], *stats)
        kept.append(logits)
        stats = [stats_out]

    all_stats = lax.all_to_all(stats[0], "label", split_axis=0, concat_axis=0, tiled=True)
    part = width // lab_count
    in_specs = [smem()] + [vmem()] * (2 + len(groups) + dp_count)
    operands = (table, pos_blocks, all_stats, *kept, *rows)
    loss_type = jax.ShapeDtypeStruct((block_count, BLK), jnp.float32)
    lse_scratch = pltpu.VMEM((block_count, BLK), jnp.float32)
    if part % 128 or lab_count % 2:
        loss, parts = pl.pallas_call(
            functools.partial(grad_kernel, groups, lab_count),
            out_shape=[
                loss_type,
                jax.ShapeDtypeStruct((lab_count, inst_count, part), jnp.bfloat16),
            ],
            in_specs=in_specs,
            out_specs=[vmem(), vmem()],
            scratch_shapes=[lse_scratch, pltpu.VMEM((block_count, BLK, width), jnp.float32)],
            compiler_params=params,
            name="grads",
        )(*operands)
        gathered = lax.all_to_all(parts, "label", split_axis=0, concat_axis=0, tiled=True)
        grads = jnp.sum(gathered.astype(jnp.float32), axis=0).astype(jnp.bfloat16)
        return loss.reshape(inst_count), grads

    pairs = lab_count // 2
    half_rows = inst_count // 2
    finals = []
    for side in range(2):
        loss, keep, send = pl.pallas_call(
            functools.partial(half_kernel, side, groups, lab_count),
            out_shape=[
                loss_type,
                jax.ShapeDtypeStruct((pairs, half_rows, part), jnp.float32),
                jax.ShapeDtypeStruct((pairs, half_rows, part), jnp.bfloat16),
            ],
            in_specs=in_specs,
            out_specs=[vmem()] * 3,
            scratch_shapes=[lse_scratch, pltpu.VMEM((block_count // 2, BLK, width), jnp.float32)],
            compiler_params=params,
            cost_estimate=pl.CostEstimate(
                flops=dp_count * 2 * BLK * cluster_size * width,
                bytes_accessed=dp_count * cluster_size * width * 2,
                transcendentals=0,
            ),
            name="grads",
        )(*operands)
        got = lax.ppermute(send, "label", [(i, i ^ 1) for i in range(lab_count)])
        own, *outgoing = pl.pallas_call(
            pair_kernel,
            out_shape=[jax.ShapeDtypeStruct((half_rows, part), jnp.float32)]
            + [jax.ShapeDtypeStruct((half_rows, part), jnp.bfloat16)] * (pairs - 1),
            in_specs=[vmem()] * 2,
            out_specs=[vmem()] * pairs,
            compiler_params=params,
            name="pair_sums",
        )(keep, got)
        finals.append(own)
        for j in range(1, pairs):
            hop = [(i, i ^ (2 * j)) for i in range(lab_count)]
            finals.append(lax.ppermute(outgoing[j - 1], "label", hop))
    grads = pl.pallas_call(
        functools.partial(last_kernel, pairs),
        out_shape=jax.ShapeDtypeStruct((inst_count, part), jnp.bfloat16),
        in_specs=[vmem()] * (2 * pairs),
        out_specs=vmem(),
        compiler_params=params,
        name="last_sums",
    )(*finals)
    return loss.reshape(inst_count), grads


def solution(mesh):
    in_specs = (P("dp", None), P(("dp", "label"), None, None), P(), P(), P("dp", None))
    out_specs = (P("dp"), P("dp", "label"))
    return jax.shard_map(shards, mesh=mesh, in_specs=in_specs, out_specs=out_specs, check_vma=False)
```

```python
import functools

import jax
import jax.numpy as jnp
from jax import lax
from jax.experimental import pallas as pl
from jax.experimental.pallas import tpu as pltpu
from jax.sharding import PartitionSpec as P

BLK = 128
NEG_FILL = -1e30
VMEM_BYTES = 32 * 1024 * 1024
VMEM_PICK = 56 * 1024 * 1024


def divide(value, by):
    if by & (by - 1) == 0:
        return lax.shift_right_logical(value, jnp.int32(by.bit_length() - 1))
    return lax.div(value, jnp.int32(by))


def remainder(value, by):
    if by & (by - 1) == 0:
        return value & jnp.int32(by - 1)
    return lax.rem(value, jnp.int32(by))


def each_entry(count, short_count, body, carry):
    if count <= 64:
        for e in range(count):
            carry = body(e // short_count, e % short_count, carry)
        return carry
    step = lambda e, c: body(divide(e, short_count), remainder(e, short_count), c)
    return lax.fori_loop(0, count, step, carry)


def find_slots(sizes, wanted, lists_ref, slot_ref):
    lab_count, stored, block_count, short_count = sizes
    dp_index, lab_index = lax.axis_index("dp"), lax.axis_index("label")
    mine = dp_index * lab_count + lab_index
    found = []
    for k in wanted:
        base = (dp_index ^ k) * block_count

        def look(row, column, slot_here, base=base):
            slot = slot_ref[lists_ref[base + row, column]]
            return jnp.where(divide(slot, stored) == mine, remainder(slot, stored), slot_here)

        count = block_count // 2 * short_count
        found.append(each_entry(count, short_count, look, jnp.int32(0)))
    return found


def far_kernel(sizes, wanted, lists_hbm, slot_hbm, weights_ref, *rest):
    outs = rest[: len(wanted)]
    held, lists_ref, slot_ref, sems = rest[len(wanted) :]
    tables = [
        pltpu.make_async_copy(lists_hbm, lists_ref, sems.at[0]),
        pltpu.make_async_copy(slot_hbm, slot_ref, sems.at[1]),
    ]
    stage = pltpu.make_async_copy(weights_ref, held, sems.at[2])
    for copy in tables:
        copy.start()
    stage.start()
    for copy in tables:
        copy.wait()
    found = find_slots(sizes, wanted, lists_ref, slot_ref)
    stage.wait()
    copies = []
    for i, slot in enumerate(found):
        copies.append(pltpu.make_async_copy(held.at[slot], outs[i], sems.at[3 + i]))
        copies[-1].start()
    for copy in copies:
        copy.wait()


def near_kernel(sizes, lists_ref, slot_ref, weights_ref, after_ref, table_ref, *rest):
    lab_count, stored, block_count, short_count = sizes
    outs, sems = rest[:-1], rest[-1]
    copies = []
    for k, slot in enumerate(find_slots(sizes, range(2), lists_ref, slot_ref)):
        copies.append(pltpu.make_async_copy(weights_ref.at[slot], outs[k], sems.at[k]))
        copies[-1].start()
    dp_index, lab_index = lax.axis_index("dp"), lax.axis_index("label")
    half = block_count // 2
    for side in range(2):

        def note(row, column, carry, side=side):
            block = side * half + row
            cluster = lists_ref[dp_index * block_count + block, column]
            device = divide(slot_ref[cluster], stored)

            @pl.when(remainder(device, lab_count) == lab_index)
            def _():
                entry = divide(device, lab_count) ^ dp_index
                table_ref[entry, 0] = cluster
                table_ref[entry, 1 + side] = jnp.int32(block)

            return carry

        each_entry(half * short_count, short_count, note, jnp.int32(0))
    for copy in copies:
        copy.wait()


def target_of(pos_ref, block, first, cluster_size):
    labels = lax.broadcasted_iota(jnp.int32, (cluster_size, BLK), 0) + first
    pos = pos_ref[block]
    hit = pos[0:1, :] == labels
    for p in range(1, pos.shape[0]):
        hit = hit | (pos[p : p + 1, :] == labels)
    return hit


def logit_kernel(slots, table_ref, feats_ref, pos_ref, *rest):
    count = len(slots)
    rows = rest[:count]
    stats_in = rest[count] if slots[0] else None
    logits_ref, stats_ref = rest[-2:]
    cluster_size = rows[0].shape[0]
    if stats_in is None:
        stats_ref[0] = jnp.full(stats_ref.shape[1:], NEG_FILL, jnp.float32)
        stats_ref[1] = jnp.zeros(stats_ref.shape[1:], jnp.float32)
        stats_ref[2] = jnp.zeros(stats_ref.shape[1:], jnp.float32)
    else:
        stats_ref[...] = stats_in[...]
    for s, ref in zip(slots, rows):
        first = table_ref[s, 0] * cluster_size
        for side in range(2):
            block = table_ref[s, 1 + side]
            logits = lax.dot_general(
                ref[...],
                feats_ref[block],
                (((1,), (1,)), ((), ())),
                preferred_element_type=jnp.float32,
            )
            logits_ref[s - slots[0], :, side * BLK : (side + 1) * BLK] = logits
            hit = target_of(pos_ref, block, first, cluster_size)
            highest = jnp.max(logits, axis=0, keepdims=True)
            total = jnp.sum(jnp.exp(logits - highest), axis=0, keepdims=True)
            positive = jnp.sum(jnp.where(hit, logits, 0.0), axis=0, keepdims=True)
            row = pl.ds(block, 1)
            before = stats_ref[0, row, :]
            after = jnp.maximum(before, highest)
            stats_ref[0, row, :] = after
            stats_ref[1, row, :] = stats_ref[1, row, :] * jnp.exp(before - after) + total * jnp.exp(
                highest - after
            )
            stats_ref[2, row, :] = stats_ref[2, row, :] + positive


def merged(refs):
    highest = refs[0][0]
    for ref in refs[1:]:
        highest = jnp.maximum(highest, ref[0])
    summed = jnp.zeros_like(highest)
    positive = jnp.zeros_like(highest)
    for ref in refs:
        summed = summed + ref[1] * jnp.exp(ref[0] - highest)
        positive = positive + ref[2]
    return highest, summed, positive


def merge_kernel(own_ref, got_ref, out_ref):
    for i, value in enumerate(merged((own_ref, got_ref))):
        out_ref[i] = value


def row_sums(stats_refs):
    highest, summed, positive = merged(stats_refs)
    return highest + jnp.log(summed), positive


def add_slot(side, s, table_ref, pos_ref, logits_ref, rows_ref, lse_ref, total_ref, first_block):
    cluster_size = rows_ref.shape[0]
    pos_count = pos_ref.shape[1]
    block = table_ref[s, 1 + side]
    hit = target_of(pos_ref, block, table_ref[s, 0] * cluster_size, cluster_size)
    dlogit = jnp.exp(
        logits_ref[:, side * BLK : (side + 1) * BLK] - lse_ref[pl.ds(block, 1), :]
    ) - jnp.where(hit, 1.0 / pos_count, 0.0)
    total_ref[block - first_block] += lax.dot_general(
        dlogit.T.astype(jnp.bfloat16),
        rows_ref[...],
        (((1,), (0,)), ((), ())),
        preferred_element_type=jnp.float32,
    )


def half_kernel(side, groups, lab_count, mask, table_ref, pos_ref, *rest):
    dp_count = groups[-1][-1] + 1
    stats_refs, rest = rest[: lab_count // 2], rest[lab_count // 2 :]
    logits_refs = rest[: len(groups)]
    rows = rest[len(groups) : len(groups) + dp_count]
    loss_ref, keep_ref, send_ref, lse_ref, total_ref = rest[len(groups) + dp_count :]
    lse, positive = row_sums(stats_refs)
    lse_ref[...] = lse
    loss_ref[...] = lse - positive / pos_ref.shape[1]
    total_ref[...] = jnp.zeros_like(total_ref)
    half = total_ref.shape[0]
    for slots, logits_ref in zip(groups, logits_refs):
        for s in slots:
            add_slot(
                side,
                s,
                table_ref,
                pos_ref,
                logits_ref.at[s - slots[0]],
                rows[s],
                lse_ref,
                total_ref,
                side * half,
            )
    part = keep_ref.shape[2]
    lab_index = lax.axis_index("label")
    for i, offset in enumerate(o for o in range(lab_count) if not o & mask):
        mine = pl.ds(pl.multiple_of((lab_index ^ offset) * part, part), part)
        other = pl.ds(pl.multiple_of((lab_index ^ (offset | mask)) * part, part), part)
        for b in range(half):
            here = pl.ds(b * BLK, BLK)
            keep_ref[i, here, :] = total_ref[b, :, mine]
            send_ref[i, here, :] = total_ref[b, :, other].astype(jnp.bfloat16)


def step_kernel(kept, sent, keep_ref, got_ref, next_ref, send_ref):
    for i, at in enumerate(kept):
        next_ref[i] = keep_ref[at] + got_ref[at].astype(jnp.float32)
    for i, at in enumerate(sent):
        send_ref[i] = (keep_ref[at] + got_ref[at].astype(jnp.float32)).astype(jnp.bfloat16)


def last_kernel(*refs):
    out_ref = refs[-1]
    for h in range(len(refs) // 2):
        total = refs[2 * h][0] + refs[2 * h + 1][0].astype(jnp.float32)
        rows = total.shape[0]
        out_ref[h * rows : (h + 1) * rows, :] = total.astype(jnp.bfloat16)


def grad_kernel(groups, lab_count, table_ref, pos_ref, *rest):
    dp_count = groups[-1][-1] + 1
    stats_refs, rest = rest[: lab_count // 2], rest[lab_count // 2 :]
    logits_refs = rest[: len(groups)]
    rows = rest[len(groups) : len(groups) + dp_count]
    loss_ref, out_ref, lse_ref, total_ref = rest[len(groups) + dp_count :]
    lse, positive = row_sums(stats_refs)
    lse_ref[...] = lse
    loss_ref[...] = lse - positive / pos_ref.shape[1]
    total_ref[...] = jnp.zeros_like(total_ref)
    for slots, logits_ref in zip(groups, logits_refs):
        for s in slots:

            @pl.when(table_ref[s, 0] >= 0)
            def _(s=s, logits_ref=logits_ref.at[s - slots[0]]):
                for side in range(2):
                    add_slot(
                        side, s, table_ref, pos_ref, logits_ref, rows[s], lse_ref, total_ref, 0
                    )

    part = out_ref.shape[2]
    for j in range(lab_count):
        for b in range(total_ref.shape[0]):
            out_ref[j, b * BLK : (b + 1) * BLK, :] = total_ref[
                b, :, j * part : (j + 1) * part
            ].astype(jnp.bfloat16)


def smem():
    return pl.BlockSpec(memory_space=pltpu.SMEM)


def vmem():
    return pl.BlockSpec(memory_space=pltpu.VMEM)


def anywhere():
    return pl.BlockSpec(memory_space=pl.ANY)


def shards(feats, weights, shortlist, slot_of, positives):
    dp_count = lax.axis_size("dp")
    lab_count = lax.axis_size("label")
    stored, cluster_size, width = weights.shape
    inst_count = feats.shape[0]
    pos_count = positives.shape[1]
    block_count = inst_count // BLK
    short_count = shortlist.shape[1]
    params = pltpu.CompilerParams(vmem_limit_bytes=VMEM_BYTES)
    row_type = jax.ShapeDtypeStruct((cluster_size, width), weights.dtype)
    stat_shape = (3, block_count, BLK)

    sizes = (lab_count, stored, block_count, short_count)
    far = range(2, dp_count)
    far_rows = pl.pallas_call(
        functools.partial(far_kernel, sizes, far),
        out_shape=[row_type] * len(far),
        in_specs=[anywhere()] * 3,
        out_specs=[anywhere()] * len(far),
        scratch_shapes=[
            pltpu.VMEM(weights.shape, weights.dtype),
            pltpu.SMEM(shortlist.shape, jnp.int32),
            pltpu.SMEM(slot_of.shape, jnp.int32),
            pltpu.SemaphoreType.DMA((3 + len(far),)),
        ],
        compiler_params=pltpu.CompilerParams(vmem_limit_bytes=VMEM_PICK),
        name="pick_far",
    )(shortlist, slot_of, weights)
    table, *rows = pl.pallas_call(
        functools.partial(near_kernel, sizes),
        out_shape=[jax.ShapeDtypeStruct((dp_count, 4), jnp.int32)] + [row_type] * 2,
        in_specs=[smem(), smem(), anywhere(), anywhere()],
        out_specs=[smem()] + [vmem()] * 2,
        scratch_shapes=[pltpu.SemaphoreType.DMA((2,))],
        compiler_params=params,
        name="pick_near",
    )(shortlist, slot_of, weights, far_rows[0])
    rows += far_rows
    for k in range(1, dp_count):
        rows[k] = lax.ppermute(rows[k], "dp", [(i, i ^ k) for i in range(dp_count)])

    feat_blocks = feats.reshape(block_count, BLK, width)
    pos_blocks = positives.reshape(block_count, BLK, pos_count).transpose(0, 2, 1)
    cuts = (0, dp_count // 2, dp_count * 3 // 4, dp_count)
    groups = [tuple(range(a, b)) for a, b in zip(cuts[:-1], cuts[1:])]
    kept = []
    stats = []
    for slots in groups:
        count = len(slots)
        logits, stats_out = pl.pallas_call(
            functools.partial(logit_kernel, slots),
            out_shape=[
                jax.ShapeDtypeStruct((count, cluster_size, 2 * BLK), jnp.float32),
                jax.ShapeDtypeStruct(stat_shape, jnp.float32),
            ],
            in_specs=[smem()] + [vmem()] * (2 + count + len(stats)),
            out_specs=[vmem(), vmem()],
            compiler_params=params,
            cost_estimate=pl.CostEstimate(
                flops=count * 4 * BLK * cluster_size * width,
                bytes_accessed=count * cluster_size * width * 2,
                transcendentals=0,
            ),
            name="logits",
        )(table, feat_blocks, pos_blocks, *[rows[s] for s in slots], *stats)
        kept.append(logits)
        stats = [stats_out]

    got = lax.ppermute(stats[0], "label", [(i, i ^ 1) for i in range(lab_count)])
    pair_stats = pl.pallas_call(
        merge_kernel,
        out_shape=jax.ShapeDtypeStruct(stat_shape, jnp.float32),
        in_specs=[vmem()] * 2,
        out_specs=vmem(),
        compiler_params=params,
        name="merge_stats",
    )(stats[0], got)
    all_stats = [pair_stats] + [
        lax.ppermute(pair_stats, "label", [(i, i ^ (2 * j)) for i in range(lab_count)])
        for j in range(1, lab_count // 2)
    ]
    part = width // lab_count
    in_specs = [smem()] + [vmem()] * (1 + len(all_stats) + len(groups) + dp_count)
    operands = (table, pos_blocks, *all_stats, *kept, *rows)
    loss_type = jax.ShapeDtypeStruct((block_count, BLK), jnp.float32)
    lse_scratch = pltpu.VMEM((block_count, BLK), jnp.float32)
    if part % 128 or lab_count % 2:
        loss, parts = pl.pallas_call(
            functools.partial(grad_kernel, groups, lab_count),
            out_shape=[
                loss_type,
                jax.ShapeDtypeStruct((lab_count, inst_count, part), jnp.bfloat16),
            ],
            in_specs=in_specs,
            out_specs=[vmem(), vmem()],
            scratch_shapes=[lse_scratch, pltpu.VMEM((block_count, BLK, width), jnp.float32)],
            compiler_params=params,
            name="grads",
        )(*operands)
        gathered = lax.all_to_all(parts, "label", split_axis=0, concat_axis=0, tiled=True)
        grads = jnp.sum(gathered.astype(jnp.float32), axis=0).astype(jnp.bfloat16)
        return loss.reshape(inst_count), grads

    half_rows = inst_count // 2
    masks = [1 << i for i in range(lab_count.bit_length() - 1)]
    finals = []
    for side in range(2):
        order = masks if side == 0 else masks[1::-1] + masks[2:]
        count = lab_count // 2
        loss, keep, send = pl.pallas_call(
            functools.partial(half_kernel, side, groups, lab_count, order[0]),
            out_shape=[
                loss_type,
                jax.ShapeDtypeStruct((count, half_rows, part), jnp.float32),
                jax.ShapeDtypeStruct((count, half_rows, part), jnp.bfloat16),
            ],
            in_specs=in_specs,
            out_specs=[vmem()] * 3,
            scratch_shapes=[lse_scratch, pltpu.VMEM((block_count // 2, BLK, width), jnp.float32)],
            compiler_params=params,
            cost_estimate=pl.CostEstimate(
                flops=dp_count * 2 * BLK * cluster_size * width,
                bytes_accessed=dp_count * cluster_size * width * 2,
                transcendentals=0,
            ),
            name="grads",
        )(*operands)
        offsets = [o for o in range(lab_count) if not o & order[0]]
        got = lax.ppermute(send, "label", [(i, i ^ order[0]) for i in range(lab_count)])
        for mask in order[1:]:
            kept_at = [i for i, o in enumerate(offsets) if not o & mask]
            sent_at = [offsets.index(offsets[i] | mask) for i in kept_at]
            offsets = [offsets[i] for i in kept_at]
            count = count // 2
            keep, send = pl.pallas_call(
                functools.partial(step_kernel, kept_at, sent_at),
                out_shape=[
                    jax.ShapeDtypeStruct((count, half_rows, part), jnp.float32),
                    jax.ShapeDtypeStruct((count, half_rows, part), jnp.bfloat16),
                ],
                in_specs=[vmem()] * 2,
                out_specs=[vmem()] * 2,
                compiler_params=params,
                name="step_sums",
            )(keep, got)
            got = lax.ppermute(send, "label", [(i, i ^ mask) for i in range(lab_count)])
        finals += [keep, got]
    grads = pl.pallas_call(
        last_kernel,
        out_shape=jax.ShapeDtypeStruct((inst_count, part), jnp.bfloat16),
        in_specs=[vmem()] * len(finals),
        out_specs=vmem(),
        compiler_params=params,
        name="last_sums",
    )(*finals)
    return loss.reshape(inst_count), grads


def solution(mesh):
    in_specs = (P("dp", None), P(("dp", "label"), None, None), P(), P(), P("dp", None))
    out_specs = (P("dp"), P("dp", "label"))
    return jax.shard_map(shards, mesh=mesh, in_specs=in_specs, out_specs=out_specs, check_vma=False)
```

```python
import functools

import jax
import jax.numpy as jnp
from jax import lax
from jax.experimental import pallas as pl
from jax.experimental.pallas import tpu as pltpu
from jax.sharding import PartitionSpec as P

BLK = 128
NEG_FILL = -1e30
VMEM_BYTES = 32 * 1024 * 1024
VMEM_PICK = 56 * 1024 * 1024


def divide(value, by):
    if by & (by - 1) == 0:
        return lax.shift_right_logical(value, jnp.int32(by.bit_length() - 1))
    return lax.div(value, jnp.int32(by))


def remainder(value, by):
    if by & (by - 1) == 0:
        return value & jnp.int32(by - 1)
    return lax.rem(value, jnp.int32(by))


def each_entry(count, short_count, body, carry):
    if count <= 64:
        for e in range(count):
            carry = body(e // short_count, e % short_count, carry)
        return carry
    step = lambda e, c: body(divide(e, short_count), remainder(e, short_count), c)
    return lax.fori_loop(0, count, step, carry)


def find_slots(sizes, wanted, lists_ref, slot_ref):
    lab_count, stored, block_count, short_count = sizes
    dp_index, lab_index = lax.axis_index("dp"), lax.axis_index("label")
    mine = dp_index * lab_count + lab_index
    found = []
    for k in wanted:
        base = (dp_index ^ k) * block_count

        def look(row, column, slot_here, base=base):
            slot = slot_ref[lists_ref[base + row, column]]
            return jnp.where(divide(slot, stored) == mine, remainder(slot, stored), slot_here)

        count = block_count // 2 * short_count
        found.append(each_entry(count, short_count, look, jnp.int32(0)))
    return found


def far_kernel(sizes, wanted, lists_hbm, slot_hbm, weights_ref, *rest):
    outs = rest[: len(wanted)]
    held, lists_ref, slot_ref, sems = rest[len(wanted) :]
    tables = [
        pltpu.make_async_copy(lists_hbm, lists_ref, sems.at[0]),
        pltpu.make_async_copy(slot_hbm, slot_ref, sems.at[1]),
    ]
    stage = pltpu.make_async_copy(weights_ref, held, sems.at[2])
    for copy in tables:
        copy.start()
    stage.start()
    for copy in tables:
        copy.wait()
    found = find_slots(sizes, wanted, lists_ref, slot_ref)
    stage.wait()
    copies = []
    for i, slot in enumerate(found):
        copies.append(pltpu.make_async_copy(held.at[slot], outs[i], sems.at[3 + i]))
        copies[-1].start()
    for copy in copies:
        copy.wait()


def near_kernel(sizes, lists_ref, slot_ref, weights_ref, table_ref, *rest):
    lab_count, stored, block_count, short_count = sizes
    outs, sems = rest[:-1], rest[-1]
    copies = []
    for k, slot in enumerate(find_slots(sizes, range(1), lists_ref, slot_ref)):
        copies.append(pltpu.make_async_copy(weights_ref.at[slot], outs[k], sems.at[k]))
        copies[-1].start()
    dp_index, lab_index = lax.axis_index("dp"), lax.axis_index("label")
    half = block_count // 2
    for side in range(2):

        def note(row, column, carry, side=side):
            block = side * half + row
            cluster = lists_ref[dp_index * block_count + block, column]
            device = divide(slot_ref[cluster], stored)

            @pl.when(remainder(device, lab_count) == lab_index)
            def _():
                entry = divide(device, lab_count) ^ dp_index
                table_ref[entry, 0] = cluster
                table_ref[entry, 1 + side] = jnp.int32(block)

            return carry

        each_entry(half * short_count, short_count, note, jnp.int32(0))
    for copy in copies:
        copy.wait()


def target_of(pos_ref, block, first, cluster_size):
    labels = lax.broadcasted_iota(jnp.int32, (cluster_size, BLK), 0) + first
    pos = pos_ref[block]
    hit = pos[0:1, :] == labels
    for p in range(1, pos.shape[0]):
        hit = hit | (pos[p : p + 1, :] == labels)
    return hit


def logit_kernel(slots, copies, table_ref, feats_ref, pos_ref, *rest):
    count = len(slots)
    rows = rest[:count]
    stats_in = rest[count] if slots[0] else None
    logits_ref, out_ref, stats_ref = rest[-3:]
    cluster_size = rows[0].shape[0]
    if stats_in is None:
        stats_ref[0] = jnp.full(stats_ref.shape[1:], NEG_FILL, jnp.float32)
        stats_ref[1] = jnp.zeros(stats_ref.shape[1:], jnp.float32)
        stats_ref[2] = jnp.zeros(stats_ref.shape[1:], jnp.float32)
    else:
        stats_ref[...] = stats_in[0]
    for s, ref in zip(slots, rows):
        first = table_ref[s, 0] * cluster_size
        for side in range(2):
            block = table_ref[s, 1 + side]
            logits = lax.dot_general(
                ref[...],
                feats_ref[block],
                (((1,), (1,)), ((), ())),
                preferred_element_type=jnp.float32,
            )
            logits_ref[s - slots[0], :, side * BLK : (side + 1) * BLK] = logits
            hit = target_of(pos_ref, block, first, cluster_size)
            highest = jnp.max(logits, axis=0, keepdims=True)
            total = jnp.sum(jnp.exp(logits - highest), axis=0, keepdims=True)
            positive = jnp.sum(jnp.where(hit, logits, 0.0), axis=0, keepdims=True)
            row = pl.ds(block, 1)
            before = stats_ref[0, row, :]
            after = jnp.maximum(before, highest)
            stats_ref[0, row, :] = after
            stats_ref[1, row, :] = stats_ref[1, row, :] * jnp.exp(before - after) + total * jnp.exp(
                highest - after
            )
            stats_ref[2, row, :] = stats_ref[2, row, :] + positive
    for i in range(copies):
        out_ref[i] = stats_ref[...]


def row_sums(stats_ref, lab_count):
    highest = stats_ref[0, 0]
    for i in range(1, lab_count):
        highest = jnp.maximum(highest, stats_ref[i, 0])
    summed = jnp.zeros_like(highest)
    positive = jnp.zeros_like(highest)
    for i in range(lab_count):
        summed = summed + stats_ref[i, 1] * jnp.exp(stats_ref[i, 0] - highest)
        positive = positive + stats_ref[i, 2]
    return highest + jnp.log(summed), positive


def add_slot(side, s, table_ref, pos_ref, logits_ref, rows_ref, lse_ref, total_ref, first_block):
    cluster_size = rows_ref.shape[0]
    pos_count = pos_ref.shape[1]
    block = table_ref[s, 1 + side]
    hit = target_of(pos_ref, block, table_ref[s, 0] * cluster_size, cluster_size)
    dlogit = jnp.exp(
        logits_ref[:, side * BLK : (side + 1) * BLK] - lse_ref[pl.ds(block, 1), :]
    ) - jnp.where(hit, 1.0 / pos_count, 0.0)
    total_ref[block - first_block] += lax.dot_general(
        dlogit.T.astype(jnp.bfloat16),
        rows_ref[...],
        (((1,), (0,)), ((), ())),
        preferred_element_type=jnp.float32,
    )


def half_kernel(side, groups, lab_count, table_ref, pos_ref, stats_ref, *rest):
    dp_count = groups[-1][-1] + 1
    logits_refs = rest[: len(groups)]
    rows = rest[len(groups) : len(groups) + dp_count]
    loss_ref, keep_ref, send_ref, lse_ref, total_ref = rest[len(groups) + dp_count :]
    lse, positive = row_sums(stats_ref, lab_count)
    lse_ref[...] = lse
    loss_ref[...] = lse - positive / pos_ref.shape[1]
    total_ref[...] = jnp.zeros_like(total_ref)
    half = total_ref.shape[0]
    for slots, logits_ref in zip(groups, logits_refs):
        for s in slots:
            add_slot(
                side,
                s,
                table_ref,
                pos_ref,
                logits_ref.at[s - slots[0]],
                rows[s],
                lse_ref,
                total_ref,
                side * half,
            )
    part = keep_ref.shape[2]
    lab_index = lax.axis_index("label")
    for j in range(lab_count // 2):
        mine = pl.ds(pl.multiple_of((lab_index ^ (2 * j)) * part, part), part)
        other = pl.ds(pl.multiple_of((lab_index ^ (2 * j + 1)) * part, part), part)
        for b in range(half):
            here = pl.ds(b * BLK, BLK)
            keep_ref[j, here, :] = total_ref[b, :, mine]
            send_ref[j, here, :] = total_ref[b, :, other].astype(jnp.bfloat16)


def pair_kernel(keep_ref, got_ref, *outs):
    outs[0][...] = keep_ref[0] + got_ref[0].astype(jnp.float32)
    for j in range(1, len(outs)):
        outs[j][...] = (keep_ref[j] + got_ref[j].astype(jnp.float32)).astype(jnp.bfloat16)


def last_kernel(count, *refs):
    out_ref = refs[-1]
    for h in range(len(refs[:-1]) // count):
        total = refs[h * count][...]
        for ref in refs[h * count + 1 : (h + 1) * count]:
            total = total + ref[...].astype(jnp.float32)
        rows = total.shape[0]
        out_ref[h * rows : (h + 1) * rows, :] = total.astype(jnp.bfloat16)


def grad_kernel(groups, lab_count, table_ref, pos_ref, stats_ref, *rest):
    dp_count = groups[-1][-1] + 1
    logits_refs = rest[: len(groups)]
    rows = rest[len(groups) : len(groups) + dp_count]
    loss_ref, out_ref, lse_ref, total_ref = rest[len(groups) + dp_count :]
    lse, positive = row_sums(stats_ref, lab_count)
    lse_ref[...] = lse
    loss_ref[...] = lse - positive / pos_ref.shape[1]
    total_ref[...] = jnp.zeros_like(total_ref)
    for slots, logits_ref in zip(groups, logits_refs):
        for s in slots:

            @pl.when(table_ref[s, 0] >= 0)
            def _(s=s, logits_ref=logits_ref.at[s - slots[0]]):
                for side in range(2):
                    add_slot(
                        side, s, table_ref, pos_ref, logits_ref, rows[s], lse_ref, total_ref, 0
                    )

    part = out_ref.shape[2]
    for j in range(lab_count):
        for b in range(total_ref.shape[0]):
            out_ref[j, b * BLK : (b + 1) * BLK, :] = total_ref[
                b, :, j * part : (j + 1) * part
            ].astype(jnp.bfloat16)


def smem():
    return pl.BlockSpec(memory_space=pltpu.SMEM)


def vmem():
    return pl.BlockSpec(memory_space=pltpu.VMEM)


def anywhere():
    return pl.BlockSpec(memory_space=pl.ANY)


def shards(feats, weights, shortlist, slot_of, positives):
    dp_count = lax.axis_size("dp")
    lab_count = lax.axis_size("label")
    stored, cluster_size, width = weights.shape
    inst_count = feats.shape[0]
    pos_count = positives.shape[1]
    block_count = inst_count // BLK
    short_count = shortlist.shape[1]
    params = pltpu.CompilerParams(vmem_limit_bytes=VMEM_BYTES)
    row_type = jax.ShapeDtypeStruct((cluster_size, width), weights.dtype)
    stat_shape = (3, block_count, BLK)

    sizes = (lab_count, stored, block_count, short_count)
    far = range(1, dp_count)
    far_rows = pl.pallas_call(
        functools.partial(far_kernel, sizes, far),
        out_shape=[row_type] * len(far),
        in_specs=[anywhere()] * 3,
        out_specs=[anywhere()] * len(far),
        scratch_shapes=[
            pltpu.VMEM(weights.shape, weights.dtype),
            pltpu.SMEM(shortlist.shape, jnp.int32),
            pltpu.SMEM(slot_of.shape, jnp.int32),
            pltpu.SemaphoreType.DMA((3 + len(far),)),
        ],
        compiler_params=pltpu.CompilerParams(vmem_limit_bytes=VMEM_PICK),
        name="pick_far",
    )(shortlist, slot_of, weights)
    table, *rows = pl.pallas_call(
        functools.partial(near_kernel, sizes),
        out_shape=[jax.ShapeDtypeStruct((dp_count, 4), jnp.int32)] + [row_type],
        in_specs=[smem(), smem(), anywhere()],
        out_specs=[smem(), vmem()],
        scratch_shapes=[pltpu.SemaphoreType.DMA((1,))],
        compiler_params=params,
        name="pick_near",
    )(shortlist, slot_of, weights)
    rows += far_rows
    for k in range(1, dp_count):
        rows[k] = lax.ppermute(rows[k], "dp", [(i, i ^ k) for i in range(dp_count)])

    feat_blocks = feats.reshape(block_count, BLK, width)
    pos_blocks = positives.reshape(block_count, BLK, pos_count).transpose(0, 2, 1)
    cuts = (0, dp_count // 2, dp_count * 3 // 4, dp_count)
    groups = [tuple(range(a, b)) for a, b in zip(cuts[:-1], cuts[1:])]
    kept = []
    stats = []
    for slots in groups:
        count = len(slots)
        copies = lab_count if slots is groups[-1] else 1
        logits, stats_out = pl.pallas_call(
            functools.partial(logit_kernel, slots, copies),
            out_shape=[
                jax.ShapeDtypeStruct((count, cluster_size, 2 * BLK), jnp.float32),
                jax.ShapeDtypeStruct((copies,) + stat_shape, jnp.float32),
            ],
            in_specs=[smem()] + [vmem()] * (2 + count + len(stats)),
            out_specs=[vmem(), vmem()],
            scratch_shapes=[pltpu.VMEM(stat_shape, jnp.float32)],
            compiler_params=params,
            cost_estimate=pl.CostEstimate(
                flops=count * 4 * BLK * cluster_size * width,
                bytes_accessed=count * cluster_size * width * 2,
                transcendentals=0,
            ),
            name="logits",
        )(table, feat_blocks, pos_blocks, *[rows[s] for s in slots], *stats)
        kept.append(logits)
        stats = [stats_out]

    all_stats = lax.all_to_all(stats[0], "label", split_axis=0, concat_axis=0, tiled=True)
    part = width // lab_count
    in_specs = [smem()] + [vmem()] * (2 + len(groups) + dp_count)
    operands = (table, pos_blocks, all_stats, *kept, *rows)
    loss_type = jax.ShapeDtypeStruct((block_count, BLK), jnp.float32)
    lse_scratch = pltpu.VMEM((block_count, BLK), jnp.float32)
    if part % 128 or lab_count % 2:
        loss, parts = pl.pallas_call(
            functools.partial(grad_kernel, groups, lab_count),
            out_shape=[
                loss_type,
                jax.ShapeDtypeStruct((lab_count, inst_count, part), jnp.bfloat16),
            ],
            in_specs=in_specs,
            out_specs=[vmem(), vmem()],
            scratch_shapes=[lse_scratch, pltpu.VMEM((block_count, BLK, width), jnp.float32)],
            compiler_params=params,
            name="grads",
        )(*operands)
        gathered = lax.all_to_all(parts, "label", split_axis=0, concat_axis=0, tiled=True)
        grads = jnp.sum(gathered.astype(jnp.float32), axis=0).astype(jnp.bfloat16)
        return loss.reshape(inst_count), grads

    pairs = lab_count // 2
    half_rows = inst_count // 2
    finals = []
    for side in range(2):
        loss, keep, send = pl.pallas_call(
            functools.partial(half_kernel, side, groups, lab_count),
            out_shape=[
                loss_type,
                jax.ShapeDtypeStruct((pairs, half_rows, part), jnp.float32),
                jax.ShapeDtypeStruct((pairs, half_rows, part), jnp.bfloat16),
            ],
            in_specs=in_specs,
            out_specs=[vmem()] * 3,
            scratch_shapes=[lse_scratch, pltpu.VMEM((block_count // 2, BLK, width), jnp.float32)],
            compiler_params=params,
            cost_estimate=pl.CostEstimate(
                flops=dp_count * 2 * BLK * cluster_size * width,
                bytes_accessed=dp_count * cluster_size * width * 2,
                transcendentals=0,
            ),
            name="grads",
        )(*operands)
        if side:
            send, got = lax.optimization_barrier((send, got))
        got = lax.ppermute(send, "label", [(i, i ^ 1) for i in range(lab_count)])
        own, *outgoing = pl.pallas_call(
            pair_kernel,
            out_shape=[jax.ShapeDtypeStruct((half_rows, part), jnp.float32)]
            + [jax.ShapeDtypeStruct((half_rows, part), jnp.bfloat16)] * (pairs - 1),
            in_specs=[vmem()] * 2,
            out_specs=[vmem()] * pairs,
            compiler_params=params,
            name="pair_sums",
        )(keep, got)
        finals.append(own)
        for j in range(1, pairs):
            hop = [(i, i ^ (2 * j)) for i in range(lab_count)]
            finals.append(lax.ppermute(outgoing[j - 1], "label", hop))
    grads = pl.pallas_call(
        functools.partial(last_kernel, pairs),
        out_shape=jax.ShapeDtypeStruct((inst_count, part), jnp.bfloat16),
        in_specs=[vmem()] * (2 * pairs),
        out_specs=vmem(),
        compiler_params=params,
        name="last_sums",
    )(*finals)
    return loss.reshape(inst_count), grads


def solution(mesh):
    in_specs = (P("dp", None), P(("dp", "label"), None, None), P(), P(), P("dp", None))
    out_specs = (P("dp"), P("dp", "label"))
    return jax.shard_map(shards, mesh=mesh, in_specs=in_specs, out_specs=out_specs, check_vma=False)
```

```python
import functools

import jax
import jax.numpy as jnp
from jax import lax
from jax.experimental import pallas as pl
from jax.experimental.pallas import tpu as pltpu
from jax.sharding import PartitionSpec as P

BLK = 128
NEG_FILL = -1e30
VMEM_BYTES = 32 * 1024 * 1024
VMEM_PICK = 56 * 1024 * 1024


def divide(value, by):
    if by & (by - 1) == 0:
        return lax.shift_right_logical(value, jnp.int32(by.bit_length() - 1))
    return lax.div(value, jnp.int32(by))


def remainder(value, by):
    if by & (by - 1) == 0:
        return value & jnp.int32(by - 1)
    return lax.rem(value, jnp.int32(by))


def each_entry(count, short_count, body, carry):
    if count <= 64:
        for e in range(count):
            carry = body(e // short_count, e % short_count, carry)
        return carry
    step = lambda e, c: body(divide(e, short_count), remainder(e, short_count), c)
    return lax.fori_loop(0, count, step, carry)


def find_slots(sizes, wanted, lists_ref, slot_ref):
    lab_count, stored, block_count, short_count = sizes
    dp_index, lab_index = lax.axis_index("dp"), lax.axis_index("label")
    mine = dp_index * lab_count + lab_index
    found = []
    for k in wanted:
        base = (dp_index ^ k) * block_count

        def look(row, column, slot_here, base=base):
            slot = slot_ref[lists_ref[base + row, column]]
            return jnp.where(divide(slot, stored) == mine, remainder(slot, stored), slot_here)

        count = block_count // 2 * short_count
        found.append(each_entry(count, short_count, look, jnp.int32(0)))
    return found


def far_kernel(sizes, wanted, lists_hbm, slot_hbm, weights_ref, *rest):
    outs = rest[: len(wanted)]
    held, lists_ref, slot_ref, sems = rest[len(wanted) :]
    tables = [
        pltpu.make_async_copy(lists_hbm, lists_ref, sems.at[0]),
        pltpu.make_async_copy(slot_hbm, slot_ref, sems.at[1]),
    ]
    stage = pltpu.make_async_copy(weights_ref, held, sems.at[2])
    for copy in tables:
        copy.start()
    stage.start()
    for copy in tables:
        copy.wait()
    found = find_slots(sizes, wanted, lists_ref, slot_ref)
    stage.wait()
    copies = []
    for i, slot in enumerate(found):
        copies.append(pltpu.make_async_copy(held.at[slot], outs[i], sems.at[3 + i]))
        copies[-1].start()
    for copy in copies:
        copy.wait()


def near_kernel(sizes, lists_ref, slot_ref, weights_ref, table_ref, *rest):
    lab_count, stored, block_count, short_count = sizes
    outs, sems = rest[:-1], rest[-1]
    copies = []
    for k, slot in enumerate(find_slots(sizes, range(1), lists_ref, slot_ref)):
        copies.append(pltpu.make_async_copy(weights_ref.at[slot], outs[k], sems.at[k]))
        copies[-1].start()
    dp_index, lab_index = lax.axis_index("dp"), lax.axis_index("label")
    half = block_count // 2
    for side in range(2):

        def note(row, column, carry, side=side):
            block = side * half + row
            cluster = lists_ref[dp_index * block_count + block, column]
            device = divide(slot_ref[cluster], stored)

            @pl.when(remainder(device, lab_count) == lab_index)
            def _():
                entry = divide(device, lab_count) ^ dp_index
                table_ref[entry, 0] = cluster
                table_ref[entry, 1 + side] = jnp.int32(block)

            return carry

        each_entry(half * short_count, short_count, note, jnp.int32(0))
    for copy in copies:
        copy.wait()


def target_of(pos_ref, block, first, cluster_size):
    labels = lax.broadcasted_iota(jnp.int32, (cluster_size, BLK), 0) + first
    pos = pos_ref[block]
    hit = pos[0:1, :] == labels
    for p in range(1, pos.shape[0]):
        hit = hit | (pos[p : p + 1, :] == labels)
    return hit


def logit_kernel(slots, copies, table_ref, feats_ref, pos_ref, *rest):
    count = len(slots)
    rows = rest[:count]
    stats_in = rest[count] if slots[0] else None
    logits_ref, out_ref, stats_ref = rest[-3:]
    cluster_size = rows[0].shape[0]
    if stats_in is None:
        stats_ref[0] = jnp.full(stats_ref.shape[1:], NEG_FILL, jnp.float32)
        stats_ref[1] = jnp.zeros(stats_ref.shape[1:], jnp.float32)
        stats_ref[2] = jnp.zeros(stats_ref.shape[1:], jnp.float32)
    else:
        stats_ref[...] = stats_in[0]
    for s, ref in zip(slots, rows):
        first = table_ref[s, 0] * cluster_size
        for side in range(2):
            block = table_ref[s, 1 + side]
            logits = lax.dot_general(
                ref[...],
                feats_ref[block],
                (((1,), (1,)), ((), ())),
                preferred_element_type=jnp.float32,
            )
            logits_ref[s - slots[0], :, side * BLK : (side + 1) * BLK] = logits
            hit = target_of(pos_ref, block, first, cluster_size)
            highest = jnp.max(logits, axis=0, keepdims=True)
            total = jnp.sum(jnp.exp(logits - highest), axis=0, keepdims=True)
            positive = jnp.sum(jnp.where(hit, logits, 0.0), axis=0, keepdims=True)
            row = pl.ds(block, 1)
            before = stats_ref[0, row, :]
            after = jnp.maximum(before, highest)
            stats_ref[0, row, :] = after
            stats_ref[1, row, :] = stats_ref[1, row, :] * jnp.exp(before - after) + total * jnp.exp(
                highest - after
            )
            stats_ref[2, row, :] = stats_ref[2, row, :] + positive
    for i in range(copies):
        out_ref[i] = stats_ref[...]


def row_sums(stats_ref, lab_count):
    highest = stats_ref[0, 0]
    for i in range(1, lab_count):
        highest = jnp.maximum(highest, stats_ref[i, 0])
    summed = jnp.zeros_like(highest)
    positive = jnp.zeros_like(highest)
    for i in range(lab_count):
        summed = summed + stats_ref[i, 1] * jnp.exp(stats_ref[i, 0] - highest)
        positive = positive + stats_ref[i, 2]
    return highest + jnp.log(summed), positive


def add_slot(side, s, table_ref, pos_ref, logits_ref, rows_ref, lse_ref, total_ref, first_block):
    cluster_size = rows_ref.shape[0]
    pos_count = pos_ref.shape[1]
    block = table_ref[s, 1 + side]
    hit = target_of(pos_ref, block, table_ref[s, 0] * cluster_size, cluster_size)
    dlogit = jnp.exp(
        logits_ref[:, side * BLK : (side + 1) * BLK] - lse_ref[pl.ds(block, 1), :]
    ) - jnp.where(hit, 1.0 / pos_count, 0.0)
    total_ref[block - first_block] += lax.dot_general(
        dlogit.T.astype(jnp.bfloat16),
        rows_ref[...],
        (((1,), (0,)), ((), ())),
        preferred_element_type=jnp.float32,
    )


def half_kernel(side, groups, lab_count, table_ref, pos_ref, stats_ref, *rest):
    dp_count = groups[-1][-1] + 1
    logits_refs = rest[: len(groups)]
    rows = rest[len(groups) : len(groups) + dp_count]
    loss_ref, keep_ref, send_ref, lse_ref, total_ref = rest[len(groups) + dp_count :]
    lse, positive = row_sums(stats_ref, lab_count)
    lse_ref[...] = lse
    loss_ref[...] = lse - positive / pos_ref.shape[1]
    total_ref[...] = jnp.zeros_like(total_ref)
    half = total_ref.shape[0]
    for slots, logits_ref in zip(groups, logits_refs):
        for s in slots:
            add_slot(
                side,
                s,
                table_ref,
                pos_ref,
                logits_ref.at[s - slots[0]],
                rows[s],
                lse_ref,
                total_ref,
                side * half,
            )
    part = keep_ref.shape[2]
    lab_index = lax.axis_index("label")
    for j in range(lab_count // 2):
        mine = pl.ds(pl.multiple_of((lab_index ^ (2 * j)) * part, part), part)
        other = pl.ds(pl.multiple_of((lab_index ^ (2 * j + 1)) * part, part), part)
        for b in range(half):
            here = pl.ds(b * BLK, BLK)
            keep_ref[j, here, :] = total_ref[b, :, mine]
            send_ref[j, here, :] = total_ref[b, :, other].astype(jnp.bfloat16)


def pair_kernel(keep_ref, got_ref, *outs):
    outs[0][...] = keep_ref[0] + got_ref[0].astype(jnp.float32)
    for j in range(1, len(outs)):
        outs[j][...] = (keep_ref[j] + got_ref[j].astype(jnp.float32)).astype(jnp.bfloat16)


def last_kernel(cores, count, *refs):
    loss_ref, out_ref = refs[-2:]
    each = 2 * count + 1

    def finish(loss_in, *parts):
        loss_ref[...] = loss_in[...]
        for h in range(2):
            total = parts[h * count][...]
            for ref in parts[h * count + 1 : (h + 1) * count]:
                total = total + ref[...].astype(jnp.float32)
            rows = total.shape[0]
            out_ref[h * rows : (h + 1) * rows, :] = total.astype(jnp.bfloat16)

    for i, core in enumerate(cores):
        only(core, functools.partial(finish, *refs[i * each : (i + 1) * each]))


def grad_kernel(groups, lab_count, table_ref, pos_ref, stats_ref, *rest):
    dp_count = groups[-1][-1] + 1
    logits_refs = rest[: len(groups)]
    rows = rest[len(groups) : len(groups) + dp_count]
    loss_ref, out_ref, lse_ref, total_ref = rest[len(groups) + dp_count :]
    lse, positive = row_sums(stats_ref, lab_count)
    lse_ref[...] = lse
    loss_ref[...] = lse - positive / pos_ref.shape[1]
    total_ref[...] = jnp.zeros_like(total_ref)
    for slots, logits_ref in zip(groups, logits_refs):
        for s in slots:

            @pl.when(table_ref[s, 0] >= 0)
            def _(s=s, logits_ref=logits_ref.at[s - slots[0]]):
                for side in range(2):
                    add_slot(
                        side, s, table_ref, pos_ref, logits_ref, rows[s], lse_ref, total_ref, 0
                    )

    part = out_ref.shape[2]
    for j in range(lab_count):
        for b in range(total_ref.shape[0]):
            out_ref[j, b * BLK : (b + 1) * BLK, :] = total_ref[
                b, :, j * part : (j + 1) * part
            ].astype(jnp.bfloat16)


def only(core, body):
    if core is None:
        body()
    else:
        pl.when((lax.axis_index("dp") & 1) == core)(body)


def on_core(core, kernel):
    return lambda *refs: only(core, functools.partial(kernel, *refs))


def smem():
    return pl.BlockSpec(memory_space=pltpu.SMEM)


def vmem():
    return pl.BlockSpec(memory_space=pltpu.VMEM)


def anywhere():
    return pl.BlockSpec(memory_space=pl.ANY)


def shards(feats, weights, shortlist, slot_of, positives):
    dp_count = lax.axis_size("dp")
    lab_count = lax.axis_size("label")
    stored, cluster_size, width = weights.shape
    inst_count = feats.shape[0]
    pos_count = positives.shape[1]
    block_count = inst_count // BLK
    short_count = shortlist.shape[1]
    params = pltpu.CompilerParams(vmem_limit_bytes=VMEM_BYTES)
    row_type = jax.ShapeDtypeStruct((cluster_size, width), weights.dtype)
    stat_shape = (3, block_count, BLK)

    sizes = (lab_count, stored, block_count, short_count)
    far = range(1, dp_count)
    far_rows = pl.pallas_call(
        functools.partial(far_kernel, sizes, far),
        out_shape=[row_type] * len(far),
        in_specs=[anywhere()] * 3,
        out_specs=[anywhere()] * len(far),
        scratch_shapes=[
            pltpu.VMEM(weights.shape, weights.dtype),
            pltpu.SMEM(shortlist.shape, jnp.int32),
            pltpu.SMEM(slot_of.shape, jnp.int32),
            pltpu.SemaphoreType.DMA((3 + len(far),)),
        ],
        compiler_params=pltpu.CompilerParams(vmem_limit_bytes=VMEM_PICK),
        name="pick_far",
    )(shortlist, slot_of, weights)
    table, *rows = pl.pallas_call(
        functools.partial(near_kernel, sizes),
        out_shape=[jax.ShapeDtypeStruct((dp_count, 4), jnp.int32)] + [row_type],
        in_specs=[smem(), smem(), anywhere()],
        out_specs=[smem(), vmem()],
        scratch_shapes=[pltpu.SemaphoreType.DMA((1,))],
        compiler_params=params,
        name="pick_near",
    )(shortlist, slot_of, weights)
    part = width // lab_count
    staggered = dp_count == 4 and part % 128 == 0 and lab_count % 2 == 0
    cores = (0, 1) if staggered else (None,)

    def swap_dp(x, k, core):
        pairs = [(i, i ^ k) for i in range(dp_count) if core is None or (i ^ k) & 1 == core]
        return lax.ppermute(x, "dp", pairs)

    def swap_label(x, mask, core):
        pairs = [
            (d * lab_count + i, d * lab_count + (i ^ mask))
            for d in range(dp_count)
            for i in range(lab_count)
            if core is None or d & 1 == core
        ]
        return lax.ppermute(x, ("dp", "label"), pairs)

    near_rows = rows + [swap_dp(far_rows[0], 1, None)]
    crossing = [[swap_dp(x, k + 2, core) for k, x in enumerate(far_rows[1:])] for core in cores]

    feat_blocks = feats.reshape(block_count, BLK, width)
    pos_blocks = positives.reshape(block_count, BLK, pos_count).transpose(0, 2, 1)

    def logits_of(slots, rows, stats, copies, core):
        count = len(slots)
        return pl.pallas_call(
            on_core(core, functools.partial(logit_kernel, slots, copies)),
            out_shape=[
                jax.ShapeDtypeStruct((count, cluster_size, 2 * BLK), jnp.float32),
                jax.ShapeDtypeStruct((copies,) + stat_shape, jnp.float32),
            ],
            in_specs=[smem()] + [vmem()] * (2 + count + len(stats)),
            out_specs=[vmem(), vmem()],
            scratch_shapes=[pltpu.VMEM(stat_shape, jnp.float32)],
            compiler_params=params,
            name="logits",
        )(table, feat_blocks, pos_blocks, *rows, *stats)

    near_logits, near_stats = logits_of((0, 1), near_rows, [], 1, None)
    far_slots = tuple(range(2, dp_count))
    groups = [(0, 1), far_slots]
    in_specs = [smem()] + [vmem()] * (2 + len(groups) + dp_count)
    loss_type = jax.ShapeDtypeStruct((block_count, BLK), jnp.float32)
    lse_scratch = pltpu.VMEM((block_count, BLK), jnp.float32)
    if not staggered:
        far_logits, stats = logits_of(far_slots, crossing[0], [near_stats], lab_count, None)
        all_stats = lax.all_to_all(stats, "label", split_axis=0, concat_axis=0, tiled=True)
        operands = (table, pos_blocks, all_stats, near_logits, far_logits, *near_rows, *crossing[0])
        loss, parts = pl.pallas_call(
            functools.partial(grad_kernel, groups, lab_count),
            out_shape=[
                loss_type,
                jax.ShapeDtypeStruct((lab_count, inst_count, part), jnp.bfloat16),
            ],
            in_specs=in_specs,
            out_specs=[vmem(), vmem()],
            scratch_shapes=[lse_scratch, pltpu.VMEM((block_count, BLK, width), jnp.float32)],
            compiler_params=params,
            name="grads",
        )(*operands)
        gathered = lax.all_to_all(parts, "label", split_axis=0, concat_axis=0, tiled=True)
        grads = jnp.sum(gathered.astype(jnp.float32), axis=0).astype(jnp.bfloat16)
        return loss.reshape(inst_count), grads

    pairs = lab_count // 2
    half_rows = inst_count // 2
    finals = []
    sent = None
    for core in cores:
        far_rows = crossing[core]
        if core:
            *far_rows, sent = lax.optimization_barrier((*far_rows, sent))
        far_logits, stats = logits_of(far_slots, far_rows, [near_stats], lab_count, core)
        all_stats = lax.all_to_all(stats, "label", split_axis=0, concat_axis=0, tiled=True)
        operands = (table, pos_blocks, all_stats, near_logits, far_logits, *near_rows, *far_rows)
        got = None
        ends = []
        for side in range(2):
            loss, keep, send = pl.pallas_call(
                on_core(core, functools.partial(half_kernel, side, groups, lab_count)),
                out_shape=[
                    loss_type,
                    jax.ShapeDtypeStruct((pairs, half_rows, part), jnp.float32),
                    jax.ShapeDtypeStruct((pairs, half_rows, part), jnp.bfloat16),
                ],
                in_specs=in_specs,
                out_specs=[vmem()] * 3,
                scratch_shapes=[
                    lse_scratch,
                    pltpu.VMEM((block_count // 2, BLK, width), jnp.float32),
                ],
                compiler_params=params,
                name="grads",
            )(*operands)
            if side:
                send, got = lax.optimization_barrier((send, got))
            got = swap_label(send, 1, core)
            if not side:
                sent = got
            own, *outgoing = pl.pallas_call(
                on_core(core, pair_kernel),
                out_shape=[jax.ShapeDtypeStruct((half_rows, part), jnp.float32)]
                + [jax.ShapeDtypeStruct((half_rows, part), jnp.bfloat16)] * (pairs - 1),
                in_specs=[vmem()] * 2,
                out_specs=[vmem()] * pairs,
                compiler_params=params,
                name="pair_sums",
            )(keep, got)
            ends.append(own)
            ends += [swap_label(x, 2 * j + 2, core) for j, x in enumerate(outgoing)]
        finals += [loss, *ends]
    loss, grads = pl.pallas_call(
        functools.partial(last_kernel, cores, pairs),
        out_shape=[loss_type, jax.ShapeDtypeStruct((inst_count, part), jnp.bfloat16)],
        in_specs=[vmem()] * len(finals),
        out_specs=[vmem()] * 2,
        compiler_params=params,
        name="last_sums",
    )(*finals)
    return loss.reshape(inst_count), grads


def solution(mesh):
    in_specs = (P("dp", None), P(("dp", "label"), None, None), P(), P(), P("dp", None))
    out_specs = (P("dp"), P("dp", "label"))
    return jax.shard_map(shards, mesh=mesh, in_specs=in_specs, out_specs=out_specs, check_vma=False)
```

```python
import functools

import jax
import jax.numpy as jnp
from jax import lax
from jax.experimental import pallas as pl
from jax.experimental.pallas import tpu as pltpu
from jax.sharding import PartitionSpec as P

BLK = 128
NEG_FILL = -1e30
VMEM_BYTES = 32 * 1024 * 1024
VMEM_PICK = 56 * 1024 * 1024


def divide(value, by):
    if by & (by - 1) == 0:
        return lax.shift_right_logical(value, jnp.int32(by.bit_length() - 1))
    return lax.div(value, jnp.int32(by))


def remainder(value, by):
    if by & (by - 1) == 0:
        return value & jnp.int32(by - 1)
    return lax.rem(value, jnp.int32(by))


def each_entry(count, short_count, body, carry):
    if count <= 64:
        for e in range(count):
            carry = body(e // short_count, e % short_count, carry)
        return carry
    step = lambda e, c: body(divide(e, short_count), remainder(e, short_count), c)
    return lax.fori_loop(0, count, step, carry)


def find_slots(sizes, wanted, lists_ref, slot_ref):
    lab_count, stored, block_count, short_count = sizes
    dp_index, lab_index = lax.axis_index("dp"), lax.axis_index("label")
    mine = dp_index * lab_count + lab_index
    found = []
    for k in wanted:
        base = (dp_index ^ k) * block_count

        def look(row, column, slot_here, base=base):
            slot = slot_ref[lists_ref[base + row, column]]
            return jnp.where(divide(slot, stored) == mine, remainder(slot, stored), slot_here)

        count = block_count // 2 * short_count
        found.append(each_entry(count, short_count, look, jnp.int32(0)))
    return found


def far_kernel(sizes, wanted, lists_hbm, slot_hbm, weights_ref, *rest):
    outs = rest[: len(wanted)]
    held, lists_ref, slot_ref, sems = rest[len(wanted) :]
    tables = [
        pltpu.make_async_copy(lists_hbm, lists_ref, sems.at[0]),
        pltpu.make_async_copy(slot_hbm, slot_ref, sems.at[1]),
    ]
    stage = pltpu.make_async_copy(weights_ref, held, sems.at[2])
    for copy in tables:
        copy.start()
    stage.start()
    for copy in tables:
        copy.wait()
    found = find_slots(sizes, wanted, lists_ref, slot_ref)
    stage.wait()
    copies = []
    for i, slot in enumerate(found):
        copies.append(pltpu.make_async_copy(held.at[slot], outs[i], sems.at[3 + i]))
        copies[-1].start()
    for copy in copies:
        copy.wait()


def near_kernel(sizes, lists_ref, slot_ref, weights_ref, table_ref, *rest):
    lab_count, stored, block_count, short_count = sizes
    outs, sems = rest[:-1], rest[-1]
    copies = []
    for k, slot in enumerate(find_slots(sizes, range(1), lists_ref, slot_ref)):
        copies.append(pltpu.make_async_copy(weights_ref.at[slot], outs[k], sems.at[k]))
        copies[-1].start()
    dp_index, lab_index = lax.axis_index("dp"), lax.axis_index("label")
    half = block_count // 2
    for side in range(2):

        def note(row, column, carry, side=side):
            block = side * half + row
            cluster = lists_ref[dp_index * block_count + block, column]
            device = divide(slot_ref[cluster], stored)

            @pl.when(remainder(device, lab_count) == lab_index)
            def _():
                entry = divide(device, lab_count) ^ dp_index
                table_ref[entry, 0] = cluster
                table_ref[entry, 1 + side] = jnp.int32(block)

            return carry

        each_entry(half * short_count, short_count, note, jnp.int32(0))
    for copy in copies:
        copy.wait()


def after_kernel(rows_ref, token_ref, out_ref):
    pass


def target_of(pos_ref, block, first, cluster_size):
    labels = lax.broadcasted_iota(jnp.int32, (cluster_size, BLK), 0) + first
    pos = pos_ref[block]
    hit = pos[0:1, :] == labels
    for p in range(1, pos.shape[0]):
        hit = hit | (pos[p : p + 1, :] == labels)
    return hit


def logit_kernel(slots, copies, table_ref, feats_ref, pos_ref, *rest):
    count = len(slots)
    rows = rest[:count]
    stats_in = rest[count] if slots[0] else None
    logits_ref, out_ref, stats_ref = rest[-3:]
    cluster_size = rows[0].shape[0]
    if stats_in is None:
        stats_ref[0] = jnp.full(stats_ref.shape[1:], NEG_FILL, jnp.float32)
        stats_ref[1] = jnp.zeros(stats_ref.shape[1:], jnp.float32)
        stats_ref[2] = jnp.zeros(stats_ref.shape[1:], jnp.float32)
    else:
        stats_ref[...] = stats_in[0]
    for s, ref in zip(slots, rows):
        first = table_ref[s, 0] * cluster_size
        for side in range(2):
            block = table_ref[s, 1 + side]
            logits = lax.dot_general(
                ref[...],
                feats_ref[block],
                (((1,), (1,)), ((), ())),
                preferred_element_type=jnp.float32,
            )
            logits_ref[s - slots[0], :, side * BLK : (side + 1) * BLK] = logits
            hit = target_of(pos_ref, block, first, cluster_size)
            highest = jnp.max(logits, axis=0, keepdims=True)
            total = jnp.sum(jnp.exp(logits - highest), axis=0, keepdims=True)
            positive = jnp.sum(jnp.where(hit, logits, 0.0), axis=0, keepdims=True)
            row = pl.ds(block, 1)
            before = stats_ref[0, row, :]
            after = jnp.maximum(before, highest)
            stats_ref[0, row, :] = after
            stats_ref[1, row, :] = stats_ref[1, row, :] * jnp.exp(before - after) + total * jnp.exp(
                highest - after
            )
            stats_ref[2, row, :] = stats_ref[2, row, :] + positive
    for i in range(copies):
        out_ref[i] = stats_ref[...]


def row_sums(stats_ref, lab_count):
    highest = stats_ref[0, 0]
    for i in range(1, lab_count):
        highest = jnp.maximum(highest, stats_ref[i, 0])
    summed = jnp.zeros_like(highest)
    positive = jnp.zeros_like(highest)
    for i in range(lab_count):
        summed = summed + stats_ref[i, 1] * jnp.exp(stats_ref[i, 0] - highest)
        positive = positive + stats_ref[i, 2]
    return highest + jnp.log(summed), positive


def add_slot(side, s, table_ref, pos_ref, logits_ref, rows_ref, lse_ref, total_ref, first_block):
    cluster_size = rows_ref.shape[0]
    pos_count = pos_ref.shape[1]
    block = table_ref[s, 1 + side]
    hit = target_of(pos_ref, block, table_ref[s, 0] * cluster_size, cluster_size)
    dlogit = jnp.exp(
        logits_ref[:, side * BLK : (side + 1) * BLK] - lse_ref[pl.ds(block, 1), :]
    ) - jnp.where(hit, 1.0 / pos_count, 0.0)
    total_ref[block - first_block] += lax.dot_general(
        dlogit.T.astype(jnp.bfloat16),
        rows_ref[...],
        (((1,), (0,)), ((), ())),
        preferred_element_type=jnp.float32,
    )


def half_kernel(side, groups, lab_count, table_ref, pos_ref, stats_ref, *rest):
    dp_count = groups[-1][-1] + 1
    logits_refs = rest[: len(groups)]
    rows = rest[len(groups) : len(groups) + dp_count]
    loss_ref, keep_ref, send_ref, lse_ref, total_ref = rest[len(groups) + dp_count :]
    lse, positive = row_sums(stats_ref, lab_count)
    lse_ref[...] = lse
    loss_ref[...] = lse - positive / pos_ref.shape[1]
    total_ref[...] = jnp.zeros_like(total_ref)
    half = total_ref.shape[0]
    for slots, logits_ref in zip(groups, logits_refs):
        for s in slots:
            add_slot(
                side,
                s,
                table_ref,
                pos_ref,
                logits_ref.at[s - slots[0]],
                rows[s],
                lse_ref,
                total_ref,
                side * half,
            )
    part = keep_ref.shape[2]
    lab_index = lax.axis_index("label")
    for j in range(lab_count // 2):
        mine = pl.ds(pl.multiple_of((lab_index ^ (2 * j)) * part, part), part)
        other = pl.ds(pl.multiple_of((lab_index ^ (2 * j + 1)) * part, part), part)
        for b in range(half):
            here = pl.ds(b * BLK, BLK)
            keep_ref[j, here, :] = total_ref[b, :, mine]
            send_ref[j, here, :] = total_ref[b, :, other].astype(jnp.bfloat16)


def pair_kernel(keep_ref, got_ref, *outs):
    outs[0][...] = keep_ref[0] + got_ref[0].astype(jnp.float32)
    for j in range(1, len(outs)):
        outs[j][...] = (keep_ref[j] + got_ref[j].astype(jnp.float32)).astype(jnp.bfloat16)


def last_kernel(count, *refs):
    out_ref = refs[-1]
    for h in range(len(refs[:-1]) // count):
        total = refs[h * count][...]
        for ref in refs[h * count + 1 : (h + 1) * count]:
            total = total + ref[...].astype(jnp.float32)
        rows = total.shape[0]
        out_ref[h * rows : (h + 1) * rows, :] = total.astype(jnp.bfloat16)


def grad_kernel(groups, lab_count, table_ref, pos_ref, stats_ref, *rest):
    dp_count = groups[-1][-1] + 1
    logits_refs = rest[: len(groups)]
    rows = rest[len(groups) : len(groups) + dp_count]
    loss_ref, out_ref, lse_ref, total_ref = rest[len(groups) + dp_count :]
    lse, positive = row_sums(stats_ref, lab_count)
    lse_ref[...] = lse
    loss_ref[...] = lse - positive / pos_ref.shape[1]
    total_ref[...] = jnp.zeros_like(total_ref)
    for slots, logits_ref in zip(groups, logits_refs):
        for s in slots:

            @pl.when(table_ref[s, 0] >= 0)
            def _(s=s, logits_ref=logits_ref.at[s - slots[0]]):
                for side in range(2):
                    add_slot(
                        side, s, table_ref, pos_ref, logits_ref, rows[s], lse_ref, total_ref, 0
                    )

    part = out_ref.shape[2]
    for j in range(lab_count):
        for b in range(total_ref.shape[0]):
            out_ref[j, b * BLK : (b + 1) * BLK, :] = total_ref[
                b, :, j * part : (j + 1) * part
            ].astype(jnp.bfloat16)


def smem():
    return pl.BlockSpec(memory_space=pltpu.SMEM)


def vmem():
    return pl.BlockSpec(memory_space=pltpu.VMEM)


def anywhere():
    return pl.BlockSpec(memory_space=pl.ANY)


def shards(feats, weights, shortlist, slot_of, positives):
    dp_count = lax.axis_size("dp")
    lab_count = lax.axis_size("label")
    stored, cluster_size, width = weights.shape
    inst_count = feats.shape[0]
    pos_count = positives.shape[1]
    block_count = inst_count // BLK
    short_count = shortlist.shape[1]
    params = pltpu.CompilerParams(vmem_limit_bytes=VMEM_BYTES)
    row_type = jax.ShapeDtypeStruct((cluster_size, width), weights.dtype)
    stat_shape = (3, block_count, BLK)

    sizes = (lab_count, stored, block_count, short_count)
    far = range(1, dp_count)
    far_rows = pl.pallas_call(
        functools.partial(far_kernel, sizes, far),
        out_shape=[row_type] * len(far),
        in_specs=[anywhere()] * 3,
        out_specs=[anywhere()] * len(far),
        scratch_shapes=[
            pltpu.VMEM(weights.shape, weights.dtype),
            pltpu.SMEM(shortlist.shape, jnp.int32),
            pltpu.SMEM(slot_of.shape, jnp.int32),
            pltpu.SemaphoreType.DMA((3 + len(far),)),
        ],
        compiler_params=pltpu.CompilerParams(vmem_limit_bytes=VMEM_PICK),
        name="pick_far",
    )(shortlist, slot_of, weights)
    table, *rows = pl.pallas_call(
        functools.partial(near_kernel, sizes),
        out_shape=[jax.ShapeDtypeStruct((dp_count, 4), jnp.int32)] + [row_type],
        in_specs=[smem(), smem(), anywhere()],
        out_specs=[smem(), vmem()],
        scratch_shapes=[pltpu.SemaphoreType.DMA((1,))],
        compiler_params=params,
        name="pick_near",
    )(shortlist, slot_of, weights)
    rows += far_rows
    def swap_dp(x, mask, core=None):
        pairs = [(i, i if core == 1 - (i & 1) else i ^ mask) for i in range(dp_count)]
        return lax.ppermute(x, "dp", pairs)

    rows[1] = swap_dp(rows[1], 1)
    if dp_count == 4:
        handed = swap_dp(rows[3], 1)
        straight = swap_dp(rows[2], 2, 0)
        crossed = swap_dp(handed, 2, 0)
        token = swap_dp(straight[:16, :128].astype(jnp.float32), 1)
        straight = pl.pallas_call(
            after_kernel,
            out_shape=row_type,
            in_specs=[anywhere(), smem()],
            out_specs=anywhere(),
            input_output_aliases={0: 0},
            compiler_params=params,
            name="after_token",
        )(straight, token)
        rows[2] = swap_dp(straight, 2, 1)
        rows[3] = swap_dp(crossed, 2, 1)
    else:
        for k in range(2, dp_count):
            rows[k] = swap_dp(rows[k], k)

    feat_blocks = feats.reshape(block_count, BLK, width)
    pos_blocks = positives.reshape(block_count, BLK, pos_count).transpose(0, 2, 1)
    cuts = (0, dp_count // 2, dp_count * 3 // 4, dp_count)
    groups = [tuple(range(a, b)) for a, b in zip(cuts[:-1], cuts[1:])]
    kept = []
    stats = []
    for slots in groups:
        count = len(slots)
        copies = lab_count if slots is groups[-1] else 1
        logits, stats_out = pl.pallas_call(
            functools.partial(logit_kernel, slots, copies),
            out_shape=[
                jax.ShapeDtypeStruct((count, cluster_size, 2 * BLK), jnp.float32),
                jax.ShapeDtypeStruct((copies,) + stat_shape, jnp.float32),
            ],
            in_specs=[smem()] + [vmem()] * (2 + count + len(stats)),
            out_specs=[vmem(), vmem()],
            scratch_shapes=[pltpu.VMEM(stat_shape, jnp.float32)],
            compiler_params=params,
            cost_estimate=pl.CostEstimate(
                flops=count * 4 * BLK * cluster_size * width,
                bytes_accessed=count * cluster_size * width * 2,
                transcendentals=0,
            ),
            name="logits",
        )(table, feat_blocks, pos_blocks, *[rows[s] for s in slots], *stats)
        kept.append(logits)
        stats = [stats_out]

    all_stats = lax.all_to_all(stats[0], "label", split_axis=0, concat_axis=0, tiled=True)
    part = width // lab_count
    in_specs = [smem()] + [vmem()] * (2 + len(groups) + dp_count)
    operands = (table, pos_blocks, all_stats, *kept, *rows)
    loss_type = jax.ShapeDtypeStruct((block_count, BLK), jnp.float32)
    lse_scratch = pltpu.VMEM((block_count, BLK), jnp.float32)
    if part % 128 or lab_count % 2:
        loss, parts = pl.pallas_call(
            functools.partial(grad_kernel, groups, lab_count),
            out_shape=[
                loss_type,
                jax.ShapeDtypeStruct((lab_count, inst_count, part), jnp.bfloat16),
            ],
            in_specs=in_specs,
            out_specs=[vmem(), vmem()],
            scratch_shapes=[lse_scratch, pltpu.VMEM((block_count, BLK, width), jnp.float32)],
            compiler_params=params,
            name="grads",
        )(*operands)
        gathered = lax.all_to_all(parts, "label", split_axis=0, concat_axis=0, tiled=True)
        grads = jnp.sum(gathered.astype(jnp.float32), axis=0).astype(jnp.bfloat16)
        return loss.reshape(inst_count), grads

    pairs = lab_count // 2
    half_rows = inst_count // 2
    finals = []
    for side in range(2):
        loss, keep, send = pl.pallas_call(
            functools.partial(half_kernel, side, groups, lab_count),
            out_shape=[
                loss_type,
                jax.ShapeDtypeStruct((pairs, half_rows, part), jnp.float32),
                jax.ShapeDtypeStruct((pairs, half_rows, part), jnp.bfloat16),
            ],
            in_specs=in_specs,
            out_specs=[vmem()] * 3,
            scratch_shapes=[lse_scratch, pltpu.VMEM((block_count // 2, BLK, width), jnp.float32)],
            compiler_params=params,
            cost_estimate=pl.CostEstimate(
                flops=dp_count * 2 * BLK * cluster_size * width,
                bytes_accessed=dp_count * cluster_size * width * 2,
                transcendentals=0,
            ),
            name="grads",
        )(*operands)
        if side:
            send, got = lax.optimization_barrier((send, got))
        got = lax.ppermute(send, "label", [(i, i ^ 1) for i in range(lab_count)])
        own, *outgoing = pl.pallas_call(
            pair_kernel,
            out_shape=[jax.ShapeDtypeStruct((half_rows, part), jnp.float32)]
            + [jax.ShapeDtypeStruct((half_rows, part), jnp.bfloat16)] * (pairs - 1),
            in_specs=[vmem()] * 2,
            out_specs=[vmem()] * pairs,
            compiler_params=params,
            name="pair_sums",
        )(keep, got)
        finals.append(own)
        for j in range(1, pairs):
            hop = [(i, i ^ (2 * j)) for i in range(lab_count)]
            finals.append(lax.ppermute(outgoing[j - 1], "label", hop))
    grads = pl.pallas_call(
        functools.partial(last_kernel, pairs),
        out_shape=jax.ShapeDtypeStruct((inst_count, part), jnp.bfloat16),
        in_specs=[vmem()] * (2 * pairs),
        out_specs=vmem(),
        compiler_params=params,
        name="last_sums",
    )(*finals)
    return loss.reshape(inst_count), grads


def solution(mesh):
    in_specs = (P("dp", None), P(("dp", "label"), None, None), P(), P(), P("dp", None))
    out_specs = (P("dp"), P("dp", "label"))
    return jax.shard_map(shards, mesh=mesh, in_specs=in_specs, out_specs=out_specs, check_vma=False)
```

```python
import functools

import jax
import jax.numpy as jnp
from jax import lax
from jax.experimental import pallas as pl
from jax.experimental.pallas import tpu as pltpu
from jax.sharding import PartitionSpec as P

BLK = 128
NEG_FILL = -1e30
VMEM_BYTES = 32 * 1024 * 1024
VMEM_PICK = 56 * 1024 * 1024


def divide(value, by):
    if by & (by - 1) == 0:
        return lax.shift_right_logical(value, jnp.int32(by.bit_length() - 1))
    return lax.div(value, jnp.int32(by))


def remainder(value, by):
    if by & (by - 1) == 0:
        return value & jnp.int32(by - 1)
    return lax.rem(value, jnp.int32(by))


def each_entry(count, short_count, body, carry):
    if count <= 64:
        for e in range(count):
            carry = body(e // short_count, e % short_count, carry)
        return carry
    step = lambda e, c: body(divide(e, short_count), remainder(e, short_count), c)
    return lax.fori_loop(0, count, step, carry)


def find_slots(sizes, wanted, lists_ref, slot_ref):
    lab_count, stored, block_count, short_count = sizes
    dp_index, lab_index = lax.axis_index("dp"), lax.axis_index("label")
    mine = dp_index * lab_count + lab_index
    found = []
    for k in wanted:
        base = (dp_index ^ k) * block_count

        def look(row, column, slot_here, base=base):
            slot = slot_ref[lists_ref[base + row, column]]
            return jnp.where(divide(slot, stored) == mine, remainder(slot, stored), slot_here)

        count = block_count // 2 * short_count
        found.append(each_entry(count, short_count, look, jnp.int32(0)))
    return found


def far_kernel(sizes, wanted, lists_hbm, slot_hbm, weights_ref, *rest):
    outs = rest[: len(wanted)]
    held, lists_ref, slot_ref, sems = rest[len(wanted) :]
    tables = [
        pltpu.make_async_copy(lists_hbm, lists_ref, sems.at[0]),
        pltpu.make_async_copy(slot_hbm, slot_ref, sems.at[1]),
    ]
    stage = pltpu.make_async_copy(weights_ref, held, sems.at[2])
    for copy in tables:
        copy.start()
    stage.start()
    for copy in tables:
        copy.wait()
    found = find_slots(sizes, wanted, lists_ref, slot_ref)
    stage.wait()
    copies = []
    for i, slot in enumerate(found):
        copies.append(pltpu.make_async_copy(held.at[slot], outs[i], sems.at[3 + i]))
        copies[-1].start()
    for copy in copies:
        copy.wait()


def near_kernel(sizes, lists_ref, slot_ref, weights_ref, table_ref, *rest):
    lab_count, stored, block_count, short_count = sizes
    outs, sems = rest[:-1], rest[-1]
    copies = []
    for k, slot in enumerate(find_slots(sizes, range(1), lists_ref, slot_ref)):
        copies.append(pltpu.make_async_copy(weights_ref.at[slot], outs[k], sems.at[k]))
        copies[-1].start()
    dp_index, lab_index = lax.axis_index("dp"), lax.axis_index("label")
    half = block_count // 2
    for side in range(2):

        def note(row, column, carry, side=side):
            block = side * half + row
            cluster = lists_ref[dp_index * block_count + block, column]
            device = divide(slot_ref[cluster], stored)

            @pl.when(remainder(device, lab_count) == lab_index)
            def _():
                entry = divide(device, lab_count) ^ dp_index
                table_ref[entry, 0] = cluster
                table_ref[entry, 1 + side] = jnp.int32(block)

            return carry

        each_entry(half * short_count, short_count, note, jnp.int32(0))
    for copy in copies:
        copy.wait()


def after_kernel(rows_ref, token_ref, out_ref):
    pass


def target_of(pos_ref, block, first, cluster_size):
    labels = lax.broadcasted_iota(jnp.int32, (cluster_size, BLK), 0) + first
    pos = pos_ref[block]
    hit = pos[0:1, :] == labels
    for p in range(1, pos.shape[0]):
        hit = hit | (pos[p : p + 1, :] == labels)
    return hit


def logit_kernel(slots, copies, table_ref, feats_ref, pos_ref, *rest):
    count = len(slots)
    rows = rest[:count]
    stats_in = rest[count] if slots[0] else None
    logits_ref, out_ref, stats_ref = rest[-3:]
    cluster_size = rows[0].shape[0]
    if stats_in is None:
        stats_ref[0] = jnp.full(stats_ref.shape[1:], NEG_FILL, jnp.float32)
        stats_ref[1] = jnp.zeros(stats_ref.shape[1:], jnp.float32)
        stats_ref[2] = jnp.zeros(stats_ref.shape[1:], jnp.float32)
    else:
        stats_ref[...] = stats_in[0]
    for s, ref in zip(slots, rows):
        first = table_ref[s, 0] * cluster_size
        for side in range(2):
            block = table_ref[s, 1 + side]
            logits = lax.dot_general(
                ref[...],
                feats_ref[block],
                (((1,), (1,)), ((), ())),
                preferred_element_type=jnp.float32,
            )
            logits_ref[s - slots[0], :, side * BLK : (side + 1) * BLK] = logits
            hit = target_of(pos_ref, block, first, cluster_size)
            highest = jnp.max(logits, axis=0, keepdims=True)
            total = jnp.sum(jnp.exp(logits - highest), axis=0, keepdims=True)
            positive = jnp.sum(jnp.where(hit, logits, 0.0), axis=0, keepdims=True)
            row = pl.ds(block, 1)
            before = stats_ref[0, row, :]
            after = jnp.maximum(before, highest)
            stats_ref[0, row, :] = after
            stats_ref[1, row, :] = stats_ref[1, row, :] * jnp.exp(before - after) + total * jnp.exp(
                highest - after
            )
            stats_ref[2, row, :] = stats_ref[2, row, :] + positive
    for i in range(copies):
        out_ref[i] = stats_ref[...]


def row_sums(stats_ref, lab_count):
    highest = stats_ref[0, 0]
    for i in range(1, lab_count):
        highest = jnp.maximum(highest, stats_ref[i, 0])
    summed = jnp.zeros_like(highest)
    positive = jnp.zeros_like(highest)
    for i in range(lab_count):
        summed = summed + stats_ref[i, 1] * jnp.exp(stats_ref[i, 0] - highest)
        positive = positive + stats_ref[i, 2]
    return highest + jnp.log(summed), positive


def add_slot(side, s, table_ref, pos_ref, logits_ref, rows_ref, lse_ref, total_ref, first_block):
    cluster_size = rows_ref.shape[0]
    pos_count = pos_ref.shape[1]
    block = table_ref[s, 1 + side]
    hit = target_of(pos_ref, block, table_ref[s, 0] * cluster_size, cluster_size)
    dlogit = jnp.exp(
        logits_ref[:, side * BLK : (side + 1) * BLK] - lse_ref[pl.ds(block, 1), :]
    ) - jnp.where(hit, 1.0 / pos_count, 0.0)
    total_ref[block - first_block] += lax.dot_general(
        dlogit.T.astype(jnp.bfloat16),
        rows_ref[...],
        (((1,), (0,)), ((), ())),
        preferred_element_type=jnp.float32,
    )


def half_kernel(side, groups, lab_count, table_ref, pos_ref, stats_ref, *rest):
    dp_count = groups[-1][-1] + 1
    logits_refs = rest[: len(groups)]
    rows = rest[len(groups) : len(groups) + dp_count]
    loss_ref, keep_ref, send_ref, lse_ref, total_ref = rest[len(groups) + dp_count :]
    lse, positive = row_sums(stats_ref, lab_count)
    lse_ref[...] = lse
    loss_ref[...] = lse - positive / pos_ref.shape[1]
    total_ref[...] = jnp.zeros_like(total_ref)
    half = total_ref.shape[0]
    for slots, logits_ref in zip(groups, logits_refs):
        for s in slots:
            add_slot(
                side,
                s,
                table_ref,
                pos_ref,
                logits_ref.at[s - slots[0]],
                rows[s],
                lse_ref,
                total_ref,
                side * half,
            )
    part = keep_ref.shape[2]
    lab_index = lax.axis_index("label")
    for j in range(lab_count // 2):
        mine = pl.ds(pl.multiple_of((lab_index ^ (2 * j)) * part, part), part)
        other = pl.ds(pl.multiple_of((lab_index ^ (2 * j + 1)) * part, part), part)
        for b in range(half):
            here = pl.ds(b * BLK, BLK)
            keep_ref[j, here, :] = total_ref[b, :, mine]
            send_ref[j, here, :] = total_ref[b, :, other].astype(jnp.bfloat16)


def pair_kernel(count, *refs):
    halves, outs = refs[: 2 * count], refs[2 * count :]
    for h in range(count):
        keep_ref, got_ref = halves[2 * h : 2 * h + 2]
        rows = pl.ds(h * keep_ref.shape[1], keep_ref.shape[1])
        for j, out_ref in enumerate(outs):
            total = keep_ref[j] + got_ref[j].astype(jnp.float32)
            out_ref[rows, :] = total.astype(out_ref.dtype)


def last_kernel(*refs):
    total = refs[0][...]
    for ref in refs[1:-1]:
        total = total + ref[...].astype(jnp.float32)
    refs[-1][...] = total.astype(jnp.bfloat16)


def grad_kernel(groups, lab_count, table_ref, pos_ref, stats_ref, *rest):
    dp_count = groups[-1][-1] + 1
    logits_refs = rest[: len(groups)]
    rows = rest[len(groups) : len(groups) + dp_count]
    loss_ref, out_ref, lse_ref, total_ref = rest[len(groups) + dp_count :]
    lse, positive = row_sums(stats_ref, lab_count)
    lse_ref[...] = lse
    loss_ref[...] = lse - positive / pos_ref.shape[1]
    total_ref[...] = jnp.zeros_like(total_ref)
    for slots, logits_ref in zip(groups, logits_refs):
        for s in slots:

            @pl.when(table_ref[s, 0] >= 0)
            def _(s=s, logits_ref=logits_ref.at[s - slots[0]]):
                for side in range(2):
                    add_slot(
                        side, s, table_ref, pos_ref, logits_ref, rows[s], lse_ref, total_ref, 0
                    )

    part = out_ref.shape[2]
    for j in range(lab_count):
        for b in range(total_ref.shape[0]):
            out_ref[j, b * BLK : (b + 1) * BLK, :] = total_ref[
                b, :, j * part : (j + 1) * part
            ].astype(jnp.bfloat16)


def smem():
    return pl.BlockSpec(memory_space=pltpu.SMEM)


def vmem():
    return pl.BlockSpec(memory_space=pltpu.VMEM)


def anywhere():
    return pl.BlockSpec(memory_space=pl.ANY)


def shards(feats, weights, shortlist, slot_of, positives):
    dp_count = lax.axis_size("dp")
    lab_count = lax.axis_size("label")
    stored, cluster_size, width = weights.shape
    inst_count = feats.shape[0]
    pos_count = positives.shape[1]
    block_count = inst_count // BLK
    short_count = shortlist.shape[1]
    params = pltpu.CompilerParams(vmem_limit_bytes=VMEM_BYTES)
    row_type = jax.ShapeDtypeStruct((cluster_size, width), weights.dtype)
    stat_shape = (3, block_count, BLK)

    sizes = (lab_count, stored, block_count, short_count)
    far = range(1, dp_count)
    far_rows = pl.pallas_call(
        functools.partial(far_kernel, sizes, far),
        out_shape=[row_type] * len(far),
        in_specs=[anywhere()] * 3,
        out_specs=[anywhere()] * len(far),
        scratch_shapes=[
            pltpu.VMEM(weights.shape, weights.dtype),
            pltpu.SMEM(shortlist.shape, jnp.int32),
            pltpu.SMEM(slot_of.shape, jnp.int32),
            pltpu.SemaphoreType.DMA((3 + len(far),)),
        ],
        compiler_params=pltpu.CompilerParams(vmem_limit_bytes=VMEM_PICK),
        name="pick_far",
    )(shortlist, slot_of, weights)
    table, *rows = pl.pallas_call(
        functools.partial(near_kernel, sizes),
        out_shape=[jax.ShapeDtypeStruct((dp_count, 4), jnp.int32)] + [row_type],
        in_specs=[smem(), smem(), anywhere()],
        out_specs=[smem(), vmem()],
        scratch_shapes=[pltpu.SemaphoreType.DMA((1,))],
        compiler_params=params,
        name="pick_near",
    )(shortlist, slot_of, weights)
    rows += far_rows
    def swap_dp(x, mask, core=None):
        pairs = [(i, i if core == 1 - (i & 1) else i ^ mask) for i in range(dp_count)]
        return lax.ppermute(x, "dp", pairs)

    rows[1] = swap_dp(rows[1], 1)
    if dp_count == 4:
        handed = swap_dp(rows[3], 1)
        straight = swap_dp(rows[2], 2, 0)
        crossed = swap_dp(handed, 2, 0)
        token = swap_dp(straight[:16, :128].astype(jnp.float32), 1)
        straight = pl.pallas_call(
            after_kernel,
            out_shape=row_type,
            in_specs=[anywhere(), anywhere()],
            out_specs=anywhere(),
            input_output_aliases={0: 0},
            compiler_params=params,
            name="after_token",
        )(straight, token)
        rows[2] = swap_dp(straight, 2, 1)
        rows[3] = swap_dp(crossed, 2, 1)
    else:
        for k in range(2, dp_count):
            rows[k] = swap_dp(rows[k], k)

    feat_blocks = feats.reshape(block_count, BLK, width)
    pos_blocks = positives.reshape(block_count, BLK, pos_count).transpose(0, 2, 1)
    cuts = (0, dp_count // 2, dp_count * 3 // 4, dp_count)
    groups = [tuple(range(a, b)) for a, b in zip(cuts[:-1], cuts[1:])]
    kept = []
    stats = []
    for slots in groups:
        count = len(slots)
        copies = lab_count if slots is groups[-1] else 1
        logits, stats_out = pl.pallas_call(
            functools.partial(logit_kernel, slots, copies),
            out_shape=[
                jax.ShapeDtypeStruct((count, cluster_size, 2 * BLK), jnp.float32),
                jax.ShapeDtypeStruct((copies,) + stat_shape, jnp.float32),
            ],
            in_specs=[smem()] + [vmem()] * (2 + count + len(stats)),
            out_specs=[vmem(), vmem()],
            scratch_shapes=[pltpu.VMEM(stat_shape, jnp.float32)],
            compiler_params=params,
            cost_estimate=pl.CostEstimate(
                flops=count * 4 * BLK * cluster_size * width,
                bytes_accessed=count * cluster_size * width * 2,
                transcendentals=0,
            ),
            name="logits",
        )(table, feat_blocks, pos_blocks, *[rows[s] for s in slots], *stats)
        kept.append(logits)
        stats = [stats_out]

    all_stats = lax.all_to_all(stats[0], "label", split_axis=0, concat_axis=0, tiled=True)
    part = width // lab_count
    in_specs = [smem()] + [vmem()] * (2 + len(groups) + dp_count)
    operands = (table, pos_blocks, all_stats, *kept, *rows)
    loss_type = jax.ShapeDtypeStruct((block_count, BLK), jnp.float32)
    lse_scratch = pltpu.VMEM((block_count, BLK), jnp.float32)
    if part % 128 or lab_count % 2:
        loss, parts = pl.pallas_call(
            functools.partial(grad_kernel, groups, lab_count),
            out_shape=[
                loss_type,
                jax.ShapeDtypeStruct((lab_count, inst_count, part), jnp.bfloat16),
            ],
            in_specs=in_specs,
            out_specs=[vmem(), vmem()],
            scratch_shapes=[lse_scratch, pltpu.VMEM((block_count, BLK, width), jnp.float32)],
            compiler_params=params,
            name="grads",
        )(*operands)
        gathered = lax.all_to_all(parts, "label", split_axis=0, concat_axis=0, tiled=True)
        grads = jnp.sum(gathered.astype(jnp.float32), axis=0).astype(jnp.bfloat16)
        return loss.reshape(inst_count), grads

    pairs = lab_count // 2
    half_rows = inst_count // 2
    halves = []
    for side in range(2):
        loss, keep, send = pl.pallas_call(
            functools.partial(half_kernel, side, groups, lab_count),
            out_shape=[
                loss_type,
                jax.ShapeDtypeStruct((pairs, half_rows, part), jnp.float32),
                jax.ShapeDtypeStruct((pairs, half_rows, part), jnp.bfloat16),
            ],
            in_specs=in_specs,
            out_specs=[vmem()] * 3,
            scratch_shapes=[lse_scratch, pltpu.VMEM((block_count // 2, BLK, width), jnp.float32)],
            compiler_params=params,
            cost_estimate=pl.CostEstimate(
                flops=dp_count * 2 * BLK * cluster_size * width,
                bytes_accessed=dp_count * cluster_size * width * 2,
                transcendentals=0,
            ),
            name="grads",
        )(*operands)
        halves += [keep, lax.ppermute(send, "label", [(i, i ^ 1) for i in range(lab_count)])]
    own, *outgoing = pl.pallas_call(
        functools.partial(pair_kernel, 2),
        out_shape=[jax.ShapeDtypeStruct((inst_count, part), jnp.float32)]
        + [jax.ShapeDtypeStruct((inst_count, part), jnp.bfloat16)] * (pairs - 1),
        in_specs=[vmem()] * 4,
        out_specs=[vmem()] * pairs,
        compiler_params=params,
        name="pair_sums",
    )(*halves)
    arrived = [
        lax.ppermute(x, "label", [(i, i ^ (2 * j + 2)) for i in range(lab_count)])
        for j, x in enumerate(outgoing)
    ]
    grads = pl.pallas_call(
        last_kernel,
        out_shape=jax.ShapeDtypeStruct((inst_count, part), jnp.bfloat16),
        in_specs=[vmem()] * pairs,
        out_specs=vmem(),
        compiler_params=params,
        name="last_sums",
    )(own, *arrived)
    return loss.reshape(inst_count), grads


def solution(mesh):
    in_specs = (P("dp", None), P(("dp", "label"), None, None), P(), P(), P("dp", None))
    out_specs = (P("dp"), P("dp", "label"))
    return jax.shard_map(shards, mesh=mesh, in_specs=in_specs, out_specs=out_specs, check_vma=False)
```

```python
import functools

import jax
import jax.numpy as jnp
from jax import lax
from jax.experimental import pallas as pl
from jax.experimental.pallas import tpu as pltpu
from jax.sharding import PartitionSpec as P

BLK = 128
NEG_FILL = -1e30
VMEM_BYTES = 32 * 1024 * 1024
VMEM_PICK = 56 * 1024 * 1024


def divide(value, by):
    if by & (by - 1) == 0:
        return lax.shift_right_logical(value, jnp.int32(by.bit_length() - 1))
    return lax.div(value, jnp.int32(by))


def remainder(value, by):
    if by & (by - 1) == 0:
        return value & jnp.int32(by - 1)
    return lax.rem(value, jnp.int32(by))


def each_entry(count, short_count, body, carry):
    if count <= 64:
        for e in range(count):
            carry = body(e // short_count, e % short_count, carry)
        return carry
    step = lambda e, c: body(divide(e, short_count), remainder(e, short_count), c)
    return lax.fori_loop(0, count, step, carry)


def find_slots(sizes, wanted, lists_ref, slot_ref):
    lab_count, stored, block_count, short_count = sizes
    dp_index, lab_index = lax.axis_index("dp"), lax.axis_index("label")
    mine = dp_index * lab_count + lab_index
    found = []
    for k in wanted:
        base = (dp_index ^ k) * block_count

        def look(row, column, slot_here, base=base):
            slot = slot_ref[lists_ref[base + row, column]]
            return jnp.where(divide(slot, stored) == mine, remainder(slot, stored), slot_here)

        count = block_count // 2 * short_count
        found.append(each_entry(count, short_count, look, jnp.int32(0)))
    return found


def far_kernel(sizes, wanted, lists_hbm, slot_hbm, weights_ref, *rest):
    outs = rest[: len(wanted)]
    held, lists_ref, slot_ref, sems = rest[len(wanted) :]
    tables = [
        pltpu.make_async_copy(lists_hbm, lists_ref, sems.at[0]),
        pltpu.make_async_copy(slot_hbm, slot_ref, sems.at[1]),
    ]
    stage = pltpu.make_async_copy(weights_ref, held, sems.at[2])
    for copy in tables:
        copy.start()
    stage.start()
    for copy in tables:
        copy.wait()
    found = find_slots(sizes, wanted, lists_ref, slot_ref)
    stage.wait()
    copies = []
    for i, slot in enumerate(found):
        copies.append(pltpu.make_async_copy(held.at[slot], outs[i], sems.at[3 + i]))
        copies[-1].start()
    for copy in copies:
        copy.wait()


def near_kernel(sizes, lists_ref, slot_ref, weights_ref, table_ref, *rest):
    lab_count, stored, block_count, short_count = sizes
    outs, sems = rest[:-1], rest[-1]
    copies = []
    for k, slot in enumerate(find_slots(sizes, range(1), lists_ref, slot_ref)):
        copies.append(pltpu.make_async_copy(weights_ref.at[slot], outs[k], sems.at[k]))
        copies[-1].start()
    dp_index, lab_index = lax.axis_index("dp"), lax.axis_index("label")
    half = block_count // 2
    for side in range(2):

        def note(row, column, carry, side=side):
            block = side * half + row
            cluster = lists_ref[dp_index * block_count + block, column]
            device = divide(slot_ref[cluster], stored)

            @pl.when(remainder(device, lab_count) == lab_index)
            def _():
                entry = divide(device, lab_count) ^ dp_index
                table_ref[entry, 0] = cluster
                table_ref[entry, 1 + side] = jnp.int32(block)

            return carry

        each_entry(half * short_count, short_count, note, jnp.int32(0))
    for copy in copies:
        copy.wait()


def target_kernel(early, table_ref, pos_ref, hits_ref, shares_ref):
    count, cluster_size, _ = hits_ref.shape
    pos_count = pos_ref.shape[1]

    def one_slot(s):
        labels = lax.broadcasted_iota(jnp.int32, (cluster_size, BLK), 0) + table_ref[s, 0] * cluster_size
        for side in range(2):
            pos = pos_ref[table_ref[s, 1 + side]]
            hit = pos[0:1, :] == labels
            for p in range(1, pos_count):
                hit = hit | (pos[p : p + 1, :] == labels)
            hits = jnp.where(hit, 1.0, 0.0)
            columns = pl.ds(side * BLK, BLK)
            hits_ref[s, :, columns] = hits
            if s in early:
                shares_ref[early.index(s), columns, :] = (hits / pos_count).T

    for s in range(count):
        pl.when(table_ref[s, 0] >= 0)(functools.partial(one_slot, s))


def logit_kernel(slots, turned, copies, table_ref, feats_ref, hits_ref, *rest):
    count = len(slots)
    rows = rest[:count]
    logits_ref, out_ref, stats_ref = rest[-3:]
    if len(rest) == count + 3:
        stats_ref[0] = jnp.full(stats_ref.shape[1:], NEG_FILL, jnp.float32)
        stats_ref[1] = jnp.zeros(stats_ref.shape[1:], jnp.float32)
        stats_ref[2] = jnp.zeros(stats_ref.shape[1:], jnp.float32)
    else:
        stats_ref[...] = rest[count][0]
    for i, (s, ref) in enumerate(zip(slots, rows)):
        for side in range(2):
            block = table_ref[s, 1 + side]
            logits = lax.dot_general(
                ref[...],
                feats_ref[block],
                (((1,), (1,)), ((), ())),
                preferred_element_type=jnp.float32,
            )
            columns = pl.ds(side * BLK, BLK)
            if turned:
                logits_ref[i, columns, :] = logits.T
            else:
                logits_ref[i, :, columns] = logits
            highest = jnp.max(logits, axis=0, keepdims=True)
            total = jnp.sum(jnp.exp(logits - highest), axis=0, keepdims=True)
            positive = jnp.sum(hits_ref[s, :, columns] * logits, axis=0, keepdims=True)
            row = pl.ds(block, 1)
            before = stats_ref[0, row, :]
            after = jnp.maximum(before, highest)
            stats_ref[0, row, :] = after
            stats_ref[1, row, :] = stats_ref[1, row, :] * jnp.exp(before - after) + total * jnp.exp(
                highest - after
            )
            stats_ref[2, row, :] = stats_ref[2, row, :] + positive
    for i in range(copies):
        out_ref[i] = stats_ref[...]


def row_sums(stats_ref, lab_count):
    highest = stats_ref[0, 0]
    for i in range(1, lab_count):
        highest = jnp.maximum(highest, stats_ref[i, 0])
    summed = jnp.zeros_like(highest)
    positive = jnp.zeros_like(highest)
    for i in range(lab_count):
        summed = summed + stats_ref[i, 1] * jnp.exp(stats_ref[i, 0] - highest)
        positive = positive + stats_ref[i, 2]
    return highest + jnp.log(summed), positive


def prepare(stats_ref, pos_count, lab_count, loss_ref, lse_ref, columns_ref, total_ref, first):
    lse, positive = row_sums(stats_ref, lab_count)
    lse_ref[...] = lse
    loss_ref[...] = lse - positive / pos_count
    for b in range(columns_ref.shape[0]):
        columns_ref[b] = jnp.broadcast_to(lse[first + b : first + b + 1, :], (BLK, BLK)).T
    total_ref[...] = jnp.zeros_like(total_ref)


def add_slots(sides, groups, pos_count, first, table_ref, hits_ref, shares_ref, logits_refs, rows, sums):
    lse_ref, columns_ref, total_ref = sums
    early = [s for slots in groups[:-1] for s in slots]
    cluster_size = rows[0].shape[0]

    def one_slot(s, logits_ref):
        for side in sides:
            block = table_ref[s, 1 + side]
            here = pl.ds(side * BLK, BLK)
            if s in early:
                column = columns_ref[block - first]
                column = jnp.concatenate([column] * (cluster_size // BLK), axis=1)
                dlogit = jnp.exp(logits_ref[here, :] - column) - shares_ref[early.index(s), here, :]
            else:
                row = lse_ref[pl.ds(block, 1), :]
                dlogit = jnp.exp(logits_ref[:, here] - row) - hits_ref[s, :, here] / pos_count
                dlogit = dlogit.T
            total_ref[block - first] += lax.dot_general(
                dlogit.astype(jnp.bfloat16),
                rows[s][...],
                (((1,), (0,)), ((), ())),
                preferred_element_type=jnp.float32,
            )

    for slots, logits_ref in zip(groups, logits_refs):
        for i, s in enumerate(slots):
            body = functools.partial(one_slot, s, logits_ref.at[i])
            if len(rows) <= 4:
                body()
            else:
                pl.when(table_ref[s, 0] >= 0)(body)


def half_kernel(side, groups, lab_count, pos_count, table_ref, hits_ref, shares_ref, stats_ref, *rest):
    logits_refs = rest[: len(groups)]
    rows = rest[len(groups) : -6]
    loss_ref, keep_ref, send_ref, lse_ref, columns_ref, total_ref = rest[-6:]
    half = total_ref.shape[0]
    prepare(
        stats_ref, pos_count, lab_count, loss_ref, lse_ref, columns_ref, total_ref, side * half
    )
    add_slots(
        (side,),
        groups,
        pos_count,
        side * half,
        table_ref,
        hits_ref,
        shares_ref,
        logits_refs,
        rows,
        (lse_ref, columns_ref, total_ref),
    )
    part = keep_ref.shape[2]
    lab_index = lax.axis_index("label")
    for j in range(lab_count // 2):
        mine = pl.ds(pl.multiple_of((lab_index ^ (2 * j)) * part, part), part)
        other = pl.ds(pl.multiple_of((lab_index ^ (2 * j + 1)) * part, part), part)
        for b in range(half):
            here = pl.ds(b * BLK, BLK)
            keep_ref[j, here, :] = total_ref[b, :, mine]
            send_ref[j, here, :] = total_ref[b, :, other].astype(jnp.bfloat16)


def pair_kernel(keep_ref, got_ref, *outs):
    outs[0][...] = keep_ref[0] + got_ref[0].astype(jnp.float32)
    for j in range(1, len(outs)):
        outs[j][...] = (keep_ref[j] + got_ref[j].astype(jnp.float32)).astype(jnp.bfloat16)


def last_kernel(count, *refs):
    out_ref = refs[-1]
    for h in range(len(refs[:-1]) // count):
        total = refs[h * count][...]
        for ref in refs[h * count + 1 : (h + 1) * count]:
            total = total + ref[...].astype(jnp.float32)
        rows = total.shape[0]
        out_ref[h * rows : (h + 1) * rows, :] = total.astype(jnp.bfloat16)


def grad_kernel(groups, lab_count, pos_count, table_ref, hits_ref, shares_ref, stats_ref, *rest):
    logits_refs = rest[: len(groups)]
    rows = rest[len(groups) : -5]
    loss_ref, out_ref, lse_ref, columns_ref, total_ref = rest[-5:]
    prepare(stats_ref, pos_count, lab_count, loss_ref, lse_ref, columns_ref, total_ref, 0)
    add_slots(
        (0, 1),
        groups,
        pos_count,
        0,
        table_ref,
        hits_ref,
        shares_ref,
        logits_refs,
        rows,
        (lse_ref, columns_ref, total_ref),
    )
    part = out_ref.shape[2]
    for j in range(lab_count):
        for b in range(total_ref.shape[0]):
            out_ref[j, b * BLK : (b + 1) * BLK, :] = total_ref[
                b, :, j * part : (j + 1) * part
            ].astype(jnp.bfloat16)


def smem():
    return pl.BlockSpec(memory_space=pltpu.SMEM)


def vmem():
    return pl.BlockSpec(memory_space=pltpu.VMEM)


def anywhere():
    return pl.BlockSpec(memory_space=pl.ANY)


def shards(feats, weights, shortlist, slot_of, positives):
    dp_count = lax.axis_size("dp")
    lab_count = lax.axis_size("label")
    stored, cluster_size, width = weights.shape
    inst_count = feats.shape[0]
    pos_count = positives.shape[1]
    block_count = inst_count // BLK
    short_count = shortlist.shape[1]
    params = pltpu.CompilerParams(vmem_limit_bytes=VMEM_BYTES)
    row_type = jax.ShapeDtypeStruct((cluster_size, width), weights.dtype)
    stat_shape = (3, block_count, BLK)

    sizes = (lab_count, stored, block_count, short_count)
    far = range(1, dp_count)
    far_rows = pl.pallas_call(
        functools.partial(far_kernel, sizes, far),
        out_shape=[row_type] * len(far),
        in_specs=[anywhere()] * 3,
        out_specs=[anywhere()] * len(far),
        scratch_shapes=[
            pltpu.VMEM(weights.shape, weights.dtype),
            pltpu.SMEM(shortlist.shape, jnp.int32),
            pltpu.SMEM(slot_of.shape, jnp.int32),
            pltpu.SemaphoreType.DMA((3 + len(far),)),
        ],
        compiler_params=pltpu.CompilerParams(vmem_limit_bytes=VMEM_PICK),
        name="pick_far",
    )(shortlist, slot_of, weights)
    table, *rows = pl.pallas_call(
        functools.partial(near_kernel, sizes),
        out_shape=[jax.ShapeDtypeStruct((dp_count, 4), jnp.int32)] + [row_type],
        in_specs=[smem(), smem(), anywhere()],
        out_specs=[smem(), vmem()],
        scratch_shapes=[pltpu.SemaphoreType.DMA((1,))],
        compiler_params=params,
        name="pick_near",
    )(shortlist, slot_of, weights)
    rows += far_rows
    for k in range(1, dp_count):
        rows[k] = lax.ppermute(rows[k], "dp", [(i, i ^ k) for i in range(dp_count)])

    feat_blocks = feats.reshape(block_count, BLK, width)
    pos_blocks = positives.reshape(block_count, BLK, pos_count).transpose(0, 2, 1)
    cuts = (0, dp_count // 2, dp_count * 3 // 4, dp_count)
    groups = [tuple(range(a, b)) for a, b in zip(cuts[:-1], cuts[1:])]
    if dp_count == 4:
        groups = [(2,), (0, 1), (3,)]
    early = [s for slots in groups[:-1] for s in slots]
    hits, shares = pl.pallas_call(
        functools.partial(target_kernel, early),
        out_shape=[
            jax.ShapeDtypeStruct((dp_count, cluster_size, 2 * BLK), jnp.float32),
            jax.ShapeDtypeStruct((len(early), 2 * BLK, cluster_size), jnp.float32),
        ],
        in_specs=[smem(), vmem()],
        out_specs=[vmem()] * 2,
        compiler_params=params,
        name="targets",
    )(table, pos_blocks)
    kept = []
    stats = []
    for slots in groups:
        count = len(slots)
        last = slots is groups[-1]
        copies = lab_count if last else 1
        shape = (cluster_size, 2 * BLK) if last else (2 * BLK, cluster_size)
        logits, stats_out = pl.pallas_call(
            functools.partial(logit_kernel, slots, not last, copies),
            out_shape=[
                jax.ShapeDtypeStruct((count,) + shape, jnp.float32),
                jax.ShapeDtypeStruct((copies,) + stat_shape, jnp.float32),
            ],
            in_specs=[smem()] + [vmem()] * (2 + count + len(stats)),
            out_specs=[vmem(), vmem()],
            scratch_shapes=[pltpu.VMEM(stat_shape, jnp.float32)],
            compiler_params=params,
            cost_estimate=pl.CostEstimate(
                flops=count * 4 * BLK * cluster_size * width,
                bytes_accessed=count * cluster_size * width * 2,
                transcendentals=0,
            ),
            name="logits",
        )(table, feat_blocks, hits, *[rows[s] for s in slots], *stats)
        kept.append(logits)
        stats = [stats_out]

    all_stats = lax.all_to_all(stats[0], "label", split_axis=0, concat_axis=0, tiled=True)
    part = width // lab_count
    in_specs = [smem()] + [vmem()] * (3 + len(groups) + dp_count)
    operands = (table, hits, shares, all_stats, *kept, *rows)
    loss_type = jax.ShapeDtypeStruct((block_count, BLK), jnp.float32)
    lse_scratch = pltpu.VMEM((block_count, BLK), jnp.float32)
    if part % 128 or lab_count % 2:
        loss, parts = pl.pallas_call(
            functools.partial(grad_kernel, groups, lab_count, pos_count),
            out_shape=[
                loss_type,
                jax.ShapeDtypeStruct((lab_count, inst_count, part), jnp.bfloat16),
            ],
            in_specs=in_specs,
            out_specs=[vmem(), vmem()],
            scratch_shapes=[
                lse_scratch,
                pltpu.VMEM((block_count, BLK, BLK), jnp.float32),
                pltpu.VMEM((block_count, BLK, width), jnp.float32),
            ],
            compiler_params=params,
            name="grads",
        )(*operands)
        gathered = lax.all_to_all(parts, "label", split_axis=0, concat_axis=0, tiled=True)
        grads = jnp.sum(gathered.astype(jnp.float32), axis=0).astype(jnp.bfloat16)
        return loss.reshape(inst_count), grads

    pairs = lab_count // 2
    half_rows = inst_count // 2
    finals = []
    for side in range(2):
        loss, keep, send = pl.pallas_call(
            functools.partial(half_kernel, side, groups, lab_count, pos_count),
            out_shape=[
                loss_type,
                jax.ShapeDtypeStruct((pairs, half_rows, part), jnp.float32),
                jax.ShapeDtypeStruct((pairs, half_rows, part), jnp.bfloat16),
            ],
            in_specs=in_specs,
            out_specs=[vmem()] * 3,
            scratch_shapes=[
                lse_scratch,
                pltpu.VMEM((block_count // 2, BLK, BLK), jnp.float32),
                pltpu.VMEM((block_count // 2, BLK, width), jnp.float32),
            ],
            compiler_params=params,
            cost_estimate=pl.CostEstimate(
                flops=dp_count * 2 * BLK * cluster_size * width,
                bytes_accessed=dp_count * cluster_size * width * 2,
                transcendentals=0,
            ),
            name="grads",
        )(*operands)
        if side:
            send, got = lax.optimization_barrier((send, got))
        got = lax.ppermute(send, "label", [(i, i ^ 1) for i in range(lab_count)])
        own, *outgoing = pl.pallas_call(
            pair_kernel,
            out_shape=[jax.ShapeDtypeStruct((half_rows, part), jnp.float32)]
            + [jax.ShapeDtypeStruct((half_rows, part), jnp.bfloat16)] * (pairs - 1),
            in_specs=[vmem()] * 2,
            out_specs=[vmem()] * pairs,
            compiler_params=params,
            name="pair_sums",
        )(keep, got)
        finals.append(own)
        for j in range(1, pairs):
            hop = [(i, i ^ (2 * j)) for i in range(lab_count)]
            finals.append(lax.ppermute(outgoing[j - 1], "label", hop))
    grads = pl.pallas_call(
        functools.partial(last_kernel, pairs),
        out_shape=jax.ShapeDtypeStruct((inst_count, part), jnp.bfloat16),
        in_specs=[vmem()] * (2 * pairs),
        out_specs=vmem(),
        compiler_params=params,
        name="last_sums",
    )(*finals)
    return loss.reshape(inst_count), grads


def solution(mesh):
    in_specs = (P("dp", None), P(("dp", "label"), None, None), P(), P(), P("dp", None))
    out_specs = (P("dp"), P("dp", "label"))
    return jax.shard_map(shards, mesh=mesh, in_specs=in_specs, out_specs=out_specs, check_vma=False)
```

```python
import functools

import jax
import jax.numpy as jnp
from jax import lax
from jax.experimental import pallas as pl
from jax.experimental.pallas import tpu as pltpu
from jax.sharding import PartitionSpec as P

BLK = 128
NEG_FILL = -1e30
VMEM_BYTES = 32 * 1024 * 1024
VMEM_PICK = 56 * 1024 * 1024


def divide(value, by):
    if by & (by - 1) == 0:
        return lax.shift_right_logical(value, jnp.int32(by.bit_length() - 1))
    return lax.div(value, jnp.int32(by))


def remainder(value, by):
    if by & (by - 1) == 0:
        return value & jnp.int32(by - 1)
    return lax.rem(value, jnp.int32(by))


def each_entry(count, short_count, body, carry):
    if count <= 64:
        for e in range(count):
            carry = body(e // short_count, e % short_count, carry)
        return carry
    step = lambda e, c: body(divide(e, short_count), remainder(e, short_count), c)
    return lax.fori_loop(0, count, step, carry)


def find_slots(sizes, wanted, lists_ref, slot_ref):
    lab_count, stored, block_count, short_count = sizes
    dp_index, lab_index = lax.axis_index("dp"), lax.axis_index("label")
    mine = dp_index * lab_count + lab_index
    found = []
    for k in wanted:
        base = (dp_index ^ k) * block_count

        def look(row, column, slot_here, base=base):
            slot = slot_ref[lists_ref[base + row, column]]
            return jnp.where(divide(slot, stored) == mine, remainder(slot, stored), slot_here)

        count = block_count // 2 * short_count
        found.append(each_entry(count, short_count, look, jnp.int32(0)))
    return found


def far_kernel(sizes, wanted, lists_hbm, slot_hbm, weights_ref, *rest):
    outs = rest[: len(wanted)]
    held, lists_ref, slot_ref, sems = rest[len(wanted) :]
    tables = [
        pltpu.make_async_copy(lists_hbm, lists_ref, sems.at[0]),
        pltpu.make_async_copy(slot_hbm, slot_ref, sems.at[1]),
    ]
    stage = pltpu.make_async_copy(weights_ref, held, sems.at[2])
    for copy in tables:
        copy.start()
    stage.start()
    for copy in tables:
        copy.wait()
    found = find_slots(sizes, wanted, lists_ref, slot_ref)
    stage.wait()
    copies = []
    for i, slot in enumerate(found):
        copies.append(pltpu.make_async_copy(held.at[slot], outs[i], sems.at[3 + i]))
        copies[-1].start()
    for copy in copies:
        copy.wait()


def near_kernel(sizes, lists_ref, slot_ref, weights_ref, table_ref, *rest):
    lab_count, stored, block_count, short_count = sizes
    outs, sems = rest[:-1], rest[-1]
    copies = []
    for k, slot in enumerate(find_slots(sizes, range(1), lists_ref, slot_ref)):
        copies.append(pltpu.make_async_copy(weights_ref.at[slot], outs[k], sems.at[k]))
        copies[-1].start()
    dp_index, lab_index = lax.axis_index("dp"), lax.axis_index("label")
    half = block_count // 2
    for side in range(2):

        def note(row, column, carry, side=side):
            block = side * half + row
            cluster = lists_ref[dp_index * block_count + block, column]
            device = divide(slot_ref[cluster], stored)

            @pl.when(remainder(device, lab_count) == lab_index)
            def _():
                entry = divide(device, lab_count) ^ dp_index
                table_ref[entry, 0] = cluster
                table_ref[entry, 1 + side] = jnp.int32(block)

            return carry

        each_entry(half * short_count, short_count, note, jnp.int32(0))
    for copy in copies:
        copy.wait()


def target_kernel(early, table_ref, pos_ref, hits_ref, shares_ref):
    count, cluster_size, _ = hits_ref.shape
    pos_count = pos_ref.shape[1]

    def one_slot(s):
        labels = lax.broadcasted_iota(jnp.int32, (cluster_size, BLK), 0) + table_ref[s, 0] * cluster_size
        for side in range(2):
            pos = pos_ref[table_ref[s, 1 + side]]
            hit = pos[0:1, :] == labels
            for p in range(1, pos_count):
                hit = hit | (pos[p : p + 1, :] == labels)
            hits = jnp.where(hit, 1.0, 0.0)
            columns = pl.ds(side * BLK, BLK)
            hits_ref[s, :, columns] = hits
            if s in early:
                shares_ref[early.index(s), columns, :] = (hits / pos_count).T

    for s in range(count):
        pl.when(table_ref[s, 0] >= 0)(functools.partial(one_slot, s))


def logit_kernel(slots, turned, copies, table_ref, feats_ref, hits_ref, *rest):
    count = len(slots)
    rows = rest[:count]
    logits_ref, out_ref, stats_ref = rest[-3:]
    if len(rest) == count + 3:
        stats_ref[0] = jnp.full(stats_ref.shape[1:], NEG_FILL, jnp.float32)
        stats_ref[1] = jnp.zeros(stats_ref.shape[1:], jnp.float32)
        stats_ref[2] = jnp.zeros(stats_ref.shape[1:], jnp.float32)
    else:
        stats_ref[...] = rest[count][0]
    for i, (s, ref) in enumerate(zip(slots, rows)):
        for side in range(2):
            block = table_ref[s, 1 + side]
            logits = lax.dot_general(
                ref[...],
                feats_ref[block],
                (((1,), (1,)), ((), ())),
                preferred_element_type=jnp.float32,
            )
            columns = pl.ds(side * BLK, BLK)
            if turned:
                logits_ref[i, columns, :] = logits.T
            else:
                logits_ref[i, :, columns] = logits
            highest = jnp.max(logits, axis=0, keepdims=True)
            total = jnp.sum(jnp.exp(logits - highest), axis=0, keepdims=True)
            positive = jnp.sum(hits_ref[s, :, columns] * logits, axis=0, keepdims=True)
            row = pl.ds(block, 1)
            before = stats_ref[0, row, :]
            after = jnp.maximum(before, highest)
            stats_ref[0, row, :] = after
            stats_ref[1, row, :] = stats_ref[1, row, :] * jnp.exp(before - after) + total * jnp.exp(
                highest - after
            )
            stats_ref[2, row, :] = stats_ref[2, row, :] + positive
    for i in range(copies):
        out_ref[i] = stats_ref[...]


def row_sums(stats_ref, lab_count):
    highest = stats_ref[0, 0]
    for i in range(1, lab_count):
        highest = jnp.maximum(highest, stats_ref[i, 0])
    summed = jnp.zeros_like(highest)
    positive = jnp.zeros_like(highest)
    for i in range(lab_count):
        summed = summed + stats_ref[i, 1] * jnp.exp(stats_ref[i, 0] - highest)
        positive = positive + stats_ref[i, 2]
    return highest + jnp.log(summed), positive


def prepare(stats_ref, pos_count, lab_count, loss_ref, lse_ref, columns_ref, total_ref, first):
    lse, positive = row_sums(stats_ref, lab_count)
    lse_ref[...] = lse
    loss_ref[...] = lse - positive / pos_count
    for b in range(columns_ref.shape[0]):
        columns_ref[b] = jnp.broadcast_to(lse[first + b : first + b + 1, :], (BLK, BLK)).T
    total_ref[...] = jnp.zeros_like(total_ref)


def add_slots(sides, groups, pos_count, first, table_ref, hits_ref, shares_ref, logits_refs, rows, sums):
    lse_ref, columns_ref, total_ref = sums
    early = [s for slots in groups[:-1] for s in slots]
    cluster_size = rows[0].shape[0]

    def one_slot(s, logits_ref):
        for side in sides:
            block = table_ref[s, 1 + side]
            here = pl.ds(side * BLK, BLK)
            if s in early:
                column = columns_ref[block - first]
                column = jnp.concatenate([column] * (cluster_size // BLK), axis=1)
                dlogit = jnp.exp(logits_ref[here, :] - column) - shares_ref[early.index(s), here, :]
            else:
                row = lse_ref[pl.ds(block, 1), :]
                dlogit = jnp.exp(logits_ref[:, here] - row) - hits_ref[s, :, here] / pos_count
                dlogit = dlogit.T
            total_ref[block - first] += lax.dot_general(
                dlogit.astype(jnp.bfloat16),
                rows[s][...],
                (((1,), (0,)), ((), ())),
                preferred_element_type=jnp.float32,
            )

    for slots, logits_ref in zip(groups, logits_refs):
        for i, s in enumerate(slots):
            body = functools.partial(one_slot, s, logits_ref.at[i])
            if len(rows) <= 4:
                body()
            else:
                pl.when(table_ref[s, 0] >= 0)(body)


def half_kernel(side, groups, lab_count, pos_count, table_ref, hits_ref, shares_ref, stats_ref, *rest):
    logits_refs = rest[: len(groups)]
    dp_count = sum(len(slots) for slots in groups)
    rows = rest[len(groups) : len(groups) + dp_count]
    loss_ref, keep_ref, *send_refs, lse_ref, columns_ref, total_ref = rest[len(groups) + dp_count :]
    half = total_ref.shape[0]
    prepare(
        stats_ref, pos_count, lab_count, loss_ref, lse_ref, columns_ref, total_ref, side * half
    )
    add_slots(
        (side,),
        groups,
        pos_count,
        side * half,
        table_ref,
        hits_ref,
        shares_ref,
        logits_refs,
        rows,
        (lse_ref, columns_ref, total_ref),
    )
    part = keep_ref.shape[2]
    lab_index = lax.axis_index("label")

    def cut(ref, i, offset):
        features = pl.ds(pl.multiple_of((lab_index ^ offset) * part, part), part)
        for b in range(half):
            ref[i, b * BLK : (b + 1) * BLK, :] = total_ref[b, :, features].astype(ref.dtype)

    if side == 0:
        for j in range(lab_count // 2):
            cut(keep_ref, j, 2 * j)
            cut(send_refs[0], j, 2 * j + 1)
    else:
        for x in range(2):
            cut(keep_ref, x, x)
            for j, ref in enumerate(send_refs):
                cut(ref, x, 2 * j + 2 + x)


def pair_kernel(keep_ref, got_ref, *outs):
    for j, out_ref in enumerate(outs):
        out_ref[...] = (keep_ref[j] + got_ref[j].astype(jnp.float32)).astype(out_ref.dtype)


def line_kernel(keep_ref, *refs):
    for x, out_ref in enumerate(refs[-2:]):
        total = keep_ref[x]
        for ref in refs[:-2]:
            total = total + ref[x].astype(jnp.float32)
        out_ref[...] = total.astype(out_ref.dtype)


def last_kernel(count, *refs):
    out_ref = refs[-1]
    at = 0
    for parts in (refs[:count], refs[count:-1]):
        total = parts[0][...]
        for ref in parts[1:]:
            total = total + ref[...].astype(jnp.float32)
        out_ref[at : at + total.shape[0], :] = total.astype(jnp.bfloat16)
        at += total.shape[0]


def grad_kernel(groups, lab_count, pos_count, table_ref, hits_ref, shares_ref, stats_ref, *rest):
    logits_refs = rest[: len(groups)]
    rows = rest[len(groups) : -5]
    loss_ref, out_ref, lse_ref, columns_ref, total_ref = rest[-5:]
    prepare(stats_ref, pos_count, lab_count, loss_ref, lse_ref, columns_ref, total_ref, 0)
    add_slots(
        (0, 1),
        groups,
        pos_count,
        0,
        table_ref,
        hits_ref,
        shares_ref,
        logits_refs,
        rows,
        (lse_ref, columns_ref, total_ref),
    )
    part = out_ref.shape[2]
    for j in range(lab_count):
        for b in range(total_ref.shape[0]):
            out_ref[j, b * BLK : (b + 1) * BLK, :] = total_ref[
                b, :, j * part : (j + 1) * part
            ].astype(jnp.bfloat16)


def smem():
    return pl.BlockSpec(memory_space=pltpu.SMEM)


def vmem():
    return pl.BlockSpec(memory_space=pltpu.VMEM)


def anywhere():
    return pl.BlockSpec(memory_space=pl.ANY)


def shards(feats, weights, shortlist, slot_of, positives):
    dp_count = lax.axis_size("dp")
    lab_count = lax.axis_size("label")
    stored, cluster_size, width = weights.shape
    inst_count = feats.shape[0]
    pos_count = positives.shape[1]
    block_count = inst_count // BLK
    short_count = shortlist.shape[1]
    params = pltpu.CompilerParams(vmem_limit_bytes=VMEM_BYTES)
    row_type = jax.ShapeDtypeStruct((cluster_size, width), weights.dtype)
    stat_shape = (3, block_count, BLK)

    sizes = (lab_count, stored, block_count, short_count)
    far = range(1, dp_count)
    far_rows = pl.pallas_call(
        functools.partial(far_kernel, sizes, far),
        out_shape=[row_type] * len(far),
        in_specs=[anywhere()] * 3,
        out_specs=[anywhere()] * len(far),
        scratch_shapes=[
            pltpu.VMEM(weights.shape, weights.dtype),
            pltpu.SMEM(shortlist.shape, jnp.int32),
            pltpu.SMEM(slot_of.shape, jnp.int32),
            pltpu.SemaphoreType.DMA((3 + len(far),)),
        ],
        compiler_params=pltpu.CompilerParams(vmem_limit_bytes=VMEM_PICK),
        name="pick_far",
    )(shortlist, slot_of, weights)
    table, *rows = pl.pallas_call(
        functools.partial(near_kernel, sizes),
        out_shape=[jax.ShapeDtypeStruct((dp_count, 4), jnp.int32)] + [row_type],
        in_specs=[smem(), smem(), anywhere()],
        out_specs=[smem(), vmem()],
        scratch_shapes=[pltpu.SemaphoreType.DMA((1,))],
        compiler_params=params,
        name="pick_near",
    )(shortlist, slot_of, weights)
    rows += far_rows
    for k in range(1, dp_count):
        rows[k] = lax.ppermute(rows[k], "dp", [(i, i ^ k) for i in range(dp_count)])

    feat_blocks = feats.reshape(block_count, BLK, width)
    pos_blocks = positives.reshape(block_count, BLK, pos_count).transpose(0, 2, 1)
    cuts = (0, dp_count // 2, dp_count * 3 // 4, dp_count)
    groups = [tuple(range(a, b)) for a, b in zip(cuts[:-1], cuts[1:])]
    if dp_count == 4:
        groups = [(2,), (0, 1), (3,)]
    early = [s for slots in groups[:-1] for s in slots]
    hits, shares = pl.pallas_call(
        functools.partial(target_kernel, early),
        out_shape=[
            jax.ShapeDtypeStruct((dp_count, cluster_size, 2 * BLK), jnp.float32),
            jax.ShapeDtypeStruct((len(early), 2 * BLK, cluster_size), jnp.float32),
        ],
        in_specs=[smem(), vmem()],
        out_specs=[vmem()] * 2,
        compiler_params=params,
        name="targets",
    )(table, pos_blocks)
    kept = []
    stats = []
    for slots in groups:
        count = len(slots)
        last = slots is groups[-1]
        copies = lab_count if last else 1
        shape = (cluster_size, 2 * BLK) if last else (2 * BLK, cluster_size)
        logits, stats_out = pl.pallas_call(
            functools.partial(logit_kernel, slots, not last, copies),
            out_shape=[
                jax.ShapeDtypeStruct((count,) + shape, jnp.float32),
                jax.ShapeDtypeStruct((copies,) + stat_shape, jnp.float32),
            ],
            in_specs=[smem()] + [vmem()] * (2 + count + len(stats)),
            out_specs=[vmem(), vmem()],
            scratch_shapes=[pltpu.VMEM(stat_shape, jnp.float32)],
            compiler_params=params,
            cost_estimate=pl.CostEstimate(
                flops=count * 4 * BLK * cluster_size * width,
                bytes_accessed=count * cluster_size * width * 2,
                transcendentals=0,
            ),
            name="logits",
        )(table, feat_blocks, hits, *[rows[s] for s in slots], *stats)
        kept.append(logits)
        stats = [stats_out]

    all_stats = lax.all_to_all(stats[0], "label", split_axis=0, concat_axis=0, tiled=True)
    part = width // lab_count
    in_specs = [smem()] + [vmem()] * (3 + len(groups) + dp_count)
    operands = (table, hits, shares, all_stats, *kept, *rows)
    loss_type = jax.ShapeDtypeStruct((block_count, BLK), jnp.float32)
    lse_scratch = pltpu.VMEM((block_count, BLK), jnp.float32)
    if part % 128 or lab_count % 2:
        loss, parts = pl.pallas_call(
            functools.partial(grad_kernel, groups, lab_count, pos_count),
            out_shape=[
                loss_type,
                jax.ShapeDtypeStruct((lab_count, inst_count, part), jnp.bfloat16),
            ],
            in_specs=in_specs,
            out_specs=[vmem(), vmem()],
            scratch_shapes=[
                lse_scratch,
                pltpu.VMEM((block_count, BLK, BLK), jnp.float32),
                pltpu.VMEM((block_count, BLK, width), jnp.float32),
            ],
            compiler_params=params,
            name="grads",
        )(*operands)
        gathered = lax.all_to_all(parts, "label", split_axis=0, concat_axis=0, tiled=True)
        grads = jnp.sum(gathered.astype(jnp.float32), axis=0).astype(jnp.bfloat16)
        return loss.reshape(inst_count), grads

    pairs = lab_count // 2
    half_rows = inst_count // 2
    wide = jax.ShapeDtypeStruct((half_rows, part), jnp.float32)
    narrow = jax.ShapeDtypeStruct((half_rows, part), jnp.bfloat16)

    def stack(count, one):
        return jax.ShapeDtypeStruct((count,) + one.shape, one.dtype)

    def swap(x, mask):
        return lax.ppermute(x, "label", [(i, i ^ mask) for i in range(lab_count)])

    def call(kernel, name, out_shape, *arrays):
        return pl.pallas_call(
            kernel,
            out_shape=out_shape,
            in_specs=[vmem()] * len(arrays),
            out_specs=jax.tree.map(lambda _: vmem(), out_shape),
            compiler_params=params,
            name=name,
        )(*arrays)

    def half(side, outs):
        return pl.pallas_call(
            functools.partial(half_kernel, side, groups, lab_count, pos_count),
            out_shape=[loss_type] + outs,
            in_specs=in_specs,
            out_specs=[vmem()] * (1 + len(outs)),
            scratch_shapes=[
                lse_scratch,
                pltpu.VMEM((block_count // 2, BLK, BLK), jnp.float32),
                pltpu.VMEM((block_count // 2, BLK, width), jnp.float32),
            ],
            compiler_params=params,
            name="grads",
        )(*operands)

    loss, keep, send = half(0, [stack(pairs, wide), stack(pairs, narrow)])
    got = swap(send, 1)
    _, line_keep, *line_send = half(1, [stack(2, wide)] + [stack(2, narrow)] * (pairs - 1))
    line_got = [swap(x, 2 * j + 2) for j, x in enumerate(line_send)]
    own, *sends = call(pair_kernel, "pair_sums", [wide] + [narrow] * (pairs - 1), keep, got)
    line_keep, *sends = lax.optimization_barrier((line_keep, *sends))
    first = [own] + [swap(x, 2 * j + 2) for j, x in enumerate(sends)]
    line_own, line_out = call(line_kernel, "line_sums", [wide, narrow], line_keep, *line_got)
    second = [line_own, swap(line_out, 1)]
    grads = call(
        functools.partial(last_kernel, len(first)),
        "last_sums",
        jax.ShapeDtypeStruct((inst_count, part), jnp.bfloat16),
        *first,
        *second,
    )
    return loss.reshape(inst_count), grads


def solution(mesh):
    in_specs = (P("dp", None), P(("dp", "label"), None, None), P(), P(), P("dp", None))
    out_specs = (P("dp"), P("dp", "label"))
    return jax.shard_map(shards, mesh=mesh, in_specs=in_specs, out_specs=out_specs, check_vma=False)
```

```python
import functools

import jax
import jax.numpy as jnp
from jax import lax
from jax.experimental import pallas as pl
from jax.experimental.pallas import tpu as pltpu
from jax.sharding import PartitionSpec as P

BLK = 128
NEG_FILL = -1e30
VMEM_BYTES = 32 * 1024 * 1024
VMEM_PICK = 56 * 1024 * 1024


def divide(value, by):
    if by & (by - 1) == 0:
        return lax.shift_right_logical(value, jnp.int32(by.bit_length() - 1))
    return lax.div(value, jnp.int32(by))


def remainder(value, by):
    if by & (by - 1) == 0:
        return value & jnp.int32(by - 1)
    return lax.rem(value, jnp.int32(by))


def each_entry(count, short_count, body, carry):
    if count <= 64:
        for e in range(count):
            carry = body(e // short_count, e % short_count, carry)
        return carry
    step = lambda e, c: body(divide(e, short_count), remainder(e, short_count), c)
    return lax.fori_loop(0, count, step, carry)


def find_slots(sizes, wanted, lists_ref, slot_ref):
    lab_count, stored, block_count, short_count = sizes
    dp_index, lab_index = lax.axis_index("dp"), lax.axis_index("label")
    mine = dp_index * lab_count + lab_index
    found = []
    for k in wanted:
        base = (dp_index ^ k) * block_count

        def look(row, column, slot_here, base=base):
            slot = slot_ref[lists_ref[base + row, column]]
            return jnp.where(divide(slot, stored) == mine, remainder(slot, stored), slot_here)

        count = block_count // 2 * short_count
        found.append(each_entry(count, short_count, look, jnp.int32(0)))
    return found


def far_kernel(sizes, wanted, lists_hbm, slot_hbm, weights_ref, *rest):
    outs = rest[: len(wanted)]
    held, lists_ref, slot_ref, sems = rest[len(wanted) :]
    tables = [
        pltpu.make_async_copy(lists_hbm, lists_ref, sems.at[0]),
        pltpu.make_async_copy(slot_hbm, slot_ref, sems.at[1]),
    ]
    stage = pltpu.make_async_copy(weights_ref, held, sems.at[2])
    for copy in tables:
        copy.start()
    stage.start()
    for copy in tables:
        copy.wait()
    found = find_slots(sizes, wanted, lists_ref, slot_ref)
    stage.wait()
    copies = []
    for i, slot in enumerate(found):
        copies.append(pltpu.make_async_copy(held.at[slot], outs[i], sems.at[3 + i]))
        copies[-1].start()
    for copy in copies:
        copy.wait()


def near_kernel(sizes, lists_hbm, slot_hbm, weights_ref, table_ref, row_ref, lists_ref, slot_ref, sems):
    lab_count, stored, block_count, short_count = sizes
    tables = [
        pltpu.make_async_copy(lists_hbm, lists_ref, sems.at[0]),
        pltpu.make_async_copy(slot_hbm, slot_ref, sems.at[1]),
    ]
    for copy in tables:
        copy.start()
    for copy in tables:
        copy.wait()
    (slot,) = find_slots(sizes, range(1), lists_ref, slot_ref)
    own = pltpu.make_async_copy(weights_ref.at[slot], row_ref, sems.at[2])
    own.start()
    dp_index, lab_index = lax.axis_index("dp"), lax.axis_index("label")
    half = block_count // 2
    for side in range(2):

        def note(row, column, carry, side=side):
            block = side * half + row
            cluster = lists_ref[dp_index * block_count + block, column]
            device = divide(slot_ref[cluster], stored)

            @pl.when(remainder(device, lab_count) == lab_index)
            def _():
                entry = divide(device, lab_count) ^ dp_index
                table_ref[entry, 0] = cluster
                table_ref[entry, 1 + side] = jnp.int32(block)

            return carry

        each_entry(half * short_count, short_count, note, jnp.int32(0))
    own.wait()


def before_kernel(sizes, early, lists, slots, weights, pos, *rest):
    table, row, hits, shares, lists_ref, slot_ref, sems = rest[2:]

    @pl.when((lax.axis_index("dp") & 1) == 1)
    def _():
        near_kernel(sizes, lists, slots, weights, table, row, lists_ref, slot_ref, sems)
        target_kernel(early, table, pos, hits, shares)


def after_kernel(sizes, early, lists, slots, weights, pos, *rest):
    done, (table, row, hits, shares, lists_ref, slot_ref, sems) = rest[:4], rest[4:]
    core = lax.axis_index("dp") & 1

    @pl.when(core == 0)
    def _():
        near_kernel(sizes, lists, slots, weights, table, row, lists_ref, slot_ref, sems)
        target_kernel(early, table, pos, hits, shares)

    @pl.when(core == 1)
    def _():
        for i in range(table.shape[0]):
            for j in range(table.shape[1] - 1):
                table[i, j] = done[0][i, j]
        row[...] = done[1][...]
        hits[...] = done[2][...]
        shares[...] = done[3][...]


def target_kernel(early, table_ref, pos_ref, hits_ref, shares_ref):
    count, cluster_size, _ = hits_ref.shape
    pos_count = pos_ref.shape[1]

    def one_slot(s):
        labels = lax.broadcasted_iota(jnp.int32, (cluster_size, BLK), 0) + table_ref[s, 0] * cluster_size
        for side in range(2):
            pos = pos_ref[table_ref[s, 1 + side]]
            hit = pos[0:1, :] == labels
            for p in range(1, pos_count):
                hit = hit | (pos[p : p + 1, :] == labels)
            hits = jnp.where(hit, 1.0, 0.0)
            columns = pl.ds(side * BLK, BLK)
            hits_ref[s, :, columns] = hits
            if s in early:
                shares_ref[early.index(s), columns, :] = (hits / pos_count).T

    for s in range(count):
        pl.when(table_ref[s, 0] >= 0)(functools.partial(one_slot, s))


def logit_kernel(slots, turned, copies, table_ref, feats_ref, hits_ref, *rest):
    count = len(slots)
    rows = rest[:count]
    logits_ref, out_ref, stats_ref = rest[-3:]
    if len(rest) == count + 3:
        stats_ref[0] = jnp.full(stats_ref.shape[1:], NEG_FILL, jnp.float32)
        stats_ref[1] = jnp.zeros(stats_ref.shape[1:], jnp.float32)
        stats_ref[2] = jnp.zeros(stats_ref.shape[1:], jnp.float32)
    else:
        stats_ref[...] = rest[count][0]
    for i, (s, ref) in enumerate(zip(slots, rows)):
        for side in range(2):
            block = table_ref[s, 1 + side]
            logits = lax.dot_general(
                ref[...],
                feats_ref[block],
                (((1,), (1,)), ((), ())),
                preferred_element_type=jnp.float32,
            )
            columns = pl.ds(side * BLK, BLK)
            if turned:
                logits_ref[i, columns, :] = logits.T
            else:
                logits_ref[i, :, columns] = logits
            highest = jnp.max(logits, axis=0, keepdims=True)
            total = jnp.sum(jnp.exp(logits - highest), axis=0, keepdims=True)
            positive = jnp.sum(hits_ref[s, :, columns] * logits, axis=0, keepdims=True)
            row = pl.ds(block, 1)
            before = stats_ref[0, row, :]
            after = jnp.maximum(before, highest)
            stats_ref[0, row, :] = after
            stats_ref[1, row, :] = stats_ref[1, row, :] * jnp.exp(before - after) + total * jnp.exp(
                highest - after
            )
            stats_ref[2, row, :] = stats_ref[2, row, :] + positive
    for i in range(copies):
        out_ref[i] = stats_ref[...]


def row_sums(stats_ref, lab_count):
    highest = stats_ref[0, 0]
    for i in range(1, lab_count):
        highest = jnp.maximum(highest, stats_ref[i, 0])
    summed = jnp.zeros_like(highest)
    positive = jnp.zeros_like(highest)
    for i in range(lab_count):
        summed = summed + stats_ref[i, 1] * jnp.exp(stats_ref[i, 0] - highest)
        positive = positive + stats_ref[i, 2]
    return highest + jnp.log(summed), positive


def prepare(stats_ref, pos_count, lab_count, loss_ref, lse_ref, columns_ref, total_ref, first):
    lse, positive = row_sums(stats_ref, lab_count)
    lse_ref[...] = lse
    loss_ref[...] = lse - positive / pos_count
    for b in range(columns_ref.shape[0]):
        columns_ref[b] = jnp.broadcast_to(lse[first + b : first + b + 1, :], (BLK, BLK)).T
    total_ref[...] = jnp.zeros_like(total_ref)


def add_slots(sides, groups, pos_count, first, table_ref, hits_ref, shares_ref, logits_refs, rows, sums):
    lse_ref, columns_ref, total_ref = sums
    early = [s for slots in groups[:-1] for s in slots]
    cluster_size = rows[0].shape[0]

    def one_slot(s, logits_ref):
        for side in sides:
            block = table_ref[s, 1 + side]
            here = pl.ds(side * BLK, BLK)
            if s in early:
                column = columns_ref[block - first]
                column = jnp.concatenate([column] * (cluster_size // BLK), axis=1)
                dlogit = jnp.exp(logits_ref[here, :] - column) - shares_ref[early.index(s), here, :]
            else:
                row = lse_ref[pl.ds(block, 1), :]
                dlogit = jnp.exp(logits_ref[:, here] - row) - hits_ref[s, :, here] / pos_count
                dlogit = dlogit.T
            total_ref[block - first] += lax.dot_general(
                dlogit.astype(jnp.bfloat16),
                rows[s][...],
                (((1,), (0,)), ((), ())),
                preferred_element_type=jnp.float32,
            )

    for slots, logits_ref in zip(groups, logits_refs):
        for i, s in enumerate(slots):
            body = functools.partial(one_slot, s, logits_ref.at[i])
            if len(rows) <= 4:
                body()
            else:
                pl.when(table_ref[s, 0] >= 0)(body)


def half_kernel(side, groups, lab_count, pos_count, table_ref, hits_ref, shares_ref, stats_ref, *rest):
    logits_refs = rest[: len(groups)]
    rows = rest[len(groups) : -6]
    loss_ref, keep_ref, send_ref, lse_ref, columns_ref, total_ref = rest[-6:]
    half = total_ref.shape[0]
    prepare(
        stats_ref, pos_count, lab_count, loss_ref, lse_ref, columns_ref, total_ref, side * half
    )
    add_slots(
        (side,),
        groups,
        pos_count,
        side * half,
        table_ref,
        hits_ref,
        shares_ref,
        logits_refs,
        rows,
        (lse_ref, columns_ref, total_ref),
    )
    part = keep_ref.shape[2]
    lab_index = lax.axis_index("label")
    for j in range(lab_count // 2):
        mine = pl.ds(pl.multiple_of((lab_index ^ (2 * j)) * part, part), part)
        other = pl.ds(pl.multiple_of((lab_index ^ (2 * j + 1)) * part, part), part)
        for b in range(half):
            here = pl.ds(b * BLK, BLK)
            keep_ref[j, here, :] = total_ref[b, :, mine]
            send_ref[j, here, :] = total_ref[b, :, other].astype(jnp.bfloat16)


def pair_kernel(keep_ref, got_ref, *outs):
    outs[0][...] = keep_ref[0] + got_ref[0].astype(jnp.float32)
    for j in range(1, len(outs)):
        outs[j][...] = (keep_ref[j] + got_ref[j].astype(jnp.float32)).astype(jnp.bfloat16)


def last_kernel(count, *refs):
    out_ref = refs[-1]
    for h in range(len(refs[:-1]) // count):
        total = refs[h * count][...]
        for ref in refs[h * count + 1 : (h + 1) * count]:
            total = total + ref[...].astype(jnp.float32)
        rows = total.shape[0]
        out_ref[h * rows : (h + 1) * rows, :] = total.astype(jnp.bfloat16)


def grad_kernel(groups, lab_count, pos_count, table_ref, hits_ref, shares_ref, stats_ref, *rest):
    logits_refs = rest[: len(groups)]
    rows = rest[len(groups) : -5]
    loss_ref, out_ref, lse_ref, columns_ref, total_ref = rest[-5:]
    prepare(stats_ref, pos_count, lab_count, loss_ref, lse_ref, columns_ref, total_ref, 0)
    add_slots(
        (0, 1),
        groups,
        pos_count,
        0,
        table_ref,
        hits_ref,
        shares_ref,
        logits_refs,
        rows,
        (lse_ref, columns_ref, total_ref),
    )
    part = out_ref.shape[2]
    for j in range(lab_count):
        for b in range(total_ref.shape[0]):
            out_ref[j, b * BLK : (b + 1) * BLK, :] = total_ref[
                b, :, j * part : (j + 1) * part
            ].astype(jnp.bfloat16)


def smem():
    return pl.BlockSpec(memory_space=pltpu.SMEM)


def vmem():
    return pl.BlockSpec(memory_space=pltpu.VMEM)


def anywhere():
    return pl.BlockSpec(memory_space=pl.ANY)


def shards(feats, weights, shortlist, slot_of, positives):
    dp_count = lax.axis_size("dp")
    lab_count = lax.axis_size("label")
    stored, cluster_size, width = weights.shape
    inst_count = feats.shape[0]
    pos_count = positives.shape[1]
    block_count = inst_count // BLK
    short_count = shortlist.shape[1]
    params = pltpu.CompilerParams(vmem_limit_bytes=VMEM_BYTES)
    row_type = jax.ShapeDtypeStruct((cluster_size, width), weights.dtype)
    stat_shape = (3, block_count, BLK)

    sizes = (lab_count, stored, block_count, short_count)
    far = range(1, dp_count)
    far_rows = pl.pallas_call(
        functools.partial(far_kernel, sizes, far),
        out_shape=[row_type] * len(far),
        in_specs=[anywhere()] * 3,
        out_specs=[anywhere()] * len(far),
        scratch_shapes=[
            pltpu.VMEM(weights.shape, weights.dtype),
            pltpu.SMEM(shortlist.shape, jnp.int32),
            pltpu.SMEM(slot_of.shape, jnp.int32),
            pltpu.SemaphoreType.DMA((3 + len(far),)),
        ],
        compiler_params=pltpu.CompilerParams(vmem_limit_bytes=VMEM_PICK),
        name="pick_far",
    )(shortlist, slot_of, weights)
    pos_blocks = positives.reshape(block_count, BLK, pos_count).transpose(0, 2, 1)
    cuts = (0, dp_count // 2, dp_count * 3 // 4, dp_count)
    groups = [tuple(range(a, b)) for a, b in zip(cuts[:-1], cuts[1:])]
    if dp_count == 4:
        groups = [(2,), (0, 1), (3,)]
    early = [s for slots in groups[:-1] for s in slots]
    near_types = [
        jax.ShapeDtypeStruct((dp_count, 4), jnp.int32),
        row_type,
        jax.ShapeDtypeStruct((dp_count, cluster_size, 2 * BLK), jnp.float32),
        jax.ShapeDtypeStruct((len(early), 2 * BLK, cluster_size), jnp.float32),
    ]
    near_operands = (shortlist, slot_of, weights, pos_blocks)
    near_specs = [anywhere()] * 3 + [vmem()]
    near_scratch = [
        pltpu.SMEM(shortlist.shape, jnp.int32),
        pltpu.SMEM(slot_of.shape, jnp.int32),
        pltpu.SemaphoreType.DMA((3,)),
    ]

    def swap_dp(x, mask):
        return lax.ppermute(x, "dp", [(i, i ^ mask) for i in range(dp_count)])

    handed = [swap_dp(x, 1) if k % 2 == 0 and k else x for k, x in enumerate(far_rows)]
    *sent, table, row, hits, shares = pl.pallas_call(
        functools.partial(before_kernel, sizes, early),
        out_shape=[row_type] + near_types,
        in_specs=near_specs + [anywhere()],
        out_specs=[anywhere(), smem()] + [vmem()] * 3,
        input_output_aliases={4: 0},
        scratch_shapes=near_scratch,
        compiler_params=params,
        name="near_core1",
    )(*near_operands, far_rows[1])
    table, row, hits, shares = pl.pallas_call(
        functools.partial(after_kernel, sizes, early),
        out_shape=near_types,
        in_specs=near_specs + [smem()] + [vmem()] * 3,
        out_specs=[smem()] + [vmem()] * 3,
        scratch_shapes=near_scratch,
        compiler_params=params,
        name="near_core0",
    )(*near_operands, table, row, hits, shares)
    rows = [row, swap_dp(far_rows[0], 1), swap_dp(sent[0], 2)]
    rows += [swap_dp(x, (k + 1) & ~1) for k, x in enumerate(handed) if k >= 2]

    feat_blocks = feats.reshape(block_count, BLK, width)
    kept = []
    stats = []
    for slots in groups:
        count = len(slots)
        last = slots is groups[-1]
        copies = lab_count if last else 1
        shape = (cluster_size, 2 * BLK) if last else (2 * BLK, cluster_size)
        logits, stats_out = pl.pallas_call(
            functools.partial(logit_kernel, slots, not last, copies),
            out_shape=[
                jax.ShapeDtypeStruct((count,) + shape, jnp.float32),
                jax.ShapeDtypeStruct((copies,) + stat_shape, jnp.float32),
            ],
            in_specs=[smem()] + [vmem()] * (2 + count + len(stats)),
            out_specs=[vmem(), vmem()],
            scratch_shapes=[pltpu.VMEM(stat_shape, jnp.float32)],
            compiler_params=params,
            cost_estimate=pl.CostEstimate(
                flops=count * 4 * BLK * cluster_size * width,
                bytes_accessed=count * cluster_size * width * 2,
                transcendentals=0,
            ),
            name="logits",
        )(table, feat_blocks, hits, *[rows[s] for s in slots], *stats)
        kept.append(logits)
        stats = [stats_out]

    all_stats = lax.all_to_all(stats[0], "label", split_axis=0, concat_axis=0, tiled=True)
    part = width // lab_count
    in_specs = [smem()] + [vmem()] * (3 + len(groups) + dp_count)
    operands = (table, hits, shares, all_stats, *kept, *rows)
    loss_type = jax.ShapeDtypeStruct((block_count, BLK), jnp.float32)
    lse_scratch = pltpu.VMEM((block_count, BLK), jnp.float32)
    if part % 128 or lab_count % 2:
        loss, parts = pl.pallas_call(
            functools.partial(grad_kernel, groups, lab_count, pos_count),
            out_shape=[
                loss_type,
                jax.ShapeDtypeStruct((lab_count, inst_count, part), jnp.bfloat16),
            ],
            in_specs=in_specs,
            out_specs=[vmem(), vmem()],
            scratch_shapes=[
                lse_scratch,
                pltpu.VMEM((block_count, BLK, BLK), jnp.float32),
                pltpu.VMEM((block_count, BLK, width), jnp.float32),
            ],
            compiler_params=params,
            name="grads",
        )(*operands)
        gathered = lax.all_to_all(parts, "label", split_axis=0, concat_axis=0, tiled=True)
        grads = jnp.sum(gathered.astype(jnp.float32), axis=0).astype(jnp.bfloat16)
        return loss.reshape(inst_count), grads

    pairs = lab_count // 2
    half_rows = inst_count // 2
    finals = []
    for side in range(2):
        loss, keep, send = pl.pallas_call(
            functools.partial(half_kernel, side, groups, lab_count, pos_count),
            out_shape=[
                loss_type,
                jax.ShapeDtypeStruct((pairs, half_rows, part), jnp.float32),
                jax.ShapeDtypeStruct((pairs, half_rows, part), jnp.bfloat16),
            ],
            in_specs=in_specs,
            out_specs=[vmem()] * 3,
            scratch_shapes=[
                lse_scratch,
                pltpu.VMEM((block_count // 2, BLK, BLK), jnp.float32),
                pltpu.VMEM((block_count // 2, BLK, width), jnp.float32),
            ],
            compiler_params=params,
            cost_estimate=pl.CostEstimate(
                flops=dp_count * 2 * BLK * cluster_size * width,
                bytes_accessed=dp_count * cluster_size * width * 2,
                transcendentals=0,
            ),
            name="grads",
        )(*operands)
        if side:
            send, got = lax.optimization_barrier((send, got))
        got = lax.ppermute(send, "label", [(i, i ^ 1) for i in range(lab_count)])
        own, *outgoing = pl.pallas_call(
            pair_kernel,
            out_shape=[jax.ShapeDtypeStruct((half_rows, part), jnp.float32)]
            + [jax.ShapeDtypeStruct((half_rows, part), jnp.bfloat16)] * (pairs - 1),
            in_specs=[vmem()] * 2,
            out_specs=[vmem()] * pairs,
            compiler_params=params,
            name="pair_sums",
        )(keep, got)
        finals.append(own)
        for j in range(1, pairs):
            hop = [(i, i ^ (2 * j)) for i in range(lab_count)]
            finals.append(lax.ppermute(outgoing[j - 1], "label", hop))
    grads = pl.pallas_call(
        functools.partial(last_kernel, pairs),
        out_shape=jax.ShapeDtypeStruct((inst_count, part), jnp.bfloat16),
        in_specs=[vmem()] * (2 * pairs),
        out_specs=vmem(),
        compiler_params=params,
        name="last_sums",
    )(*finals)
    return loss.reshape(inst_count), grads


def solution(mesh):
    in_specs = (P("dp", None), P(("dp", "label"), None, None), P(), P(), P("dp", None))
    out_specs = (P("dp"), P("dp", "label"))
    return jax.shard_map(shards, mesh=mesh, in_specs=in_specs, out_specs=out_specs, check_vma=False)
```

```python
import functools

import jax
import jax.numpy as jnp
from jax import lax
from jax.experimental import pallas as pl
from jax.experimental.pallas import tpu as pltpu
from jax.sharding import PartitionSpec as P

BLK = 128
NEG_FILL = -1e30
VMEM_BYTES = 32 * 1024 * 1024
VMEM_PICK = 56 * 1024 * 1024


def divide(value, by):
    if by & (by - 1) == 0:
        return lax.shift_right_logical(value, jnp.int32(by.bit_length() - 1))
    return lax.div(value, jnp.int32(by))


def remainder(value, by):
    if by & (by - 1) == 0:
        return value & jnp.int32(by - 1)
    return lax.rem(value, jnp.int32(by))


def each_entry(count, short_count, body, carry):
    if count <= 64:
        for e in range(count):
            carry = body(e // short_count, e % short_count, carry)
        return carry
    step = lambda e, c: body(divide(e, short_count), remainder(e, short_count), c)
    return lax.fori_loop(0, count, step, carry)


def find_slots(sizes, wanted, lists_ref, slot_ref):
    lab_count, stored, block_count, short_count = sizes
    dp_index, lab_index = lax.axis_index("dp"), lax.axis_index("label")
    mine = dp_index * lab_count + lab_index
    found = []
    for k in wanted:
        base = (dp_index ^ k) * block_count

        def look(row, column, slot_here, base=base):
            slot = slot_ref[lists_ref[base + row, column]]
            return jnp.where(divide(slot, stored) == mine, remainder(slot, stored), slot_here)

        count = block_count // 2 * short_count
        found.append(each_entry(count, short_count, look, jnp.int32(0)))
    return found


def far_kernel(sizes, wanted, lists_hbm, slot_hbm, weights_ref, *rest):
    outs = rest[: len(wanted)]
    held, lists_ref, slot_ref, sems = rest[len(wanted) :]
    tables = [
        pltpu.make_async_copy(lists_hbm, lists_ref, sems.at[0]),
        pltpu.make_async_copy(slot_hbm, slot_ref, sems.at[1]),
    ]
    stage = pltpu.make_async_copy(weights_ref, held, sems.at[2])
    for copy in tables:
        copy.start()
    stage.start()
    for copy in tables:
        copy.wait()
    found = find_slots(sizes, wanted, lists_ref, slot_ref)
    stage.wait()
    copies = []
    for i, slot in enumerate(found):
        copies.append(pltpu.make_async_copy(held.at[slot], outs[i], sems.at[3 + i]))
        copies[-1].start()
    for copy in copies:
        copy.wait()


def near_kernel(sizes, lists_ref, slot_ref, weights_ref, table_ref, *rest):
    lab_count, stored, block_count, short_count = sizes
    outs, sems = rest[:-1], rest[-1]
    copies = []
    for k, slot in enumerate(find_slots(sizes, range(1), lists_ref, slot_ref)):
        copies.append(pltpu.make_async_copy(weights_ref.at[slot], outs[k], sems.at[k]))
        copies[-1].start()
    dp_index, lab_index = lax.axis_index("dp"), lax.axis_index("label")
    half = block_count // 2
    for side in range(2):

        def note(row, column, carry, side=side):
            block = side * half + row
            cluster = lists_ref[dp_index * block_count + block, column]
            device = divide(slot_ref[cluster], stored)

            @pl.when(remainder(device, lab_count) == lab_index)
            def _():
                entry = divide(device, lab_count) ^ dp_index
                table_ref[entry, 0] = cluster
                table_ref[entry, 1 + side] = jnp.int32(block)

            return carry

        each_entry(half * short_count, short_count, note, jnp.int32(0))
    for copy in copies:
        copy.wait()


def target_kernel(early, late, table_ref, pos_ref, feats_ref, hits_ref, shares_ref, turned_ref):
    count, cluster_size, _ = hits_ref.shape
    pos_count = pos_ref.shape[1]

    def one_slot(s):
        labels = lax.broadcasted_iota(jnp.int32, (cluster_size, BLK), 0) + table_ref[s, 0] * cluster_size
        for side in range(2):
            pos = pos_ref[table_ref[s, 1 + side]]
            hit = pos[0:1, :] == labels
            for p in range(1, pos_count):
                hit = hit | (pos[p : p + 1, :] == labels)
            hits = jnp.where(hit, 1.0, 0.0)
            columns = pl.ds(side * BLK, BLK)
            hits_ref[s, :, columns] = hits
            if s in early:
                shares_ref[early.index(s), columns, :] = (hits / pos_count).T
            else:
                feats = feats_ref[table_ref[s, 1 + side]].astype(jnp.float32)
                turned_ref[late.index(s), :, columns] = feats.T.astype(jnp.bfloat16)

    for s in range(count):
        pl.when(table_ref[s, 0] >= 0)(functools.partial(one_slot, s))


def logit_kernel(slots, turned, copies, table_ref, feats_ref, hits_ref, *rest):
    count = len(slots)
    rows = rest[:count]
    logits_ref, out_ref, stats_ref = rest[-3:]
    if len(rest) == count + 3:
        stats_ref[0] = jnp.full(stats_ref.shape[1:], NEG_FILL, jnp.float32)
        stats_ref[1] = jnp.zeros(stats_ref.shape[1:], jnp.float32)
        stats_ref[2] = jnp.zeros(stats_ref.shape[1:], jnp.float32)
    else:
        stats_ref[...] = rest[count][0]
    for i, (s, ref) in enumerate(zip(slots, rows)):
        if not turned:
            logits_ref[i] = jnp.dot(ref[...], feats_ref[i], preferred_element_type=jnp.float32)
        for side in range(2):
            block = table_ref[s, 1 + side]
            columns = pl.ds(side * BLK, BLK)
            if turned:
                logits = lax.dot_general(
                    ref[...],
                    feats_ref[block],
                    (((1,), (1,)), ((), ())),
                    preferred_element_type=jnp.float32,
                )
                logits_ref[i, columns, :] = logits.T
            else:
                logits = logits_ref[i, :, columns]
            highest = jnp.max(logits, axis=0, keepdims=True)
            total = jnp.sum(jnp.exp(logits - highest), axis=0, keepdims=True)
            positive = jnp.sum(hits_ref[s, :, columns] * logits, axis=0, keepdims=True)
            row = pl.ds(block, 1)
            before = stats_ref[0, row, :]
            after = jnp.maximum(before, highest)
            stats_ref[0, row, :] = after
            stats_ref[1, row, :] = stats_ref[1, row, :] * jnp.exp(before - after) + total * jnp.exp(
                highest - after
            )
            stats_ref[2, row, :] = stats_ref[2, row, :] + positive
    for i in range(copies):
        out_ref[i] = stats_ref[...]


def row_sums(stats_ref, lab_count):
    highest = stats_ref[0, 0]
    for i in range(1, lab_count):
        highest = jnp.maximum(highest, stats_ref[i, 0])
    summed = jnp.zeros_like(highest)
    positive = jnp.zeros_like(highest)
    for i in range(lab_count):
        summed = summed + stats_ref[i, 1] * jnp.exp(stats_ref[i, 0] - highest)
        positive = positive + stats_ref[i, 2]
    return highest + jnp.log(summed), positive


def prepare(stats_ref, pos_count, lab_count, loss_ref, lse_ref, columns_ref, first):
    lse, positive = row_sums(stats_ref, lab_count)
    lse_ref[...] = lse
    loss_ref[...] = lse - positive / pos_count
    for b in range(columns_ref.shape[0]):
        columns_ref[b] = jnp.broadcast_to(lse[first + b : first + b + 1, :], (BLK, BLK)).T


def add_slots(sides, groups, pos_count, first, table_ref, hits_ref, shares_ref, logits_refs, rows, sums):
    lse_ref, columns_ref, total_ref = sums
    early = [s for slots in groups[:-1] for s in slots]
    cluster_size = rows[0].shape[0]

    def one_slot(s, logits_ref):
        for side in sides:
            block = table_ref[s, 1 + side]
            here = pl.ds(side * BLK, BLK)
            if s in early:
                column = columns_ref[block - first]
                column = jnp.concatenate([column] * (cluster_size // BLK), axis=1)
                dlogit = jnp.exp(logits_ref[here, :] - column) - shares_ref[early.index(s), here, :]
            else:
                row = lse_ref[pl.ds(block, 1), :]
                dlogit = jnp.exp(logits_ref[:, here] - row) - hits_ref[s, :, here] / pos_count
                dlogit = dlogit.T
            total_ref[block - first] += lax.dot_general(
                dlogit.astype(jnp.bfloat16),
                rows[s][...],
                (((1,), (0,)), ((), ())),
                preferred_element_type=jnp.float32,
            )

    for slots, logits_ref in zip(groups, logits_refs):
        for i, s in enumerate(slots):
            body = functools.partial(one_slot, s, logits_ref.at[i])
            if len(rows) <= 4:
                body()
            else:
                pl.when(table_ref[s, 0] >= 0)(body)


def half_sums(side, groups, pos_count, table_ref, hits_ref, shares_ref, logits_refs, rows, sums):
    lse_ref, columns_ref, dlogit_ref, total_ref = sums
    half = columns_ref.shape[0]
    cluster_size = rows[0].shape[0]
    early = [s for slots in groups[:-1] for s in slots]
    here = pl.ds(side * BLK, BLK)
    dlogit_ref[...] = jnp.zeros_like(dlogit_ref)
    for slots, logits_ref in zip(groups, logits_refs):
        for i, s in enumerate(slots):
            block = table_ref[s, 1 + side]
            if s in early:
                column = columns_ref[block - side * half]
                column = jnp.concatenate([column] * (cluster_size // BLK), axis=1)
                dlogit = jnp.exp(logits_ref[i, here, :] - column) - shares_ref[early.index(s), here, :]
            else:
                row = lse_ref[pl.ds(block, 1), :]
                dlogit = jnp.exp(logits_ref[i, :, here] - row) - hits_ref[s, :, here] / pos_count
                dlogit = dlogit.T
            at = pl.ds(pl.multiple_of((block - side * half) * BLK, BLK), BLK)
            labels = pl.ds(s * cluster_size, cluster_size)
            dlogit_ref[at, labels] = dlogit.astype(jnp.bfloat16)
    total_ref[...] = jnp.dot(
        dlogit_ref[...],
        jnp.concatenate([ref[...] for ref in rows], axis=0),
        preferred_element_type=jnp.float32,
    )


def half_kernel(side, groups, lab_count, pos_count, table_ref, hits_ref, shares_ref, stats_ref, *rest):
    logits_refs = rest[: len(groups)]
    rows = rest[len(groups) : -7]
    loss_ref, keep_ref, send_ref, lse_ref, columns_ref, dlogit_ref, total_ref = rest[-7:]
    half = columns_ref.shape[0]
    prepare(stats_ref, pos_count, lab_count, loss_ref, lse_ref, columns_ref, side * half)
    half_sums(
        side,
        groups,
        pos_count,
        table_ref,
        hits_ref,
        shares_ref,
        logits_refs,
        rows,
        (lse_ref, columns_ref, dlogit_ref, total_ref),
    )
    part = keep_ref.shape[2]
    lab_index = lax.axis_index("label")
    for j in range(lab_count // 2):
        mine = pl.ds(pl.multiple_of((lab_index ^ (2 * j)) * part, part), part)
        other = pl.ds(pl.multiple_of((lab_index ^ (2 * j + 1)) * part, part), part)
        for b in range(half):
            here = pl.ds(b * BLK, BLK)
            keep_ref[j, here, :] = total_ref[here, mine]
            send_ref[j, here, :] = total_ref[here, other].astype(jnp.bfloat16)


def pair_kernel(keep_ref, got_ref, *outs):
    outs[0][...] = keep_ref[0] + got_ref[0].astype(jnp.float32)
    for j in range(1, len(outs)):
        outs[j][...] = (keep_ref[j] + got_ref[j].astype(jnp.float32)).astype(jnp.bfloat16)


def last_kernel(count, *refs):
    out_ref = refs[-1]
    for h in range(len(refs[:-1]) // count):
        total = refs[h * count][...]
        for ref in refs[h * count + 1 : (h + 1) * count]:
            total = total + ref[...].astype(jnp.float32)
        rows = total.shape[0]
        out_ref[h * rows : (h + 1) * rows, :] = total.astype(jnp.bfloat16)


def grad_kernel(groups, lab_count, pos_count, table_ref, hits_ref, shares_ref, stats_ref, *rest):
    logits_refs = rest[: len(groups)]
    rows = rest[len(groups) : -5]
    loss_ref, out_ref, lse_ref, columns_ref, total_ref = rest[-5:]
    prepare(stats_ref, pos_count, lab_count, loss_ref, lse_ref, columns_ref, 0)
    total_ref[...] = jnp.zeros_like(total_ref)
    add_slots(
        (0, 1),
        groups,
        pos_count,
        0,
        table_ref,
        hits_ref,
        shares_ref,
        logits_refs,
        rows,
        (lse_ref, columns_ref, total_ref),
    )
    part = out_ref.shape[2]
    for j in range(lab_count):
        for b in range(total_ref.shape[0]):
            out_ref[j, b * BLK : (b + 1) * BLK, :] = total_ref[
                b, :, j * part : (j + 1) * part
            ].astype(jnp.bfloat16)


def smem():
    return pl.BlockSpec(memory_space=pltpu.SMEM)


def vmem():
    return pl.BlockSpec(memory_space=pltpu.VMEM)


def anywhere():
    return pl.BlockSpec(memory_space=pl.ANY)


def shards(feats, weights, shortlist, slot_of, positives):
    dp_count = lax.axis_size("dp")
    lab_count = lax.axis_size("label")
    stored, cluster_size, width = weights.shape
    inst_count = feats.shape[0]
    pos_count = positives.shape[1]
    block_count = inst_count // BLK
    short_count = shortlist.shape[1]
    params = pltpu.CompilerParams(vmem_limit_bytes=VMEM_BYTES)
    row_type = jax.ShapeDtypeStruct((cluster_size, width), weights.dtype)
    stat_shape = (3, block_count, BLK)

    sizes = (lab_count, stored, block_count, short_count)
    far = range(1, dp_count)
    far_rows = pl.pallas_call(
        functools.partial(far_kernel, sizes, far),
        out_shape=[row_type] * len(far),
        in_specs=[anywhere()] * 3,
        out_specs=[anywhere()] * len(far),
        scratch_shapes=[
            pltpu.VMEM(weights.shape, weights.dtype),
            pltpu.SMEM(shortlist.shape, jnp.int32),
            pltpu.SMEM(slot_of.shape, jnp.int32),
            pltpu.SemaphoreType.DMA((3 + len(far),)),
        ],
        compiler_params=pltpu.CompilerParams(vmem_limit_bytes=VMEM_PICK),
        name="pick_far",
    )(shortlist, slot_of, weights)
    table, *rows = pl.pallas_call(
        functools.partial(near_kernel, sizes),
        out_shape=[jax.ShapeDtypeStruct((dp_count, 4), jnp.int32)] + [row_type],
        in_specs=[smem(), smem(), anywhere()],
        out_specs=[smem(), vmem()],
        scratch_shapes=[pltpu.SemaphoreType.DMA((1,))],
        compiler_params=params,
        name="pick_near",
    )(shortlist, slot_of, weights)
    rows += far_rows
    for k in range(1, dp_count):
        rows[k] = lax.ppermute(rows[k], "dp", [(i, i ^ k) for i in range(dp_count)])

    feat_blocks = feats.reshape(block_count, BLK, width)
    pos_blocks = positives.reshape(block_count, BLK, pos_count).transpose(0, 2, 1)
    cuts = (0, dp_count // 2, dp_count * 3 // 4, dp_count)
    groups = [tuple(range(a, b)) for a, b in zip(cuts[:-1], cuts[1:])]
    if dp_count == 4:
        groups = [(2,), (0, 1), (3,)]
    early = [s for slots in groups[:-1] for s in slots]
    late = list(groups[-1])
    hits, shares, turned = pl.pallas_call(
        functools.partial(target_kernel, early, late),
        out_shape=[
            jax.ShapeDtypeStruct((dp_count, cluster_size, 2 * BLK), jnp.float32),
            jax.ShapeDtypeStruct((len(early), 2 * BLK, cluster_size), jnp.float32),
            jax.ShapeDtypeStruct((len(late), width, 2 * BLK), feats.dtype),
        ],
        in_specs=[smem()] + [vmem()] * 2,
        out_specs=[vmem()] * 3,
        compiler_params=params,
        name="targets",
    )(table, pos_blocks, feat_blocks)
    kept = []
    stats = []
    for slots in groups:
        count = len(slots)
        last = slots is groups[-1]
        copies = lab_count if last else 1
        shape = (cluster_size, 2 * BLK) if last else (2 * BLK, cluster_size)
        logits, stats_out = pl.pallas_call(
            functools.partial(logit_kernel, slots, not last, copies),
            out_shape=[
                jax.ShapeDtypeStruct((count,) + shape, jnp.float32),
                jax.ShapeDtypeStruct((copies,) + stat_shape, jnp.float32),
            ],
            in_specs=[smem()] + [vmem()] * (2 + count + len(stats)),
            out_specs=[vmem(), vmem()],
            scratch_shapes=[pltpu.VMEM(stat_shape, jnp.float32)],
            compiler_params=params,
            cost_estimate=pl.CostEstimate(
                flops=count * 4 * BLK * cluster_size * width,
                bytes_accessed=count * cluster_size * width * 2,
                transcendentals=0,
            ),
            name="logits",
        )(table, turned if last else feat_blocks, hits, *[rows[s] for s in slots], *stats)
        kept.append(logits)
        stats = [stats_out]

    all_stats = lax.all_to_all(stats[0], "label", split_axis=0, concat_axis=0, tiled=True)
    part = width // lab_count
    in_specs = [smem()] + [vmem()] * (3 + len(groups) + dp_count)
    operands = (table, hits, shares, all_stats, *kept, *rows)
    loss_type = jax.ShapeDtypeStruct((block_count, BLK), jnp.float32)
    lse_scratch = pltpu.VMEM((block_count, BLK), jnp.float32)
    if part % 128 or lab_count % 2:
        loss, parts = pl.pallas_call(
            functools.partial(grad_kernel, groups, lab_count, pos_count),
            out_shape=[
                loss_type,
                jax.ShapeDtypeStruct((lab_count, inst_count, part), jnp.bfloat16),
            ],
            in_specs=in_specs,
            out_specs=[vmem(), vmem()],
            scratch_shapes=[
                lse_scratch,
                pltpu.VMEM((block_count, BLK, BLK), jnp.float32),
                pltpu.VMEM((block_count, BLK, width), jnp.float32),
            ],
            compiler_params=params,
            name="grads",
        )(*operands)
        gathered = lax.all_to_all(parts, "label", split_axis=0, concat_axis=0, tiled=True)
        grads = jnp.sum(gathered.astype(jnp.float32), axis=0).astype(jnp.bfloat16)
        return loss.reshape(inst_count), grads

    pairs = lab_count // 2
    half_rows = inst_count // 2
    finals = []
    for side in range(2):
        loss, keep, send = pl.pallas_call(
            functools.partial(half_kernel, side, groups, lab_count, pos_count),
            out_shape=[
                loss_type,
                jax.ShapeDtypeStruct((pairs, half_rows, part), jnp.float32),
                jax.ShapeDtypeStruct((pairs, half_rows, part), jnp.bfloat16),
            ],
            in_specs=in_specs,
            out_specs=[vmem()] * 3,
            scratch_shapes=[
                lse_scratch,
                pltpu.VMEM((block_count // 2, BLK, BLK), jnp.float32),
                pltpu.VMEM((half_rows, dp_count * cluster_size), jnp.bfloat16),
                pltpu.VMEM((half_rows, width), jnp.float32),
            ],
            compiler_params=params,
            cost_estimate=pl.CostEstimate(
                flops=dp_count * 2 * BLK * cluster_size * width,
                bytes_accessed=dp_count * cluster_size * width * 2,
                transcendentals=0,
            ),
            name="grads",
        )(*operands)
        if side:
            send, got = lax.optimization_barrier((send, got))
        got = lax.ppermute(send, "label", [(i, i ^ 1) for i in range(lab_count)])
        own, *outgoing = pl.pallas_call(
            pair_kernel,
            out_shape=[jax.ShapeDtypeStruct((half_rows, part), jnp.float32)]
            + [jax.ShapeDtypeStruct((half_rows, part), jnp.bfloat16)] * (pairs - 1),
            in_specs=[vmem()] * 2,
            out_specs=[vmem()] * pairs,
            compiler_params=params,
            name="pair_sums",
        )(keep, got)
        finals.append(own)
        for j in range(1, pairs):
            hop = [(i, i ^ (2 * j)) for i in range(lab_count)]
            finals.append(lax.ppermute(outgoing[j - 1], "label", hop))
    grads = pl.pallas_call(
        functools.partial(last_kernel, pairs),
        out_shape=jax.ShapeDtypeStruct((inst_count, part), jnp.bfloat16),
        in_specs=[vmem()] * (2 * pairs),
        out_specs=vmem(),
        compiler_params=params,
        name="last_sums",
    )(*finals)
    return loss.reshape(inst_count), grads


def solution(mesh):
    in_specs = (P("dp", None), P(("dp", "label"), None, None), P(), P(), P("dp", None))
    out_specs = (P("dp"), P("dp", "label"))
    return jax.shard_map(shards, mesh=mesh, in_specs=in_specs, out_specs=out_specs, check_vma=False)
```

```python
import functools

import jax
import jax.numpy as jnp
from jax import lax
from jax.experimental import pallas as pl
from jax.experimental.pallas import tpu as pltpu
from jax.sharding import PartitionSpec as P

BLK = 128
NEG_FILL = -1e30
VMEM_BYTES = 32 * 1024 * 1024
VMEM_PICK = 56 * 1024 * 1024


def divide(value, by):
    if by & (by - 1) == 0:
        return lax.shift_right_logical(value, jnp.int32(by.bit_length() - 1))
    return lax.div(value, jnp.int32(by))


def remainder(value, by):
    if by & (by - 1) == 0:
        return value & jnp.int32(by - 1)
    return lax.rem(value, jnp.int32(by))


def each_entry(count, short_count, body, carry):
    if count <= 64:
        for e in range(count):
            carry = body(e // short_count, e % short_count, carry)
        return carry
    step = lambda e, c: body(divide(e, short_count), remainder(e, short_count), c)
    return lax.fori_loop(0, count, step, carry)


class Plan:
    def __init__(self, square, dp_count, lab_count, stored, block_count, short_count):
        self.square, self.dp_count, self.lab_count = square, dp_count, lab_count
        self.stored, self.block_count, self.short_count = stored, block_count, short_count

    def here(self):
        return lax.axis_index("dp"), lax.axis_index("label")

    def home(self):
        dp, lab = self.here()
        return (dp & ~1) | (lab & 1) if self.square else dp

    def flips(self, entry, core):
        return [(0, 0), (core, 1 - core), (1 - core, core), (1, 1)][entry]

    def wanted_by(self, entry):
        dp, lab = self.here()
        if not self.square:
            return dp ^ entry
        flip_x, flip_y = self.flips(entry, dp & 1)
        return ((dp >> 1) ^ flip_y) * 2 + ((lab & 1) ^ flip_x)

    def entry_of(self, device):
        dp, lab = self.here()
        that_dp, that_lab = divide(device, self.lab_count), remainder(device, self.lab_count)
        if not self.square:
            return that_lab == lab, that_dp ^ dp
        match = ((that_dp & 1) == (dp & 1)) & ((that_lab >> 1) == (lab >> 1))
        flip_y, flip_x = (that_dp ^ dp) >> 1, (that_lab ^ lab) & 1
        core = dp & 1
        lone = jnp.where(flip_y == 1 - core, 1, 2)
        entry = jnp.where(flip_x + flip_y == 1, lone, flip_x + flip_y + (flip_x & flip_y))
        return match, entry

    def pairs(self, entry):
        result = []
        for dp in range(self.dp_count):
            for lab in range(self.lab_count):
                if self.square:
                    flip_x, flip_y = self.flips(entry, dp & 1)
                    target = (dp ^ (2 * flip_y)) * self.lab_count + (lab ^ flip_x)
                else:
                    target = (dp ^ entry) * self.lab_count + lab
                result.append((dp * self.lab_count + lab, target))
        return result


def find_slots(plan, wanted, lists_ref, slot_ref):
    dp_index, lab_index = plan.here()
    mine = dp_index * plan.lab_count + lab_index
    stored, short_count = plan.stored, plan.short_count
    found = []
    for k in wanted:
        base = plan.wanted_by(k) * plan.block_count

        def look(row, column, slot_here, base=base):
            slot = slot_ref[lists_ref[base + row, column]]
            return jnp.where(divide(slot, stored) == mine, remainder(slot, stored), slot_here)

        count = plan.block_count // 2 * short_count
        found.append(each_entry(count, short_count, look, jnp.int32(0)))
    return found


def far_kernel(plan, wanted, lists_hbm, slot_hbm, weights_ref, *rest):
    outs = rest[: len(wanted)]
    held, lists_ref, slot_ref, sems = rest[len(wanted) :]
    tables = [
        pltpu.make_async_copy(lists_hbm, lists_ref, sems.at[0]),
        pltpu.make_async_copy(slot_hbm, slot_ref, sems.at[1]),
    ]
    stage = pltpu.make_async_copy(weights_ref, held, sems.at[2])
    for copy in tables:
        copy.start()
    stage.start()
    for copy in tables:
        copy.wait()
    found = find_slots(plan, wanted, lists_ref, slot_ref)
    stage.wait()
    copies = []
    for i, slot in enumerate(found):
        copies.append(pltpu.make_async_copy(held.at[slot], outs[i], sems.at[3 + i]))
        copies[-1].start()
    for copy in copies:
        copy.wait()


def near_kernel(plan, lists_ref, slot_ref, weights_ref, table_ref, *rest):
    block_count, short_count = plan.block_count, plan.short_count
    outs, sems = rest[:-1], rest[-1]
    copies = []
    for k, slot in enumerate(find_slots(plan, range(1), lists_ref, slot_ref)):
        copies.append(pltpu.make_async_copy(weights_ref.at[slot], outs[k], sems.at[k]))
        copies[-1].start()
    home = plan.home()
    half = block_count // 2
    for side in range(2):

        def note(row, column, carry, side=side):
            block = side * half + row
            cluster = lists_ref[home * block_count + block, column]
            match, entry = plan.entry_of(divide(slot_ref[cluster], plan.stored))

            @pl.when(match)
            def _():
                table_ref[entry, 0] = cluster
                table_ref[entry, 1 + side] = jnp.int32(block)

            return carry

        each_entry(half * short_count, short_count, note, jnp.int32(0))
    for copy in copies:
        copy.wait()


def home_kernel(feats_ref, pos_ref, other_feats_ref, other_pos_ref, home_feats_ref, home_pos_ref):
    same = (lax.axis_index("dp") & 1) == (lax.axis_index("label") & 1)

    @pl.when(same)
    def _():
        home_feats_ref[...] = feats_ref[...]
        home_pos_ref[...] = pos_ref[...]

    @pl.when(jnp.logical_not(same))
    def _():
        home_feats_ref[...] = other_feats_ref[...]
        home_pos_ref[...] = other_pos_ref[...]


def target_kernel(early, late, table_ref, pos_ref, feats_ref, hits_ref, shares_ref, turned_ref):
    count, cluster_size, _ = hits_ref.shape
    pos_count = pos_ref.shape[1]

    def one_slot(s):
        labels = lax.broadcasted_iota(jnp.int32, (cluster_size, BLK), 0) + table_ref[s, 0] * cluster_size
        for side in range(2):
            pos = pos_ref[table_ref[s, 1 + side]]
            hit = pos[0:1, :] == labels
            for p in range(1, pos_count):
                hit = hit | (pos[p : p + 1, :] == labels)
            hits = jnp.where(hit, 1.0, 0.0)
            columns = pl.ds(side * BLK, BLK)
            hits_ref[s, :, columns] = hits
            if s in early:
                shares_ref[early.index(s), columns, :] = (hits / pos_count).T
            else:
                feats = feats_ref[table_ref[s, 1 + side]].astype(jnp.float32)
                turned_ref[late.index(s), :, columns] = feats.T.astype(jnp.bfloat16)

    for s in range(count):
        pl.when(table_ref[s, 0] >= 0)(functools.partial(one_slot, s))


def logit_kernel(slots, turned, copies, table_ref, feats_ref, hits_ref, *rest):
    count = len(slots)
    rows = rest[:count]
    logits_ref, out_ref, stats_ref = rest[-3:]
    if len(rest) == count + 3:
        stats_ref[0] = jnp.full(stats_ref.shape[1:], NEG_FILL, jnp.float32)
        stats_ref[1] = jnp.zeros(stats_ref.shape[1:], jnp.float32)
        stats_ref[2] = jnp.zeros(stats_ref.shape[1:], jnp.float32)
    else:
        stats_ref[...] = rest[count][0]
    for i, (s, ref) in enumerate(zip(slots, rows)):
        if not turned:
            logits_ref[i] = jnp.dot(ref[...], feats_ref[i], preferred_element_type=jnp.float32)
        for side in range(2):
            block = table_ref[s, 1 + side]
            columns = pl.ds(side * BLK, BLK)
            if turned:
                logits = lax.dot_general(
                    ref[...],
                    feats_ref[block],
                    (((1,), (1,)), ((), ())),
                    preferred_element_type=jnp.float32,
                )
                logits_ref[i, columns, :] = logits.T
            else:
                logits = logits_ref[i, :, columns]
            highest = jnp.max(logits, axis=0, keepdims=True)
            total = jnp.sum(jnp.exp(logits - highest), axis=0, keepdims=True)
            positive = jnp.sum(hits_ref[s, :, columns] * logits, axis=0, keepdims=True)
            row = pl.ds(block, 1)
            before = stats_ref[0, row, :]
            after = jnp.maximum(before, highest)
            stats_ref[0, row, :] = after
            stats_ref[1, row, :] = stats_ref[1, row, :] * jnp.exp(before - after) + total * jnp.exp(
                highest - after
            )
            stats_ref[2, row, :] = stats_ref[2, row, :] + positive
    for i in range(copies):
        out_ref[i] = stats_ref[...]


def row_sums(stats_ref, lab_count):
    highest = stats_ref[0, 0]
    for i in range(1, lab_count):
        highest = jnp.maximum(highest, stats_ref[i, 0])
    summed = jnp.zeros_like(highest)
    positive = jnp.zeros_like(highest)
    for i in range(lab_count):
        summed = summed + stats_ref[i, 1] * jnp.exp(stats_ref[i, 0] - highest)
        positive = positive + stats_ref[i, 2]
    return highest + jnp.log(summed), positive


def prepare(stats_ref, pos_count, lab_count, loss_ref, lse_ref, columns_ref, total_ref, first):
    lse, positive = row_sums(stats_ref, lab_count)
    lse_ref[...] = lse
    loss_ref[...] = lse - positive / pos_count
    for b in range(columns_ref.shape[0]):
        columns_ref[b] = jnp.broadcast_to(lse[first + b : first + b + 1, :], (BLK, BLK)).T
    total_ref[...] = jnp.zeros_like(total_ref)


def add_slots(sides, groups, pos_count, first, table_ref, hits_ref, shares_ref, logits_refs, rows, sums):
    lse_ref, columns_ref, total_ref = sums
    early = [s for slots in groups[:-1] for s in slots]
    cluster_size = rows[0].shape[0]

    def one_slot(s, logits_ref):
        for side in sides:
            block = table_ref[s, 1 + side]
            here = pl.ds(side * BLK, BLK)
            if s in early:
                column = columns_ref[block - first]
                column = jnp.concatenate([column] * (cluster_size // BLK), axis=1)
                dlogit = jnp.exp(logits_ref[here, :] - column) - shares_ref[early.index(s), here, :]
            else:
                row = lse_ref[pl.ds(block, 1), :]
                dlogit = jnp.exp(logits_ref[:, here] - row) - hits_ref[s, :, here] / pos_count
                dlogit = dlogit.T
            total_ref[block - first] += lax.dot_general(
                dlogit.astype(jnp.bfloat16),
                rows[s][...],
                (((1,), (0,)), ((), ())),
                preferred_element_type=jnp.float32,
            )

    for slots, logits_ref in zip(groups, logits_refs):
        for i, s in enumerate(slots):
            body = functools.partial(one_slot, s, logits_ref.at[i])
            if len(rows) <= 4:
                body()
            else:
                pl.when(table_ref[s, 0] >= 0)(body)


def half_kernel(side, groups, lab_count, pos_count, table_ref, hits_ref, shares_ref, stats_ref, *rest):
    logits_refs = rest[: len(groups)]
    rows = rest[len(groups) : -6]
    loss_ref, keep_ref, send_ref, lse_ref, columns_ref, total_ref = rest[-6:]
    half = total_ref.shape[0]
    prepare(
        stats_ref, pos_count, lab_count, loss_ref, lse_ref, columns_ref, total_ref, side * half
    )
    add_slots(
        (side,),
        groups,
        pos_count,
        side * half,
        table_ref,
        hits_ref,
        shares_ref,
        logits_refs,
        rows,
        (lse_ref, columns_ref, total_ref),
    )
    part = keep_ref.shape[2]
    core, line = lax.axis_index("dp") & 1, lax.axis_index("label") >> 1
    for j in range(lab_count // 2):
        first = (line ^ j) * 2
        mine = pl.ds(pl.multiple_of((first + 1 - core) * part, part), part)
        other = pl.ds(pl.multiple_of((first + core) * part, part), part)
        for b in range(half):
            here = pl.ds(b * BLK, BLK)
            keep_ref[j, here, :] = total_ref[b, :, mine]
            send_ref[j, here, :] = total_ref[b, :, other].astype(jnp.bfloat16)


def pair_kernel(keep_ref, got_ref, *outs):
    for j, out_ref in enumerate(outs):
        out_ref[...] = (keep_ref[j] + got_ref[j].astype(jnp.float32)).astype(out_ref.dtype)


def line_kernel(*refs):
    total = refs[0][...]
    for ref in refs[1:-1]:
        total = total + ref[...].astype(jnp.float32)
    refs[-1][...] = total.astype(jnp.bfloat16)


def join_kernel(low_ref, high_ref, out_ref):
    rows = low_ref.shape[0]
    out_ref[:rows, :] = low_ref[...]
    out_ref[rows:, :] = high_ref[...]


def grad_kernel(groups, lab_count, pos_count, table_ref, hits_ref, shares_ref, stats_ref, *rest):
    logits_refs = rest[: len(groups)]
    rows = rest[len(groups) : -5]
    loss_ref, out_ref, lse_ref, columns_ref, total_ref = rest[-5:]
    prepare(stats_ref, pos_count, lab_count, loss_ref, lse_ref, columns_ref, total_ref, 0)
    add_slots(
        (0, 1),
        groups,
        pos_count,
        0,
        table_ref,
        hits_ref,
        shares_ref,
        logits_refs,
        rows,
        (lse_ref, columns_ref, total_ref),
    )
    part = out_ref.shape[2]
    for j in range(lab_count):
        for b in range(total_ref.shape[0]):
            out_ref[j, b * BLK : (b + 1) * BLK, :] = total_ref[
                b, :, j * part : (j + 1) * part
            ].astype(jnp.bfloat16)


def smem():
    return pl.BlockSpec(memory_space=pltpu.SMEM)


def vmem():
    return pl.BlockSpec(memory_space=pltpu.VMEM)


def anywhere():
    return pl.BlockSpec(memory_space=pl.ANY)


def call(kernel, name, out_shape, in_specs, arrays, scratch=(), limit=VMEM_BYTES, out_specs=None):
    return pl.pallas_call(
        kernel,
        out_shape=out_shape,
        in_specs=in_specs,
        out_specs=out_specs or [vmem()] * len(out_shape),
        scratch_shapes=list(scratch),
        compiler_params=pltpu.CompilerParams(vmem_limit_bytes=limit),
        name=name,
    )(*arrays)


def shards(feats, weights, shortlist, slot_of, positives):
    dp_count = lax.axis_size("dp")
    lab_count = lax.axis_size("label")
    stored, cluster_size, width = weights.shape
    inst_count = feats.shape[0]
    pos_count = positives.shape[1]
    block_count = inst_count // BLK
    part = width // lab_count
    square = dp_count == 4 and lab_count == 8 and part % 128 == 0
    plan = Plan(square, dp_count, lab_count, stored, block_count, shortlist.shape[1])
    struct = jax.ShapeDtypeStruct
    row_type = struct((cluster_size, width), weights.dtype)
    stat_shape = (3, block_count, BLK)
    both = ("dp", "label")
    devices = [(dp, lab) for dp in range(dp_count) for lab in range(lab_count)]

    def move(x, target):
        pairs = []
        for dp, lab in devices:
            to_dp, to_lab = target(dp, lab)
            pairs.append((dp * lab_count + lab, to_dp * lab_count + to_lab))
        return lax.ppermute(x, both, pairs)

    feat_blocks = feats.reshape(block_count, BLK, width)
    pos_blocks = positives.reshape(block_count, BLK, pos_count).transpose(0, 2, 1)
    if square:
        other_feats = lax.ppermute(feat_blocks, "dp", [(i, i ^ 1) for i in range(dp_count)])
        other_pos = lax.ppermute(pos_blocks, "dp", [(i, i ^ 1) for i in range(dp_count)])
        feat_blocks, pos_blocks = call(
            home_kernel,
            "home",
            [struct(feat_blocks.shape, feats.dtype), struct(pos_blocks.shape, jnp.int32)],
            [vmem()] * 4,
            (feat_blocks, pos_blocks, other_feats, other_pos),
        )

    far = range(1, dp_count)
    far_rows = call(
        functools.partial(far_kernel, plan, far),
        "pick_far",
        [row_type] * len(far),
        [anywhere()] * 3,
        (shortlist, slot_of, weights),
        scratch=[
            pltpu.VMEM(weights.shape, weights.dtype),
            pltpu.SMEM(shortlist.shape, jnp.int32),
            pltpu.SMEM(slot_of.shape, jnp.int32),
            pltpu.SemaphoreType.DMA((3 + len(far),)),
        ],
        limit=VMEM_PICK,
        out_specs=[anywhere()] * len(far),
    )
    table, *rows = call(
        functools.partial(near_kernel, plan),
        "pick_near",
        [struct((dp_count, 4), jnp.int32), row_type],
        [smem(), smem(), anywhere()],
        (shortlist, slot_of, weights),
        scratch=[pltpu.SemaphoreType.DMA((1,))],
        out_specs=[smem(), vmem()],
    )
    rows += [lax.ppermute(x, both, plan.pairs(k)) for k, x in zip(far, far_rows)]

    if square:
        groups = [(0,), (1,), (2,), (3,)]
    else:
        cuts = (0, dp_count // 2, dp_count * 3 // 4, dp_count)
        groups = [tuple(range(a, b)) for a, b in zip(cuts[:-1], cuts[1:])]
    early = [s for slots in groups[:-1] for s in slots]
    late = list(groups[-1])
    hits, shares, turned = call(
        functools.partial(target_kernel, early, late),
        "targets",
        [
            struct((dp_count, cluster_size, 2 * BLK), jnp.float32),
            struct((len(early), 2 * BLK, cluster_size), jnp.float32),
            struct((len(late), width, 2 * BLK), feats.dtype),
        ],
        [smem()] + [vmem()] * 2,
        (table, pos_blocks, feat_blocks),
    )
    kept = []
    stats = []
    for slots in groups:
        last = slots is groups[-1]
        copies = lab_count if last else 1
        shape = (cluster_size, 2 * BLK) if last else (2 * BLK, cluster_size)
        logits, stats_out = call(
            functools.partial(logit_kernel, slots, not last, copies),
            "logits",
            [
                struct((len(slots),) + shape, jnp.float32),
                struct((copies,) + stat_shape, jnp.float32),
            ],
            [smem()] + [vmem()] * (2 + len(slots) + len(stats)),
            (table, turned if last else feat_blocks, hits, *[rows[s] for s in slots], *stats),
            scratch=[pltpu.VMEM(stat_shape, jnp.float32)],
        )
        kept.append(logits)
        stats = [stats_out]

    in_specs = [smem()] + [vmem()] * (3 + len(groups) + dp_count)
    loss_type = struct((block_count, BLK), jnp.float32)
    lse_scratch = pltpu.VMEM((block_count, BLK), jnp.float32)
    if not square:
        all_stats = lax.all_to_all(stats[0], "label", split_axis=0, concat_axis=0, tiled=True)
        loss, parts = call(
            functools.partial(grad_kernel, groups, lab_count, pos_count),
            "grads",
            [loss_type, struct((lab_count, inst_count, part), jnp.bfloat16)],
            in_specs,
            (table, hits, shares, all_stats, *kept, *rows),
            scratch=[
                lse_scratch,
                pltpu.VMEM((block_count, BLK, BLK), jnp.float32),
                pltpu.VMEM((block_count, BLK, width), jnp.float32),
            ],
        )
        gathered = lax.all_to_all(parts, "label", split_axis=0, concat_axis=0, tiled=True)
        grads = jnp.sum(gathered.astype(jnp.float32), axis=0).astype(jnp.bfloat16)
        return loss.reshape(inst_count), grads

    owners = [
        [(2 * y + core) * lab_count + 2 * z + x for z in range(lab_count // 2) for core in range(2)]
        for y in range(dp_count // 2)
        for x in range(2)
    ]
    all_stats = lax.all_to_all(
        stats[0], both, split_axis=0, concat_axis=0, axis_index_groups=owners, tiled=True
    )
    pairs = lab_count // 2
    half_rows = inst_count // 2
    wide = struct((half_rows, part), jnp.float32)
    narrow = struct((half_rows, part), jnp.bfloat16)

    def deliver(x):
        return move(x, lambda dp, lab: ((dp & ~1) | (lab & 1), (lab & ~1) | (1 - (dp & 1))))

    ends = []
    for side in range(2):
        loss, keep, send = call(
            functools.partial(half_kernel, side, groups, lab_count, pos_count),
            "grads",
            [
                loss_type,
                struct((pairs, half_rows, part), jnp.float32),
                struct((pairs, half_rows, part), jnp.bfloat16),
            ],
            in_specs,
            (table, hits, shares, all_stats, *kept, *rows),
            scratch=[
                lse_scratch,
                pltpu.VMEM((block_count // 2, BLK, BLK), jnp.float32),
                pltpu.VMEM((block_count // 2, BLK, width), jnp.float32),
            ],
        )
        got = lax.ppermute(send, "dp", [(i, i ^ 1) for i in range(dp_count)])
        if side:
            got, loss_here = lax.optimization_barrier((got, loss_here))
        else:
            loss_here = deliver(loss)
        own, *outgoing = call(
            pair_kernel, "pair_sums", [wide] + [narrow] * (pairs - 1), [vmem()] * 2, (keep, got)
        )
        line = [own]
        for j, x in enumerate(outgoing):
            hop = [(i, i ^ (2 * j + 2)) for i in range(lab_count)]
            line.append(lax.ppermute(x, "label", hop))
        (done,) = call(line_kernel, "line_sums", [narrow], [vmem()] * pairs, line)
        ends.append(deliver(done))
    (grads,) = call(
        join_kernel, "join", [struct((inst_count, part), jnp.bfloat16)], [vmem()] * 2, ends
    )
    return loss_here.reshape(inst_count), grads


def solution(mesh):
    in_specs = (P("dp", None), P(("dp", "label"), None, None), P(), P(), P("dp", None))
    out_specs = (P("dp"), P("dp", "label"))
    return jax.shard_map(shards, mesh=mesh, in_specs=in_specs, out_specs=out_specs, check_vma=False)
```

```python
import functools

import jax
import jax.numpy as jnp
from jax import lax
from jax.experimental import pallas as pl
from jax.experimental.pallas import tpu as pltpu
from jax.sharding import PartitionSpec as P

BLK = 128
NEG_FILL = -1e30
VMEM_BYTES = 32 * 1024 * 1024
VMEM_PICK = 56 * 1024 * 1024


def divide(value, by):
    if by & (by - 1) == 0:
        return lax.shift_right_logical(value, jnp.int32(by.bit_length() - 1))
    return lax.div(value, jnp.int32(by))


def remainder(value, by):
    if by & (by - 1) == 0:
        return value & jnp.int32(by - 1)
    return lax.rem(value, jnp.int32(by))


def each_entry(count, short_count, body, carry):
    if count <= 64:
        for e in range(count):
            carry = body(e // short_count, e % short_count, carry)
        return carry
    step = lambda e, c: body(divide(e, short_count), remainder(e, short_count), c)
    return lax.fori_loop(0, count, step, carry)


class Plan:
    def __init__(self, square, dp_count, lab_count, stored, block_count, short_count):
        self.square, self.dp_count, self.lab_count = square, dp_count, lab_count
        self.stored, self.block_count, self.short_count = stored, block_count, short_count

    def here(self):
        return lax.axis_index("dp"), lax.axis_index("label")

    def home(self):
        dp, lab = self.here()
        return (dp & ~1) | (lab & 1) if self.square else dp

    def flips(self, entry, core):
        return [(0, 0), (core, 1 - core), (1 - core, core), (1, 1)][entry]

    def wanted_by(self, entry):
        dp, lab = self.here()
        if not self.square:
            return dp ^ entry
        flip_x, flip_y = self.flips(entry, dp & 1)
        return ((dp >> 1) ^ flip_y) * 2 + ((lab & 1) ^ flip_x)

    def entry_of(self, device):
        dp, lab = self.here()
        that_dp, that_lab = divide(device, self.lab_count), remainder(device, self.lab_count)
        if not self.square:
            return that_lab == lab, that_dp ^ dp
        match = ((that_dp & 1) == (dp & 1)) & ((that_lab >> 1) == (lab >> 1))
        flip_y, flip_x = (that_dp ^ dp) >> 1, (that_lab ^ lab) & 1
        core = dp & 1
        lone = jnp.where(flip_y == 1 - core, 1, 2)
        entry = jnp.where(flip_x + flip_y == 1, lone, flip_x + flip_y + (flip_x & flip_y))
        return match, entry

    def pairs(self, entry):
        result = []
        for dp in range(self.dp_count):
            for lab in range(self.lab_count):
                if self.square:
                    flip_x, flip_y = self.flips(entry, dp & 1)
                    target = (dp ^ (2 * flip_y)) * self.lab_count + (lab ^ flip_x)
                else:
                    target = (dp ^ entry) * self.lab_count + lab
                result.append((dp * self.lab_count + lab, target))
        return result


def find_slots(plan, wanted, lists_ref, slot_ref):
    dp_index, lab_index = plan.here()
    mine = dp_index * plan.lab_count + lab_index
    stored, short_count = plan.stored, plan.short_count
    found = []
    for k in wanted:
        base = plan.wanted_by(k) * plan.block_count

        def look(row, column, slot_here, base=base):
            slot = slot_ref[lists_ref[base + row, column]]
            return jnp.where(divide(slot, stored) == mine, remainder(slot, stored), slot_here)

        count = plan.block_count // 2 * short_count
        found.append(each_entry(count, short_count, look, jnp.int32(0)))
    return found


def far_kernel(plan, wanted, lists_hbm, slot_hbm, weights_ref, *rest):
    outs = rest[: len(wanted)]
    held, lists_ref, slot_ref, sems = rest[len(wanted) :]
    tables = [
        pltpu.make_async_copy(lists_hbm, lists_ref, sems.at[0]),
        pltpu.make_async_copy(slot_hbm, slot_ref, sems.at[1]),
    ]
    stage = pltpu.make_async_copy(weights_ref, held, sems.at[2])
    for copy in tables:
        copy.start()
    stage.start()
    for copy in tables:
        copy.wait()
    found = find_slots(plan, wanted, lists_ref, slot_ref)
    stage.wait()
    copies = []
    for i, slot in enumerate(found):
        copies.append(pltpu.make_async_copy(held.at[slot], outs[i], sems.at[3 + i]))
        copies[-1].start()
    for copy in copies:
        copy.wait()


def near_kernel(plan, lists_ref, slot_ref, weights_ref, table_ref, *rest):
    block_count, short_count = plan.block_count, plan.short_count
    outs, sems = rest[:-1], rest[-1]
    copies = []
    for k, slot in enumerate(find_slots(plan, range(1), lists_ref, slot_ref)):
        copies.append(pltpu.make_async_copy(weights_ref.at[slot], outs[k], sems.at[k]))
        copies[-1].start()
    home = plan.home()
    half = block_count // 2
    for side in range(2):

        def note(row, column, carry, side=side):
            block = side * half + row
            cluster = lists_ref[home * block_count + block, column]
            match, entry = plan.entry_of(divide(slot_ref[cluster], plan.stored))

            @pl.when(match)
            def _():
                table_ref[entry, 0] = cluster
                table_ref[entry, 1 + side] = jnp.int32(block)

            return carry

        each_entry(half * short_count, short_count, note, jnp.int32(0))
    for copy in copies:
        copy.wait()


def home_kernel(feats_ref, pos_ref, other_feats_ref, other_pos_ref, home_feats_ref, home_pos_ref):
    same = (lax.axis_index("dp") & 1) == (lax.axis_index("label") & 1)

    @pl.when(same)
    def _():
        home_feats_ref[...] = feats_ref[...]
        home_pos_ref[...] = pos_ref[...]

    @pl.when(jnp.logical_not(same))
    def _():
        home_feats_ref[...] = other_feats_ref[...]
        home_pos_ref[...] = other_pos_ref[...]


def target_kernel(early, late, table_ref, pos_ref, feats_ref, hits_ref, shares_ref, turned_ref):
    count, cluster_size, _ = hits_ref.shape
    pos_count = pos_ref.shape[1]

    def one_slot(s):
        labels = lax.broadcasted_iota(jnp.int32, (cluster_size, BLK), 0) + table_ref[s, 0] * cluster_size
        for side in range(2):
            pos = pos_ref[table_ref[s, 1 + side]]
            hit = pos[0:1, :] == labels
            for p in range(1, pos_count):
                hit = hit | (pos[p : p + 1, :] == labels)
            hits = jnp.where(hit, 1.0, 0.0)
            columns = pl.ds(side * BLK, BLK)
            hits_ref[s, :, columns] = hits
            if s in early:
                shares_ref[early.index(s), columns, :] = (hits / pos_count).T
            else:
                feats = feats_ref[table_ref[s, 1 + side]].astype(jnp.float32)
                turned_ref[late.index(s), :, columns] = feats.T.astype(jnp.bfloat16)

    for s in range(count):
        pl.when(table_ref[s, 0] >= 0)(functools.partial(one_slot, s))


def logit_kernel(slots, turned, copies, table_ref, feats_ref, hits_ref, *rest):
    count = len(slots)
    rows = rest[:count]
    logits_ref, out_ref, stats_ref = rest[-3:]
    if len(rest) == count + 3:
        stats_ref[0] = jnp.full(stats_ref.shape[1:], NEG_FILL, jnp.float32)
        stats_ref[1] = jnp.zeros(stats_ref.shape[1:], jnp.float32)
        stats_ref[2] = jnp.zeros(stats_ref.shape[1:], jnp.float32)
    else:
        stats_ref[...] = rest[count][0]
    for i, (s, ref) in enumerate(zip(slots, rows)):
        if not turned:
            logits_ref[i] = jnp.dot(ref[...], feats_ref[i], preferred_element_type=jnp.float32)
        for side in range(2):
            block = table_ref[s, 1 + side]
            columns = pl.ds(side * BLK, BLK)
            if turned:
                logits = lax.dot_general(
                    ref[...],
                    feats_ref[block],
                    (((1,), (1,)), ((), ())),
                    preferred_element_type=jnp.float32,
                )
                logits_ref[i, columns, :] = logits.T
            else:
                logits = logits_ref[i, :, columns]
            highest = jnp.max(logits, axis=0, keepdims=True)
            total = jnp.sum(jnp.exp(logits - highest), axis=0, keepdims=True)
            positive = jnp.sum(hits_ref[s, :, columns] * logits, axis=0, keepdims=True)
            row = pl.ds(block, 1)
            before = stats_ref[0, row, :]
            after = jnp.maximum(before, highest)
            stats_ref[0, row, :] = after
            stats_ref[1, row, :] = stats_ref[1, row, :] * jnp.exp(before - after) + total * jnp.exp(
                highest - after
            )
            stats_ref[2, row, :] = stats_ref[2, row, :] + positive
    for i in range(copies):
        out_ref[i] = stats_ref[...]


def row_sums(stats_ref, lab_count):
    highest = stats_ref[0, 0]
    for i in range(1, lab_count):
        highest = jnp.maximum(highest, stats_ref[i, 0])
    summed = jnp.zeros_like(highest)
    positive = jnp.zeros_like(highest)
    for i in range(lab_count):
        summed = summed + stats_ref[i, 1] * jnp.exp(stats_ref[i, 0] - highest)
        positive = positive + stats_ref[i, 2]
    return highest + jnp.log(summed), positive


def prepare(stats_ref, pos_count, lab_count, loss_ref, lse_ref, columns_ref, total_ref, first):
    lse, positive = row_sums(stats_ref, lab_count)
    lse_ref[...] = lse
    loss_ref[...] = lse - positive / pos_count
    for b in range(columns_ref.shape[0]):
        columns_ref[b] = jnp.broadcast_to(lse[first + b : first + b + 1, :], (BLK, BLK)).T
    total_ref[...] = jnp.zeros_like(total_ref)


def add_slots(sides, groups, pos_count, first, table_ref, hits_ref, shares_ref, logits_refs, rows, sums):
    lse_ref, columns_ref, total_ref = sums
    early = [s for slots in groups[:-1] for s in slots]
    cluster_size = rows[0].shape[0]

    def one_slot(s, logits_ref):
        for side in sides:
            block = table_ref[s, 1 + side]
            here = pl.ds(side * BLK, BLK)
            if s in early:
                column = columns_ref[block - first]
                column = jnp.concatenate([column] * (cluster_size // BLK), axis=1)
                dlogit = jnp.exp(logits_ref[here, :] - column) - shares_ref[early.index(s), here, :]
            else:
                row = lse_ref[pl.ds(block, 1), :]
                dlogit = jnp.exp(logits_ref[:, here] - row) - hits_ref[s, :, here] / pos_count
                dlogit = dlogit.T
            total_ref[block - first] += lax.dot_general(
                dlogit.astype(jnp.bfloat16),
                rows[s][...],
                (((1,), (0,)), ((), ())),
                preferred_element_type=jnp.float32,
            )

    for slots, logits_ref in zip(groups, logits_refs):
        for i, s in enumerate(slots):
            body = functools.partial(one_slot, s, logits_ref.at[i])
            if len(rows) <= 4:
                body()
            else:
                pl.when(table_ref[s, 0] >= 0)(body)


def half_kernel(side, groups, lab_count, pos_count, table_ref, hits_ref, shares_ref, stats_ref, *rest):
    logits_refs = rest[: len(groups)]
    rows = rest[len(groups) : -6]
    loss_ref, keep_ref, send_ref, lse_ref, columns_ref, total_ref = rest[-6:]
    half = total_ref.shape[0]
    prepare(
        stats_ref, pos_count, lab_count, loss_ref, lse_ref, columns_ref, total_ref, side * half
    )
    add_slots(
        (side,),
        groups,
        pos_count,
        side * half,
        table_ref,
        hits_ref,
        shares_ref,
        logits_refs,
        rows,
        (lse_ref, columns_ref, total_ref),
    )
    part = keep_ref.shape[2]
    core, line = lax.axis_index("dp") & 1, lax.axis_index("label") >> 1
    for j in range(lab_count // 2):
        first = (line ^ j) * 2
        mine = pl.ds(pl.multiple_of((first + 1 - core) * part, part), part)
        other = pl.ds(pl.multiple_of((first + core) * part, part), part)
        for b in range(half):
            here = pl.ds(b * BLK, BLK)
            keep_ref[j, here, :] = total_ref[b, :, mine]
            send_ref[j, here, :] = total_ref[b, :, other].astype(jnp.bfloat16)


def pair_kernel(keep_ref, got_ref, *outs):
    for j, out_ref in enumerate(outs):
        out_ref[...] = (keep_ref[j] + got_ref[j].astype(jnp.float32)).astype(out_ref.dtype)


def line_kernel(count, loss_ref, *refs):
    out_ref, terms_ref = refs[-2:]
    rows = refs[0].shape[0]
    for h in range(2):
        total = refs[h * count][...]
        for ref in refs[h * count + 1 : (h + 1) * count]:
            total = total + ref[...].astype(jnp.float32)
        out_ref[h * rows : (h + 1) * rows, :] = total.astype(jnp.bfloat16)
    terms_ref[...] = jnp.zeros_like(terms_ref)
    blocks = loss_ref.shape[0]
    rest = loss_ref[...]
    for i in range(3):
        term = rest.astype(jnp.bfloat16).astype(jnp.float32)
        terms_ref[i * blocks : (i + 1) * blocks, :] = term
        rest = rest - term
    out_ref[2 * rows :, :] = terms_ref[...].astype(jnp.bfloat16)


def home_again_kernel(got_ref, loss_ref, grads_ref):
    blocks = loss_ref.shape[0]
    count = grads_ref.shape[0]
    grads_ref[...] = got_ref[:count, :]
    terms = got_ref[count:, :].astype(jnp.float32)
    loss_ref[...] = terms[:blocks] + (terms[blocks : 2 * blocks] + terms[2 * blocks : 3 * blocks])


def grad_kernel(groups, lab_count, pos_count, table_ref, hits_ref, shares_ref, stats_ref, *rest):
    logits_refs = rest[: len(groups)]
    rows = rest[len(groups) : -5]
    loss_ref, out_ref, lse_ref, columns_ref, total_ref = rest[-5:]
    prepare(stats_ref, pos_count, lab_count, loss_ref, lse_ref, columns_ref, total_ref, 0)
    add_slots(
        (0, 1),
        groups,
        pos_count,
        0,
        table_ref,
        hits_ref,
        shares_ref,
        logits_refs,
        rows,
        (lse_ref, columns_ref, total_ref),
    )
    part = out_ref.shape[2]
    for j in range(lab_count):
        for b in range(total_ref.shape[0]):
            out_ref[j, b * BLK : (b + 1) * BLK, :] = total_ref[
                b, :, j * part : (j + 1) * part
            ].astype(jnp.bfloat16)


def smem():
    return pl.BlockSpec(memory_space=pltpu.SMEM)


def vmem():
    return pl.BlockSpec(memory_space=pltpu.VMEM)


def anywhere():
    return pl.BlockSpec(memory_space=pl.ANY)


def call(kernel, name, out_shape, in_specs, arrays, scratch=(), limit=VMEM_BYTES, out_specs=None):
    return pl.pallas_call(
        kernel,
        out_shape=out_shape,
        in_specs=in_specs,
        out_specs=out_specs or [vmem()] * len(out_shape),
        scratch_shapes=list(scratch),
        compiler_params=pltpu.CompilerParams(vmem_limit_bytes=limit),
        name=name,
    )(*arrays)


def shards(feats, weights, shortlist, slot_of, positives):
    dp_count = lax.axis_size("dp")
    lab_count = lax.axis_size("label")
    stored, cluster_size, width = weights.shape
    inst_count = feats.shape[0]
    pos_count = positives.shape[1]
    block_count = inst_count // BLK
    part = width // lab_count
    square = dp_count == 4 and lab_count == 8 and part % 128 == 0
    plan = Plan(square, dp_count, lab_count, stored, block_count, shortlist.shape[1])
    struct = jax.ShapeDtypeStruct
    row_type = struct((cluster_size, width), weights.dtype)
    stat_shape = (3, block_count, BLK)
    both = ("dp", "label")
    devices = [(dp, lab) for dp in range(dp_count) for lab in range(lab_count)]

    def move(x, target):
        pairs = []
        for dp, lab in devices:
            to_dp, to_lab = target(dp, lab)
            pairs.append((dp * lab_count + lab, to_dp * lab_count + to_lab))
        return lax.ppermute(x, both, pairs)

    feat_blocks = feats.reshape(block_count, BLK, width)
    pos_blocks = positives.reshape(block_count, BLK, pos_count).transpose(0, 2, 1)
    if square:
        other_feats = lax.ppermute(feat_blocks, "dp", [(i, i ^ 1) for i in range(dp_count)])
        other_pos = lax.ppermute(pos_blocks, "dp", [(i, i ^ 1) for i in range(dp_count)])
        feat_blocks, pos_blocks = call(
            home_kernel,
            "home",
            [struct(feat_blocks.shape, feats.dtype), struct(pos_blocks.shape, jnp.int32)],
            [vmem()] * 4,
            (feat_blocks, pos_blocks, other_feats, other_pos),
        )

    far = range(1, dp_count)
    far_rows = call(
        functools.partial(far_kernel, plan, far),
        "pick_far",
        [row_type] * len(far),
        [anywhere()] * 3,
        (shortlist, slot_of, weights),
        scratch=[
            pltpu.VMEM(weights.shape, weights.dtype),
            pltpu.SMEM(shortlist.shape, jnp.int32),
            pltpu.SMEM(slot_of.shape, jnp.int32),
            pltpu.SemaphoreType.DMA((3 + len(far),)),
        ],
        limit=VMEM_PICK,
        out_specs=[anywhere()] * len(far),
    )
    table, *rows = call(
        functools.partial(near_kernel, plan),
        "pick_near",
        [struct((dp_count, 4), jnp.int32), row_type],
        [smem(), smem(), anywhere()],
        (shortlist, slot_of, weights),
        scratch=[pltpu.SemaphoreType.DMA((1,))],
        out_specs=[smem(), vmem()],
    )
    rows += [lax.ppermute(x, both, plan.pairs(k)) for k, x in zip(far, far_rows)]

    if square:
        groups = [(0,), (1,), (2,), (3,)]
    else:
        cuts = (0, dp_count // 2, dp_count * 3 // 4, dp_count)
        groups = [tuple(range(a, b)) for a, b in zip(cuts[:-1], cuts[1:])]
    early = [s for slots in groups[:-1] for s in slots]
    late = list(groups[-1])
    hits, shares, turned = call(
        functools.partial(target_kernel, early, late),
        "targets",
        [
            struct((dp_count, cluster_size, 2 * BLK), jnp.float32),
            struct((len(early), 2 * BLK, cluster_size), jnp.float32),
            struct((len(late), width, 2 * BLK), feats.dtype),
        ],
        [smem()] + [vmem()] * 2,
        (table, pos_blocks, feat_blocks),
    )
    kept = []
    stats = []
    for slots in groups:
        last = slots is groups[-1]
        copies = lab_count if last else 1
        shape = (cluster_size, 2 * BLK) if last else (2 * BLK, cluster_size)
        logits, stats_out = call(
            functools.partial(logit_kernel, slots, not last, copies),
            "logits",
            [
                struct((len(slots),) + shape, jnp.float32),
                struct((copies,) + stat_shape, jnp.float32),
            ],
            [smem()] + [vmem()] * (2 + len(slots) + len(stats)),
            (table, turned if last else feat_blocks, hits, *[rows[s] for s in slots], *stats),
            scratch=[pltpu.VMEM(stat_shape, jnp.float32)],
        )
        kept.append(logits)
        stats = [stats_out]

    in_specs = [smem()] + [vmem()] * (3 + len(groups) + dp_count)
    loss_type = struct((block_count, BLK), jnp.float32)
    lse_scratch = pltpu.VMEM((block_count, BLK), jnp.float32)
    if not square:
        all_stats = lax.all_to_all(stats[0], "label", split_axis=0, concat_axis=0, tiled=True)
        loss, parts = call(
            functools.partial(grad_kernel, groups, lab_count, pos_count),
            "grads",
            [loss_type, struct((lab_count, inst_count, part), jnp.bfloat16)],
            in_specs,
            (table, hits, shares, all_stats, *kept, *rows),
            scratch=[
                lse_scratch,
                pltpu.VMEM((block_count, BLK, BLK), jnp.float32),
                pltpu.VMEM((block_count, BLK, width), jnp.float32),
            ],
        )
        gathered = lax.all_to_all(parts, "label", split_axis=0, concat_axis=0, tiled=True)
        grads = jnp.sum(gathered.astype(jnp.float32), axis=0).astype(jnp.bfloat16)
        return loss.reshape(inst_count), grads

    owners = [
        [(2 * y + core) * lab_count + 2 * z + x for z in range(lab_count // 2) for core in range(2)]
        for y in range(dp_count // 2)
        for x in range(2)
    ]
    all_stats = lax.all_to_all(
        stats[0], both, split_axis=0, concat_axis=0, axis_index_groups=owners, tiled=True
    )
    pairs = lab_count // 2
    half_rows = inst_count // 2
    wide = struct((half_rows, part), jnp.float32)
    narrow = struct((half_rows, part), jnp.bfloat16)

    parts = []
    for side in range(2):
        loss, keep, send = call(
            functools.partial(half_kernel, side, groups, lab_count, pos_count),
            "grads",
            [
                loss_type,
                struct((pairs, half_rows, part), jnp.float32),
                struct((pairs, half_rows, part), jnp.bfloat16),
            ],
            in_specs,
            (table, hits, shares, all_stats, *kept, *rows),
            scratch=[
                lse_scratch,
                pltpu.VMEM((block_count // 2, BLK, BLK), jnp.float32),
                pltpu.VMEM((block_count // 2, BLK, width), jnp.float32),
            ],
        )
        got = lax.ppermute(send, "dp", [(i, i ^ 1) for i in range(dp_count)])
        own, *outgoing = call(
            pair_kernel, "pair_sums", [wide] + [narrow] * (pairs - 1), [vmem()] * 2, (keep, got)
        )
        parts.append(own)
        for j, x in enumerate(outgoing):
            hop = [(i, i ^ (2 * j + 2)) for i in range(lab_count)]
            parts.append(lax.ppermute(x, "label", hop))
    extra = -(-3 * block_count // 16) * 16
    (done,) = call(
        functools.partial(line_kernel, pairs),
        "line_sums",
        [struct((inst_count + extra, part), jnp.bfloat16)],
        [vmem()] * (1 + 2 * pairs),
        (loss, *parts),
        scratch=[pltpu.VMEM((extra, part), jnp.float32)],
    )
    home = move(done, lambda dp, lab: ((dp & ~1) | (lab & 1), (lab & ~1) | (1 - (dp & 1))))
    loss, grads = call(
        home_again_kernel,
        "home_again",
        [loss_type, struct((inst_count, part), jnp.bfloat16)],
        [vmem()],
        (home,),
    )
    return loss.reshape(inst_count), grads


def solution(mesh):
    in_specs = (P("dp", None), P(("dp", "label"), None, None), P(), P(), P("dp", None))
    out_specs = (P("dp"), P("dp", "label"))
    return jax.shard_map(shards, mesh=mesh, in_specs=in_specs, out_specs=out_specs, check_vma=False)
```

```python
import functools

import jax
import jax.numpy as jnp
from jax import lax
from jax.experimental import pallas as pl
from jax.experimental.pallas import tpu as pltpu
from jax.sharding import PartitionSpec as P

BLK = 128
NEG_FILL = -1e30
VMEM_BYTES = 32 * 1024 * 1024
VMEM_PICK = 56 * 1024 * 1024


def divide(value, by):
    if by & (by - 1) == 0:
        return lax.shift_right_logical(value, jnp.int32(by.bit_length() - 1))
    return lax.div(value, jnp.int32(by))


def remainder(value, by):
    if by & (by - 1) == 0:
        return value & jnp.int32(by - 1)
    return lax.rem(value, jnp.int32(by))


def each_entry(count, short_count, body, carry):
    if count <= 64:
        for e in range(count):
            carry = body(e // short_count, e % short_count, carry)
        return carry
    step = lambda e, c: body(divide(e, short_count), remainder(e, short_count), c)
    return lax.fori_loop(0, count, step, carry)


class Plan:
    def __init__(self, square, dp_count, lab_count, stored, block_count, short_count):
        self.square, self.dp_count, self.lab_count = square, dp_count, lab_count
        self.stored, self.block_count, self.short_count = stored, block_count, short_count

    def here(self):
        return lax.axis_index("dp"), lax.axis_index("label")

    def home(self):
        dp, lab = self.here()
        return (dp & ~1) | (lab & 1) if self.square else dp

    def flips(self, entry, core):
        return [(0, 0), (core, 1 - core), (1 - core, core), (1, 1)][entry]

    def wanted_by(self, entry):
        dp, lab = self.here()
        if not self.square:
            return dp ^ entry
        flip_x, flip_y = self.flips(entry, dp & 1)
        return ((dp >> 1) ^ flip_y) * 2 + ((lab & 1) ^ flip_x)

    def entry_of(self, device):
        dp, lab = self.here()
        that_dp, that_lab = divide(device, self.lab_count), remainder(device, self.lab_count)
        if not self.square:
            return that_lab == lab, that_dp ^ dp
        match = ((that_dp & 1) == (dp & 1)) & ((that_lab >> 1) == (lab >> 1))
        flip_y, flip_x = (that_dp ^ dp) >> 1, (that_lab ^ lab) & 1
        core = dp & 1
        lone = jnp.where(flip_y == 1 - core, 1, 2)
        entry = jnp.where(flip_x + flip_y == 1, lone, flip_x + flip_y + (flip_x & flip_y))
        return match, entry

    def pairs(self, entry):
        result = []
        for dp in range(self.dp_count):
            for lab in range(self.lab_count):
                if self.square:
                    flip_x, flip_y = self.flips(entry, dp & 1)
                    target = (dp ^ (2 * flip_y)) * self.lab_count + (lab ^ flip_x)
                else:
                    target = (dp ^ entry) * self.lab_count + lab
                result.append((dp * self.lab_count + lab, target))
        return result


def find_slots(plan, wanted, lists_ref, slot_ref):
    dp_index, lab_index = plan.here()
    mine = dp_index * plan.lab_count + lab_index
    stored, short_count = plan.stored, plan.short_count
    found = []
    for k in wanted:
        base = plan.wanted_by(k) * plan.block_count

        def look(row, column, slot_here, base=base):
            slot = slot_ref[lists_ref[base + row, column]]
            return jnp.where(divide(slot, stored) == mine, remainder(slot, stored), slot_here)

        count = plan.block_count // 2 * short_count
        found.append(each_entry(count, short_count, look, jnp.int32(0)))
    return found


def far_kernel(plan, wanted, lists_hbm, slot_hbm, weights_ref, *rest):
    outs = rest[: len(wanted)]
    held, lists_ref, slot_ref, sems = rest[len(wanted) :]
    tables = [
        pltpu.make_async_copy(lists_hbm, lists_ref, sems.at[0]),
        pltpu.make_async_copy(slot_hbm, slot_ref, sems.at[1]),
    ]
    stage = pltpu.make_async_copy(weights_ref, held, sems.at[2])
    for copy in tables:
        copy.start()
    stage.start()
    for copy in tables:
        copy.wait()
    found = find_slots(plan, wanted, lists_ref, slot_ref)
    stage.wait()
    copies = []
    for i, slot in enumerate(found):
        copies.append(pltpu.make_async_copy(held.at[slot], outs[i], sems.at[3 + i]))
        copies[-1].start()
    for copy in copies:
        copy.wait()


def near_kernel(plan, lists_ref, slot_ref, weights_ref, table_ref, *rest):
    block_count, short_count = plan.block_count, plan.short_count
    outs, sems = rest[:-1], rest[-1]
    copies = []
    for k, slot in enumerate(find_slots(plan, range(1), lists_ref, slot_ref)):
        copies.append(pltpu.make_async_copy(weights_ref.at[slot], outs[k], sems.at[k]))
        copies[-1].start()
    home = plan.home()
    half = block_count // 2
    for side in range(2):

        def note(row, column, carry, side=side):
            block = side * half + row
            cluster = lists_ref[home * block_count + block, column]
            match, entry = plan.entry_of(divide(slot_ref[cluster], plan.stored))

            @pl.when(match)
            def _():
                table_ref[entry, 0] = cluster
                table_ref[entry, 1 + side] = jnp.int32(block)

            return carry

        each_entry(half * short_count, short_count, note, jnp.int32(0))
    for copy in copies:
        copy.wait()


def home_kernel(feats_ref, pos_ref, other_feats_ref, other_pos_ref, home_feats_ref, home_pos_ref):
    same = (lax.axis_index("dp") & 1) == (lax.axis_index("label") & 1)

    @pl.when(same)
    def _():
        home_feats_ref[...] = feats_ref[...]
        home_pos_ref[...] = pos_ref[...]

    @pl.when(jnp.logical_not(same))
    def _():
        home_feats_ref[...] = other_feats_ref[...]
        home_pos_ref[...] = other_pos_ref[...]


def target_kernel(early, late, table_ref, pos_ref, feats_ref, hits_ref, shares_ref, turned_ref):
    count, cluster_size, _ = hits_ref.shape
    pos_count = pos_ref.shape[1]

    def one_slot(s):
        labels = lax.broadcasted_iota(jnp.int32, (cluster_size, BLK), 0) + table_ref[s, 0] * cluster_size
        for side in range(2):
            pos = pos_ref[table_ref[s, 1 + side]]
            hit = pos[0:1, :] == labels
            for p in range(1, pos_count):
                hit = hit | (pos[p : p + 1, :] == labels)
            hits = jnp.where(hit, 1.0, 0.0)
            columns = pl.ds(side * BLK, BLK)
            hits_ref[s, :, columns] = hits
            if s in early:
                shares_ref[early.index(s), columns, :] = (hits / pos_count).T
            else:
                feats = feats_ref[table_ref[s, 1 + side]].astype(jnp.float32)
                turned_ref[late.index(s), :, columns] = feats.T.astype(jnp.bfloat16)

    for s in range(count):
        pl.when(table_ref[s, 0] >= 0)(functools.partial(one_slot, s))


def logit_kernel(slots, turned, copies, table_ref, feats_ref, hits_ref, *rest):
    count = len(slots)
    rows = rest[:count]
    logits_ref, out_ref, stats_ref = rest[-3:]
    if len(rest) == count + 3:
        stats_ref[0] = jnp.full(stats_ref.shape[1:], NEG_FILL, jnp.float32)
        stats_ref[1] = jnp.zeros(stats_ref.shape[1:], jnp.float32)
        stats_ref[2] = jnp.zeros(stats_ref.shape[1:], jnp.float32)
    else:
        stats_ref[...] = rest[count][0]
    for i, (s, ref) in enumerate(zip(slots, rows)):
        if not turned:
            logits_ref[i] = jnp.dot(ref[...], feats_ref[i], preferred_element_type=jnp.float32)
        for side in range(2):
            block = table_ref[s, 1 + side]
            columns = pl.ds(side * BLK, BLK)
            if turned:
                logits = lax.dot_general(
                    ref[...],
                    feats_ref[block],
                    (((1,), (1,)), ((), ())),
                    preferred_element_type=jnp.float32,
                )
                logits_ref[i, columns, :] = logits.T
            else:
                logits = logits_ref[i, :, columns]
            highest = jnp.max(logits, axis=0, keepdims=True)
            total = jnp.sum(jnp.exp(logits - highest), axis=0, keepdims=True)
            positive = jnp.sum(hits_ref[s, :, columns] * logits, axis=0, keepdims=True)
            row = pl.ds(block, 1)
            before = stats_ref[0, row, :]
            after = jnp.maximum(before, highest)
            stats_ref[0, row, :] = after
            stats_ref[1, row, :] = stats_ref[1, row, :] * jnp.exp(before - after) + total * jnp.exp(
                highest - after
            )
            stats_ref[2, row, :] = stats_ref[2, row, :] + positive
    for i in range(copies):
        out_ref[i] = stats_ref[...]


def row_sums(stats_ref, lab_count):
    highest = stats_ref[0, 0]
    for i in range(1, lab_count):
        highest = jnp.maximum(highest, stats_ref[i, 0])
    summed = jnp.zeros_like(highest)
    positive = jnp.zeros_like(highest)
    for i in range(lab_count):
        summed = summed + stats_ref[i, 1] * jnp.exp(stats_ref[i, 0] - highest)
        positive = positive + stats_ref[i, 2]
    return highest + jnp.log(summed), positive


def prepare(stats_ref, pos_count, lab_count, loss_ref, lse_ref, columns_ref, total_ref, first):
    lse, positive = row_sums(stats_ref, lab_count)
    lse_ref[...] = lse
    loss_ref[...] = lse - positive / pos_count
    for b in range(columns_ref.shape[0]):
        columns_ref[b] = jnp.broadcast_to(lse[first + b : first + b + 1, :], (BLK, BLK)).T
    total_ref[...] = jnp.zeros_like(total_ref)


def add_slots(sides, groups, pos_count, first, table_ref, hits_ref, shares_ref, logits_refs, rows, sums):
    lse_ref, columns_ref, total_ref = sums
    early = [s for slots in groups[:-1] for s in slots]
    cluster_size = rows[0].shape[0]

    def one_slot(s, logits_ref):
        for side in sides:
            block = table_ref[s, 1 + side]
            here = pl.ds(side * BLK, BLK)
            if s in early:
                column = columns_ref[block - first]
                column = jnp.concatenate([column] * (cluster_size // BLK), axis=1)
                dlogit = jnp.exp(logits_ref[here, :] - column) - shares_ref[early.index(s), here, :]
            else:
                row = lse_ref[pl.ds(block, 1), :]
                dlogit = jnp.exp(logits_ref[:, here] - row) - hits_ref[s, :, here] / pos_count
                dlogit = dlogit.T
            total_ref[block - first] += lax.dot_general(
                dlogit.astype(jnp.bfloat16),
                rows[s][...],
                (((1,), (0,)), ((), ())),
                preferred_element_type=jnp.float32,
            )

    for slots, logits_ref in zip(groups, logits_refs):
        for i, s in enumerate(slots):
            body = functools.partial(one_slot, s, logits_ref.at[i])
            if len(rows) <= 4:
                body()
            else:
                pl.when(table_ref[s, 0] >= 0)(body)


def half_kernel(side, groups, lab_count, pos_count, table_ref, hits_ref, shares_ref, stats_ref, *rest):
    logits_refs = rest[: len(groups)]
    rows = rest[len(groups) : -6]
    loss_ref, keep_ref, send_ref, lse_ref, columns_ref, total_ref = rest[-6:]
    half = total_ref.shape[0]
    prepare(
        stats_ref, pos_count, lab_count, loss_ref, lse_ref, columns_ref, total_ref, side * half
    )
    add_slots(
        (side,),
        groups,
        pos_count,
        side * half,
        table_ref,
        hits_ref,
        shares_ref,
        logits_refs,
        rows,
        (lse_ref, columns_ref, total_ref),
    )
    part = keep_ref.shape[2]
    core, line = lax.axis_index("dp") & 1, lax.axis_index("label") >> 1
    for j in range(lab_count // 2):
        first = (line ^ j) * 2
        mine = pl.ds(pl.multiple_of((first + 1 - core) * part, part), part)
        other = pl.ds(pl.multiple_of((first + core) * part, part), part)
        for b in range(half):
            here = pl.ds(b * BLK, BLK)
            keep_ref[j, here, :] = total_ref[b, :, mine]
            send_ref[j, here, :] = total_ref[b, :, other].astype(jnp.bfloat16)


def pair_kernel(keep_ref, got_ref, next_ref, send_ref):
    for j in range(keep_ref.shape[0]):
        total = keep_ref[j] + got_ref[j].astype(jnp.float32)
        out_ref = send_ref if j % 2 else next_ref
        out_ref[j // 2] = total.astype(out_ref.dtype)


def step_kernel(keep_ref, got_ref, own_ref, send_ref):
    own_ref[...] = keep_ref[0] + got_ref[0].astype(jnp.float32)
    send_ref[...] = (keep_ref[1] + got_ref[1].astype(jnp.float32)).astype(jnp.bfloat16)


def line_kernel(count, loss_ref, *refs):
    out_ref, terms_ref = refs[-2:]
    rows = refs[0].shape[0]
    for h in range(2):
        total = refs[h * count][...]
        for ref in refs[h * count + 1 : (h + 1) * count]:
            total = total + ref[...].astype(jnp.float32)
        out_ref[h * rows : (h + 1) * rows, :] = total.astype(jnp.bfloat16)
    terms_ref[...] = jnp.zeros_like(terms_ref)
    blocks = loss_ref.shape[0]
    rest = loss_ref[...]
    for i in range(3):
        term = rest.astype(jnp.bfloat16).astype(jnp.float32)
        terms_ref[i * blocks : (i + 1) * blocks, :] = term
        rest = rest - term
    out_ref[2 * rows :, :] = terms_ref[...].astype(jnp.bfloat16)


def home_again_kernel(got_ref, loss_ref, grads_ref):
    blocks = loss_ref.shape[0]
    count = grads_ref.shape[0]
    grads_ref[...] = got_ref[:count, :]
    terms = got_ref[count:, :].astype(jnp.float32)
    loss_ref[...] = terms[:blocks] + (terms[blocks : 2 * blocks] + terms[2 * blocks : 3 * blocks])


def grad_kernel(groups, lab_count, pos_count, table_ref, hits_ref, shares_ref, stats_ref, *rest):
    logits_refs = rest[: len(groups)]
    rows = rest[len(groups) : -5]
    loss_ref, out_ref, lse_ref, columns_ref, total_ref = rest[-5:]
    prepare(stats_ref, pos_count, lab_count, loss_ref, lse_ref, columns_ref, total_ref, 0)
    add_slots(
        (0, 1),
        groups,
        pos_count,
        0,
        table_ref,
        hits_ref,
        shares_ref,
        logits_refs,
        rows,
        (lse_ref, columns_ref, total_ref),
    )
    part = out_ref.shape[2]
    for j in range(lab_count):
        for b in range(total_ref.shape[0]):
            out_ref[j, b * BLK : (b + 1) * BLK, :] = total_ref[
                b, :, j * part : (j + 1) * part
            ].astype(jnp.bfloat16)


def smem():
    return pl.BlockSpec(memory_space=pltpu.SMEM)


def vmem():
    return pl.BlockSpec(memory_space=pltpu.VMEM)


def anywhere():
    return pl.BlockSpec(memory_space=pl.ANY)


def call(kernel, name, out_shape, in_specs, arrays, scratch=(), limit=VMEM_BYTES, out_specs=None):
    return pl.pallas_call(
        kernel,
        out_shape=out_shape,
        in_specs=in_specs,
        out_specs=out_specs or [vmem()] * len(out_shape),
        scratch_shapes=list(scratch),
        compiler_params=pltpu.CompilerParams(vmem_limit_bytes=limit),
        name=name,
    )(*arrays)


def shards(feats, weights, shortlist, slot_of, positives):
    dp_count = lax.axis_size("dp")
    lab_count = lax.axis_size("label")
    stored, cluster_size, width = weights.shape
    inst_count = feats.shape[0]
    pos_count = positives.shape[1]
    block_count = inst_count // BLK
    part = width // lab_count
    square = dp_count == 4 and lab_count == 8 and part % 128 == 0
    plan = Plan(square, dp_count, lab_count, stored, block_count, shortlist.shape[1])
    struct = jax.ShapeDtypeStruct
    row_type = struct((cluster_size, width), weights.dtype)
    stat_shape = (3, block_count, BLK)
    both = ("dp", "label")
    devices = [(dp, lab) for dp in range(dp_count) for lab in range(lab_count)]

    def move(x, target):
        pairs = []
        for dp, lab in devices:
            to_dp, to_lab = target(dp, lab)
            pairs.append((dp * lab_count + lab, to_dp * lab_count + to_lab))
        return lax.ppermute(x, both, pairs)

    feat_blocks = feats.reshape(block_count, BLK, width)
    pos_blocks = positives.reshape(block_count, BLK, pos_count).transpose(0, 2, 1)
    if square:
        other_feats = lax.ppermute(feat_blocks, "dp", [(i, i ^ 1) for i in range(dp_count)])
        other_pos = lax.ppermute(pos_blocks, "dp", [(i, i ^ 1) for i in range(dp_count)])
        feat_blocks, pos_blocks = call(
            home_kernel,
            "home",
            [struct(feat_blocks.shape, feats.dtype), struct(pos_blocks.shape, jnp.int32)],
            [vmem()] * 4,
            (feat_blocks, pos_blocks, other_feats, other_pos),
        )

    far = range(1, dp_count)
    far_rows = call(
        functools.partial(far_kernel, plan, far),
        "pick_far",
        [row_type] * len(far),
        [anywhere()] * 3,
        (shortlist, slot_of, weights),
        scratch=[
            pltpu.VMEM(weights.shape, weights.dtype),
            pltpu.SMEM(shortlist.shape, jnp.int32),
            pltpu.SMEM(slot_of.shape, jnp.int32),
            pltpu.SemaphoreType.DMA((3 + len(far),)),
        ],
        limit=VMEM_PICK,
        out_specs=[anywhere()] * len(far),
    )
    table, *rows = call(
        functools.partial(near_kernel, plan),
        "pick_near",
        [struct((dp_count, 4), jnp.int32), row_type],
        [smem(), smem(), anywhere()],
        (shortlist, slot_of, weights),
        scratch=[pltpu.SemaphoreType.DMA((1,))],
        out_specs=[smem(), vmem()],
    )
    rows += [lax.ppermute(x, both, plan.pairs(k)) for k, x in zip(far, far_rows)]

    if square:
        groups = [(0,), (1,), (2,), (3,)]
    else:
        cuts = (0, dp_count // 2, dp_count * 3 // 4, dp_count)
        groups = [tuple(range(a, b)) for a, b in zip(cuts[:-1], cuts[1:])]
    early = [s for slots in groups[:-1] for s in slots]
    late = list(groups[-1])
    hits, shares, turned = call(
        functools.partial(target_kernel, early, late),
        "targets",
        [
            struct((dp_count, cluster_size, 2 * BLK), jnp.float32),
            struct((len(early), 2 * BLK, cluster_size), jnp.float32),
            struct((len(late), width, 2 * BLK), feats.dtype),
        ],
        [smem()] + [vmem()] * 2,
        (table, pos_blocks, feat_blocks),
    )
    kept = []
    stats = []
    for slots in groups:
        last = slots is groups[-1]
        copies = lab_count if last else 1
        shape = (cluster_size, 2 * BLK) if last else (2 * BLK, cluster_size)
        logits, stats_out = call(
            functools.partial(logit_kernel, slots, not last, copies),
            "logits",
            [
                struct((len(slots),) + shape, jnp.float32),
                struct((copies,) + stat_shape, jnp.float32),
            ],
            [smem()] + [vmem()] * (2 + len(slots) + len(stats)),
            (table, turned if last else feat_blocks, hits, *[rows[s] for s in slots], *stats),
            scratch=[pltpu.VMEM(stat_shape, jnp.float32)],
        )
        kept.append(logits)
        stats = [stats_out]

    in_specs = [smem()] + [vmem()] * (3 + len(groups) + dp_count)
    loss_type = struct((block_count, BLK), jnp.float32)
    lse_scratch = pltpu.VMEM((block_count, BLK), jnp.float32)
    if not square:
        all_stats = lax.all_to_all(stats[0], "label", split_axis=0, concat_axis=0, tiled=True)
        loss, parts = call(
            functools.partial(grad_kernel, groups, lab_count, pos_count),
            "grads",
            [loss_type, struct((lab_count, inst_count, part), jnp.bfloat16)],
            in_specs,
            (table, hits, shares, all_stats, *kept, *rows),
            scratch=[
                lse_scratch,
                pltpu.VMEM((block_count, BLK, BLK), jnp.float32),
                pltpu.VMEM((block_count, BLK, width), jnp.float32),
            ],
        )
        gathered = lax.all_to_all(parts, "label", split_axis=0, concat_axis=0, tiled=True)
        grads = jnp.sum(gathered.astype(jnp.float32), axis=0).astype(jnp.bfloat16)
        return loss.reshape(inst_count), grads

    owners = [
        [(2 * y + core) * lab_count + 2 * z + x for z in range(lab_count // 2) for core in range(2)]
        for y in range(dp_count // 2)
        for x in range(2)
    ]
    all_stats = lax.all_to_all(
        stats[0], both, split_axis=0, concat_axis=0, axis_index_groups=owners, tiled=True
    )
    pairs = lab_count // 2
    half_rows = inst_count // 2
    wide = struct((half_rows, part), jnp.float32)
    narrow = struct((half_rows, part), jnp.bfloat16)

    parts = []
    for side in range(2):
        loss, keep, send = call(
            functools.partial(half_kernel, side, groups, lab_count, pos_count),
            "grads",
            [
                loss_type,
                struct((pairs, half_rows, part), jnp.float32),
                struct((pairs, half_rows, part), jnp.bfloat16),
            ],
            in_specs,
            (table, hits, shares, all_stats, *kept, *rows),
            scratch=[
                lse_scratch,
                pltpu.VMEM((block_count // 2, BLK, BLK), jnp.float32),
                pltpu.VMEM((block_count // 2, BLK, width), jnp.float32),
            ],
        )
        got = lax.ppermute(send, "dp", [(i, i ^ 1) for i in range(dp_count)])
        keep, send = call(
            pair_kernel,
            "pair_sums",
            [struct((2, half_rows, part), jnp.float32), struct((2, half_rows, part), jnp.bfloat16)],
            [vmem()] * 2,
            (keep, got),
        )
        got = lax.ppermute(send, "label", [(i, i ^ 2) for i in range(lab_count)])
        own, send = call(step_kernel, "step_sums", [wide, narrow], [vmem()] * 2, (keep, got))
        parts += [own, lax.ppermute(send, "label", [(i, i ^ 4) for i in range(lab_count)])]
    extra = -(-3 * block_count // 16) * 16
    (done,) = call(
        functools.partial(line_kernel, 2),
        "line_sums",
        [struct((inst_count + extra, part), jnp.bfloat16)],
        [vmem()] * 5,
        (loss, *parts),
        scratch=[pltpu.VMEM((extra, part), jnp.float32)],
    )
    home = move(done, lambda dp, lab: ((dp & ~1) | (lab & 1), (lab & ~1) | (1 - (dp & 1))))
    loss, grads = call(
        home_again_kernel,
        "home_again",
        [loss_type, struct((inst_count, part), jnp.bfloat16)],
        [vmem()],
        (home,),
    )
    return loss.reshape(inst_count), grads


def solution(mesh):
    in_specs = (P("dp", None), P(("dp", "label"), None, None), P(), P(), P("dp", None))
    out_specs = (P("dp"), P("dp", "label"))
    return jax.shard_map(shards, mesh=mesh, in_specs=in_specs, out_specs=out_specs, check_vma=False)
```

```python
import functools

import jax
import jax.numpy as jnp
from jax import lax
from jax.experimental import pallas as pl
from jax.experimental.pallas import tpu as pltpu
from jax.sharding import PartitionSpec as P

BLK = 128
NEG_FILL = -1e30
VMEM_BYTES = 32 * 1024 * 1024
VMEM_PICK = 56 * 1024 * 1024


def divide(value, by):
    if by & (by - 1) == 0:
        return lax.shift_right_logical(value, jnp.int32(by.bit_length() - 1))
    return lax.div(value, jnp.int32(by))


def remainder(value, by):
    if by & (by - 1) == 0:
        return value & jnp.int32(by - 1)
    return lax.rem(value, jnp.int32(by))


def each_entry(count, short_count, body, carry):
    if count <= 64:
        for e in range(count):
            carry = body(e // short_count, e % short_count, carry)
        return carry
    step = lambda e, c: body(divide(e, short_count), remainder(e, short_count), c)
    return lax.fori_loop(0, count, step, carry)


class Plan:
    def __init__(self, square, dp_count, lab_count, stored, block_count, short_count):
        self.square, self.dp_count, self.lab_count = square, dp_count, lab_count
        self.stored, self.block_count, self.short_count = stored, block_count, short_count

    def here(self):
        return lax.axis_index("dp"), lax.axis_index("label")

    def home(self):
        dp, lab = self.here()
        return (dp & ~1) | (lab & 1) if self.square else dp

    def flips(self, entry, core):
        return [(0, 0), (core, 1 - core), (1 - core, core), (1, 1)][entry]

    def wanted_by(self, entry):
        dp, lab = self.here()
        if not self.square:
            return dp ^ entry
        flip_x, flip_y = self.flips(entry, dp & 1)
        return ((dp >> 1) ^ flip_y) * 2 + ((lab & 1) ^ flip_x)

    def entry_of(self, device):
        dp, lab = self.here()
        that_dp, that_lab = divide(device, self.lab_count), remainder(device, self.lab_count)
        if not self.square:
            return that_lab == lab, that_dp ^ dp
        match = ((that_dp & 1) == (dp & 1)) & ((that_lab >> 1) == (lab >> 1))
        flip_y, flip_x = (that_dp ^ dp) >> 1, (that_lab ^ lab) & 1
        core = dp & 1
        lone = jnp.where(flip_y == 1 - core, 1, 2)
        entry = jnp.where(flip_x + flip_y == 1, lone, flip_x + flip_y + (flip_x & flip_y))
        return match, entry

    def pairs(self, entry):
        result = []
        for dp in range(self.dp_count):
            for lab in range(self.lab_count):
                if self.square:
                    flip_x, flip_y = self.flips(entry, dp & 1)
                    target = (dp ^ (2 * flip_y)) * self.lab_count + (lab ^ flip_x)
                else:
                    target = (dp ^ entry) * self.lab_count + lab
                result.append((dp * self.lab_count + lab, target))
        return result


def find_slots(plan, wanted, lists_ref, slot_ref):
    dp_index, lab_index = plan.here()
    mine = dp_index * plan.lab_count + lab_index
    stored, short_count = plan.stored, plan.short_count
    found = []
    for k in wanted:
        base = plan.wanted_by(k) * plan.block_count

        def look(row, column, slot_here, base=base):
            slot = slot_ref[lists_ref[base + row, column]]
            return jnp.where(divide(slot, stored) == mine, remainder(slot, stored), slot_here)

        count = plan.block_count // 2 * short_count
        found.append(each_entry(count, short_count, look, jnp.int32(0)))
    return found


def far_kernel(plan, wanted, lists_hbm, slot_hbm, weights_ref, *rest):
    outs = rest[: len(wanted)]
    held, lists_ref, slot_ref, sems = rest[len(wanted) :]
    tables = [
        pltpu.make_async_copy(lists_hbm, lists_ref, sems.at[0]),
        pltpu.make_async_copy(slot_hbm, slot_ref, sems.at[1]),
    ]
    stage = pltpu.make_async_copy(weights_ref, held, sems.at[2])
    for copy in tables:
        copy.start()
    stage.start()
    for copy in tables:
        copy.wait()
    found = find_slots(plan, wanted, lists_ref, slot_ref)
    stage.wait()
    copies = []
    for i, slot in enumerate(found):
        copies.append(pltpu.make_async_copy(held.at[slot], outs[i], sems.at[3 + i]))
        copies[-1].start()
    for copy in copies:
        copy.wait()


def near_kernel(plan, lists_ref, slot_ref, weights_ref, table_ref, *rest):
    block_count, short_count = plan.block_count, plan.short_count
    outs, sems = rest[:-1], rest[-1]
    copies = []
    for k, slot in enumerate(find_slots(plan, range(1), lists_ref, slot_ref)):
        copies.append(pltpu.make_async_copy(weights_ref.at[slot], outs[k], sems.at[k]))
        copies[-1].start()
    home = plan.home()
    half = block_count // 2
    for side in range(2):

        def note(row, column, carry, side=side):
            block = side * half + row
            cluster = lists_ref[home * block_count + block, column]
            match, entry = plan.entry_of(divide(slot_ref[cluster], plan.stored))

            @pl.when(match)
            def _():
                table_ref[entry, 0] = cluster
                table_ref[entry, 1 + side] = jnp.int32(block)

            return carry

        each_entry(half * short_count, short_count, note, jnp.int32(0))
    for copy in copies:
        copy.wait()


def home_kernel(feats_ref, pos_ref, other_feats_ref, other_pos_ref, home_feats_ref, home_pos_ref):
    same = (lax.axis_index("dp") & 1) == (lax.axis_index("label") & 1)

    @pl.when(same)
    def _():
        home_feats_ref[...] = feats_ref[...]
        home_pos_ref[...] = pos_ref[...]

    @pl.when(jnp.logical_not(same))
    def _():
        home_feats_ref[...] = other_feats_ref[...]
        home_pos_ref[...] = other_pos_ref[...]


def target_kernel(early, late, table_ref, pos_ref, feats_ref, hits_ref, shares_ref, turned_ref):
    count, cluster_size, _ = hits_ref.shape
    pos_count = pos_ref.shape[1]

    def one_slot(s):
        labels = lax.broadcasted_iota(jnp.int32, (cluster_size, BLK), 0) + table_ref[s, 0] * cluster_size
        for side in range(2):
            pos = pos_ref[table_ref[s, 1 + side]]
            hit = pos[0:1, :] == labels
            for p in range(1, pos_count):
                hit = hit | (pos[p : p + 1, :] == labels)
            hits = jnp.where(hit, 1.0, 0.0)
            columns = pl.ds(side * BLK, BLK)
            hits_ref[s, :, columns] = hits
            if s in early:
                shares_ref[early.index(s), columns, :] = (hits / pos_count).T
            else:
                feats = feats_ref[table_ref[s, 1 + side]].astype(jnp.float32)
                turned_ref[late.index(s), :, columns] = feats.T.astype(jnp.bfloat16)

    for s in range(count):
        pl.when(table_ref[s, 0] >= 0)(functools.partial(one_slot, s))


def logit_kernel(slots, turned, copies, table_ref, feats_ref, hits_ref, *rest):
    count = len(slots)
    rows = rest[:count]
    logits_ref, out_ref, stats_ref = rest[-3:]
    if len(rest) == count + 3:
        stats_ref[0] = jnp.full(stats_ref.shape[1:], NEG_FILL, jnp.float32)
        stats_ref[1] = jnp.zeros(stats_ref.shape[1:], jnp.float32)
        stats_ref[2] = jnp.zeros(stats_ref.shape[1:], jnp.float32)
    else:
        stats_ref[...] = rest[count][0]
    for i, (s, ref) in enumerate(zip(slots, rows)):
        if not turned:
            logits_ref[i] = jnp.dot(ref[...], feats_ref[i], preferred_element_type=jnp.float32)
        for side in range(2):
            block = table_ref[s, 1 + side]
            columns = pl.ds(side * BLK, BLK)
            if turned:
                logits = lax.dot_general(
                    ref[...],
                    feats_ref[block],
                    (((1,), (1,)), ((), ())),
                    preferred_element_type=jnp.float32,
                )
                logits_ref[i, columns, :] = logits.T
            else:
                logits = logits_ref[i, :, columns]
            highest = jnp.max(logits, axis=0, keepdims=True)
            total = jnp.sum(jnp.exp(logits - highest), axis=0, keepdims=True)
            positive = jnp.sum(hits_ref[s, :, columns] * logits, axis=0, keepdims=True)
            row = pl.ds(block, 1)
            before = stats_ref[0, row, :]
            after = jnp.maximum(before, highest)
            stats_ref[0, row, :] = after
            stats_ref[1, row, :] = stats_ref[1, row, :] * jnp.exp(before - after) + total * jnp.exp(
                highest - after
            )
            stats_ref[2, row, :] = stats_ref[2, row, :] + positive
    for i in range(copies):
        out_ref[i] = stats_ref[...]


def row_sums(stats_ref, lab_count):
    highest = stats_ref[0, 0]
    for i in range(1, lab_count):
        highest = jnp.maximum(highest, stats_ref[i, 0])
    summed = jnp.zeros_like(highest)
    positive = jnp.zeros_like(highest)
    for i in range(lab_count):
        summed = summed + stats_ref[i, 1] * jnp.exp(stats_ref[i, 0] - highest)
        positive = positive + stats_ref[i, 2]
    return highest + jnp.log(summed), positive


def prepare(stats_ref, pos_count, lab_count, loss_ref, lse_ref, columns_ref, total_ref, first):
    lse, positive = row_sums(stats_ref, lab_count)
    lse_ref[...] = lse
    loss_ref[...] = lse - positive / pos_count
    for b in range(columns_ref.shape[0]):
        columns_ref[b] = jnp.broadcast_to(lse[first + b : first + b + 1, :], (BLK, BLK)).T
    total_ref[...] = jnp.zeros_like(total_ref)


def add_slots(sides, groups, pos_count, first, table_ref, hits_ref, shares_ref, logits_refs, rows, sums):
    lse_ref, columns_ref, total_ref = sums
    early = [s for slots in groups[:-1] for s in slots]
    cluster_size = rows[0].shape[0]

    def one_slot(s, logits_ref):
        for side in sides:
            block = table_ref[s, 1 + side]
            here = pl.ds(side * BLK, BLK)
            if s in early:
                column = columns_ref[block - first]
                column = jnp.concatenate([column] * (cluster_size // BLK), axis=1)
                dlogit = jnp.exp(logits_ref[here, :] - column) - shares_ref[early.index(s), here, :]
            else:
                row = lse_ref[pl.ds(block, 1), :]
                dlogit = jnp.exp(logits_ref[:, here] - row) - hits_ref[s, :, here] / pos_count
                dlogit = dlogit.T
            total_ref[block - first] += lax.dot_general(
                dlogit.astype(jnp.bfloat16),
                rows[s][...],
                (((1,), (0,)), ((), ())),
                preferred_element_type=jnp.float32,
            )

    for slots, logits_ref in zip(groups, logits_refs):
        for i, s in enumerate(slots):
            body = functools.partial(one_slot, s, logits_ref.at[i])
            if len(rows) <= 4:
                body()
            else:
                pl.when(table_ref[s, 0] >= 0)(body)


def half_kernel(side, groups, lab_count, pos_count, table_ref, hits_ref, shares_ref, stats_ref, *rest):
    logits_refs = rest[: len(groups)]
    rows = rest[len(groups) : -6]
    loss_ref, keep_ref, send_ref, lse_ref, columns_ref, total_ref = rest[-6:]
    half = total_ref.shape[0]
    prepare(
        stats_ref, pos_count, lab_count, loss_ref, lse_ref, columns_ref, total_ref, side * half
    )
    add_slots(
        (side,),
        groups,
        pos_count,
        side * half,
        table_ref,
        hits_ref,
        shares_ref,
        logits_refs,
        rows,
        (lse_ref, columns_ref, total_ref),
    )
    part = keep_ref.shape[2]
    core, line = lax.axis_index("dp") & 1, lax.axis_index("label") >> 1
    for j in range(lab_count // 2):
        first = (line ^ j) * 2
        mine = pl.ds(pl.multiple_of((first + 1 - core) * part, part), part)
        other = pl.ds(pl.multiple_of((first + core) * part, part), part)
        for b in range(half):
            here = pl.ds(b * BLK, BLK)
            keep_ref[j, here, :] = total_ref[b, :, mine]
            send_ref[j, here, :] = total_ref[b, :, other].astype(jnp.bfloat16)


def pair_kernel(keep_ref, got_ref, next_ref, send_ref):
    for j in range(keep_ref.shape[0]):
        total = keep_ref[j] + got_ref[j].astype(jnp.float32)
        out_ref = send_ref if j % 2 else next_ref
        out_ref[j // 2] = total.astype(out_ref.dtype)


def spread_kernel(keep_ref, got_ref, *outs):
    for j, out_ref in enumerate(outs):
        out_ref[...] = (keep_ref[j] + got_ref[j].astype(jnp.float32)).astype(out_ref.dtype)


def step_kernel(keep_ref, got_ref, own_ref, send_ref):
    own_ref[...] = keep_ref[0] + got_ref[0].astype(jnp.float32)
    send_ref[...] = (keep_ref[1] + got_ref[1].astype(jnp.float32)).astype(jnp.bfloat16)


def line_kernel(count, loss_ref, *refs):
    out_ref, terms_ref = refs[-2:]
    rows = refs[0].shape[0]
    for h, parts in enumerate((refs[:count], refs[count:-2])):
        total = parts[0][...]
        for ref in parts[1:]:
            total = total + ref[...].astype(jnp.float32)
        out_ref[h * rows : (h + 1) * rows, :] = total.astype(jnp.bfloat16)
    terms_ref[...] = jnp.zeros_like(terms_ref)
    blocks = loss_ref.shape[0]
    rest = loss_ref[...]
    for i in range(3):
        term = rest.astype(jnp.bfloat16).astype(jnp.float32)
        terms_ref[i * blocks : (i + 1) * blocks, :] = term
        rest = rest - term
    out_ref[2 * rows :, :] = terms_ref[...].astype(jnp.bfloat16)


def home_again_kernel(got_ref, loss_ref, grads_ref):
    blocks = loss_ref.shape[0]
    count = grads_ref.shape[0]
    grads_ref[...] = got_ref[:count, :]
    terms = got_ref[count:, :].astype(jnp.float32)
    loss_ref[...] = terms[:blocks] + (terms[blocks : 2 * blocks] + terms[2 * blocks : 3 * blocks])


def grad_kernel(groups, lab_count, pos_count, table_ref, hits_ref, shares_ref, stats_ref, *rest):
    logits_refs = rest[: len(groups)]
    rows = rest[len(groups) : -5]
    loss_ref, out_ref, lse_ref, columns_ref, total_ref = rest[-5:]
    prepare(stats_ref, pos_count, lab_count, loss_ref, lse_ref, columns_ref, total_ref, 0)
    add_slots(
        (0, 1),
        groups,
        pos_count,
        0,
        table_ref,
        hits_ref,
        shares_ref,
        logits_refs,
        rows,
        (lse_ref, columns_ref, total_ref),
    )
    part = out_ref.shape[2]
    for j in range(lab_count):
        for b in range(total_ref.shape[0]):
            out_ref[j, b * BLK : (b + 1) * BLK, :] = total_ref[
                b, :, j * part : (j + 1) * part
            ].astype(jnp.bfloat16)


def smem():
    return pl.BlockSpec(memory_space=pltpu.SMEM)


def vmem():
    return pl.BlockSpec(memory_space=pltpu.VMEM)


def anywhere():
    return pl.BlockSpec(memory_space=pl.ANY)


def call(kernel, name, out_shape, in_specs, arrays, scratch=(), limit=VMEM_BYTES, out_specs=None):
    return pl.pallas_call(
        kernel,
        out_shape=out_shape,
        in_specs=in_specs,
        out_specs=out_specs or [vmem()] * len(out_shape),
        scratch_shapes=list(scratch),
        compiler_params=pltpu.CompilerParams(vmem_limit_bytes=limit),
        name=name,
    )(*arrays)


def shards(feats, weights, shortlist, slot_of, positives):
    dp_count = lax.axis_size("dp")
    lab_count = lax.axis_size("label")
    stored, cluster_size, width = weights.shape
    inst_count = feats.shape[0]
    pos_count = positives.shape[1]
    block_count = inst_count // BLK
    part = width // lab_count
    square = dp_count == 4 and lab_count == 8 and part % 128 == 0
    plan = Plan(square, dp_count, lab_count, stored, block_count, shortlist.shape[1])
    struct = jax.ShapeDtypeStruct
    row_type = struct((cluster_size, width), weights.dtype)
    stat_shape = (3, block_count, BLK)
    both = ("dp", "label")
    devices = [(dp, lab) for dp in range(dp_count) for lab in range(lab_count)]

    def move(x, target):
        pairs = []
        for dp, lab in devices:
            to_dp, to_lab = target(dp, lab)
            pairs.append((dp * lab_count + lab, to_dp * lab_count + to_lab))
        return lax.ppermute(x, both, pairs)

    feat_blocks = feats.reshape(block_count, BLK, width)
    pos_blocks = positives.reshape(block_count, BLK, pos_count).transpose(0, 2, 1)
    if square:
        other_feats = lax.ppermute(feat_blocks, "dp", [(i, i ^ 1) for i in range(dp_count)])
        other_pos = lax.ppermute(pos_blocks, "dp", [(i, i ^ 1) for i in range(dp_count)])
        feat_blocks, pos_blocks = call(
            home_kernel,
            "home",
            [struct(feat_blocks.shape, feats.dtype), struct(pos_blocks.shape, jnp.int32)],
            [vmem()] * 4,
            (feat_blocks, pos_blocks, other_feats, other_pos),
        )

    far = range(1, dp_count)
    far_rows = call(
        functools.partial(far_kernel, plan, far),
        "pick_far",
        [row_type] * len(far),
        [anywhere()] * 3,
        (shortlist, slot_of, weights),
        scratch=[
            pltpu.VMEM(weights.shape, weights.dtype),
            pltpu.SMEM(shortlist.shape, jnp.int32),
            pltpu.SMEM(slot_of.shape, jnp.int32),
            pltpu.SemaphoreType.DMA((3 + len(far),)),
        ],
        limit=VMEM_PICK,
        out_specs=[anywhere()] * len(far),
    )
    table, *rows = call(
        functools.partial(near_kernel, plan),
        "pick_near",
        [struct((dp_count, 4), jnp.int32), row_type],
        [smem(), smem(), anywhere()],
        (shortlist, slot_of, weights),
        scratch=[pltpu.SemaphoreType.DMA((1,))],
        out_specs=[smem(), vmem()],
    )
    rows += [lax.ppermute(x, both, plan.pairs(k)) for k, x in zip(far, far_rows)]

    if square:
        groups = [(0,), (1,), (2,), (3,)]
    else:
        cuts = (0, dp_count // 2, dp_count * 3 // 4, dp_count)
        groups = [tuple(range(a, b)) for a, b in zip(cuts[:-1], cuts[1:])]
    early = [s for slots in groups[:-1] for s in slots]
    late = list(groups[-1])
    hits, shares, turned = call(
        functools.partial(target_kernel, early, late),
        "targets",
        [
            struct((dp_count, cluster_size, 2 * BLK), jnp.float32),
            struct((len(early), 2 * BLK, cluster_size), jnp.float32),
            struct((len(late), width, 2 * BLK), feats.dtype),
        ],
        [smem()] + [vmem()] * 2,
        (table, pos_blocks, feat_blocks),
    )
    kept = []
    stats = []
    for slots in groups:
        last = slots is groups[-1]
        copies = lab_count if last else 1
        shape = (cluster_size, 2 * BLK) if last else (2 * BLK, cluster_size)
        logits, stats_out = call(
            functools.partial(logit_kernel, slots, not last, copies),
            "logits",
            [
                struct((len(slots),) + shape, jnp.float32),
                struct((copies,) + stat_shape, jnp.float32),
            ],
            [smem()] + [vmem()] * (2 + len(slots) + len(stats)),
            (table, turned if last else feat_blocks, hits, *[rows[s] for s in slots], *stats),
            scratch=[pltpu.VMEM(stat_shape, jnp.float32)],
        )
        kept.append(logits)
        stats = [stats_out]

    in_specs = [smem()] + [vmem()] * (3 + len(groups) + dp_count)
    loss_type = struct((block_count, BLK), jnp.float32)
    lse_scratch = pltpu.VMEM((block_count, BLK), jnp.float32)
    if not square:
        all_stats = lax.all_to_all(stats[0], "label", split_axis=0, concat_axis=0, tiled=True)
        loss, parts = call(
            functools.partial(grad_kernel, groups, lab_count, pos_count),
            "grads",
            [loss_type, struct((lab_count, inst_count, part), jnp.bfloat16)],
            in_specs,
            (table, hits, shares, all_stats, *kept, *rows),
            scratch=[
                lse_scratch,
                pltpu.VMEM((block_count, BLK, BLK), jnp.float32),
                pltpu.VMEM((block_count, BLK, width), jnp.float32),
            ],
        )
        gathered = lax.all_to_all(parts, "label", split_axis=0, concat_axis=0, tiled=True)
        grads = jnp.sum(gathered.astype(jnp.float32), axis=0).astype(jnp.bfloat16)
        return loss.reshape(inst_count), grads

    owners = [
        [(2 * y + core) * lab_count + 2 * z + x for z in range(lab_count // 2) for core in range(2)]
        for y in range(dp_count // 2)
        for x in range(2)
    ]
    all_stats = lax.all_to_all(
        stats[0], both, split_axis=0, concat_axis=0, axis_index_groups=owners, tiled=True
    )
    pairs = lab_count // 2
    half_rows = inst_count // 2
    wide = struct((half_rows, part), jnp.float32)
    narrow = struct((half_rows, part), jnp.bfloat16)

    halves = []
    for side in range(2):
        loss, keep, send = call(
            functools.partial(half_kernel, side, groups, lab_count, pos_count),
            "grads",
            [
                loss_type,
                struct((pairs, half_rows, part), jnp.float32),
                struct((pairs, half_rows, part), jnp.bfloat16),
            ],
            in_specs,
            (table, hits, shares, all_stats, *kept, *rows),
            scratch=[
                lse_scratch,
                pltpu.VMEM((block_count // 2, BLK, BLK), jnp.float32),
                pltpu.VMEM((block_count // 2, BLK, width), jnp.float32),
            ],
        )
        halves.append((keep, lax.ppermute(send, "dp", [(i, i ^ 1) for i in range(dp_count)])))

    def hop(x, mask):
        return lax.ppermute(x, "label", [(i, i ^ mask) for i in range(lab_count)])

    keep, send = call(
        pair_kernel,
        "pair_sums",
        [struct((2, half_rows, part), jnp.float32), struct((2, half_rows, part), jnp.bfloat16)],
        [vmem()] * 2,
        halves[0],
    )
    got = hop(send, 2)
    spread = call(
        spread_kernel, "spread_sums", [wide] + [narrow] * (pairs - 1), [vmem()] * 2, halves[1]
    )
    high = [spread[0]] + [hop(x, 2 * j + 2) for j, x in enumerate(spread[1:])]
    got, *_ = lax.optimization_barrier((got, *spread))
    own, send = call(step_kernel, "step_sums", [wide, narrow], [vmem()] * 2, (keep, got))
    parts = [own, hop(send, 4)] + high
    extra = -(-3 * block_count // 16) * 16
    (done,) = call(
        functools.partial(line_kernel, 2),
        "line_sums",
        [struct((inst_count + extra, part), jnp.bfloat16)],
        [vmem()] * (1 + len(parts)),
        (loss, *parts),
        scratch=[pltpu.VMEM((extra, part), jnp.float32)],
    )
    home = move(done, lambda dp, lab: ((dp & ~1) | (lab & 1), (lab & ~1) | (1 - (dp & 1))))
    loss, grads = call(
        home_again_kernel,
        "home_again",
        [loss_type, struct((inst_count, part), jnp.bfloat16)],
        [vmem()],
        (home,),
    )
    return loss.reshape(inst_count), grads


def solution(mesh):
    in_specs = (P("dp", None), P(("dp", "label"), None, None), P(), P(), P("dp", None))
    out_specs = (P("dp"), P("dp", "label"))
    return jax.shard_map(shards, mesh=mesh, in_specs=in_specs, out_specs=out_specs, check_vma=False)
```

```python
import functools

import jax
import jax.numpy as jnp
from jax import lax
from jax.experimental import pallas as pl
from jax.experimental.pallas import tpu as pltpu
from jax.sharding import PartitionSpec as P

BLK = 128
NEG_FILL = -1e30
VMEM_BYTES = 32 * 1024 * 1024
VMEM_PICK = 56 * 1024 * 1024


def divide(value, by):
    if by & (by - 1) == 0:
        return lax.shift_right_logical(value, jnp.int32(by.bit_length() - 1))
    return lax.div(value, jnp.int32(by))


def remainder(value, by):
    if by & (by - 1) == 0:
        return value & jnp.int32(by - 1)
    return lax.rem(value, jnp.int32(by))


def each_entry(count, short_count, body, carry):
    if count <= 64:
        for e in range(count):
            carry = body(e // short_count, e % short_count, carry)
        return carry
    step = lambda e, c: body(divide(e, short_count), remainder(e, short_count), c)
    return lax.fori_loop(0, count, step, carry)


class Plan:
    def __init__(self, square, dp_count, lab_count, stored, block_count, short_count):
        self.square, self.dp_count, self.lab_count = square, dp_count, lab_count
        self.stored, self.block_count, self.short_count = stored, block_count, short_count

    def here(self):
        return lax.axis_index("dp"), lax.axis_index("label")

    def home(self):
        dp, lab = self.here()
        return (dp & ~1) | (lab & 1) if self.square else dp

    def flips(self, entry, core):
        return [(0, 0), (core, 1 - core), (1 - core, core), (1, 1)][entry]

    def wanted_by(self, entry):
        dp, lab = self.here()
        if not self.square:
            return dp ^ entry
        flip_x, flip_y = self.flips(entry, dp & 1)
        return ((dp >> 1) ^ flip_y) * 2 + ((lab & 1) ^ flip_x)

    def entry_of(self, device):
        dp, lab = self.here()
        that_dp, that_lab = divide(device, self.lab_count), remainder(device, self.lab_count)
        if not self.square:
            return that_lab == lab, that_dp ^ dp
        match = ((that_dp & 1) == (dp & 1)) & ((that_lab >> 1) == (lab >> 1))
        flip_y, flip_x = (that_dp ^ dp) >> 1, (that_lab ^ lab) & 1
        core = dp & 1
        lone = jnp.where(flip_y == 1 - core, 1, 2)
        entry = jnp.where(flip_x + flip_y == 1, lone, flip_x + flip_y + (flip_x & flip_y))
        return match, entry

    def pairs(self, entry):
        result = []
        for dp in range(self.dp_count):
            for lab in range(self.lab_count):
                if self.square:
                    flip_x, flip_y = self.flips(entry, dp & 1)
                    target = (dp ^ (2 * flip_y)) * self.lab_count + (lab ^ flip_x)
                else:
                    target = (dp ^ entry) * self.lab_count + lab
                result.append((dp * self.lab_count + lab, target))
        return result


def find_slots(plan, wanted, lists_ref, slot_ref):
    dp_index, lab_index = plan.here()
    mine = dp_index * plan.lab_count + lab_index
    stored, short_count = plan.stored, plan.short_count
    found = []
    for k in wanted:
        base = plan.wanted_by(k) * plan.block_count

        def look(row, column, slot_here, base=base):
            slot = slot_ref[lists_ref[base + row, column]]
            return jnp.where(divide(slot, stored) == mine, remainder(slot, stored), slot_here)

        count = plan.block_count // 2 * short_count
        found.append(each_entry(count, short_count, look, jnp.int32(0)))
    return found


def far_kernel(plan, wanted, lists_hbm, slot_hbm, weights_ref, *rest):
    outs = rest[: len(wanted)]
    held, lists_ref, slot_ref, sems = rest[len(wanted) :]
    tables = [
        pltpu.make_async_copy(lists_hbm, lists_ref, sems.at[0]),
        pltpu.make_async_copy(slot_hbm, slot_ref, sems.at[1]),
    ]
    stage = pltpu.make_async_copy(weights_ref, held, sems.at[2])
    for copy in tables:
        copy.start()
    stage.start()
    for copy in tables:
        copy.wait()
    found = find_slots(plan, wanted, lists_ref, slot_ref)
    stage.wait()
    copies = []
    for i, slot in enumerate(found):
        copies.append(pltpu.make_async_copy(held.at[slot], outs[i], sems.at[3 + i]))
        copies[-1].start()
    for copy in copies:
        copy.wait()


def near_kernel(plan, lists_ref, slot_ref, weights_ref, table_ref, *rest):
    block_count, short_count = plan.block_count, plan.short_count
    outs, sems = rest[:-1], rest[-1]
    copies = []
    for k, slot in enumerate(find_slots(plan, range(1), lists_ref, slot_ref)):
        copies.append(pltpu.make_async_copy(weights_ref.at[slot], outs[k], sems.at[k]))
        copies[-1].start()
    home = plan.home()
    half = block_count // 2
    for side in range(2):

        def note(row, column, carry, side=side):
            block = side * half + row
            cluster = lists_ref[home * block_count + block, column]
            match, entry = plan.entry_of(divide(slot_ref[cluster], plan.stored))

            @pl.when(match)
            def _():
                table_ref[entry, 0] = cluster
                table_ref[entry, 1 + side] = jnp.int32(block)

            return carry

        each_entry(half * short_count, short_count, note, jnp.int32(0))
    for copy in copies:
        copy.wait()


def home_kernel(feats_ref, pos_ref, other_feats_ref, other_pos_ref, home_feats_ref, home_pos_ref):
    same = (lax.axis_index("dp") & 1) == (lax.axis_index("label") & 1)

    @pl.when(same)
    def _():
        home_feats_ref[...] = feats_ref[...]
        home_pos_ref[...] = pos_ref[...]

    @pl.when(jnp.logical_not(same))
    def _():
        home_feats_ref[...] = other_feats_ref[...]
        home_pos_ref[...] = other_pos_ref[...]


def target_kernel(early, late, table_ref, pos_ref, feats_ref, hits_ref, shares_ref, turned_ref):
    count, cluster_size, _ = hits_ref.shape
    pos_count = pos_ref.shape[1]

    def one_slot(s):
        labels = lax.broadcasted_iota(jnp.int32, (cluster_size, BLK), 0) + table_ref[s, 0] * cluster_size
        for side in range(2):
            pos = pos_ref[table_ref[s, 1 + side]]
            hit = pos[0:1, :] == labels
            for p in range(1, pos_count):
                hit = hit | (pos[p : p + 1, :] == labels)
            hits = jnp.where(hit, 1.0, 0.0)
            columns = pl.ds(side * BLK, BLK)
            hits_ref[s, :, columns] = hits
            if s in early:
                shares_ref[early.index(s), columns, :] = (hits / pos_count).T
            else:
                feats = feats_ref[table_ref[s, 1 + side]].astype(jnp.float32)
                turned_ref[late.index(s), :, columns] = feats.T.astype(jnp.bfloat16)

    for s in range(count):
        pl.when(table_ref[s, 0] >= 0)(functools.partial(one_slot, s))


def logit_kernel(slots, turned, copies, table_ref, feats_ref, hits_ref, *rest):
    count = len(slots)
    rows = rest[:count]
    logits_ref, out_ref, stats_ref = rest[-3:]
    if len(rest) == count + 3:
        stats_ref[0] = jnp.full(stats_ref.shape[1:], NEG_FILL, jnp.float32)
        stats_ref[1] = jnp.zeros(stats_ref.shape[1:], jnp.float32)
        stats_ref[2] = jnp.zeros(stats_ref.shape[1:], jnp.float32)
    else:
        stats_ref[...] = rest[count][0]
    for i, (s, ref) in enumerate(zip(slots, rows)):
        if not turned:
            logits_ref[i] = jnp.dot(ref[...], feats_ref[i], preferred_element_type=jnp.float32)
        for side in range(2):
            block = table_ref[s, 1 + side]
            columns = pl.ds(side * BLK, BLK)
            if turned:
                logits = lax.dot_general(
                    ref[...],
                    feats_ref[block],
                    (((1,), (1,)), ((), ())),
                    preferred_element_type=jnp.float32,
                )
                logits_ref[i, columns, :] = logits.T
            else:
                logits = logits_ref[i, :, columns]
            highest = jnp.max(logits, axis=0, keepdims=True)
            total = jnp.sum(jnp.exp(logits - highest), axis=0, keepdims=True)
            positive = jnp.sum(hits_ref[s, :, columns] * logits, axis=0, keepdims=True)
            row = pl.ds(block, 1)
            before = stats_ref[0, row, :]
            after = jnp.maximum(before, highest)
            stats_ref[0, row, :] = after
            stats_ref[1, row, :] = stats_ref[1, row, :] * jnp.exp(before - after) + total * jnp.exp(
                highest - after
            )
            stats_ref[2, row, :] = stats_ref[2, row, :] + positive
    for i in range(copies):
        out_ref[i] = stats_ref[...]


def row_sums(stats_ref, lab_count):
    highest = stats_ref[0, 0]
    for i in range(1, lab_count):
        highest = jnp.maximum(highest, stats_ref[i, 0])
    summed = jnp.zeros_like(highest)
    positive = jnp.zeros_like(highest)
    for i in range(lab_count):
        summed = summed + stats_ref[i, 1] * jnp.exp(stats_ref[i, 0] - highest)
        positive = positive + stats_ref[i, 2]
    return highest + jnp.log(summed), positive


def prepare(stats_ref, pos_count, lab_count, loss_ref, lse_ref, columns_ref, total_ref, first):
    lse, positive = row_sums(stats_ref, lab_count)
    lse_ref[...] = lse
    loss_ref[...] = lse - positive / pos_count
    for b in range(columns_ref.shape[0]):
        columns_ref[b] = jnp.broadcast_to(lse[first + b : first + b + 1, :], (BLK, BLK)).T
    total_ref[...] = jnp.zeros_like(total_ref)


def add_slots(sides, groups, pos_count, first, table_ref, hits_ref, shares_ref, logits_refs, rows, sums):
    lse_ref, columns_ref, total_ref = sums
    early = [s for slots in groups[:-1] for s in slots]
    cluster_size = rows[0].shape[0]

    def one_slot(s, logits_ref):
        for side in sides:
            block = table_ref[s, 1 + side]
            here = pl.ds(side * BLK, BLK)
            if s in early:
                column = columns_ref[block - first]
                column = jnp.concatenate([column] * (cluster_size // BLK), axis=1)
                dlogit = jnp.exp(logits_ref[here, :] - column) - shares_ref[early.index(s), here, :]
            else:
                row = lse_ref[pl.ds(block, 1), :]
                dlogit = jnp.exp(logits_ref[:, here] - row) - hits_ref[s, :, here] / pos_count
                dlogit = dlogit.T
            total_ref[block - first] += lax.dot_general(
                dlogit.astype(jnp.bfloat16),
                rows[s][...],
                (((1,), (0,)), ((), ())),
                preferred_element_type=jnp.float32,
            )

    for slots, logits_ref in zip(groups, logits_refs):
        for i, s in enumerate(slots):
            body = functools.partial(one_slot, s, logits_ref.at[i])
            if len(rows) <= 4:
                body()
            else:
                pl.when(table_ref[s, 0] >= 0)(body)


def half_kernel(side, groups, lab_count, pos_count, table_ref, hits_ref, shares_ref, stats_ref, *rest):
    logits_refs = rest[: len(groups)]
    rows = rest[len(groups) : -6]
    loss_ref, keep_ref, send_ref, lse_ref, columns_ref, total_ref = rest[-6:]
    half = total_ref.shape[0]
    prepare(
        stats_ref, pos_count, lab_count, loss_ref, lse_ref, columns_ref, total_ref, side * half
    )
    add_slots(
        (side,),
        groups,
        pos_count,
        side * half,
        table_ref,
        hits_ref,
        shares_ref,
        logits_refs,
        rows,
        (lse_ref, columns_ref, total_ref),
    )
    part = keep_ref.shape[2]
    core, line = lax.axis_index("dp") & 1, lax.axis_index("label") >> 1
    for j in range(lab_count // 2):
        first = (line ^ j) * 2
        mine = pl.ds(pl.multiple_of((first + 1 - core) * part, part), part)
        other = pl.ds(pl.multiple_of((first + core) * part, part), part)
        for b in range(half):
            here = pl.ds(b * BLK, BLK)
            keep_ref[j, here, :] = total_ref[b, :, mine]
            send_ref[j, here, :] = total_ref[b, :, other].astype(jnp.bfloat16)


def pair_kernel(keep_ref, got_ref, next_ref, send_ref):
    for j in range(keep_ref.shape[0]):
        total = keep_ref[j] + got_ref[j].astype(jnp.float32)
        out_ref = send_ref if j % 2 else next_ref
        out_ref[j // 2] = total.astype(out_ref.dtype)


def spread_kernel(keep_ref, got_ref, *outs):
    for j, out_ref in enumerate(outs):
        out_ref[...] = (keep_ref[j] + got_ref[j].astype(jnp.float32)).astype(out_ref.dtype)


def step_kernel(keep_ref, got_ref, own_ref, send_ref):
    own_ref[...] = keep_ref[0] + got_ref[0].astype(jnp.float32)
    send_ref[...] = (keep_ref[1] + got_ref[1].astype(jnp.float32)).astype(jnp.bfloat16)


def line_kernel(*refs):
    total = refs[0][...]
    for ref in refs[1:-1]:
        total = total + ref[...].astype(jnp.float32)
    refs[-1][...] = total.astype(jnp.bfloat16)


def line_and_loss_kernel(loss_ref, *refs):
    out_ref, terms_ref = refs[-2:]
    rows = refs[0].shape[0]
    line_kernel(*refs[:-2], out_ref.at[:rows, :])
    terms_ref[...] = jnp.zeros_like(terms_ref)
    blocks = loss_ref.shape[0]
    rest = loss_ref[...]
    for i in range(3):
        term = rest.astype(jnp.bfloat16).astype(jnp.float32)
        terms_ref[i * blocks : (i + 1) * blocks, :] = term
        rest = rest - term
    out_ref[rows:, :] = terms_ref[...].astype(jnp.bfloat16)


def home_again_kernel(low_ref, high_ref, loss_ref, grads_ref):
    blocks = loss_ref.shape[0]
    rows = high_ref.shape[0]
    grads_ref[:rows, :] = low_ref[:rows, :]
    grads_ref[rows:, :] = high_ref[...]
    terms = low_ref[rows:, :].astype(jnp.float32)
    loss_ref[...] = terms[:blocks] + (terms[blocks : 2 * blocks] + terms[2 * blocks : 3 * blocks])


def grad_kernel(groups, lab_count, pos_count, table_ref, hits_ref, shares_ref, stats_ref, *rest):
    logits_refs = rest[: len(groups)]
    rows = rest[len(groups) : -5]
    loss_ref, out_ref, lse_ref, columns_ref, total_ref = rest[-5:]
    prepare(stats_ref, pos_count, lab_count, loss_ref, lse_ref, columns_ref, total_ref, 0)
    add_slots(
        (0, 1),
        groups,
        pos_count,
        0,
        table_ref,
        hits_ref,
        shares_ref,
        logits_refs,
        rows,
        (lse_ref, columns_ref, total_ref),
    )
    part = out_ref.shape[2]
    for j in range(lab_count):
        for b in range(total_ref.shape[0]):
            out_ref[j, b * BLK : (b + 1) * BLK, :] = total_ref[
                b, :, j * part : (j + 1) * part
            ].astype(jnp.bfloat16)


def smem():
    return pl.BlockSpec(memory_space=pltpu.SMEM)


def vmem():
    return pl.BlockSpec(memory_space=pltpu.VMEM)


def anywhere():
    return pl.BlockSpec(memory_space=pl.ANY)


def call(kernel, name, out_shape, in_specs, arrays, scratch=(), limit=VMEM_BYTES, out_specs=None):
    return pl.pallas_call(
        kernel,
        out_shape=out_shape,
        in_specs=in_specs,
        out_specs=out_specs or [vmem()] * len(out_shape),
        scratch_shapes=list(scratch),
        compiler_params=pltpu.CompilerParams(vmem_limit_bytes=limit),
        name=name,
    )(*arrays)


def shards(feats, weights, shortlist, slot_of, positives):
    dp_count = lax.axis_size("dp")
    lab_count = lax.axis_size("label")
    stored, cluster_size, width = weights.shape
    inst_count = feats.shape[0]
    pos_count = positives.shape[1]
    block_count = inst_count // BLK
    part = width // lab_count
    square = dp_count == 4 and lab_count == 8 and part % 128 == 0
    plan = Plan(square, dp_count, lab_count, stored, block_count, shortlist.shape[1])
    struct = jax.ShapeDtypeStruct
    row_type = struct((cluster_size, width), weights.dtype)
    stat_shape = (3, block_count, BLK)
    both = ("dp", "label")
    devices = [(dp, lab) for dp in range(dp_count) for lab in range(lab_count)]

    def move(x, target):
        pairs = []
        for dp, lab in devices:
            to_dp, to_lab = target(dp, lab)
            pairs.append((dp * lab_count + lab, to_dp * lab_count + to_lab))
        return lax.ppermute(x, both, pairs)

    feat_blocks = feats.reshape(block_count, BLK, width)
    pos_blocks = positives.reshape(block_count, BLK, pos_count).transpose(0, 2, 1)
    if square:
        other_feats = lax.ppermute(feat_blocks, "dp", [(i, i ^ 1) for i in range(dp_count)])
        other_pos = lax.ppermute(pos_blocks, "dp", [(i, i ^ 1) for i in range(dp_count)])
        feat_blocks, pos_blocks = call(
            home_kernel,
            "home",
            [struct(feat_blocks.shape, feats.dtype), struct(pos_blocks.shape, jnp.int32)],
            [vmem()] * 4,
            (feat_blocks, pos_blocks, other_feats, other_pos),
        )

    far = range(1, dp_count)
    far_rows = call(
        functools.partial(far_kernel, plan, far),
        "pick_far",
        [row_type] * len(far),
        [anywhere()] * 3,
        (shortlist, slot_of, weights),
        scratch=[
            pltpu.VMEM(weights.shape, weights.dtype),
            pltpu.SMEM(shortlist.shape, jnp.int32),
            pltpu.SMEM(slot_of.shape, jnp.int32),
            pltpu.SemaphoreType.DMA((3 + len(far),)),
        ],
        limit=VMEM_PICK,
        out_specs=[anywhere()] * len(far),
    )
    table, *rows = call(
        functools.partial(near_kernel, plan),
        "pick_near",
        [struct((dp_count, 4), jnp.int32), row_type],
        [smem(), smem(), anywhere()],
        (shortlist, slot_of, weights),
        scratch=[pltpu.SemaphoreType.DMA((1,))],
        out_specs=[smem(), vmem()],
    )
    rows += [lax.ppermute(x, both, plan.pairs(k)) for k, x in zip(far, far_rows)]

    if square:
        groups = [(0,), (1,), (2,), (3,)]
    else:
        cuts = (0, dp_count // 2, dp_count * 3 // 4, dp_count)
        groups = [tuple(range(a, b)) for a, b in zip(cuts[:-1], cuts[1:])]
    early = [s for slots in groups[:-1] for s in slots]
    late = list(groups[-1])
    hits, shares, turned = call(
        functools.partial(target_kernel, early, late),
        "targets",
        [
            struct((dp_count, cluster_size, 2 * BLK), jnp.float32),
            struct((len(early), 2 * BLK, cluster_size), jnp.float32),
            struct((len(late), width, 2 * BLK), feats.dtype),
        ],
        [smem()] + [vmem()] * 2,
        (table, pos_blocks, feat_blocks),
    )
    kept = []
    stats = []
    for slots in groups:
        last = slots is groups[-1]
        copies = lab_count if last else 1
        shape = (cluster_size, 2 * BLK) if last else (2 * BLK, cluster_size)
        logits, stats_out = call(
            functools.partial(logit_kernel, slots, not last, copies),
            "logits",
            [
                struct((len(slots),) + shape, jnp.float32),
                struct((copies,) + stat_shape, jnp.float32),
            ],
            [smem()] + [vmem()] * (2 + len(slots) + len(stats)),
            (table, turned if last else feat_blocks, hits, *[rows[s] for s in slots], *stats),
            scratch=[pltpu.VMEM(stat_shape, jnp.float32)],
        )
        kept.append(logits)
        stats = [stats_out]

    in_specs = [smem()] + [vmem()] * (3 + len(groups) + dp_count)
    loss_type = struct((block_count, BLK), jnp.float32)
    lse_scratch = pltpu.VMEM((block_count, BLK), jnp.float32)
    if not square:
        all_stats = lax.all_to_all(stats[0], "label", split_axis=0, concat_axis=0, tiled=True)
        loss, parts = call(
            functools.partial(grad_kernel, groups, lab_count, pos_count),
            "grads",
            [loss_type, struct((lab_count, inst_count, part), jnp.bfloat16)],
            in_specs,
            (table, hits, shares, all_stats, *kept, *rows),
            scratch=[
                lse_scratch,
                pltpu.VMEM((block_count, BLK, BLK), jnp.float32),
                pltpu.VMEM((block_count, BLK, width), jnp.float32),
            ],
        )
        gathered = lax.all_to_all(parts, "label", split_axis=0, concat_axis=0, tiled=True)
        grads = jnp.sum(gathered.astype(jnp.float32), axis=0).astype(jnp.bfloat16)
        return loss.reshape(inst_count), grads

    owners = [
        [(2 * y + core) * lab_count + 2 * z + x for z in range(lab_count // 2) for core in range(2)]
        for y in range(dp_count // 2)
        for x in range(2)
    ]
    all_stats = lax.all_to_all(
        stats[0], both, split_axis=0, concat_axis=0, axis_index_groups=owners, tiled=True
    )
    pairs = lab_count // 2
    half_rows = inst_count // 2
    wide = struct((half_rows, part), jnp.float32)
    narrow = struct((half_rows, part), jnp.bfloat16)

    halves = []
    for side in range(2):
        loss, keep, send = call(
            functools.partial(half_kernel, side, groups, lab_count, pos_count),
            "grads",
            [
                loss_type,
                struct((pairs, half_rows, part), jnp.float32),
                struct((pairs, half_rows, part), jnp.bfloat16),
            ],
            in_specs,
            (table, hits, shares, all_stats, *kept, *rows),
            scratch=[
                lse_scratch,
                pltpu.VMEM((block_count // 2, BLK, BLK), jnp.float32),
                pltpu.VMEM((block_count // 2, BLK, width), jnp.float32),
            ],
        )
        halves.append((keep, lax.ppermute(send, "dp", [(i, i ^ 1) for i in range(dp_count)])))

    def hop(x, mask):
        return lax.ppermute(x, "label", [(i, i ^ mask) for i in range(lab_count)])

    keep, send = call(
        pair_kernel,
        "pair_sums",
        [struct((2, half_rows, part), jnp.float32), struct((2, half_rows, part), jnp.bfloat16)],
        [vmem()] * 2,
        halves[1],
    )
    got = hop(send, 2)
    spread = call(
        spread_kernel, "spread_sums", [wide] + [narrow] * (pairs - 1), [vmem()] * 2, halves[0]
    )
    low = [spread[0]] + [hop(x, 2 * j + 2) for j, x in enumerate(spread[1:])]
    got, *_ = lax.optimization_barrier((got, *spread))
    own, send = call(step_kernel, "step_sums", [wide, narrow], [vmem()] * 2, (keep, got))
    high = [own, hop(send, 4)]
    extra = -(-3 * block_count // 16) * 16

    def deliver(x):
        return move(x, lambda dp, lab: ((dp & ~1) | (lab & 1), (lab & ~1) | (1 - (dp & 1))))

    (low,) = call(
        line_and_loss_kernel,
        "line_sums_loss",
        [struct((half_rows + extra, part), jnp.bfloat16)],
        [vmem()] * (1 + len(low)),
        (loss, *low),
        scratch=[pltpu.VMEM((extra, part), jnp.float32)],
    )
    low_home = deliver(low)
    *high, low = lax.optimization_barrier((*high, low))
    (high,) = call(line_kernel, "line_sums", [narrow], [vmem()] * 2, high)
    loss, grads = call(
        home_again_kernel,
        "home_again",
        [loss_type, struct((inst_count, part), jnp.bfloat16)],
        [vmem()] * 2,
        (low_home, deliver(high)),
    )
    return loss.reshape(inst_count), grads


def solution(mesh):
    in_specs = (P("dp", None), P(("dp", "label"), None, None), P(), P(), P("dp", None))
    out_specs = (P("dp"), P("dp", "label"))
    return jax.shard_map(shards, mesh=mesh, in_specs=in_specs, out_specs=out_specs, check_vma=False)
```

```python
import functools

import jax
import jax.numpy as jnp
from jax import lax
from jax.experimental import pallas as pl
from jax.experimental.pallas import tpu as pltpu
from jax.sharding import PartitionSpec as P

BLK = 128
NEG_FILL = -1e30
VMEM_BYTES = 32 * 1024 * 1024
VMEM_PICK = 56 * 1024 * 1024


def divide(value, by):
    if by & (by - 1) == 0:
        return lax.shift_right_logical(value, jnp.int32(by.bit_length() - 1))
    return lax.div(value, jnp.int32(by))


def remainder(value, by):
    if by & (by - 1) == 0:
        return value & jnp.int32(by - 1)
    return lax.rem(value, jnp.int32(by))


def each_entry(count, short_count, body, carry):
    if count <= 64:
        for e in range(count):
            carry = body(e // short_count, e % short_count, carry)
        return carry
    step = lambda e, c: body(divide(e, short_count), remainder(e, short_count), c)
    return lax.fori_loop(0, count, step, carry)


class Plan:
    def __init__(self, square, dp_count, lab_count, stored, block_count, short_count):
        self.square, self.dp_count, self.lab_count = square, dp_count, lab_count
        self.stored, self.block_count, self.short_count = stored, block_count, short_count

    def here(self):
        return lax.axis_index("dp"), lax.axis_index("label")

    def home(self):
        dp, lab = self.here()
        return (dp & ~1) | (lab & 1) if self.square else dp

    def flips(self, entry, core):
        return [(0, 0), (1, 1), (core, 1 - core), (1 - core, core)][entry]

    def wanted_by(self, entry):
        dp, lab = self.here()
        if not self.square:
            return dp ^ entry
        flip_x, flip_y = self.flips(entry, dp & 1)
        return ((dp >> 1) ^ flip_y) * 2 + ((lab & 1) ^ flip_x)

    def entry_of(self, device):
        dp, lab = self.here()
        that_dp, that_lab = divide(device, self.lab_count), remainder(device, self.lab_count)
        if not self.square:
            return that_lab == lab, that_dp ^ dp
        match = ((that_dp & 1) == (dp & 1)) & ((that_lab >> 1) == (lab >> 1))
        flip_y, flip_x = (that_dp ^ dp) >> 1, (that_lab ^ lab) & 1
        core = dp & 1
        lone = jnp.where(flip_y == 1 - core, 2, 3)
        entry = jnp.where(flip_x + flip_y == 1, lone, (flip_x + flip_y) >> 1)
        return match, entry

    def pairs(self, entry):
        result = []
        for dp in range(self.dp_count):
            for lab in range(self.lab_count):
                if self.square:
                    flip_x, flip_y = self.flips(entry, dp & 1)
                    target = (dp ^ (2 * flip_y)) * self.lab_count + (lab ^ flip_x)
                else:
                    target = (dp ^ entry) * self.lab_count + lab
                result.append((dp * self.lab_count + lab, target))
        return result


def find_slots(plan, wanted, lists_ref, slot_ref):
    dp_index, lab_index = plan.here()
    mine = dp_index * plan.lab_count + lab_index
    stored, short_count = plan.stored, plan.short_count
    found = []
    for k in wanted:
        base = plan.wanted_by(k) * plan.block_count

        def look(row, column, slot_here, base=base):
            slot = slot_ref[lists_ref[base + row, column]]
            return jnp.where(divide(slot, stored) == mine, remainder(slot, stored), slot_here)

        count = plan.block_count // 2 * short_count
        found.append(each_entry(count, short_count, look, jnp.int32(0)))
    return found


def far_kernel(plan, wanted, lists_hbm, slot_hbm, weights_ref, *rest):
    outs = rest[: len(wanted)]
    held, lists_ref, slot_ref, sems = rest[len(wanted) :]
    tables = [
        pltpu.make_async_copy(lists_hbm, lists_ref, sems.at[0]),
        pltpu.make_async_copy(slot_hbm, slot_ref, sems.at[1]),
    ]
    stage = pltpu.make_async_copy(weights_ref, held, sems.at[2])
    for copy in tables:
        copy.start()
    stage.start()
    for copy in tables:
        copy.wait()
    found = find_slots(plan, wanted, lists_ref, slot_ref)
    stage.wait()
    copies = []
    for i, slot in enumerate(found):
        copies.append(pltpu.make_async_copy(held.at[slot], outs[i], sems.at[3 + i]))
        copies[-1].start()
    for copy in copies:
        copy.wait()


def near_kernel(plan, lists_ref, slot_ref, weights_ref, table_ref, *rest):
    block_count, short_count = plan.block_count, plan.short_count
    outs, sems = rest[:-1], rest[-1]
    copies = []
    for k, slot in enumerate(find_slots(plan, range(1), lists_ref, slot_ref)):
        copies.append(pltpu.make_async_copy(weights_ref.at[slot], outs[k], sems.at[k]))
        copies[-1].start()
    home = plan.home()
    half = block_count // 2
    for side in range(2):

        def note(row, column, carry, side=side):
            block = side * half + row
            cluster = lists_ref[home * block_count + block, column]
            match, entry = plan.entry_of(divide(slot_ref[cluster], plan.stored))

            @pl.when(match)
            def _():
                table_ref[entry, 0] = cluster
                table_ref[entry, 1 + side] = jnp.int32(block)

            return carry

        each_entry(half * short_count, short_count, note, jnp.int32(0))
    for copy in copies:
        copy.wait()


def home_kernel(feats_ref, pos_ref, other_feats_ref, other_pos_ref, home_feats_ref, home_pos_ref):
    same = (lax.axis_index("dp") & 1) == (lax.axis_index("label") & 1)

    @pl.when(same)
    def _():
        home_feats_ref[...] = feats_ref[...]
        home_pos_ref[...] = pos_ref[...]

    @pl.when(jnp.logical_not(same))
    def _():
        home_feats_ref[...] = other_feats_ref[...]
        home_pos_ref[...] = other_pos_ref[...]


def target_kernel(early, late, table_ref, pos_ref, feats_ref, hits_ref, shares_ref, turned_ref):
    count, cluster_size, _ = hits_ref.shape
    pos_count = pos_ref.shape[1]

    def one_slot(s):
        labels = lax.broadcasted_iota(jnp.int32, (cluster_size, BLK), 0) + table_ref[s, 0] * cluster_size
        for side in range(2):
            pos = pos_ref[table_ref[s, 1 + side]]
            hit = pos[0:1, :] == labels
            for p in range(1, pos_count):
                hit = hit | (pos[p : p + 1, :] == labels)
            hits = jnp.where(hit, 1.0, 0.0)
            columns = pl.ds(side * BLK, BLK)
            hits_ref[s, :, columns] = hits
            if s in early:
                shares_ref[early.index(s), columns, :] = (hits / pos_count).T
            else:
                feats = feats_ref[table_ref[s, 1 + side]].astype(jnp.float32)
                turned_ref[late.index(s), :, columns] = feats.T.astype(jnp.bfloat16)

    for s in range(count):
        pl.when(table_ref[s, 0] >= 0)(functools.partial(one_slot, s))


def logit_kernel(slots, turned, copies, table_ref, feats_ref, hits_ref, *rest):
    count = len(slots)
    rows = rest[:count]
    logits_ref, out_ref, stats_ref = rest[-3:]
    if len(rest) == count + 3:
        stats_ref[0] = jnp.full(stats_ref.shape[1:], NEG_FILL, jnp.float32)
        stats_ref[1] = jnp.zeros(stats_ref.shape[1:], jnp.float32)
        stats_ref[2] = jnp.zeros(stats_ref.shape[1:], jnp.float32)
    else:
        stats_ref[...] = rest[count][0]
    for i, (s, ref) in enumerate(zip(slots, rows)):
        if not turned:
            logits_ref[i] = jnp.dot(ref[...], feats_ref[i], preferred_element_type=jnp.float32)
        for side in range(2):
            block = table_ref[s, 1 + side]
            columns = pl.ds(side * BLK, BLK)
            if turned:
                logits = lax.dot_general(
                    ref[...],
                    feats_ref[block],
                    (((1,), (1,)), ((), ())),
                    preferred_element_type=jnp.float32,
                )
                logits_ref[i, columns, :] = logits.T
            else:
                logits = logits_ref[i, :, columns]
            highest = jnp.max(logits, axis=0, keepdims=True)
            total = jnp.sum(jnp.exp(logits - highest), axis=0, keepdims=True)
            positive = jnp.sum(hits_ref[s, :, columns] * logits, axis=0, keepdims=True)
            row = pl.ds(block, 1)
            before = stats_ref[0, row, :]
            after = jnp.maximum(before, highest)
            stats_ref[0, row, :] = after
            stats_ref[1, row, :] = stats_ref[1, row, :] * jnp.exp(before - after) + total * jnp.exp(
                highest - after
            )
            stats_ref[2, row, :] = stats_ref[2, row, :] + positive
    for i in range(copies):
        out_ref[i] = stats_ref[...]


def row_sums(stats_ref, lab_count):
    highest = stats_ref[0, 0]
    for i in range(1, lab_count):
        highest = jnp.maximum(highest, stats_ref[i, 0])
    summed = jnp.zeros_like(highest)
    positive = jnp.zeros_like(highest)
    for i in range(lab_count):
        summed = summed + stats_ref[i, 1] * jnp.exp(stats_ref[i, 0] - highest)
        positive = positive + stats_ref[i, 2]
    return highest + jnp.log(summed), positive


def prepare(stats_ref, pos_count, lab_count, loss_ref, lse_ref, columns_ref, total_ref, first):
    lse, positive = row_sums(stats_ref, lab_count)
    lse_ref[...] = lse
    loss_ref[...] = lse - positive / pos_count
    for b in range(columns_ref.shape[0]):
        columns_ref[b] = jnp.broadcast_to(lse[first + b : first + b + 1, :], (BLK, BLK)).T
    total_ref[...] = jnp.zeros_like(total_ref)


def add_slots(sides, groups, pos_count, first, table_ref, hits_ref, shares_ref, logits_refs, rows, sums):
    lse_ref, columns_ref, total_ref = sums
    early = [s for slots in groups[:-1] for s in slots]
    cluster_size = rows[0].shape[0]

    def one_slot(s, logits_ref):
        for side in sides:
            block = table_ref[s, 1 + side]
            here = pl.ds(side * BLK, BLK)
            if s in early:
                column = columns_ref[block - first]
                column = jnp.concatenate([column] * (cluster_size // BLK), axis=1)
                dlogit = jnp.exp(logits_ref[here, :] - column) - shares_ref[early.index(s), here, :]
            else:
                row = lse_ref[pl.ds(block, 1), :]
                dlogit = jnp.exp(logits_ref[:, here] - row) - hits_ref[s, :, here] / pos_count
                dlogit = dlogit.T
            total_ref[block - first] += lax.dot_general(
                dlogit.astype(jnp.bfloat16),
                rows[s][...],
                (((1,), (0,)), ((), ())),
                preferred_element_type=jnp.float32,
            )

    for slots, logits_ref in zip(groups, logits_refs):
        for i, s in enumerate(slots):
            body = functools.partial(one_slot, s, logits_ref.at[i])
            if len(rows) <= 4:
                body()
            else:
                pl.when(table_ref[s, 0] >= 0)(body)


def half_kernel(side, groups, lab_count, pos_count, table_ref, hits_ref, shares_ref, stats_ref, *rest):
    logits_refs = rest[: len(groups)]
    rows = rest[len(groups) : -6]
    loss_ref, keep_ref, send_ref, lse_ref, columns_ref, total_ref = rest[-6:]
    half = total_ref.shape[0]
    prepare(
        stats_ref, pos_count, lab_count, loss_ref, lse_ref, columns_ref, total_ref, side * half
    )
    add_slots(
        (side,),
        groups,
        pos_count,
        side * half,
        table_ref,
        hits_ref,
        shares_ref,
        logits_refs,
        rows,
        (lse_ref, columns_ref, total_ref),
    )
    part = keep_ref.shape[2]
    core, line = lax.axis_index("dp") & 1, lax.axis_index("label") >> 1
    for j in range(lab_count // 2):
        first = (line ^ j) * 2
        mine = pl.ds(pl.multiple_of((first + 1 - core) * part, part), part)
        other = pl.ds(pl.multiple_of((first + core) * part, part), part)
        for b in range(half):
            here = pl.ds(b * BLK, BLK)
            keep_ref[j, here, :] = total_ref[b, :, mine]
            send_ref[j, here, :] = total_ref[b, :, other].astype(jnp.bfloat16)


def pair_kernel(keep_ref, got_ref, next_ref, send_ref):
    for j in range(keep_ref.shape[0]):
        total = keep_ref[j] + got_ref[j].astype(jnp.float32)
        out_ref = send_ref if j % 2 else next_ref
        out_ref[j // 2] = total.astype(out_ref.dtype)


def spread_kernel(keep_ref, got_ref, *outs):
    for j, out_ref in enumerate(outs):
        out_ref[...] = (keep_ref[j] + got_ref[j].astype(jnp.float32)).astype(out_ref.dtype)


def step_kernel(keep_ref, got_ref, own_ref, send_ref):
    own_ref[...] = keep_ref[0] + got_ref[0].astype(jnp.float32)
    send_ref[...] = (keep_ref[1] + got_ref[1].astype(jnp.float32)).astype(jnp.bfloat16)


def line_kernel(*refs):
    total = refs[0][...]
    for ref in refs[1:-1]:
        total = total + ref[...].astype(jnp.float32)
    refs[-1][...] = total.astype(jnp.bfloat16)


def line_and_loss_kernel(loss_ref, *refs):
    out_ref, terms_ref = refs[-2:]
    rows = refs[0].shape[0]
    line_kernel(*refs[:-2], out_ref.at[:rows, :])
    terms_ref[...] = jnp.zeros_like(terms_ref)
    blocks = loss_ref.shape[0]
    rest = loss_ref[...]
    for i in range(3):
        term = rest.astype(jnp.bfloat16).astype(jnp.float32)
        terms_ref[i * blocks : (i + 1) * blocks, :] = term
        rest = rest - term
    out_ref[rows:, :] = terms_ref[...].astype(jnp.bfloat16)


def home_again_kernel(low_ref, high_ref, loss_ref, grads_ref):
    blocks = loss_ref.shape[0]
    rows = high_ref.shape[0]
    grads_ref[:rows, :] = low_ref[:rows, :]
    grads_ref[rows:, :] = high_ref[...]
    terms = low_ref[rows:, :].astype(jnp.float32)
    loss_ref[...] = terms[:blocks] + (terms[blocks : 2 * blocks] + terms[2 * blocks : 3 * blocks])


def grad_kernel(groups, lab_count, pos_count, table_ref, hits_ref, shares_ref, stats_ref, *rest):
    logits_refs = rest[: len(groups)]
    rows = rest[len(groups) : -5]
    loss_ref, out_ref, lse_ref, columns_ref, total_ref = rest[-5:]
    prepare(stats_ref, pos_count, lab_count, loss_ref, lse_ref, columns_ref, total_ref, 0)
    add_slots(
        (0, 1),
        groups,
        pos_count,
        0,
        table_ref,
        hits_ref,
        shares_ref,
        logits_refs,
        rows,
        (lse_ref, columns_ref, total_ref),
    )
    part = out_ref.shape[2]
    for j in range(lab_count):
        for b in range(total_ref.shape[0]):
            out_ref[j, b * BLK : (b + 1) * BLK, :] = total_ref[
                b, :, j * part : (j + 1) * part
            ].astype(jnp.bfloat16)


def smem():
    return pl.BlockSpec(memory_space=pltpu.SMEM)


def vmem():
    return pl.BlockSpec(memory_space=pltpu.VMEM)


def anywhere():
    return pl.BlockSpec(memory_space=pl.ANY)


def call(kernel, name, out_shape, in_specs, arrays, scratch=(), limit=VMEM_BYTES, out_specs=None):
    return pl.pallas_call(
        kernel,
        out_shape=out_shape,
        in_specs=in_specs,
        out_specs=out_specs or [vmem()] * len(out_shape),
        scratch_shapes=list(scratch),
        compiler_params=pltpu.CompilerParams(vmem_limit_bytes=limit),
        name=name,
    )(*arrays)


def shards(feats, weights, shortlist, slot_of, positives):
    dp_count = lax.axis_size("dp")
    lab_count = lax.axis_size("label")
    stored, cluster_size, width = weights.shape
    inst_count = feats.shape[0]
    pos_count = positives.shape[1]
    block_count = inst_count // BLK
    part = width // lab_count
    square = dp_count == 4 and lab_count == 8 and part % 128 == 0
    plan = Plan(square, dp_count, lab_count, stored, block_count, shortlist.shape[1])
    struct = jax.ShapeDtypeStruct
    row_type = struct((cluster_size, width), weights.dtype)
    stat_shape = (3, block_count, BLK)
    both = ("dp", "label")
    devices = [(dp, lab) for dp in range(dp_count) for lab in range(lab_count)]

    def move(x, target):
        pairs = []
        for dp, lab in devices:
            to_dp, to_lab = target(dp, lab)
            pairs.append((dp * lab_count + lab, to_dp * lab_count + to_lab))
        return lax.ppermute(x, both, pairs)

    feat_blocks = feats.reshape(block_count, BLK, width)
    pos_blocks = positives.reshape(block_count, BLK, pos_count).transpose(0, 2, 1)
    if square:
        other_feats = lax.ppermute(feat_blocks, "dp", [(i, i ^ 1) for i in range(dp_count)])
        other_pos = lax.ppermute(pos_blocks, "dp", [(i, i ^ 1) for i in range(dp_count)])
        feat_blocks, pos_blocks = call(
            home_kernel,
            "home",
            [struct(feat_blocks.shape, feats.dtype), struct(pos_blocks.shape, jnp.int32)],
            [vmem()] * 4,
            (feat_blocks, pos_blocks, other_feats, other_pos),
        )

    far = range(1, dp_count)
    far_rows = call(
        functools.partial(far_kernel, plan, far),
        "pick_far",
        [row_type] * len(far),
        [anywhere()] * 3,
        (shortlist, slot_of, weights),
        scratch=[
            pltpu.VMEM(weights.shape, weights.dtype),
            pltpu.SMEM(shortlist.shape, jnp.int32),
            pltpu.SMEM(slot_of.shape, jnp.int32),
            pltpu.SemaphoreType.DMA((3 + len(far),)),
        ],
        limit=VMEM_PICK,
        out_specs=[anywhere()] * len(far),
    )
    table, *rows = call(
        functools.partial(near_kernel, plan),
        "pick_near",
        [struct((dp_count, 4), jnp.int32), row_type],
        [smem(), smem(), anywhere()],
        (shortlist, slot_of, weights),
        scratch=[pltpu.SemaphoreType.DMA((1,))],
        out_specs=[smem(), vmem()],
    )
    rows += [lax.ppermute(x, both, plan.pairs(k)) for k, x in zip(far, far_rows)]

    if square:
        groups = [(0,), (1,), (2,), (3,)]
    else:
        cuts = (0, dp_count // 2, dp_count * 3 // 4, dp_count)
        groups = [tuple(range(a, b)) for a, b in zip(cuts[:-1], cuts[1:])]
    early = [s for slots in groups[:-1] for s in slots]
    late = list(groups[-1])
    hits, shares, turned = call(
        functools.partial(target_kernel, early, late),
        "targets",
        [
            struct((dp_count, cluster_size, 2 * BLK), jnp.float32),
            struct((len(early), 2 * BLK, cluster_size), jnp.float32),
            struct((len(late), width, 2 * BLK), feats.dtype),
        ],
        [smem()] + [vmem()] * 2,
        (table, pos_blocks, feat_blocks),
    )
    kept = []
    stats = []
    for slots in groups:
        last = slots is groups[-1]
        copies = lab_count if last else 1
        shape = (cluster_size, 2 * BLK) if last else (2 * BLK, cluster_size)
        logits, stats_out = call(
            functools.partial(logit_kernel, slots, not last, copies),
            "logits",
            [
                struct((len(slots),) + shape, jnp.float32),
                struct((copies,) + stat_shape, jnp.float32),
            ],
            [smem()] + [vmem()] * (2 + len(slots) + len(stats)),
            (table, turned if last else feat_blocks, hits, *[rows[s] for s in slots], *stats),
            scratch=[pltpu.VMEM(stat_shape, jnp.float32)],
        )
        kept.append(logits)
        stats = [stats_out]

    in_specs = [smem()] + [vmem()] * (3 + len(groups) + dp_count)
    loss_type = struct((block_count, BLK), jnp.float32)
    lse_scratch = pltpu.VMEM((block_count, BLK), jnp.float32)
    if not square:
        all_stats = lax.all_to_all(stats[0], "label", split_axis=0, concat_axis=0, tiled=True)
        loss, parts = call(
            functools.partial(grad_kernel, groups, lab_count, pos_count),
            "grads",
            [loss_type, struct((lab_count, inst_count, part), jnp.bfloat16)],
            in_specs,
            (table, hits, shares, all_stats, *kept, *rows),
            scratch=[
                lse_scratch,
                pltpu.VMEM((block_count, BLK, BLK), jnp.float32),
                pltpu.VMEM((block_count, BLK, width), jnp.float32),
            ],
        )
        gathered = lax.all_to_all(parts, "label", split_axis=0, concat_axis=0, tiled=True)
        grads = jnp.sum(gathered.astype(jnp.float32), axis=0).astype(jnp.bfloat16)
        return loss.reshape(inst_count), grads

    owners = [
        [(2 * y + core) * lab_count + 2 * z + x for z in range(lab_count // 2) for core in range(2)]
        for y in range(dp_count // 2)
        for x in range(2)
    ]
    all_stats = lax.all_to_all(
        stats[0], both, split_axis=0, concat_axis=0, axis_index_groups=owners, tiled=True
    )
    pairs = lab_count // 2
    half_rows = inst_count // 2
    wide = struct((half_rows, part), jnp.float32)
    narrow = struct((half_rows, part), jnp.bfloat16)

    halves = []
    for side in range(2):
        loss, keep, send = call(
            functools.partial(half_kernel, side, groups, lab_count, pos_count),
            "grads",
            [
                loss_type,
                struct((pairs, half_rows, part), jnp.float32),
                struct((pairs, half_rows, part), jnp.bfloat16),
            ],
            in_specs,
            (table, hits, shares, all_stats, *kept, *rows),
            scratch=[
                lse_scratch,
                pltpu.VMEM((block_count // 2, BLK, BLK), jnp.float32),
                pltpu.VMEM((block_count // 2, BLK, width), jnp.float32),
            ],
        )
        halves.append((keep, lax.ppermute(send, "dp", [(i, i ^ 1) for i in range(dp_count)])))

    def hop(x, mask):
        return lax.ppermute(x, "label", [(i, i ^ mask) for i in range(lab_count)])

    keep, send = call(
        pair_kernel,
        "pair_sums",
        [struct((2, half_rows, part), jnp.float32), struct((2, half_rows, part), jnp.bfloat16)],
        [vmem()] * 2,
        halves[1],
    )
    got = hop(send, 2)
    spread = call(
        spread_kernel, "spread_sums", [wide] + [narrow] * (pairs - 1), [vmem()] * 2, halves[0]
    )
    low = [spread[0]] + [hop(x, 2 * j + 2) for j, x in enumerate(spread[1:])]
    got, *_ = lax.optimization_barrier((got, *spread))
    own, send = call(step_kernel, "step_sums", [wide, narrow], [vmem()] * 2, (keep, got))
    high = [own, hop(send, 4)]
    extra = -(-3 * block_count // 16) * 16

    def deliver(x):
        return move(x, lambda dp, lab: ((dp & ~1) | (lab & 1), (lab & ~1) | (1 - (dp & 1))))

    (low,) = call(
        line_and_loss_kernel,
        "line_sums_loss",
        [struct((half_rows + extra, part), jnp.bfloat16)],
        [vmem()] * (1 + len(low)),
        (loss, *low),
        scratch=[pltpu.VMEM((extra, part), jnp.float32)],
    )
    low_home = deliver(low)
    *high, low = lax.optimization_barrier((*high, low))
    (high,) = call(line_kernel, "line_sums", [narrow], [vmem()] * 2, high)
    loss, grads = call(
        home_again_kernel,
        "home_again",
        [loss_type, struct((inst_count, part), jnp.bfloat16)],
        [vmem()] * 2,
        (low_home, deliver(high)),
    )
    return loss.reshape(inst_count), grads


def solution(mesh):
    in_specs = (P("dp", None), P(("dp", "label"), None, None), P(), P(), P("dp", None))
    out_specs = (P("dp"), P("dp", "label"))
    return jax.shard_map(shards, mesh=mesh, in_specs=in_specs, out_specs=out_specs, check_vma=False)
```

```python
import functools

import jax
import jax.numpy as jnp
from jax import lax
from jax.experimental import pallas as pl
from jax.experimental.pallas import tpu as pltpu
from jax.sharding import PartitionSpec as P

BLK = 128
NEG_FILL = -1e30
VMEM_BYTES = 32 * 1024 * 1024
VMEM_PICK = 56 * 1024 * 1024


def divide(value, by):
    if by & (by - 1) == 0:
        return lax.shift_right_logical(value, jnp.int32(by.bit_length() - 1))
    return lax.div(value, jnp.int32(by))


def remainder(value, by):
    if by & (by - 1) == 0:
        return value & jnp.int32(by - 1)
    return lax.rem(value, jnp.int32(by))


def each_entry(count, short_count, body, carry):
    if count <= 64:
        for e in range(count):
            carry = body(e // short_count, e % short_count, carry)
        return carry
    step = lambda e, c: body(divide(e, short_count), remainder(e, short_count), c)
    return lax.fori_loop(0, count, step, carry)


class Plan:
    def __init__(self, square, dp_count, lab_count, stored, block_count, short_count):
        self.square, self.dp_count, self.lab_count = square, dp_count, lab_count
        self.stored, self.block_count, self.short_count = stored, block_count, short_count

    def here(self):
        return lax.axis_index("dp"), lax.axis_index("label")

    def home(self):
        dp, lab = self.here()
        return (dp & ~1) | (lab & 1) if self.square else dp

    def flips(self, entry, core):
        return [(0, 0), (1, 1), (core, 1 - core), (1 - core, core)][entry]

    def wanted_by(self, entry):
        dp, lab = self.here()
        if not self.square:
            return dp ^ entry
        flip_x, flip_y = self.flips(entry, dp & 1)
        return ((dp >> 1) ^ flip_y) * 2 + ((lab & 1) ^ flip_x)

    def entry_of(self, device):
        dp, lab = self.here()
        that_dp, that_lab = divide(device, self.lab_count), remainder(device, self.lab_count)
        if not self.square:
            return that_lab == lab, that_dp ^ dp
        match = ((that_dp & 1) == (dp & 1)) & ((that_lab >> 1) == (lab >> 1))
        flip_y, flip_x = (that_dp ^ dp) >> 1, (that_lab ^ lab) & 1
        core = dp & 1
        lone = jnp.where(flip_y == 1 - core, 2, 3)
        entry = jnp.where(flip_x + flip_y == 1, lone, (flip_x + flip_y) >> 1)
        return match, entry

    def pairs(self, entry):
        result = []
        for dp in range(self.dp_count):
            for lab in range(self.lab_count):
                if self.square:
                    flip_x, flip_y = self.flips(entry, dp & 1)
                    target = (dp ^ (2 * flip_y)) * self.lab_count + (lab ^ flip_x)
                else:
                    target = (dp ^ entry) * self.lab_count + lab
                result.append((dp * self.lab_count + lab, target))
        return result


def find_slots(plan, wanted, lists_ref, slot_ref):
    dp_index, lab_index = plan.here()
    mine = dp_index * plan.lab_count + lab_index
    stored, short_count = plan.stored, plan.short_count
    found = []
    for k in wanted:
        base = plan.wanted_by(k) * plan.block_count

        def look(row, column, slot_here, base=base):
            slot = slot_ref[lists_ref[base + row, column]]
            return jnp.where(divide(slot, stored) == mine, remainder(slot, stored), slot_here)

        count = plan.block_count // 2 * short_count
        found.append(each_entry(count, short_count, look, jnp.int32(0)))
    return found


def far_kernel(plan, wanted, lists_hbm, slot_hbm, weights_ref, *rest):
    outs = rest[: len(wanted)]
    held, lists_ref, slot_ref, sems = rest[len(wanted) :]
    tables = [
        pltpu.make_async_copy(lists_hbm, lists_ref, sems.at[0]),
        pltpu.make_async_copy(slot_hbm, slot_ref, sems.at[1]),
    ]
    stage = pltpu.make_async_copy(weights_ref, held, sems.at[2])
    for copy in tables:
        copy.start()
    stage.start()
    for copy in tables:
        copy.wait()
    found = find_slots(plan, wanted, lists_ref, slot_ref)
    stage.wait()
    copies = []
    for i, slot in enumerate(found):
        copies.append(pltpu.make_async_copy(held.at[slot], outs[i], sems.at[3 + i]))
        copies[-1].start()
    for copy in copies:
        copy.wait()


def near_kernel(plan, lists_ref, slot_ref, weights_ref, table_ref, *rest):
    block_count, short_count = plan.block_count, plan.short_count
    outs, sems = rest[:-1], rest[-1]
    copies = []
    for k, slot in enumerate(find_slots(plan, range(1), lists_ref, slot_ref)):
        copies.append(pltpu.make_async_copy(weights_ref.at[slot], outs[k], sems.at[k]))
        copies[-1].start()
    home = plan.home()
    half = block_count // 2
    for side in range(2):

        def note(row, column, carry, side=side):
            block = side * half + row
            cluster = lists_ref[home * block_count + block, column]
            match, entry = plan.entry_of(divide(slot_ref[cluster], plan.stored))

            @pl.when(match)
            def _():
                table_ref[entry, 0] = cluster
                table_ref[entry, 1 + side] = jnp.int32(block)

            return carry

        each_entry(half * short_count, short_count, note, jnp.int32(0))
    for copy in copies:
        copy.wait()


def home_kernel(feats_ref, pos_ref, other_feats_ref, other_pos_ref, home_feats_ref, home_pos_ref):
    same = (lax.axis_index("dp") & 1) == (lax.axis_index("label") & 1)

    @pl.when(same)
    def _():
        home_feats_ref[...] = feats_ref[...]
        home_pos_ref[...] = pos_ref[...]

    @pl.when(jnp.logical_not(same))
    def _():
        home_feats_ref[...] = other_feats_ref[...]
        home_pos_ref[...] = other_pos_ref[...]


def target_kernel(early, late, table_ref, pos_ref, feats_ref, hits_ref, shares_ref, turned_ref):
    count, cluster_size, _ = hits_ref.shape
    pos_count = pos_ref.shape[1]

    def one_slot(s):
        labels = lax.broadcasted_iota(jnp.int32, (cluster_size, BLK), 0) + table_ref[s, 0] * cluster_size
        for side in range(2):
            pos = pos_ref[table_ref[s, 1 + side]]
            hit = pos[0:1, :] == labels
            for p in range(1, pos_count):
                hit = hit | (pos[p : p + 1, :] == labels)
            hits = jnp.where(hit, 1.0, 0.0)
            columns = pl.ds(side * BLK, BLK)
            hits_ref[s, :, columns] = hits
            if s in early:
                shares_ref[early.index(s), columns, :] = (hits / pos_count).T
            else:
                feats = feats_ref[table_ref[s, 1 + side]].astype(jnp.float32)
                turned_ref[late.index(s), :, columns] = feats.T.astype(jnp.bfloat16)

    for s in range(count):
        pl.when(table_ref[s, 0] >= 0)(functools.partial(one_slot, s))


def logit_kernel(slots, turned, copies, table_ref, feats_ref, hits_ref, *rest):
    count = len(slots)
    rows = rest[:count]
    logits_ref, out_ref, stats_ref = rest[-3:]
    if len(rest) == count + 3:
        stats_ref[0] = jnp.full(stats_ref.shape[1:], NEG_FILL, jnp.float32)
        stats_ref[1] = jnp.zeros(stats_ref.shape[1:], jnp.float32)
        stats_ref[2] = jnp.zeros(stats_ref.shape[1:], jnp.float32)
    else:
        stats_ref[...] = rest[count][0]
    for i, (s, ref) in enumerate(zip(slots, rows)):
        if not turned:
            logits_ref[i] = jnp.dot(ref[...], feats_ref[i], preferred_element_type=jnp.float32)
        for side in range(2):
            block = table_ref[s, 1 + side]
            columns = pl.ds(side * BLK, BLK)
            if turned:
                logits = lax.dot_general(
                    ref[...],
                    feats_ref[block],
                    (((1,), (1,)), ((), ())),
                    preferred_element_type=jnp.float32,
                )
                logits_ref[i, columns, :] = logits.T
            else:
                logits = logits_ref[i, :, columns]
            highest = jnp.max(logits, axis=0, keepdims=True)
            total = jnp.sum(jnp.exp(logits - highest), axis=0, keepdims=True)
            positive = jnp.sum(hits_ref[s, :, columns] * logits, axis=0, keepdims=True)
            row = pl.ds(block, 1)
            before = stats_ref[0, row, :]
            after = jnp.maximum(before, highest)
            stats_ref[0, row, :] = after
            stats_ref[1, row, :] = stats_ref[1, row, :] * jnp.exp(before - after) + total * jnp.exp(
                highest - after
            )
            stats_ref[2, row, :] = stats_ref[2, row, :] + positive
    for i in range(copies):
        out_ref[i] = stats_ref[...]


def row_sums(stats_ref, lab_count):
    highest = stats_ref[0, 0]
    for i in range(1, lab_count):
        highest = jnp.maximum(highest, stats_ref[i, 0])
    summed = jnp.zeros_like(highest)
    positive = jnp.zeros_like(highest)
    for i in range(lab_count):
        summed = summed + stats_ref[i, 1] * jnp.exp(stats_ref[i, 0] - highest)
        positive = positive + stats_ref[i, 2]
    return highest + jnp.log(summed), positive


def prepare(stats_ref, pos_count, lab_count, loss_ref, lse_ref, columns_ref, total_ref, first):
    lse, positive = row_sums(stats_ref, lab_count)
    lse_ref[...] = lse
    loss_ref[...] = lse - positive / pos_count
    for b in range(columns_ref.shape[0]):
        columns_ref[b] = jnp.broadcast_to(lse[first + b : first + b + 1, :], (BLK, BLK)).T
    total_ref[...] = jnp.zeros_like(total_ref)


def add_slots(sides, groups, pos_count, first, table_ref, hits_ref, shares_ref, logits_refs, rows, sums):
    lse_ref, columns_ref, total_ref = sums
    early = [s for slots in groups[:-1] for s in slots]
    cluster_size = rows[0].shape[0]

    def one_slot(s, logits_ref):
        for side in sides:
            block = table_ref[s, 1 + side]
            here = pl.ds(side * BLK, BLK)
            if s in early:
                column = columns_ref[block - first]
                column = jnp.concatenate([column] * (cluster_size // BLK), axis=1)
                dlogit = jnp.exp(logits_ref[here, :] - column) - shares_ref[early.index(s), here, :]
            else:
                row = lse_ref[pl.ds(block, 1), :]
                dlogit = jnp.exp(logits_ref[:, here] - row) - hits_ref[s, :, here] / pos_count
                dlogit = dlogit.T
            total_ref[block - first] += lax.dot_general(
                dlogit.astype(jnp.bfloat16),
                rows[s][...],
                (((1,), (0,)), ((), ())),
                preferred_element_type=jnp.float32,
            )

    for slots, logits_ref in zip(groups, logits_refs):
        for i, s in enumerate(slots):
            body = functools.partial(one_slot, s, logits_ref.at[i])
            if len(rows) <= 4:
                body()
            else:
                pl.when(table_ref[s, 0] >= 0)(body)


def half_kernel(side, groups, lab_count, pos_count, table_ref, hits_ref, shares_ref, stats_ref, *rest):
    logits_refs = rest[: len(groups)]
    rows = rest[len(groups) : -6]
    loss_ref, keep_ref, send_ref, lse_ref, columns_ref, total_ref = rest[-6:]
    half = total_ref.shape[0]
    prepare(
        stats_ref, pos_count, lab_count, loss_ref, lse_ref, columns_ref, total_ref, side * half
    )
    add_slots(
        (side,),
        groups,
        pos_count,
        side * half,
        table_ref,
        hits_ref,
        shares_ref,
        logits_refs,
        rows,
        (lse_ref, columns_ref, total_ref),
    )
    part = keep_ref.shape[2]
    core, line = lax.axis_index("dp") & 1, lax.axis_index("label") >> 1
    for j in range(lab_count // 2):
        first = (line ^ j) * 2
        mine = pl.ds(pl.multiple_of((first + 1 - core) * part, part), part)
        other = pl.ds(pl.multiple_of((first + core) * part, part), part)
        for b in range(half):
            here = pl.ds(b * BLK, BLK)
            keep_ref[j, here, :] = total_ref[b, :, mine]
            send_ref[j, here, :] = total_ref[b, :, other].astype(jnp.bfloat16)


def pair_kernel(keep_ref, got_ref, next_ref, send_ref):
    for j in range(keep_ref.shape[0]):
        total = keep_ref[j] + got_ref[j].astype(jnp.float32)
        out_ref = send_ref if j % 2 else next_ref
        out_ref[j // 2] = total.astype(out_ref.dtype)


def spread_kernel(keep_ref, got_ref, *outs):
    for j, out_ref in enumerate(outs):
        out_ref[...] = (keep_ref[j] + got_ref[j].astype(jnp.float32)).astype(out_ref.dtype)


def step_kernel(keep_ref, got_ref, own_ref, send_ref):
    own_ref[...] = keep_ref[0] + got_ref[0].astype(jnp.float32)
    send_ref[...] = (keep_ref[1] + got_ref[1].astype(jnp.float32)).astype(jnp.bfloat16)


def line_kernel(*refs):
    total = refs[0][...]
    for ref in refs[1:-1]:
        total = total + ref[...].astype(jnp.float32)
    refs[-1][...] = total.astype(jnp.bfloat16)


def line_and_loss_kernel(loss_ref, *refs):
    out_ref, terms_ref = refs[-2:]
    rows = refs[0].shape[0]
    line_kernel(*refs[:-2], out_ref.at[:rows, :])
    terms_ref[...] = jnp.zeros_like(terms_ref)
    blocks = loss_ref.shape[0]
    rest = loss_ref[...]
    for i in range(3):
        term = rest.astype(jnp.bfloat16).astype(jnp.float32)
        terms_ref[i * blocks : (i + 1) * blocks, :] = term
        rest = rest - term
    out_ref[rows:, :] = terms_ref[...].astype(jnp.bfloat16)


def home_again_kernel(low_ref, high_ref, loss_ref, grads_ref):
    blocks = loss_ref.shape[0]
    rows = high_ref.shape[0]
    grads_ref[:rows, :] = low_ref[:rows, :]
    grads_ref[rows:, :] = high_ref[...]
    terms = low_ref[rows:, :].astype(jnp.float32)
    loss_ref[...] = terms[:blocks] + (terms[blocks : 2 * blocks] + terms[2 * blocks : 3 * blocks])


def grad_kernel(groups, lab_count, pos_count, table_ref, hits_ref, shares_ref, stats_ref, *rest):
    logits_refs = rest[: len(groups)]
    rows = rest[len(groups) : -5]
    loss_ref, out_ref, lse_ref, columns_ref, total_ref = rest[-5:]
    prepare(stats_ref, pos_count, lab_count, loss_ref, lse_ref, columns_ref, total_ref, 0)
    add_slots(
        (0, 1),
        groups,
        pos_count,
        0,
        table_ref,
        hits_ref,
        shares_ref,
        logits_refs,
        rows,
        (lse_ref, columns_ref, total_ref),
    )
    part = out_ref.shape[2]
    for j in range(lab_count):
        for b in range(total_ref.shape[0]):
            out_ref[j, b * BLK : (b + 1) * BLK, :] = total_ref[
                b, :, j * part : (j + 1) * part
            ].astype(jnp.bfloat16)


def smem():
    return pl.BlockSpec(memory_space=pltpu.SMEM)


def vmem():
    return pl.BlockSpec(memory_space=pltpu.VMEM)


def anywhere():
    return pl.BlockSpec(memory_space=pl.ANY)


def call(kernel, name, out_shape, in_specs, arrays, scratch=(), limit=VMEM_BYTES, out_specs=None):
    return pl.pallas_call(
        kernel,
        out_shape=out_shape,
        in_specs=in_specs,
        out_specs=out_specs or [vmem()] * len(out_shape),
        scratch_shapes=list(scratch),
        compiler_params=pltpu.CompilerParams(vmem_limit_bytes=limit),
        name=name,
    )(*arrays)


def shards(feats, weights, shortlist, slot_of, positives):
    dp_count = lax.axis_size("dp")
    lab_count = lax.axis_size("label")
    stored, cluster_size, width = weights.shape
    inst_count = feats.shape[0]
    pos_count = positives.shape[1]
    block_count = inst_count // BLK
    part = width // lab_count
    square = dp_count == 4 and lab_count == 8 and part % 128 == 0
    plan = Plan(square, dp_count, lab_count, stored, block_count, shortlist.shape[1])
    struct = jax.ShapeDtypeStruct
    row_type = struct((cluster_size, width), weights.dtype)
    stat_shape = (3, block_count, BLK)
    both = ("dp", "label")
    devices = [(dp, lab) for dp in range(dp_count) for lab in range(lab_count)]

    def move(x, target):
        pairs = []
        for dp, lab in devices:
            to_dp, to_lab = target(dp, lab)
            pairs.append((dp * lab_count + lab, to_dp * lab_count + to_lab))
        return lax.ppermute(x, both, pairs)

    feat_blocks = feats.reshape(block_count, BLK, width)
    pos_blocks = positives.reshape(block_count, BLK, pos_count).transpose(0, 2, 1)
    if square:
        other_feats = lax.ppermute(feat_blocks, "dp", [(i, i ^ 1) for i in range(dp_count)])
        other_pos = lax.ppermute(pos_blocks, "dp", [(i, i ^ 1) for i in range(dp_count)])
        feat_blocks, pos_blocks = call(
            home_kernel,
            "home",
            [struct(feat_blocks.shape, feats.dtype), struct(pos_blocks.shape, jnp.int32)],
            [vmem()] * 4,
            (feat_blocks, pos_blocks, other_feats, other_pos),
        )

    far = range(1, dp_count)
    far_rows = call(
        functools.partial(far_kernel, plan, far),
        "pick_far",
        [row_type] * len(far),
        [anywhere()] * 3,
        (shortlist, slot_of, weights),
        scratch=[
            pltpu.VMEM(weights.shape, weights.dtype),
            pltpu.SMEM(shortlist.shape, jnp.int32),
            pltpu.SMEM(slot_of.shape, jnp.int32),
            pltpu.SemaphoreType.DMA((3 + len(far),)),
        ],
        limit=VMEM_PICK,
        out_specs=[anywhere()] * len(far),
    )
    table, *rows = call(
        functools.partial(near_kernel, plan),
        "pick_near",
        [struct((dp_count, 4), jnp.int32), row_type],
        [smem(), smem(), anywhere()],
        (shortlist, slot_of, weights),
        scratch=[pltpu.SemaphoreType.DMA((1,))],
        out_specs=[smem(), vmem()],
    )
    for k, x in zip(far, far_rows):
        if square and k == 3:
            x, rows[1] = lax.optimization_barrier((x, rows[1]))
        rows.append(lax.ppermute(x, both, plan.pairs(k)))

    if square:
        groups = [(0,), (1,), (2,), (3,)]
    else:
        cuts = (0, dp_count // 2, dp_count * 3 // 4, dp_count)
        groups = [tuple(range(a, b)) for a, b in zip(cuts[:-1], cuts[1:])]
    early = [s for slots in groups[:-1] for s in slots]
    late = list(groups[-1])
    hits, shares, turned = call(
        functools.partial(target_kernel, early, late),
        "targets",
        [
            struct((dp_count, cluster_size, 2 * BLK), jnp.float32),
            struct((len(early), 2 * BLK, cluster_size), jnp.float32),
            struct((len(late), width, 2 * BLK), feats.dtype),
        ],
        [smem()] + [vmem()] * 2,
        (table, pos_blocks, feat_blocks),
    )
    kept = []
    stats = []
    for slots in groups:
        last = slots is groups[-1]
        copies = lab_count if last else 1
        shape = (cluster_size, 2 * BLK) if last else (2 * BLK, cluster_size)
        logits, stats_out = call(
            functools.partial(logit_kernel, slots, not last, copies),
            "logits",
            [
                struct((len(slots),) + shape, jnp.float32),
                struct((copies,) + stat_shape, jnp.float32),
            ],
            [smem()] + [vmem()] * (2 + len(slots) + len(stats)),
            (table, turned if last else feat_blocks, hits, *[rows[s] for s in slots], *stats),
            scratch=[pltpu.VMEM(stat_shape, jnp.float32)],
        )
        kept.append(logits)
        stats = [stats_out]

    in_specs = [smem()] + [vmem()] * (3 + len(groups) + dp_count)
    loss_type = struct((block_count, BLK), jnp.float32)
    lse_scratch = pltpu.VMEM((block_count, BLK), jnp.float32)
    if not square:
        all_stats = lax.all_to_all(stats[0], "label", split_axis=0, concat_axis=0, tiled=True)
        loss, parts = call(
            functools.partial(grad_kernel, groups, lab_count, pos_count),
            "grads",
            [loss_type, struct((lab_count, inst_count, part), jnp.bfloat16)],
            in_specs,
            (table, hits, shares, all_stats, *kept, *rows),
            scratch=[
                lse_scratch,
                pltpu.VMEM((block_count, BLK, BLK), jnp.float32),
                pltpu.VMEM((block_count, BLK, width), jnp.float32),
            ],
        )
        gathered = lax.all_to_all(parts, "label", split_axis=0, concat_axis=0, tiled=True)
        grads = jnp.sum(gathered.astype(jnp.float32), axis=0).astype(jnp.bfloat16)
        return loss.reshape(inst_count), grads

    owners = [
        [(2 * y + core) * lab_count + 2 * z + x for z in range(lab_count // 2) for core in range(2)]
        for y in range(dp_count // 2)
        for x in range(2)
    ]
    all_stats = lax.all_to_all(
        stats[0], both, split_axis=0, concat_axis=0, axis_index_groups=owners, tiled=True
    )
    pairs = lab_count // 2
    half_rows = inst_count // 2
    wide = struct((half_rows, part), jnp.float32)
    narrow = struct((half_rows, part), jnp.bfloat16)

    halves = []
    for side in range(2):
        loss, keep, send = call(
            functools.partial(half_kernel, side, groups, lab_count, pos_count),
            "grads",
            [
                loss_type,
                struct((pairs, half_rows, part), jnp.float32),
                struct((pairs, half_rows, part), jnp.bfloat16),
            ],
            in_specs,
            (table, hits, shares, all_stats, *kept, *rows),
            scratch=[
                lse_scratch,
                pltpu.VMEM((block_count // 2, BLK, BLK), jnp.float32),
                pltpu.VMEM((block_count // 2, BLK, width), jnp.float32),
            ],
        )
        halves.append((keep, lax.ppermute(send, "dp", [(i, i ^ 1) for i in range(dp_count)])))

    def hop(x, mask):
        return lax.ppermute(x, "label", [(i, i ^ mask) for i in range(lab_count)])

    keep, send = call(
        pair_kernel,
        "pair_sums",
        [struct((2, half_rows, part), jnp.float32), struct((2, half_rows, part), jnp.bfloat16)],
        [vmem()] * 2,
        halves[1],
    )
    got = hop(send, 2)
    spread = call(
        spread_kernel, "spread_sums", [wide] + [narrow] * (pairs - 1), [vmem()] * 2, halves[0]
    )
    low = [spread[0]] + [hop(x, 2 * j + 2) for j, x in enumerate(spread[1:])]
    got, *_ = lax.optimization_barrier((got, *spread))
    own, send = call(step_kernel, "step_sums", [wide, narrow], [vmem()] * 2, (keep, got))
    high = [own, hop(send, 4)]
    extra = -(-3 * block_count // 16) * 16

    def deliver(x):
        return move(x, lambda dp, lab: ((dp & ~1) | (lab & 1), (lab & ~1) | (1 - (dp & 1))))

    (low,) = call(
        line_and_loss_kernel,
        "line_sums_loss",
        [struct((half_rows + extra, part), jnp.bfloat16)],
        [vmem()] * (1 + len(low)),
        (loss, *low),
        scratch=[pltpu.VMEM((extra, part), jnp.float32)],
    )
    low_home = deliver(low)
    *high, low = lax.optimization_barrier((*high, low))
    (high,) = call(line_kernel, "line_sums", [narrow], [vmem()] * 2, high)
    loss, grads = call(
        home_again_kernel,
        "home_again",
        [loss_type, struct((inst_count, part), jnp.bfloat16)],
        [vmem()] * 2,
        (low_home, deliver(high)),
    )
    return loss.reshape(inst_count), grads


def solution(mesh):
    in_specs = (P("dp", None), P(("dp", "label"), None, None), P(), P(), P("dp", None))
    out_specs = (P("dp"), P("dp", "label"))
    return jax.shard_map(shards, mesh=mesh, in_specs=in_specs, out_specs=out_specs, check_vma=False)
```

```python
import functools

import jax
import jax.numpy as jnp
from jax import lax
from jax.experimental import pallas as pl
from jax.experimental.pallas import tpu as pltpu
from jax.sharding import PartitionSpec as P

BLK = 128
NEG_FILL = -1e30
VMEM_BYTES = 32 * 1024 * 1024
VMEM_PICK = 56 * 1024 * 1024


def divide(value, by):
    if by & (by - 1) == 0:
        return lax.shift_right_logical(value, jnp.int32(by.bit_length() - 1))
    return lax.div(value, jnp.int32(by))


def remainder(value, by):
    if by & (by - 1) == 0:
        return value & jnp.int32(by - 1)
    return lax.rem(value, jnp.int32(by))


def each_entry(count, short_count, body, carry):
    if count <= 64:
        for e in range(count):
            carry = body(e // short_count, e % short_count, carry)
        return carry
    step = lambda e, c: body(divide(e, short_count), remainder(e, short_count), c)
    return lax.fori_loop(0, count, step, carry)


class Plan:
    def __init__(self, square, dp_count, lab_count, stored, block_count, short_count):
        self.square, self.dp_count, self.lab_count = square, dp_count, lab_count
        self.stored, self.block_count, self.short_count = stored, block_count, short_count

    def here(self):
        return lax.axis_index("dp"), lax.axis_index("label")

    def home(self):
        dp, lab = self.here()
        return (dp & ~1) | (lab & 1) if self.square else dp

    def flips(self, entry, core):
        return [(0, 0), (1, 1), (core, 1 - core), (1 - core, core)][entry]

    def wanted_by(self, entry):
        dp, lab = self.here()
        if not self.square:
            return dp ^ entry
        flip_x, flip_y = self.flips(entry, dp & 1)
        return ((dp >> 1) ^ flip_y) * 2 + ((lab & 1) ^ flip_x)

    def entry_of(self, device):
        dp, lab = self.here()
        that_dp, that_lab = divide(device, self.lab_count), remainder(device, self.lab_count)
        if not self.square:
            return that_lab == lab, that_dp ^ dp
        match = ((that_dp & 1) == (dp & 1)) & ((that_lab >> 1) == (lab >> 1))
        flip_y, flip_x = (that_dp ^ dp) >> 1, (that_lab ^ lab) & 1
        core = dp & 1
        lone = jnp.where(flip_y == 1 - core, 2, 3)
        entry = jnp.where(flip_x + flip_y == 1, lone, (flip_x + flip_y) >> 1)
        return match, entry

    def pairs(self, entry):
        result = []
        for dp in range(self.dp_count):
            for lab in range(self.lab_count):
                if self.square:
                    flip_x, flip_y = self.flips(entry, dp & 1)
                    target = (dp ^ (2 * flip_y)) * self.lab_count + (lab ^ flip_x)
                else:
                    target = (dp ^ entry) * self.lab_count + lab
                result.append((dp * self.lab_count + lab, target))
        return result


def find_slots(plan, wanted, lists_ref, slot_ref):
    dp_index, lab_index = plan.here()
    mine = dp_index * plan.lab_count + lab_index
    stored, short_count = plan.stored, plan.short_count
    found = []
    for k in wanted:
        base = plan.wanted_by(k) * plan.block_count

        def look(row, column, slot_here, base=base):
            slot = slot_ref[lists_ref[base + row, column]]
            return jnp.where(divide(slot, stored) == mine, remainder(slot, stored), slot_here)

        count = plan.block_count // 2 * short_count
        found.append(each_entry(count, short_count, look, jnp.int32(0)))
    return found


def far_kernel(plan, wanted, lists_hbm, slot_hbm, weights_ref, *rest):
    outs = rest[: len(wanted)]
    held, lists_ref, slot_ref, sems = rest[len(wanted) :]
    tables = [
        pltpu.make_async_copy(lists_hbm, lists_ref, sems.at[0]),
        pltpu.make_async_copy(slot_hbm, slot_ref, sems.at[1]),
    ]
    stage = pltpu.make_async_copy(weights_ref, held, sems.at[2])
    for copy in tables:
        copy.start()
    stage.start()
    for copy in tables:
        copy.wait()
    found = find_slots(plan, wanted, lists_ref, slot_ref)
    stage.wait()
    copies = []
    for i, slot in enumerate(found):
        copies.append(pltpu.make_async_copy(held.at[slot], outs[i], sems.at[3 + i]))
        copies[-1].start()
    for copy in copies:
        copy.wait()


def near_kernel(plan, lists_ref, slot_ref, weights_ref, table_ref, *rest):
    block_count, short_count = plan.block_count, plan.short_count
    outs, sems = rest[:-1], rest[-1]
    copies = []
    for k, slot in enumerate(find_slots(plan, range(1), lists_ref, slot_ref)):
        copies.append(pltpu.make_async_copy(weights_ref.at[slot], outs[k], sems.at[k]))
        copies[-1].start()
    home = plan.home()
    half = block_count // 2
    for side in range(2):

        def note(row, column, carry, side=side):
            block = side * half + row
            cluster = lists_ref[home * block_count + block, column]
            match, entry = plan.entry_of(divide(slot_ref[cluster], plan.stored))

            @pl.when(match)
            def _():
                table_ref[entry, 0] = cluster
                table_ref[entry, 1 + side] = jnp.int32(block)

            return carry

        each_entry(half * short_count, short_count, note, jnp.int32(0))
    for copy in copies:
        copy.wait()


def home_kernel(feats_ref, pos_ref, other_feats_ref, other_pos_ref, home_feats_ref, home_pos_ref):
    same = (lax.axis_index("dp") & 1) == (lax.axis_index("label") & 1)

    @pl.when(same)
    def _():
        home_feats_ref[...] = feats_ref[...]
        home_pos_ref[...] = pos_ref[...]

    @pl.when(jnp.logical_not(same))
    def _():
        home_feats_ref[...] = other_feats_ref[...]
        home_pos_ref[...] = other_pos_ref[...]


def target_kernel(early, late, table_ref, pos_ref, feats_ref, hits_ref, shares_ref, turned_ref):
    count, cluster_size, _ = hits_ref.shape
    pos_count = pos_ref.shape[1]

    def one_slot(s):
        labels = lax.broadcasted_iota(jnp.int32, (cluster_size, BLK), 0) + table_ref[s, 0] * cluster_size
        for side in range(2):
            pos = pos_ref[table_ref[s, 1 + side]]
            hit = pos[0:1, :] == labels
            for p in range(1, pos_count):
                hit = hit | (pos[p : p + 1, :] == labels)
            hits = jnp.where(hit, 1.0, 0.0)
            columns = pl.ds(side * BLK, BLK)
            hits_ref[s, :, columns] = hits
            if s in early:
                shares_ref[early.index(s), columns, :] = (hits / pos_count).T
            else:
                feats = feats_ref[table_ref[s, 1 + side]].astype(jnp.float32)
                turned_ref[late.index(s), :, columns] = feats.T.astype(jnp.bfloat16)

    for s in range(count):
        pl.when(table_ref[s, 0] >= 0)(functools.partial(one_slot, s))


def logit_kernel(slots, turned, copies, table_ref, feats_ref, hits_ref, *rest):
    count = len(slots)
    rows = rest[:count]
    logits_ref, out_ref, stats_ref = rest[-3:]
    if len(rest) == count + 3:
        stats_ref[0] = jnp.full(stats_ref.shape[1:], NEG_FILL, jnp.float32)
        stats_ref[1] = jnp.zeros(stats_ref.shape[1:], jnp.float32)
        stats_ref[2] = jnp.zeros(stats_ref.shape[1:], jnp.float32)
    else:
        stats_ref[...] = rest[count][0]
    for i, (s, ref) in enumerate(zip(slots, rows)):
        if not turned:
            logits_ref[i] = jnp.dot(ref[...], feats_ref[i], preferred_element_type=jnp.float32)
        for side in range(2):
            block = table_ref[s, 1 + side]
            columns = pl.ds(side * BLK, BLK)
            if turned:
                logits = lax.dot_general(
                    ref[...],
                    feats_ref[block],
                    (((1,), (1,)), ((), ())),
                    preferred_element_type=jnp.float32,
                )
                logits_ref[i, columns, :] = logits.T
            else:
                logits = logits_ref[i, :, columns]
            highest = jnp.max(logits, axis=0, keepdims=True)
            total = jnp.sum(jnp.exp(logits - highest), axis=0, keepdims=True)
            positive = jnp.sum(hits_ref[s, :, columns] * logits, axis=0, keepdims=True)
            row = pl.ds(block, 1)
            before = stats_ref[0, row, :]
            after = jnp.maximum(before, highest)
            stats_ref[0, row, :] = after
            stats_ref[1, row, :] = stats_ref[1, row, :] * jnp.exp(before - after) + total * jnp.exp(
                highest - after
            )
            stats_ref[2, row, :] = stats_ref[2, row, :] + positive
    for i in range(copies):
        out_ref[i] = stats_ref[...]


def row_sums(stats_ref, lab_count):
    highest = stats_ref[0, 0]
    for i in range(1, lab_count):
        highest = jnp.maximum(highest, stats_ref[i, 0])
    summed = jnp.zeros_like(highest)
    positive = jnp.zeros_like(highest)
    for i in range(lab_count):
        summed = summed + stats_ref[i, 1] * jnp.exp(stats_ref[i, 0] - highest)
        positive = positive + stats_ref[i, 2]
    return highest + jnp.log(summed), positive


def prepare(stats_ref, pos_count, lab_count, loss_ref, lse_ref, columns_ref, total_ref, first):
    lse, positive = row_sums(stats_ref, lab_count)
    lse_ref[...] = lse
    loss_ref[...] = lse - positive / pos_count
    for b in range(columns_ref.shape[0]):
        columns_ref[b] = jnp.broadcast_to(lse[first + b : first + b + 1, :], (BLK, BLK)).T
    total_ref[...] = jnp.zeros_like(total_ref)


def add_slots(sides, groups, pos_count, first, table_ref, hits_ref, shares_ref, logits_refs, rows, sums):
    lse_ref, columns_ref, total_ref = sums
    early = [s for slots in groups[:-1] for s in slots]
    cluster_size = rows[0].shape[0]

    def one_slot(s, logits_ref):
        for side in sides:
            block = table_ref[s, 1 + side]
            here = pl.ds(side * BLK, BLK)
            if s in early:
                column = columns_ref[block - first]
                column = jnp.concatenate([column] * (cluster_size // BLK), axis=1)
                dlogit = jnp.exp(logits_ref[here, :] - column) - shares_ref[early.index(s), here, :]
            else:
                row = lse_ref[pl.ds(block, 1), :]
                dlogit = jnp.exp(logits_ref[:, here] - row) - hits_ref[s, :, here] / pos_count
                dlogit = dlogit.T
            total_ref[block - first] += lax.dot_general(
                dlogit.astype(jnp.bfloat16),
                rows[s][...],
                (((1,), (0,)), ((), ())),
                preferred_element_type=jnp.float32,
            )

    for slots, logits_ref in zip(groups, logits_refs):
        for i, s in enumerate(slots):
            body = functools.partial(one_slot, s, logits_ref.at[i])
            if len(rows) <= 4:
                body()
            else:
                pl.when(table_ref[s, 0] >= 0)(body)


def half_kernel(side, groups, lab_count, pos_count, table_ref, hits_ref, shares_ref, stats_ref, *rest):
    logits_refs = rest[: len(groups)]
    rows = rest[len(groups) : -6]
    loss_ref, keep_ref, send_ref, lse_ref, columns_ref, total_ref = rest[-6:]
    half = total_ref.shape[0]
    prepare(
        stats_ref, pos_count, lab_count, loss_ref, lse_ref, columns_ref, total_ref, side * half
    )
    add_slots(
        (side,),
        groups,
        pos_count,
        side * half,
        table_ref,
        hits_ref,
        shares_ref,
        logits_refs,
        rows,
        (lse_ref, columns_ref, total_ref),
    )
    part = keep_ref.shape[2]
    core, line = lax.axis_index("dp") & 1, lax.axis_index("label") >> 1
    for j in range(lab_count // 2):
        first = (line ^ j) * 2
        mine = pl.ds(pl.multiple_of((first + 1 - core) * part, part), part)
        other = pl.ds(pl.multiple_of((first + core) * part, part), part)
        for b in range(half):
            here = pl.ds(b * BLK, BLK)
            keep_ref[j, here, :] = total_ref[b, :, mine]
            send_ref[j, here, :] = total_ref[b, :, other].astype(jnp.bfloat16)


def pair_kernel(keep_ref, got_ref, next_ref, send_ref):
    for j in range(keep_ref.shape[0]):
        total = keep_ref[j] + got_ref[j].astype(jnp.float32)
        out_ref = send_ref if j % 2 else next_ref
        out_ref[j // 2] = total.astype(out_ref.dtype)


def spread_kernel(keep_ref, got_ref, *outs):
    for j, out_ref in enumerate(outs):
        out_ref[...] = (keep_ref[j] + got_ref[j].astype(jnp.float32)).astype(out_ref.dtype)


def step_kernel(keep_ref, got_ref, own_ref, send_ref):
    own_ref[...] = keep_ref[0] + got_ref[0].astype(jnp.float32)
    send_ref[...] = (keep_ref[1] + got_ref[1].astype(jnp.float32)).astype(jnp.bfloat16)


def line_kernel(*refs):
    total = refs[0][...]
    for ref in refs[1:-1]:
        total = total + ref[...].astype(jnp.float32)
    refs[-1][...] = total.astype(jnp.bfloat16)


def line_and_loss_kernel(loss_ref, *refs):
    out_ref, terms_ref = refs[-2:]
    rows = refs[0].shape[0]
    line_kernel(*refs[:-2], out_ref.at[:rows, :])
    terms_ref[...] = jnp.zeros_like(terms_ref)
    blocks = loss_ref.shape[0]
    rest = loss_ref[...]
    for i in range(3):
        term = rest.astype(jnp.bfloat16).astype(jnp.float32)
        terms_ref[i * blocks : (i + 1) * blocks, :] = term
        rest = rest - term
    out_ref[rows:, :] = terms_ref[...].astype(jnp.bfloat16)


def home_again_kernel(low_ref, high_ref, loss_ref, grads_ref):
    blocks = loss_ref.shape[0]
    rows = high_ref.shape[0]
    grads_ref[:rows, :] = low_ref[:rows, :]
    grads_ref[rows:, :] = high_ref[...]
    terms = low_ref[rows:, :].astype(jnp.float32)
    loss_ref[...] = terms[:blocks] + (terms[blocks : 2 * blocks] + terms[2 * blocks : 3 * blocks])


def grad_kernel(groups, lab_count, pos_count, table_ref, hits_ref, shares_ref, stats_ref, *rest):
    logits_refs = rest[: len(groups)]
    rows = rest[len(groups) : -5]
    loss_ref, out_ref, lse_ref, columns_ref, total_ref = rest[-5:]
    prepare(stats_ref, pos_count, lab_count, loss_ref, lse_ref, columns_ref, total_ref, 0)
    add_slots(
        (0, 1),
        groups,
        pos_count,
        0,
        table_ref,
        hits_ref,
        shares_ref,
        logits_refs,
        rows,
        (lse_ref, columns_ref, total_ref),
    )
    part = out_ref.shape[2]
    for j in range(lab_count):
        for b in range(total_ref.shape[0]):
            out_ref[j, b * BLK : (b + 1) * BLK, :] = total_ref[
                b, :, j * part : (j + 1) * part
            ].astype(jnp.bfloat16)


def smem():
    return pl.BlockSpec(memory_space=pltpu.SMEM)


def vmem():
    return pl.BlockSpec(memory_space=pltpu.VMEM)


def anywhere():
    return pl.BlockSpec(memory_space=pl.ANY)


def call(kernel, name, out_shape, in_specs, arrays, scratch=(), limit=VMEM_BYTES, out_specs=None):
    return pl.pallas_call(
        kernel,
        out_shape=out_shape,
        in_specs=in_specs,
        out_specs=out_specs or [vmem()] * len(out_shape),
        scratch_shapes=list(scratch),
        compiler_params=pltpu.CompilerParams(vmem_limit_bytes=limit),
        name=name,
    )(*arrays)


def shards(feats, weights, shortlist, slot_of, positives):
    dp_count = lax.axis_size("dp")
    lab_count = lax.axis_size("label")
    stored, cluster_size, width = weights.shape
    inst_count = feats.shape[0]
    pos_count = positives.shape[1]
    block_count = inst_count // BLK
    part = width // lab_count
    square = dp_count == 4 and lab_count == 8 and part % 128 == 0
    plan = Plan(square, dp_count, lab_count, stored, block_count, shortlist.shape[1])
    struct = jax.ShapeDtypeStruct
    row_type = struct((cluster_size, width), weights.dtype)
    stat_shape = (3, block_count, BLK)
    both = ("dp", "label")
    devices = [(dp, lab) for dp in range(dp_count) for lab in range(lab_count)]

    def move(x, target):
        pairs = []
        for dp, lab in devices:
            to_dp, to_lab = target(dp, lab)
            pairs.append((dp * lab_count + lab, to_dp * lab_count + to_lab))
        return lax.ppermute(x, both, pairs)

    feat_blocks = feats.reshape(block_count, BLK, width)
    pos_blocks = positives.reshape(block_count, BLK, pos_count).transpose(0, 2, 1)
    if square:
        other_feats = lax.ppermute(feat_blocks, "dp", [(i, i ^ 1) for i in range(dp_count)])
        other_pos = lax.ppermute(pos_blocks, "dp", [(i, i ^ 1) for i in range(dp_count)])
        feat_blocks, pos_blocks = call(
            home_kernel,
            "home",
            [struct(feat_blocks.shape, feats.dtype), struct(pos_blocks.shape, jnp.int32)],
            [vmem()] * 4,
            (feat_blocks, pos_blocks, other_feats, other_pos),
        )

    far = range(1, dp_count)
    far_rows = []
    for some in (far[:1], far[1:]) if square else (far,):
        far_rows += call(
            functools.partial(far_kernel, plan, some),
            "pick_far",
            [row_type] * len(some),
            [anywhere()] * 3,
            (shortlist, slot_of, weights),
            scratch=[
                pltpu.VMEM(weights.shape, weights.dtype),
                pltpu.SMEM(shortlist.shape, jnp.int32),
                pltpu.SMEM(slot_of.shape, jnp.int32),
                pltpu.SemaphoreType.DMA((3 + len(some),)),
            ],
            limit=VMEM_PICK,
            out_specs=[anywhere()] * len(some),
        )
    table, *rows = call(
        functools.partial(near_kernel, plan),
        "pick_near",
        [struct((dp_count, 4), jnp.int32), row_type],
        [smem(), smem(), anywhere()],
        (shortlist, slot_of, weights),
        scratch=[pltpu.SemaphoreType.DMA((1,))],
        out_specs=[smem(), vmem()],
    )
    for k, x in zip(far, far_rows):
        if square and k == 3:
            x, rows[1] = lax.optimization_barrier((x, rows[1]))
        rows.append(lax.ppermute(x, both, plan.pairs(k)))

    if square:
        groups = [(0,), (1,), (2,), (3,)]
    else:
        cuts = (0, dp_count // 2, dp_count * 3 // 4, dp_count)
        groups = [tuple(range(a, b)) for a, b in zip(cuts[:-1], cuts[1:])]
    early = [s for slots in groups[:-1] for s in slots]
    late = list(groups[-1])
    hits, shares, turned = call(
        functools.partial(target_kernel, early, late),
        "targets",
        [
            struct((dp_count, cluster_size, 2 * BLK), jnp.float32),
            struct((len(early), 2 * BLK, cluster_size), jnp.float32),
            struct((len(late), width, 2 * BLK), feats.dtype),
        ],
        [smem()] + [vmem()] * 2,
        (table, pos_blocks, feat_blocks),
    )
    kept = []
    stats = []
    for slots in groups:
        last = slots is groups[-1]
        copies = lab_count if last else 1
        shape = (cluster_size, 2 * BLK) if last else (2 * BLK, cluster_size)
        logits, stats_out = call(
            functools.partial(logit_kernel, slots, not last, copies),
            "logits",
            [
                struct((len(slots),) + shape, jnp.float32),
                struct((copies,) + stat_shape, jnp.float32),
            ],
            [smem()] + [vmem()] * (2 + len(slots) + len(stats)),
            (table, turned if last else feat_blocks, hits, *[rows[s] for s in slots], *stats),
            scratch=[pltpu.VMEM(stat_shape, jnp.float32)],
        )
        kept.append(logits)
        stats = [stats_out]

    in_specs = [smem()] + [vmem()] * (3 + len(groups) + dp_count)
    loss_type = struct((block_count, BLK), jnp.float32)
    lse_scratch = pltpu.VMEM((block_count, BLK), jnp.float32)
    if not square:
        all_stats = lax.all_to_all(stats[0], "label", split_axis=0, concat_axis=0, tiled=True)
        loss, parts = call(
            functools.partial(grad_kernel, groups, lab_count, pos_count),
            "grads",
            [loss_type, struct((lab_count, inst_count, part), jnp.bfloat16)],
            in_specs,
            (table, hits, shares, all_stats, *kept, *rows),
            scratch=[
                lse_scratch,
                pltpu.VMEM((block_count, BLK, BLK), jnp.float32),
                pltpu.VMEM((block_count, BLK, width), jnp.float32),
            ],
        )
        gathered = lax.all_to_all(parts, "label", split_axis=0, concat_axis=0, tiled=True)
        grads = jnp.sum(gathered.astype(jnp.float32), axis=0).astype(jnp.bfloat16)
        return loss.reshape(inst_count), grads

    owners = [
        [(2 * y + core) * lab_count + 2 * z + x for z in range(lab_count // 2) for core in range(2)]
        for y in range(dp_count // 2)
        for x in range(2)
    ]
    all_stats = lax.all_to_all(
        stats[0], both, split_axis=0, concat_axis=0, axis_index_groups=owners, tiled=True
    )
    pairs = lab_count // 2
    half_rows = inst_count // 2
    wide = struct((half_rows, part), jnp.float32)
    narrow = struct((half_rows, part), jnp.bfloat16)

    halves = []
    for side in range(2):
        loss, keep, send = call(
            functools.partial(half_kernel, side, groups, lab_count, pos_count),
            "grads",
            [
                loss_type,
                struct((pairs, half_rows, part), jnp.float32),
                struct((pairs, half_rows, part), jnp.bfloat16),
            ],
            in_specs,
            (table, hits, shares, all_stats, *kept, *rows),
            scratch=[
                lse_scratch,
                pltpu.VMEM((block_count // 2, BLK, BLK), jnp.float32),
                pltpu.VMEM((block_count // 2, BLK, width), jnp.float32),
            ],
        )
        halves.append((keep, lax.ppermute(send, "dp", [(i, i ^ 1) for i in range(dp_count)])))

    def hop(x, mask):
        return lax.ppermute(x, "label", [(i, i ^ mask) for i in range(lab_count)])

    keep, send = call(
        pair_kernel,
        "pair_sums",
        [struct((2, half_rows, part), jnp.float32), struct((2, half_rows, part), jnp.bfloat16)],
        [vmem()] * 2,
        halves[1],
    )
    got = hop(send, 2)
    spread = call(
        spread_kernel, "spread_sums", [wide] + [narrow] * (pairs - 1), [vmem()] * 2, halves[0]
    )
    low = [spread[0]] + [hop(x, 2 * j + 2) for j, x in enumerate(spread[1:])]
    got, *_ = lax.optimization_barrier((got, *spread))
    own, send = call(step_kernel, "step_sums", [wide, narrow], [vmem()] * 2, (keep, got))
    high = [own, hop(send, 4)]
    extra = -(-3 * block_count // 16) * 16

    def deliver(x):
        return move(x, lambda dp, lab: ((dp & ~1) | (lab & 1), (lab & ~1) | (1 - (dp & 1))))

    (low,) = call(
        line_and_loss_kernel,
        "line_sums_loss",
        [struct((half_rows + extra, part), jnp.bfloat16)],
        [vmem()] * (1 + len(low)),
        (loss, *low),
        scratch=[pltpu.VMEM((extra, part), jnp.float32)],
    )
    low_home = deliver(low)
    *high, low = lax.optimization_barrier((*high, low))
    (high,) = call(line_kernel, "line_sums", [narrow], [vmem()] * 2, high)
    loss, grads = call(
        home_again_kernel,
        "home_again",
        [loss_type, struct((inst_count, part), jnp.bfloat16)],
        [vmem()] * 2,
        (low_home, deliver(high)),
    )
    return loss.reshape(inst_count), grads


def solution(mesh):
    in_specs = (P("dp", None), P(("dp", "label"), None, None), P(), P(), P("dp", None))
    out_specs = (P("dp"), P("dp", "label"))
    return jax.shard_map(shards, mesh=mesh, in_specs=in_specs, out_specs=out_specs, check_vma=False)
```

```python
import functools

import jax
import jax.numpy as jnp
from jax import lax
from jax.experimental import pallas as pl
from jax.experimental.pallas import tpu as pltpu
from jax.sharding import PartitionSpec as P

BLK = 128
NEG_FILL = -1e30
VMEM_BYTES = 32 * 1024 * 1024
VMEM_PICK = 56 * 1024 * 1024


def divide(value, by):
    if by & (by - 1) == 0:
        return lax.shift_right_logical(value, jnp.int32(by.bit_length() - 1))
    return lax.div(value, jnp.int32(by))


def remainder(value, by):
    if by & (by - 1) == 0:
        return value & jnp.int32(by - 1)
    return lax.rem(value, jnp.int32(by))


def each_entry(count, short_count, body, carry):
    if count <= 64:
        for e in range(count):
            carry = body(e // short_count, e % short_count, carry)
        return carry
    step = lambda e, c: body(divide(e, short_count), remainder(e, short_count), c)
    return lax.fori_loop(0, count, step, carry)


class Plan:
    def __init__(self, square, dp_count, lab_count, stored, block_count, short_count):
        self.square, self.dp_count, self.lab_count = square, dp_count, lab_count
        self.stored, self.block_count, self.short_count = stored, block_count, short_count

    def here(self):
        return lax.axis_index("dp"), lax.axis_index("label")

    def home(self):
        dp, lab = self.here()
        return (dp & ~1) | (lab & 1) if self.square else dp

    def flips(self, entry, core):
        return [(0, 0), (1, 1), (core, 1 - core), (1 - core, core)][entry]

    def wanted_by(self, entry):
        dp, lab = self.here()
        if not self.square:
            return dp ^ entry
        flip_x, flip_y = self.flips(entry, dp & 1)
        return ((dp >> 1) ^ flip_y) * 2 + ((lab & 1) ^ flip_x)

    def entry_of(self, device):
        dp, lab = self.here()
        that_dp, that_lab = divide(device, self.lab_count), remainder(device, self.lab_count)
        if not self.square:
            return that_lab == lab, that_dp ^ dp
        match = ((that_dp & 1) == (dp & 1)) & ((that_lab >> 1) == (lab >> 1))
        flip_y, flip_x = (that_dp ^ dp) >> 1, (that_lab ^ lab) & 1
        core = dp & 1
        lone = jnp.where(flip_y == 1 - core, 2, 3)
        entry = jnp.where(flip_x + flip_y == 1, lone, (flip_x + flip_y) >> 1)
        return match, entry

    def pairs(self, entry):
        result = []
        for dp in range(self.dp_count):
            for lab in range(self.lab_count):
                if self.square:
                    flip_x, flip_y = self.flips(entry, dp & 1)
                    target = (dp ^ (2 * flip_y)) * self.lab_count + (lab ^ flip_x)
                else:
                    target = (dp ^ entry) * self.lab_count + lab
                result.append((dp * self.lab_count + lab, target))
        return result


def find_slots(plan, wanted, lists_ref, slot_ref):
    dp_index, lab_index = plan.here()
    mine = dp_index * plan.lab_count + lab_index
    stored, short_count = plan.stored, plan.short_count
    found = []
    for k in wanted:
        base = plan.wanted_by(k) * plan.block_count

        def look(row, column, slot_here, base=base):
            slot = slot_ref[lists_ref[base + row, column]]
            return jnp.where(divide(slot, stored) == mine, remainder(slot, stored), slot_here)

        count = plan.block_count // 2 * short_count
        found.append(each_entry(count, short_count, look, jnp.int32(0)))
    return found


def far_kernel(plan, wanted, lists_hbm, slot_hbm, weights_ref, *rest):
    outs = rest[: len(wanted)]
    held, lists_ref, slot_ref, sems = rest[len(wanted) :]
    tables = [
        pltpu.make_async_copy(lists_hbm, lists_ref, sems.at[0]),
        pltpu.make_async_copy(slot_hbm, slot_ref, sems.at[1]),
    ]
    stage = pltpu.make_async_copy(weights_ref, held, sems.at[2])
    for copy in tables:
        copy.start()
    stage.start()
    for copy in tables:
        copy.wait()
    found = find_slots(plan, wanted, lists_ref, slot_ref)
    stage.wait()
    copies = []
    for i, slot in enumerate(found):
        copies.append(pltpu.make_async_copy(held.at[slot], outs[i], sems.at[3 + i]))
        copies[-1].start()
    for copy in copies:
        copy.wait()


def near_kernel(plan, lists_ref, slot_ref, weights_ref, table_ref, *rest):
    block_count, short_count = plan.block_count, plan.short_count
    outs, sems = rest[:-1], rest[-1]
    copies = []
    for k, slot in enumerate(find_slots(plan, range(1), lists_ref, slot_ref)):
        copies.append(pltpu.make_async_copy(weights_ref.at[slot], outs[k], sems.at[k]))
        copies[-1].start()
    home = plan.home()
    half = block_count // 2
    for side in range(2):

        def note(row, column, carry, side=side):
            block = side * half + row
            cluster = lists_ref[home * block_count + block, column]
            match, entry = plan.entry_of(divide(slot_ref[cluster], plan.stored))

            @pl.when(match)
            def _():
                table_ref[entry, 0] = cluster
                table_ref[entry, 1 + side] = jnp.int32(block)

            return carry

        each_entry(half * short_count, short_count, note, jnp.int32(0))
    for copy in copies:
        copy.wait()


def home_kernel(feats_ref, pos_ref, other_feats_ref, other_pos_ref, home_feats_ref, home_pos_ref):
    same = (lax.axis_index("dp") & 1) == (lax.axis_index("label") & 1)

    @pl.when(same)
    def _():
        home_feats_ref[...] = feats_ref[...]
        home_pos_ref[...] = pos_ref[...]

    @pl.when(jnp.logical_not(same))
    def _():
        home_feats_ref[...] = other_feats_ref[...]
        home_pos_ref[...] = other_pos_ref[...]


def target_kernel(early, late, table_ref, pos_ref, feats_ref, hits_ref, shares_ref, turned_ref):
    count, cluster_size, _ = hits_ref.shape
    pos_count = pos_ref.shape[1]

    def one_slot(s):
        labels = lax.broadcasted_iota(jnp.int32, (cluster_size, BLK), 0) + table_ref[s, 0] * cluster_size
        for side in range(2):
            pos = pos_ref[table_ref[s, 1 + side]]
            hit = pos[0:1, :] == labels
            for p in range(1, pos_count):
                hit = hit | (pos[p : p + 1, :] == labels)
            hits = jnp.where(hit, 1.0, 0.0)
            columns = pl.ds(side * BLK, BLK)
            hits_ref[s, :, columns] = hits
            if s in early:
                shares_ref[early.index(s), columns, :] = (hits / pos_count).T
            else:
                feats = feats_ref[table_ref[s, 1 + side]].astype(jnp.float32)
                turned_ref[late.index(s), :, columns] = feats.T.astype(jnp.bfloat16)

    for s in range(count):
        pl.when(table_ref[s, 0] >= 0)(functools.partial(one_slot, s))


def logit_kernel(slots, turned, copies, table_ref, feats_ref, hits_ref, *rest):
    count = len(slots)
    rows = rest[:count]
    logits_ref, out_ref, stats_ref = rest[-3:]
    if len(rest) == count + 3:
        stats_ref[0] = jnp.full(stats_ref.shape[1:], NEG_FILL, jnp.float32)
        stats_ref[1] = jnp.zeros(stats_ref.shape[1:], jnp.float32)
        stats_ref[2] = jnp.zeros(stats_ref.shape[1:], jnp.float32)
    else:
        stats_ref[...] = rest[count][0]
    for i, (s, ref) in enumerate(zip(slots, rows)):
        if not turned:
            logits_ref[i] = jnp.dot(ref[...], feats_ref[i], preferred_element_type=jnp.float32)
        for side in range(2):
            block = table_ref[s, 1 + side]
            columns = pl.ds(side * BLK, BLK)
            if turned:
                logits = lax.dot_general(
                    ref[...],
                    feats_ref[block],
                    (((1,), (1,)), ((), ())),
                    preferred_element_type=jnp.float32,
                )
                logits_ref[i, columns, :] = logits.T
            else:
                logits = logits_ref[i, :, columns]
            highest = jnp.max(logits, axis=0, keepdims=True)
            total = jnp.sum(jnp.exp(logits - highest), axis=0, keepdims=True)
            positive = jnp.sum(hits_ref[s, :, columns] * logits, axis=0, keepdims=True)
            row = pl.ds(block, 1)
            before = stats_ref[0, row, :]
            after = jnp.maximum(before, highest)
            stats_ref[0, row, :] = after
            stats_ref[1, row, :] = stats_ref[1, row, :] * jnp.exp(before - after) + total * jnp.exp(
                highest - after
            )
            stats_ref[2, row, :] = stats_ref[2, row, :] + positive
    for i in range(copies):
        out_ref[i] = stats_ref[...]


def row_sums(stats_ref, lab_count):
    highest = stats_ref[0, 0]
    for i in range(1, lab_count):
        highest = jnp.maximum(highest, stats_ref[i, 0])
    summed = jnp.zeros_like(highest)
    positive = jnp.zeros_like(highest)
    for i in range(lab_count):
        summed = summed + stats_ref[i, 1] * jnp.exp(stats_ref[i, 0] - highest)
        positive = positive + stats_ref[i, 2]
    return highest + jnp.log(summed), positive


def prepare(stats_ref, pos_count, lab_count, loss_ref, lse_ref, columns_ref, total_ref, first):
    lse, positive = row_sums(stats_ref, lab_count)
    lse_ref[...] = lse
    loss_ref[...] = lse - positive / pos_count
    for b in range(columns_ref.shape[0]):
        columns_ref[b] = jnp.broadcast_to(lse[first + b : first + b + 1, :], (BLK, BLK)).T
    total_ref[...] = jnp.zeros_like(total_ref)


def add_slots(sides, groups, pos_count, first, table_ref, hits_ref, shares_ref, logits_refs, rows, sums):
    lse_ref, columns_ref, total_ref = sums
    early = [s for slots in groups[:-1] for s in slots]
    cluster_size = rows[0].shape[0]

    def one_slot(s, logits_ref):
        for side in sides:
            block = table_ref[s, 1 + side]
            here = pl.ds(side * BLK, BLK)
            if s in early:
                column = columns_ref[block - first]
                column = jnp.concatenate([column] * (cluster_size // BLK), axis=1)
                dlogit = jnp.exp(logits_ref[here, :] - column) - shares_ref[early.index(s), here, :]
            else:
                row = lse_ref[pl.ds(block, 1), :]
                dlogit = jnp.exp(logits_ref[:, here] - row) - hits_ref[s, :, here] / pos_count
                dlogit = dlogit.T
            total_ref[block - first] += lax.dot_general(
                dlogit.astype(jnp.bfloat16),
                rows[s][...],
                (((1,), (0,)), ((), ())),
                preferred_element_type=jnp.float32,
            )

    for slots, logits_ref in zip(groups, logits_refs):
        for i, s in enumerate(slots):
            body = functools.partial(one_slot, s, logits_ref.at[i])
            if len(rows) <= 4:
                body()
            else:
                pl.when(table_ref[s, 0] >= 0)(body)


def half_kernel(side, groups, lab_count, pos_count, table_ref, hits_ref, shares_ref, stats_ref, *rest):
    logits_refs = rest[: len(groups)]
    rows = rest[len(groups) : -6]
    loss_ref, keep_ref, send_ref, lse_ref, columns_ref, total_ref = rest[-6:]
    half = total_ref.shape[0]
    prepare(
        stats_ref, pos_count, lab_count, loss_ref, lse_ref, columns_ref, total_ref, side * half
    )
    add_slots(
        (side,),
        groups,
        pos_count,
        side * half,
        table_ref,
        hits_ref,
        shares_ref,
        logits_refs,
        rows,
        (lse_ref, columns_ref, total_ref),
    )
    part = keep_ref.shape[2]
    core, line = lax.axis_index("dp") & 1, lax.axis_index("label") >> 1
    for j in range(lab_count // 2):
        first = (line ^ j) * 2
        mine = pl.ds(pl.multiple_of((first + 1 - core) * part, part), part)
        other = pl.ds(pl.multiple_of((first + core) * part, part), part)
        for b in range(half):
            here = pl.ds(b * BLK, BLK)
            keep_ref[j, here, :] = total_ref[b, :, mine]
            send_ref[j, here, :] = total_ref[b, :, other].astype(jnp.bfloat16)


def pair_kernel(keep_ref, got_ref, next_ref, send_ref):
    for j in range(keep_ref.shape[0]):
        total = keep_ref[j] + got_ref[j].astype(jnp.float32)
        out_ref = send_ref if j % 2 else next_ref
        out_ref[j // 2] = total.astype(out_ref.dtype)


def spread_kernel(keep_ref, got_ref, *outs):
    for j, out_ref in enumerate(outs):
        out_ref[...] = (keep_ref[j] + got_ref[j].astype(jnp.float32)).astype(out_ref.dtype)


def step_kernel(keep_ref, got_ref, own_ref, send_ref):
    own_ref[...] = keep_ref[0] + got_ref[0].astype(jnp.float32)
    send_ref[...] = (keep_ref[1] + got_ref[1].astype(jnp.float32)).astype(jnp.bfloat16)


def line_kernel(*refs):
    total = refs[0][...]
    for ref in refs[1:-1]:
        total = total + ref[...].astype(jnp.float32)
    refs[-1][...] = total.astype(jnp.bfloat16)


def line_and_loss_kernel(loss_ref, *refs):
    out_ref, terms_ref = refs[-2:]
    rows = refs[0].shape[0]
    line_kernel(*refs[:-2], out_ref.at[:rows, :])
    terms_ref[...] = jnp.zeros_like(terms_ref)
    blocks = loss_ref.shape[0]
    rest = loss_ref[...]
    for i in range(3):
        term = rest.astype(jnp.bfloat16).astype(jnp.float32)
        terms_ref[i * blocks : (i + 1) * blocks, :] = term
        rest = rest - term
    out_ref[rows:, :] = terms_ref[...].astype(jnp.bfloat16)


def home_again_kernel(low_ref, high_ref, loss_ref, grads_ref):
    blocks = loss_ref.shape[0]
    rows = high_ref.shape[0]
    grads_ref[:rows, :] = low_ref[:rows, :]
    grads_ref[rows:, :] = high_ref[...]
    terms = low_ref[rows:, :].astype(jnp.float32)
    loss_ref[...] = terms[:blocks] + (terms[blocks : 2 * blocks] + terms[2 * blocks : 3 * blocks])


def grad_kernel(groups, lab_count, pos_count, table_ref, hits_ref, shares_ref, stats_ref, *rest):
    logits_refs = rest[: len(groups)]
    rows = rest[len(groups) : -5]
    loss_ref, out_ref, lse_ref, columns_ref, total_ref = rest[-5:]
    prepare(stats_ref, pos_count, lab_count, loss_ref, lse_ref, columns_ref, total_ref, 0)
    add_slots(
        (0, 1),
        groups,
        pos_count,
        0,
        table_ref,
        hits_ref,
        shares_ref,
        logits_refs,
        rows,
        (lse_ref, columns_ref, total_ref),
    )
    part = out_ref.shape[2]
    for j in range(lab_count):
        for b in range(total_ref.shape[0]):
            out_ref[j, b * BLK : (b + 1) * BLK, :] = total_ref[
                b, :, j * part : (j + 1) * part
            ].astype(jnp.bfloat16)


def smem():
    return pl.BlockSpec(memory_space=pltpu.SMEM)


def vmem():
    return pl.BlockSpec(memory_space=pltpu.VMEM)


def anywhere():
    return pl.BlockSpec(memory_space=pl.ANY)


def call(kernel, name, out_shape, in_specs, arrays, scratch=(), limit=VMEM_BYTES, out_specs=None):
    return pl.pallas_call(
        kernel,
        out_shape=out_shape,
        in_specs=in_specs,
        out_specs=out_specs or [vmem()] * len(out_shape),
        scratch_shapes=list(scratch),
        compiler_params=pltpu.CompilerParams(vmem_limit_bytes=limit),
        name=name,
    )(*arrays)


def shards(feats, weights, shortlist, slot_of, positives):
    dp_count = lax.axis_size("dp")
    lab_count = lax.axis_size("label")
    stored, cluster_size, width = weights.shape
    inst_count = feats.shape[0]
    pos_count = positives.shape[1]
    block_count = inst_count // BLK
    part = width // lab_count
    square = dp_count == 4 and lab_count == 8 and part % 128 == 0
    plan = Plan(square, dp_count, lab_count, stored, block_count, shortlist.shape[1])
    struct = jax.ShapeDtypeStruct
    row_type = struct((cluster_size, width), weights.dtype)
    stat_shape = (3, block_count, BLK)
    both = ("dp", "label")
    devices = [(dp, lab) for dp in range(dp_count) for lab in range(lab_count)]

    def move(x, target):
        pairs = []
        for dp, lab in devices:
            to_dp, to_lab = target(dp, lab)
            pairs.append((dp * lab_count + lab, to_dp * lab_count + to_lab))
        return lax.ppermute(x, both, pairs)

    feat_blocks = feats.reshape(block_count, BLK, width)
    pos_blocks = positives.reshape(block_count, BLK, pos_count).transpose(0, 2, 1)
    if square:
        other_feats = lax.ppermute(feat_blocks, "dp", [(i, i ^ 1) for i in range(dp_count)])
        other_pos = lax.ppermute(pos_blocks, "dp", [(i, i ^ 1) for i in range(dp_count)])
        feat_blocks, pos_blocks = call(
            home_kernel,
            "home",
            [struct(feat_blocks.shape, feats.dtype), struct(pos_blocks.shape, jnp.int32)],
            [vmem()] * 4,
            (feat_blocks, pos_blocks, other_feats, other_pos),
        )

    far = range(1, dp_count)
    far_rows = []
    for some in (far[:1], far[1:]) if square else (far,):
        far_rows += call(
            functools.partial(far_kernel, plan, some),
            "pick_far",
            [row_type] * len(some),
            [anywhere()] * 3,
            (shortlist, slot_of, weights),
            scratch=[
                pltpu.VMEM(weights.shape, weights.dtype),
                pltpu.SMEM(shortlist.shape, jnp.int32),
                pltpu.SMEM(slot_of.shape, jnp.int32),
                pltpu.SemaphoreType.DMA((3 + len(some),)),
            ],
            limit=VMEM_PICK,
            out_specs=[anywhere()] * len(some),
        )
    table, *rows = call(
        functools.partial(near_kernel, plan),
        "pick_near",
        [struct((dp_count, 4), jnp.int32), row_type],
        [smem(), smem(), anywhere()],
        (shortlist, slot_of, weights),
        scratch=[pltpu.SemaphoreType.DMA((1,))],
        out_specs=[smem(), vmem()],
    )
    for k, x in zip(far, far_rows):
        if square and k == 3:
            x, rows[1] = lax.optimization_barrier((x, rows[1]))
        rows.append(lax.ppermute(x, both, plan.pairs(k)))

    if square:
        groups = [(0,), (1,), (2,), (3,)]
    else:
        cuts = (0, dp_count // 2, dp_count * 3 // 4, dp_count)
        groups = [tuple(range(a, b)) for a, b in zip(cuts[:-1], cuts[1:])]
    early = [s for slots in groups[:-1] for s in slots]
    late = list(groups[-1])
    hits, shares, turned = call(
        functools.partial(target_kernel, early, late),
        "targets",
        [
            struct((dp_count, cluster_size, 2 * BLK), jnp.float32),
            struct((len(early), 2 * BLK, cluster_size), jnp.float32),
            struct((len(late), width, 2 * BLK), feats.dtype),
        ],
        [smem()] + [vmem()] * 2,
        (table, pos_blocks, feat_blocks),
    )
    kept = []
    stats = []
    for slots in groups:
        last = slots is groups[-1]
        copies = lab_count if last else 1
        shape = (cluster_size, 2 * BLK) if last else (2 * BLK, cluster_size)
        logits, stats_out = call(
            functools.partial(logit_kernel, slots, not last, copies),
            "logits",
            [
                struct((len(slots),) + shape, jnp.float32),
                struct((copies,) + stat_shape, jnp.float32),
            ],
            [smem()] + [vmem()] * (2 + len(slots) + len(stats)),
            (table, turned if last else feat_blocks, hits, *[rows[s] for s in slots], *stats),
            scratch=[pltpu.VMEM(stat_shape, jnp.float32)],
        )
        kept.append(logits)
        stats = [stats_out]

    in_specs = [smem()] + [vmem()] * (3 + len(groups) + dp_count)
    loss_type = struct((block_count, BLK), jnp.float32)
    lse_scratch = pltpu.VMEM((block_count, BLK), jnp.float32)
    if not square:
        all_stats = lax.all_to_all(stats[0], "label", split_axis=0, concat_axis=0, tiled=True)
        loss, parts = call(
            functools.partial(grad_kernel, groups, lab_count, pos_count),
            "grads",
            [loss_type, struct((lab_count, inst_count, part), jnp.bfloat16)],
            in_specs,
            (table, hits, shares, all_stats, *kept, *rows),
            scratch=[
                lse_scratch,
                pltpu.VMEM((block_count, BLK, BLK), jnp.float32),
                pltpu.VMEM((block_count, BLK, width), jnp.float32),
            ],
        )
        gathered = lax.all_to_all(parts, "label", split_axis=0, concat_axis=0, tiled=True)
        grads = jnp.sum(gathered.astype(jnp.float32), axis=0).astype(jnp.bfloat16)
        return loss.reshape(inst_count), grads

    owners = [
        [(2 * y + core) * lab_count + 2 * z + x for z in range(lab_count // 2) for core in range(2)]
        for y in range(dp_count // 2)
        for x in range(2)
    ]
    all_stats = lax.all_to_all(
        stats[0], both, split_axis=0, concat_axis=0, axis_index_groups=owners, tiled=True
    )
    pairs = lab_count // 2
    half_rows = inst_count // 2
    wide = struct((half_rows, part), jnp.float32)
    narrow = struct((half_rows, part), jnp.bfloat16)

    halves = []
    for side in range(2):
        loss, keep, send = call(
            functools.partial(half_kernel, side, groups, lab_count, pos_count),
            "grads",
            [
                loss_type,
                struct((pairs, half_rows, part), jnp.float32),
                struct((pairs, half_rows, part), jnp.bfloat16),
            ],
            in_specs,
            (table, hits, shares, all_stats, *kept, *rows),
            scratch=[
                lse_scratch,
                pltpu.VMEM((block_count // 2, BLK, BLK), jnp.float32),
                pltpu.VMEM((block_count // 2, BLK, width), jnp.float32),
            ],
        )
        halves.append((keep, lax.ppermute(send, "dp", [(i, i ^ 1) for i in range(dp_count)])))

    def hop(x, mask):
        return lax.ppermute(x, "label", [(i, i ^ mask) for i in range(lab_count)])

    keep, send = call(
        pair_kernel,
        "pair_sums",
        [struct((2, half_rows, part), jnp.float32), struct((2, half_rows, part), jnp.bfloat16)],
        [vmem()] * 2,
        halves[1],
    )
    got = hop(send, 2)
    spread = call(
        spread_kernel, "spread_sums", [wide] + [narrow] * (pairs - 1), [vmem()] * 2, halves[0]
    )
    low = [spread[0]] + [hop(spread[j], 2 * j) for j in range(pairs - 1, 0, -1)]
    got, *_ = lax.optimization_barrier((got, *spread))
    own, send = call(step_kernel, "step_sums", [wide, narrow], [vmem()] * 2, (keep, got))
    high = [own, hop(send, 4)]
    extra = -(-3 * block_count // 16) * 16

    def deliver(x):
        return move(x, lambda dp, lab: ((dp & ~1) | (lab & 1), (lab & ~1) | (1 - (dp & 1))))

    (low,) = call(
        line_and_loss_kernel,
        "line_sums_loss",
        [struct((half_rows + extra, part), jnp.bfloat16)],
        [vmem()] * (1 + len(low)),
        (loss, *low),
        scratch=[pltpu.VMEM((extra, part), jnp.float32)],
    )
    low_home = deliver(low)
    *high, low = lax.optimization_barrier((*high, low))
    (high,) = call(line_kernel, "line_sums", [narrow], [vmem()] * 2, high)
    loss, grads = call(
        home_again_kernel,
        "home_again",
        [loss_type, struct((inst_count, part), jnp.bfloat16)],
        [vmem()] * 2,
        (low_home, deliver(high)),
    )
    return loss.reshape(inst_count), grads


def solution(mesh):
    in_specs = (P("dp", None), P(("dp", "label"), None, None), P(), P(), P("dp", None))
    out_specs = (P("dp"), P("dp", "label"))
    return jax.shard_map(shards, mesh=mesh, in_specs=in_specs, out_specs=out_specs, check_vma=False)
```

```python
import functools

import jax
import jax.numpy as jnp
from jax import lax
from jax.experimental import pallas as pl
from jax.experimental.pallas import tpu as pltpu
from jax.sharding import PartitionSpec as P

BLK = 128
NEG_FILL = -1e30
VMEM_BYTES = 32 * 1024 * 1024
VMEM_PICK = 56 * 1024 * 1024


def divide(value, by):
    if by & (by - 1) == 0:
        return lax.shift_right_logical(value, jnp.int32(by.bit_length() - 1))
    return lax.div(value, jnp.int32(by))


def remainder(value, by):
    if by & (by - 1) == 0:
        return value & jnp.int32(by - 1)
    return lax.rem(value, jnp.int32(by))


def each_entry(count, short_count, body, carry):
    if count <= 64:
        for e in range(count):
            carry = body(e // short_count, e % short_count, carry)
        return carry
    step = lambda e, c: body(divide(e, short_count), remainder(e, short_count), c)
    return lax.fori_loop(0, count, step, carry)


class Plan:
    def __init__(self, square, dp_count, lab_count, stored, block_count, short_count):
        self.square, self.dp_count, self.lab_count = square, dp_count, lab_count
        self.stored, self.block_count, self.short_count = stored, block_count, short_count

    def here(self):
        return lax.axis_index("dp"), lax.axis_index("label")

    def home(self):
        dp, lab = self.here()
        return (dp & ~1) | (lab & 1) if self.square else dp

    def flips(self, entry, core):
        return [(0, 0), (1, 1), (core, 1 - core), (1 - core, core)][entry]

    def wanted_by(self, entry):
        dp, lab = self.here()
        if not self.square:
            return dp ^ entry
        flip_x, flip_y = self.flips(entry, dp & 1)
        return ((dp >> 1) ^ flip_y) * 2 + ((lab & 1) ^ flip_x)

    def entry_of(self, device):
        dp, lab = self.here()
        that_dp, that_lab = divide(device, self.lab_count), remainder(device, self.lab_count)
        if not self.square:
            return that_lab == lab, that_dp ^ dp
        match = ((that_dp & 1) == (dp & 1)) & ((that_lab >> 1) == (lab >> 1))
        flip_y, flip_x = (that_dp ^ dp) >> 1, (that_lab ^ lab) & 1
        core = dp & 1
        lone = jnp.where(flip_y == 1 - core, 2, 3)
        entry = jnp.where(flip_x + flip_y == 1, lone, (flip_x + flip_y) >> 1)
        return match, entry

    def pairs(self, entry):
        result = []
        for dp in range(self.dp_count):
            for lab in range(self.lab_count):
                if self.square:
                    flip_x, flip_y = self.flips(entry, dp & 1)
                    target = (dp ^ (2 * flip_y)) * self.lab_count + (lab ^ flip_x)
                else:
                    target = (dp ^ entry) * self.lab_count + lab
                result.append((dp * self.lab_count + lab, target))
        return result


def find_slots(plan, wanted, lists_ref, slot_ref):
    dp_index, lab_index = plan.here()
    mine = dp_index * plan.lab_count + lab_index
    stored, short_count = plan.stored, plan.short_count
    found = []
    for k in wanted:
        base = plan.wanted_by(k) * plan.block_count

        def look(row, column, slot_here, base=base):
            slot = slot_ref[lists_ref[base + row, column]]
            return jnp.where(divide(slot, stored) == mine, remainder(slot, stored), slot_here)

        count = plan.block_count // 2 * short_count
        found.append(each_entry(count, short_count, look, jnp.int32(0)))
    return found


def far_kernel(plan, wanted, lists_hbm, slot_hbm, weights_ref, *rest):
    outs = rest[: len(wanted)]
    held, lists_ref, slot_ref, sems = rest[len(wanted) :]
    tables = [
        pltpu.make_async_copy(lists_hbm, lists_ref, sems.at[0]),
        pltpu.make_async_copy(slot_hbm, slot_ref, sems.at[1]),
    ]
    stage = pltpu.make_async_copy(weights_ref, held, sems.at[2])
    for copy in tables:
        copy.start()
    stage.start()
    for copy in tables:
        copy.wait()
    found = find_slots(plan, wanted, lists_ref, slot_ref)
    stage.wait()
    copies = []
    for i, slot in enumerate(found):
        copies.append(pltpu.make_async_copy(held.at[slot], outs[i], sems.at[3 + i]))
        copies[-1].start()
    for copy in copies:
        copy.wait()


def near_kernel(plan, lists_ref, slot_ref, weights_ref, table_ref, *rest):
    block_count, short_count = plan.block_count, plan.short_count
    outs, sems = rest[:-1], rest[-1]
    copies = []
    for k, slot in enumerate(find_slots(plan, range(1), lists_ref, slot_ref)):
        copies.append(pltpu.make_async_copy(weights_ref.at[slot], outs[k], sems.at[k]))
        copies[-1].start()
    home = plan.home()
    half = block_count // 2
    for side in range(2):

        def note(row, column, carry, side=side):
            block = side * half + row
            cluster = lists_ref[home * block_count + block, column]
            match, entry = plan.entry_of(divide(slot_ref[cluster], plan.stored))

            @pl.when(match)
            def _():
                table_ref[entry, 0] = cluster
                table_ref[entry, 1 + side] = jnp.int32(block)

            return carry

        each_entry(half * short_count, short_count, note, jnp.int32(0))
    for copy in copies:
        copy.wait()


def home_kernel(feats_ref, pos_ref, other_feats_ref, other_pos_ref, home_feats_ref, home_pos_ref):
    same = (lax.axis_index("dp") & 1) == (lax.axis_index("label") & 1)

    @pl.when(same)
    def _():
        home_feats_ref[...] = feats_ref[...]
        home_pos_ref[...] = pos_ref[...]

    @pl.when(jnp.logical_not(same))
    def _():
        home_feats_ref[...] = other_feats_ref[...]
        home_pos_ref[...] = other_pos_ref[...]


def target_kernel(early, late, table_ref, pos_ref, feats_ref, hits_ref, shares_ref, turned_ref):
    count, cluster_size, _ = hits_ref.shape
    pos_count = pos_ref.shape[1]

    def one_slot(s):
        labels = lax.broadcasted_iota(jnp.int32, (cluster_size, BLK), 0) + table_ref[s, 0] * cluster_size
        for side in range(2):
            pos = pos_ref[table_ref[s, 1 + side]]
            hit = pos[0:1, :] == labels
            for p in range(1, pos_count):
                hit = hit | (pos[p : p + 1, :] == labels)
            hits = jnp.where(hit, 1.0, 0.0)
            columns = pl.ds(side * BLK, BLK)
            hits_ref[s, :, columns] = hits
            if s in early:
                shares_ref[early.index(s), columns, :] = (hits / pos_count).T
            else:
                feats = feats_ref[table_ref[s, 1 + side]].astype(jnp.float32)
                turned_ref[late.index(s), :, columns] = feats.T.astype(jnp.bfloat16)

    for s in range(count):
        pl.when(table_ref[s, 0] >= 0)(functools.partial(one_slot, s))


def logit_kernel(slots, turned, copies, table_ref, feats_ref, hits_ref, *rest):
    count = len(slots)
    rows = rest[:count]
    logits_ref, out_ref, stats_ref = rest[-3:]
    if len(rest) == count + 3:
        stats_ref[0] = jnp.full(stats_ref.shape[1:], NEG_FILL, jnp.float32)
        stats_ref[1] = jnp.zeros(stats_ref.shape[1:], jnp.float32)
        stats_ref[2] = jnp.zeros(stats_ref.shape[1:], jnp.float32)
    else:
        stats_ref[...] = rest[count][0]
    for i, (s, ref) in enumerate(zip(slots, rows)):
        if not turned:
            logits_ref[i] = jnp.dot(ref[...], feats_ref[i], preferred_element_type=jnp.float32)
        for side in range(2):
            block = table_ref[s, 1 + side]
            columns = pl.ds(side * BLK, BLK)
            if turned:
                logits = lax.dot_general(
                    ref[...],
                    feats_ref[block],
                    (((1,), (1,)), ((), ())),
                    preferred_element_type=jnp.float32,
                )
                logits_ref[i, columns, :] = logits.T
            else:
                logits = logits_ref[i, :, columns]
            highest = jnp.max(logits, axis=0, keepdims=True)
            total = jnp.sum(jnp.exp(logits - highest), axis=0, keepdims=True)
            positive = jnp.sum(hits_ref[s, :, columns] * logits, axis=0, keepdims=True)
            row = pl.ds(block, 1)
            before = stats_ref[0, row, :]
            after = jnp.maximum(before, highest)
            stats_ref[0, row, :] = after
            stats_ref[1, row, :] = stats_ref[1, row, :] * jnp.exp(before - after) + total * jnp.exp(
                highest - after
            )
            stats_ref[2, row, :] = stats_ref[2, row, :] + positive
    for i in range(copies):
        out_ref[i] = stats_ref[...]


def row_sums(stats_ref, lab_count):
    highest = stats_ref[0, 0]
    for i in range(1, lab_count):
        highest = jnp.maximum(highest, stats_ref[i, 0])
    summed = jnp.zeros_like(highest)
    positive = jnp.zeros_like(highest)
    for i in range(lab_count):
        summed = summed + stats_ref[i, 1] * jnp.exp(stats_ref[i, 0] - highest)
        positive = positive + stats_ref[i, 2]
    return highest + jnp.log(summed), positive


def prepare(stats_ref, pos_count, lab_count, loss_ref, lse_ref, columns_ref, total_ref, first):
    lse, positive = row_sums(stats_ref, lab_count)
    lse_ref[...] = lse
    loss_ref[...] = lse - positive / pos_count
    for b in range(columns_ref.shape[0]):
        columns_ref[b] = jnp.broadcast_to(lse[first + b : first + b + 1, :], (BLK, BLK)).T
    total_ref[...] = jnp.zeros_like(total_ref)


def add_slots(sides, groups, pos_count, first, table_ref, hits_ref, shares_ref, logits_refs, rows, sums):
    lse_ref, columns_ref, total_ref = sums
    early = [s for slots in groups[:-1] for s in slots]
    cluster_size = rows[0].shape[0]

    def one_slot(s, logits_ref):
        for side in sides:
            block = table_ref[s, 1 + side]
            here = pl.ds(side * BLK, BLK)
            if s in early:
                column = columns_ref[block - first]
                column = jnp.concatenate([column] * (cluster_size // BLK), axis=1)
                dlogit = jnp.exp(logits_ref[here, :] - column) - shares_ref[early.index(s), here, :]
            else:
                row = lse_ref[pl.ds(block, 1), :]
                dlogit = jnp.exp(logits_ref[:, here] - row) - hits_ref[s, :, here] / pos_count
                dlogit = dlogit.T
            total_ref[block - first] += lax.dot_general(
                dlogit.astype(jnp.bfloat16),
                rows[s][...],
                (((1,), (0,)), ((), ())),
                preferred_element_type=jnp.float32,
            )

    for slots, logits_ref in zip(groups, logits_refs):
        for i, s in enumerate(slots):
            body = functools.partial(one_slot, s, logits_ref.at[i])
            if len(rows) <= 4:
                body()
            else:
                pl.when(table_ref[s, 0] >= 0)(body)


def half_kernel(side, groups, lab_count, pos_count, table_ref, hits_ref, shares_ref, stats_ref, *rest):
    logits_refs = rest[: len(groups)]
    rows = rest[len(groups) : -6]
    loss_ref, keep_ref, send_ref, lse_ref, columns_ref, total_ref = rest[-6:]
    half = total_ref.shape[0]
    prepare(
        stats_ref, pos_count, lab_count, loss_ref, lse_ref, columns_ref, total_ref, side * half
    )
    add_slots(
        (side,),
        groups,
        pos_count,
        side * half,
        table_ref,
        hits_ref,
        shares_ref,
        logits_refs,
        rows,
        (lse_ref, columns_ref, total_ref),
    )
    part = keep_ref.shape[2]
    core, line = lax.axis_index("dp") & 1, lax.axis_index("label") >> 1
    for j in range(lab_count // 2):
        first = (line ^ j) * 2
        mine = pl.ds(pl.multiple_of((first + 1 - core) * part, part), part)
        other = pl.ds(pl.multiple_of((first + core) * part, part), part)
        for b in range(half):
            here = pl.ds(b * BLK, BLK)
            keep_ref[j, here, :] = total_ref[b, :, mine]
            send_ref[j, here, :] = total_ref[b, :, other].astype(jnp.bfloat16)


def pair_kernel(keep_ref, got_ref, next_ref, send_ref):
    for j in range(keep_ref.shape[0]):
        total = keep_ref[j] + got_ref[j].astype(jnp.float32)
        out_ref = send_ref if j % 2 else next_ref
        out_ref[j // 2] = total.astype(out_ref.dtype)


def spread_kernel(keep_ref, got_ref, *outs):
    for j, out_ref in enumerate(outs):
        out_ref[...] = (keep_ref[j] + got_ref[j].astype(jnp.float32)).astype(out_ref.dtype)


def step_kernel(keep_ref, got_ref, own_ref, send_ref):
    own_ref[...] = keep_ref[0] + got_ref[0].astype(jnp.float32)
    send_ref[...] = (keep_ref[1] + got_ref[1].astype(jnp.float32)).astype(jnp.bfloat16)


def line_kernel(*refs):
    total = refs[0][...]
    for ref in refs[1:-1]:
        total = total + ref[...].astype(jnp.float32)
    refs[-1][...] = total.astype(jnp.bfloat16)


def line_and_loss_kernel(loss_ref, *refs):
    out_ref, terms_ref = refs[-2:]
    rows = refs[0].shape[0]
    line_kernel(*refs[:-2], out_ref.at[:rows, :])
    terms_ref[...] = jnp.zeros_like(terms_ref)
    blocks = loss_ref.shape[0]
    rest = loss_ref[...]
    for i in range(3):
        term = rest.astype(jnp.bfloat16).astype(jnp.float32)
        terms_ref[i * blocks : (i + 1) * blocks, :] = term
        rest = rest - term
    out_ref[rows:, :] = terms_ref[...].astype(jnp.bfloat16)


def home_again_kernel(low_ref, high_ref, loss_ref, grads_ref):
    blocks = loss_ref.shape[0]
    rows = high_ref.shape[0]
    grads_ref[:rows, :] = low_ref[:rows, :]
    grads_ref[rows:, :] = high_ref[...]
    terms = low_ref[rows:, :].astype(jnp.float32)
    loss_ref[...] = terms[:blocks] + (terms[blocks : 2 * blocks] + terms[2 * blocks : 3 * blocks])


def grad_kernel(groups, lab_count, pos_count, table_ref, hits_ref, shares_ref, stats_ref, *rest):
    logits_refs = rest[: len(groups)]
    rows = rest[len(groups) : -5]
    loss_ref, out_ref, lse_ref, columns_ref, total_ref = rest[-5:]
    prepare(stats_ref, pos_count, lab_count, loss_ref, lse_ref, columns_ref, total_ref, 0)
    add_slots(
        (0, 1),
        groups,
        pos_count,
        0,
        table_ref,
        hits_ref,
        shares_ref,
        logits_refs,
        rows,
        (lse_ref, columns_ref, total_ref),
    )
    part = out_ref.shape[2]
    for j in range(lab_count):
        for b in range(total_ref.shape[0]):
            out_ref[j, b * BLK : (b + 1) * BLK, :] = total_ref[
                b, :, j * part : (j + 1) * part
            ].astype(jnp.bfloat16)


def smem():
    return pl.BlockSpec(memory_space=pltpu.SMEM)


def vmem():
    return pl.BlockSpec(memory_space=pltpu.VMEM)


def anywhere():
    return pl.BlockSpec(memory_space=pl.ANY)


def call(kernel, name, out_shape, in_specs, arrays, scratch=(), limit=VMEM_BYTES, out_specs=None):
    return pl.pallas_call(
        kernel,
        out_shape=out_shape,
        in_specs=in_specs,
        out_specs=out_specs or [vmem()] * len(out_shape),
        scratch_shapes=list(scratch),
        compiler_params=pltpu.CompilerParams(vmem_limit_bytes=limit),
        name=name,
    )(*arrays)


def shards(feats, weights, shortlist, slot_of, positives):
    dp_count = lax.axis_size("dp")
    lab_count = lax.axis_size("label")
    stored, cluster_size, width = weights.shape
    inst_count = feats.shape[0]
    pos_count = positives.shape[1]
    block_count = inst_count // BLK
    part = width // lab_count
    square = dp_count == 4 and lab_count == 8 and part % 128 == 0
    plan = Plan(square, dp_count, lab_count, stored, block_count, shortlist.shape[1])
    struct = jax.ShapeDtypeStruct
    row_type = struct((cluster_size, width), weights.dtype)
    stat_shape = (3, block_count, BLK)
    both = ("dp", "label")
    devices = [(dp, lab) for dp in range(dp_count) for lab in range(lab_count)]

    def move(x, target):
        pairs = []
        for dp, lab in devices:
            to_dp, to_lab = target(dp, lab)
            pairs.append((dp * lab_count + lab, to_dp * lab_count + to_lab))
        return lax.ppermute(x, both, pairs)

    feat_blocks = feats.reshape(block_count, BLK, width)
    pos_blocks = positives.reshape(block_count, BLK, pos_count).transpose(0, 2, 1)
    if square:
        other_feats = lax.ppermute(feat_blocks, "dp", [(i, i ^ 1) for i in range(dp_count)])
        other_pos = lax.ppermute(pos_blocks, "dp", [(i, i ^ 1) for i in range(dp_count)])
        feat_blocks, pos_blocks = call(
            home_kernel,
            "home",
            [struct(feat_blocks.shape, feats.dtype), struct(pos_blocks.shape, jnp.int32)],
            [vmem()] * 4,
            (feat_blocks, pos_blocks, other_feats, other_pos),
        )

    far = range(1, dp_count)
    far_rows = []
    for some in (far[:1], far[1:]) if square else (far,):
        far_rows += call(
            functools.partial(far_kernel, plan, some),
            "pick_far",
            [row_type] * len(some),
            [anywhere()] * 3,
            (shortlist, slot_of, weights),
            scratch=[
                pltpu.VMEM(weights.shape, weights.dtype),
                pltpu.SMEM(shortlist.shape, jnp.int32),
                pltpu.SMEM(slot_of.shape, jnp.int32),
                pltpu.SemaphoreType.DMA((3 + len(some),)),
            ],
            limit=VMEM_PICK,
            out_specs=[anywhere()] * len(some),
        )
    table, *rows = call(
        functools.partial(near_kernel, plan),
        "pick_near",
        [struct((dp_count, 4), jnp.int32), row_type],
        [smem(), smem(), anywhere()],
        (shortlist, slot_of, weights),
        scratch=[pltpu.SemaphoreType.DMA((1,))],
        out_specs=[smem(), vmem()],
    )
    for k, x in zip(far, far_rows):
        if square and k == 3:
            x, rows[1] = lax.optimization_barrier((x, rows[1]))
        rows.append(lax.ppermute(x, both, plan.pairs(k)))

    if square:
        groups = [(0,), (1,), (2,), (3,)]
    else:
        cuts = (0, dp_count // 2, dp_count * 3 // 4, dp_count)
        groups = [tuple(range(a, b)) for a, b in zip(cuts[:-1], cuts[1:])]
    early = [s for slots in groups[:-1] for s in slots]
    late = list(groups[-1])
    hits, shares, turned = call(
        functools.partial(target_kernel, early, late),
        "targets",
        [
            struct((dp_count, cluster_size, 2 * BLK), jnp.float32),
            struct((len(early), 2 * BLK, cluster_size), jnp.float32),
            struct((len(late), width, 2 * BLK), feats.dtype),
        ],
        [smem()] + [vmem()] * 2,
        (table, pos_blocks, feat_blocks),
    )
    kept = []
    stats = []
    for slots in groups:
        last = slots is groups[-1]
        copies = lab_count if last else 1
        shape = (cluster_size, 2 * BLK) if last else (2 * BLK, cluster_size)
        logits, stats_out = call(
            functools.partial(logit_kernel, slots, not last, copies),
            "logits",
            [
                struct((len(slots),) + shape, jnp.float32),
                struct((copies,) + stat_shape, jnp.float32),
            ],
            [smem()] + [vmem()] * (2 + len(slots) + len(stats)),
            (table, turned if last else feat_blocks, hits, *[rows[s] for s in slots], *stats),
            scratch=[pltpu.VMEM(stat_shape, jnp.float32)],
        )
        kept.append(logits)
        stats = [stats_out]

    in_specs = [smem()] + [vmem()] * (3 + len(groups) + dp_count)
    loss_type = struct((block_count, BLK), jnp.float32)
    lse_scratch = pltpu.VMEM((block_count, BLK), jnp.float32)
    if not square:
        all_stats = lax.all_to_all(stats[0], "label", split_axis=0, concat_axis=0, tiled=True)
        loss, parts = call(
            functools.partial(grad_kernel, groups, lab_count, pos_count),
            "grads",
            [loss_type, struct((lab_count, inst_count, part), jnp.bfloat16)],
            in_specs,
            (table, hits, shares, all_stats, *kept, *rows),
            scratch=[
                lse_scratch,
                pltpu.VMEM((block_count, BLK, BLK), jnp.float32),
                pltpu.VMEM((block_count, BLK, width), jnp.float32),
            ],
        )
        gathered = lax.all_to_all(parts, "label", split_axis=0, concat_axis=0, tiled=True)
        grads = jnp.sum(gathered.astype(jnp.float32), axis=0).astype(jnp.bfloat16)
        return loss.reshape(inst_count), grads

    owners = [
        [(2 * y + core) * lab_count + 2 * z + x for z in range(lab_count // 2) for core in range(2)]
        for y in range(dp_count // 2)
        for x in range(2)
    ]
    all_stats = lax.all_to_all(
        stats[0], both, split_axis=0, concat_axis=0, axis_index_groups=owners, tiled=True
    )
    pairs = lab_count // 2
    half_rows = inst_count // 2
    wide = struct((half_rows, part), jnp.float32)
    narrow = struct((half_rows, part), jnp.bfloat16)

    halves = []
    for side in range(2):
        loss, keep, send = call(
            functools.partial(half_kernel, side, groups, lab_count, pos_count),
            "grads",
            [
                loss_type,
                struct((pairs, half_rows, part), jnp.float32),
                struct((pairs, half_rows, part), jnp.bfloat16),
            ],
            in_specs,
            (table, hits, shares, all_stats, *kept, *rows),
            scratch=[
                lse_scratch,
                pltpu.VMEM((block_count // 2, BLK, BLK), jnp.float32),
                pltpu.VMEM((block_count // 2, BLK, width), jnp.float32),
            ],
        )
        halves.append((keep, lax.ppermute(send, "dp", [(i, i ^ 1) for i in range(dp_count)])))

    def hop(x, mask):
        return lax.ppermute(x, "label", [(i, i ^ mask) for i in range(lab_count)])

    keep, send = call(
        pair_kernel,
        "pair_sums",
        [struct((2, half_rows, part), jnp.float32), struct((2, half_rows, part), jnp.bfloat16)],
        [vmem()] * 2,
        halves[1],
    )
    got = hop(send, 2)
    spread = call(
        spread_kernel, "spread_sums", [wide] + [narrow] * (pairs - 1), [vmem()] * 2, halves[0]
    )
    low = [spread[0]] + [hop(spread[j], 2 * j) for j in (2, 3, 1)]
    got, *_ = lax.optimization_barrier((got, *spread))
    own, send = call(step_kernel, "step_sums", [wide, narrow], [vmem()] * 2, (keep, got))
    high = [own, hop(send, 4)]
    extra = -(-3 * block_count // 16) * 16

    def deliver(x):
        return move(x, lambda dp, lab: ((dp & ~1) | (lab & 1), (lab & ~1) | (1 - (dp & 1))))

    (low,) = call(
        line_and_loss_kernel,
        "line_sums_loss",
        [struct((half_rows + extra, part), jnp.bfloat16)],
        [vmem()] * (1 + len(low)),
        (loss, *low),
        scratch=[pltpu.VMEM((extra, part), jnp.float32)],
    )
    low_home = deliver(low)
    *high, low = lax.optimization_barrier((*high, low))
    (high,) = call(line_kernel, "line_sums", [narrow], [vmem()] * 2, high)
    loss, grads = call(
        home_again_kernel,
        "home_again",
        [loss_type, struct((inst_count, part), jnp.bfloat16)],
        [vmem()] * 2,
        (low_home, deliver(high)),
    )
    return loss.reshape(inst_count), grads


def solution(mesh):
    in_specs = (P("dp", None), P(("dp", "label"), None, None), P(), P(), P("dp", None))
    out_specs = (P("dp"), P("dp", "label"))
    return jax.shard_map(shards, mesh=mesh, in_specs=in_specs, out_specs=out_specs, check_vma=False)
```

```python
import functools

import jax
import jax.numpy as jnp
from jax import lax
from jax.experimental import pallas as pl
from jax.experimental.pallas import tpu as pltpu
from jax.sharding import PartitionSpec as P

BLK = 128
NEG_FILL = -1e30
VMEM_BYTES = 32 * 1024 * 1024
VMEM_PICK = 56 * 1024 * 1024


def divide(value, by):
    if by & (by - 1) == 0:
        return lax.shift_right_logical(value, jnp.int32(by.bit_length() - 1))
    return lax.div(value, jnp.int32(by))


def remainder(value, by):
    if by & (by - 1) == 0:
        return value & jnp.int32(by - 1)
    return lax.rem(value, jnp.int32(by))


def each_entry(count, short_count, body, carry):
    if count <= 64:
        for e in range(count):
            carry = body(e // short_count, e % short_count, carry)
        return carry
    step = lambda e, c: body(divide(e, short_count), remainder(e, short_count), c)
    return lax.fori_loop(0, count, step, carry)


class Plan:
    def __init__(self, square, dp_count, lab_count, stored, block_count, short_count):
        self.square, self.dp_count, self.lab_count = square, dp_count, lab_count
        self.stored, self.block_count, self.short_count = stored, block_count, short_count

    def here(self):
        return lax.axis_index("dp"), lax.axis_index("label")

    def home(self):
        dp, lab = self.here()
        return (dp & ~1) | (lab & 1) if self.square else dp

    def flips(self, entry, core):
        return [(0, 0), (1, 1), (1 - core, core), (core, 1 - core)][entry]

    def wanted_by(self, entry):
        dp, lab = self.here()
        if not self.square:
            return dp ^ entry
        flip_x, flip_y = self.flips(entry, dp & 1)
        return ((dp >> 1) ^ flip_y) * 2 + ((lab & 1) ^ flip_x)

    def entry_of(self, device):
        dp, lab = self.here()
        that_dp, that_lab = divide(device, self.lab_count), remainder(device, self.lab_count)
        if not self.square:
            return that_lab == lab, that_dp ^ dp
        match = ((that_dp & 1) == (dp & 1)) & ((that_lab >> 1) == (lab >> 1))
        flip_y, flip_x = (that_dp ^ dp) >> 1, (that_lab ^ lab) & 1
        core = dp & 1
        lone = jnp.where(flip_y == core, 2, 3)
        entry = jnp.where(flip_x + flip_y == 1, lone, (flip_x + flip_y) >> 1)
        return match, entry

    def pairs(self, entry):
        result = []
        for dp in range(self.dp_count):
            for lab in range(self.lab_count):
                if self.square:
                    flip_x, flip_y = self.flips(entry, dp & 1)
                    target = (dp ^ (2 * flip_y)) * self.lab_count + (lab ^ flip_x)
                else:
                    target = (dp ^ entry) * self.lab_count + lab
                result.append((dp * self.lab_count + lab, target))
        return result


def find_slots(plan, wanted, lists_ref, slot_ref):
    dp_index, lab_index = plan.here()
    mine = dp_index * plan.lab_count + lab_index
    stored, short_count = plan.stored, plan.short_count
    found = []
    for k in wanted:
        base = plan.wanted_by(k) * plan.block_count

        def look(row, column, slot_here, base=base):
            slot = slot_ref[lists_ref[base + row, column]]
            return jnp.where(divide(slot, stored) == mine, remainder(slot, stored), slot_here)

        count = plan.block_count // 2 * short_count
        found.append(each_entry(count, short_count, look, jnp.int32(0)))
    return found


def far_kernel(plan, wanted, lists_hbm, slot_hbm, weights_ref, *rest):
    outs = rest[: len(wanted)]
    held, lists_ref, slot_ref, sems = rest[len(wanted) :]
    tables = [
        pltpu.make_async_copy(lists_hbm, lists_ref, sems.at[0]),
        pltpu.make_async_copy(slot_hbm, slot_ref, sems.at[1]),
    ]
    stage = pltpu.make_async_copy(weights_ref, held, sems.at[2])
    for copy in tables:
        copy.start()
    stage.start()
    for copy in tables:
        copy.wait()
    found = find_slots(plan, wanted, lists_ref, slot_ref)
    stage.wait()
    copies = []
    for i, slot in enumerate(found):
        copies.append(pltpu.make_async_copy(held.at[slot], outs[i], sems.at[3 + i]))
        copies[-1].start()
    for copy in copies:
        copy.wait()


def near_kernel(plan, lists_ref, slot_ref, weights_ref, table_ref, *rest):
    block_count, short_count = plan.block_count, plan.short_count
    outs, sems = rest[:-1], rest[-1]
    copies = []
    for k, slot in enumerate(find_slots(plan, range(1), lists_ref, slot_ref)):
        copies.append(pltpu.make_async_copy(weights_ref.at[slot], outs[k], sems.at[k]))
        copies[-1].start()
    home = plan.home()
    half = block_count // 2
    for side in range(2):

        def note(row, column, carry, side=side):
            block = side * half + row
            cluster = lists_ref[home * block_count + block, column]
            match, entry = plan.entry_of(divide(slot_ref[cluster], plan.stored))

            @pl.when(match)
            def _():
                table_ref[entry, 0] = cluster
                table_ref[entry, 1 + side] = jnp.int32(block)

            return carry

        each_entry(half * short_count, short_count, note, jnp.int32(0))
    for copy in copies:
        copy.wait()


def home_kernel(feats_ref, pos_ref, other_feats_ref, other_pos_ref, home_feats_ref, home_pos_ref):
    same = (lax.axis_index("dp") & 1) == (lax.axis_index("label") & 1)

    @pl.when(same)
    def _():
        home_feats_ref[...] = feats_ref[...]
        home_pos_ref[...] = pos_ref[...]

    @pl.when(jnp.logical_not(same))
    def _():
        home_feats_ref[...] = other_feats_ref[...]
        home_pos_ref[...] = other_pos_ref[...]


def target_kernel(early, late, table_ref, pos_ref, feats_ref, hits_ref, shares_ref, turned_ref):
    count, cluster_size, _ = hits_ref.shape
    pos_count = pos_ref.shape[1]

    def one_slot(s):
        labels = lax.broadcasted_iota(jnp.int32, (cluster_size, BLK), 0) + table_ref[s, 0] * cluster_size
        for side in range(2):
            pos = pos_ref[table_ref[s, 1 + side]]
            hit = pos[0:1, :] == labels
            for p in range(1, pos_count):
                hit = hit | (pos[p : p + 1, :] == labels)
            hits = jnp.where(hit, 1.0, 0.0)
            columns = pl.ds(side * BLK, BLK)
            hits_ref[s, :, columns] = hits
            if s in early:
                shares_ref[early.index(s), columns, :] = (hits / pos_count).T
            else:
                feats = feats_ref[table_ref[s, 1 + side]].astype(jnp.float32)
                turned_ref[late.index(s), :, columns] = feats.T.astype(jnp.bfloat16)

    for s in range(count):
        pl.when(table_ref[s, 0] >= 0)(functools.partial(one_slot, s))


def logit_kernel(slots, turned, copies, table_ref, feats_ref, hits_ref, *rest):
    count = len(slots)
    rows = rest[:count]
    logits_ref, out_ref, stats_ref = rest[-3:]
    if len(rest) == count + 3:
        stats_ref[0] = jnp.full(stats_ref.shape[1:], NEG_FILL, jnp.float32)
        stats_ref[1] = jnp.zeros(stats_ref.shape[1:], jnp.float32)
        stats_ref[2] = jnp.zeros(stats_ref.shape[1:], jnp.float32)
    else:
        stats_ref[...] = rest[count][0]
    for i, (s, ref) in enumerate(zip(slots, rows)):
        if not turned:
            logits_ref[i] = jnp.dot(ref[...], feats_ref[i], preferred_element_type=jnp.float32)
        for side in range(2):
            block = table_ref[s, 1 + side]
            columns = pl.ds(side * BLK, BLK)
            if turned:
                logits = lax.dot_general(
                    ref[...],
                    feats_ref[block],
                    (((1,), (1,)), ((), ())),
                    preferred_element_type=jnp.float32,
                )
                logits_ref[i, columns, :] = logits.T
            else:
                logits = logits_ref[i, :, columns]
            highest = jnp.max(logits, axis=0, keepdims=True)
            total = jnp.sum(jnp.exp(logits - highest), axis=0, keepdims=True)
            positive = jnp.sum(hits_ref[s, :, columns] * logits, axis=0, keepdims=True)
            row = pl.ds(block, 1)
            before = stats_ref[0, row, :]
            after = jnp.maximum(before, highest)
            stats_ref[0, row, :] = after
            stats_ref[1, row, :] = stats_ref[1, row, :] * jnp.exp(before - after) + total * jnp.exp(
                highest - after
            )
            stats_ref[2, row, :] = stats_ref[2, row, :] + positive
    for i in range(copies):
        out_ref[i] = stats_ref[...]


def row_sums(stats_ref, lab_count):
    highest = stats_ref[0, 0]
    for i in range(1, lab_count):
        highest = jnp.maximum(highest, stats_ref[i, 0])
    summed = jnp.zeros_like(highest)
    positive = jnp.zeros_like(highest)
    for i in range(lab_count):
        summed = summed + stats_ref[i, 1] * jnp.exp(stats_ref[i, 0] - highest)
        positive = positive + stats_ref[i, 2]
    return highest + jnp.log(summed), positive


def prepare(stats_ref, pos_count, lab_count, loss_ref, lse_ref, columns_ref, total_ref, first):
    lse, positive = row_sums(stats_ref, lab_count)
    lse_ref[...] = lse
    loss_ref[...] = lse - positive / pos_count
    for b in range(columns_ref.shape[0]):
        columns_ref[b] = jnp.broadcast_to(lse[first + b : first + b + 1, :], (BLK, BLK)).T
    total_ref[...] = jnp.zeros_like(total_ref)


def add_slots(sides, groups, pos_count, first, table_ref, hits_ref, shares_ref, logits_refs, rows, sums):
    lse_ref, columns_ref, total_ref = sums
    early = [s for slots in groups[:-1] for s in slots]
    cluster_size = rows[0].shape[0]

    def one_slot(s, logits_ref):
        for side in sides:
            block = table_ref[s, 1 + side]
            here = pl.ds(side * BLK, BLK)
            if s in early:
                column = columns_ref[block - first]
                column = jnp.concatenate([column] * (cluster_size // BLK), axis=1)
                dlogit = jnp.exp(logits_ref[here, :] - column) - shares_ref[early.index(s), here, :]
            else:
                row = lse_ref[pl.ds(block, 1), :]
                dlogit = jnp.exp(logits_ref[:, here] - row) - hits_ref[s, :, here] / pos_count
                dlogit = dlogit.T
            total_ref[block - first] += lax.dot_general(
                dlogit.astype(jnp.bfloat16),
                rows[s][...],
                (((1,), (0,)), ((), ())),
                preferred_element_type=jnp.float32,
            )

    for slots, logits_ref in zip(groups, logits_refs):
        for i, s in enumerate(slots):
            body = functools.partial(one_slot, s, logits_ref.at[i])
            if len(rows) <= 4:
                body()
            else:
                pl.when(table_ref[s, 0] >= 0)(body)


def half_kernel(side, groups, lab_count, pos_count, table_ref, hits_ref, shares_ref, stats_ref, *rest):
    logits_refs = rest[: len(groups)]
    rows = rest[len(groups) : -6]
    loss_ref, keep_ref, send_ref, lse_ref, columns_ref, total_ref = rest[-6:]
    half = total_ref.shape[0]
    prepare(
        stats_ref, pos_count, lab_count, loss_ref, lse_ref, columns_ref, total_ref, side * half
    )
    add_slots(
        (side,),
        groups,
        pos_count,
        side * half,
        table_ref,
        hits_ref,
        shares_ref,
        logits_refs,
        rows,
        (lse_ref, columns_ref, total_ref),
    )
    part = keep_ref.shape[2]
    core, line = lax.axis_index("dp") & 1, lax.axis_index("label") >> 1
    for j in range(lab_count // 2):
        first = (line ^ j) * 2
        mine = pl.ds(pl.multiple_of((first + 1 - core) * part, part), part)
        other = pl.ds(pl.multiple_of((first + core) * part, part), part)
        for b in range(half):
            here = pl.ds(b * BLK, BLK)
            keep_ref[j, here, :] = total_ref[b, :, mine]
            send_ref[j, here, :] = total_ref[b, :, other].astype(jnp.bfloat16)


def pair_kernel(keep_ref, got_ref, next_ref, send_ref):
    for j in range(keep_ref.shape[0]):
        total = keep_ref[j] + got_ref[j].astype(jnp.float32)
        out_ref = send_ref if j % 2 else next_ref
        out_ref[j // 2] = total.astype(out_ref.dtype)


def spread_kernel(keep_ref, got_ref, *outs):
    for j, out_ref in enumerate(outs):
        out_ref[...] = (keep_ref[j] + got_ref[j].astype(jnp.float32)).astype(out_ref.dtype)


def step_kernel(keep_ref, got_ref, own_ref, send_ref):
    own_ref[...] = keep_ref[0] + got_ref[0].astype(jnp.float32)
    send_ref[...] = (keep_ref[1] + got_ref[1].astype(jnp.float32)).astype(jnp.bfloat16)


def line_kernel(*refs):
    total = refs[0][...]
    for ref in refs[1:-1]:
        total = total + ref[...].astype(jnp.float32)
    refs[-1][...] = total.astype(jnp.bfloat16)


def line_and_loss_kernel(loss_ref, *refs):
    out_ref, terms_ref = refs[-2:]
    rows = refs[0].shape[0]
    line_kernel(*refs[:-2], out_ref.at[:rows, :])
    terms_ref[...] = jnp.zeros_like(terms_ref)
    blocks = loss_ref.shape[0]
    rest = loss_ref[...]
    for i in range(3):
        term = rest.astype(jnp.bfloat16).astype(jnp.float32)
        terms_ref[i * blocks : (i + 1) * blocks, :] = term
        rest = rest - term
    out_ref[rows:, :] = terms_ref[...].astype(jnp.bfloat16)


def home_again_kernel(low_ref, high_ref, loss_ref, grads_ref):
    blocks = loss_ref.shape[0]
    rows = high_ref.shape[0]
    grads_ref[:rows, :] = low_ref[:rows, :]
    grads_ref[rows:, :] = high_ref[...]
    terms = low_ref[rows:, :].astype(jnp.float32)
    loss_ref[...] = terms[:blocks] + (terms[blocks : 2 * blocks] + terms[2 * blocks : 3 * blocks])


def grad_kernel(groups, lab_count, pos_count, table_ref, hits_ref, shares_ref, stats_ref, *rest):
    logits_refs = rest[: len(groups)]
    rows = rest[len(groups) : -5]
    loss_ref, out_ref, lse_ref, columns_ref, total_ref = rest[-5:]
    prepare(stats_ref, pos_count, lab_count, loss_ref, lse_ref, columns_ref, total_ref, 0)
    add_slots(
        (0, 1),
        groups,
        pos_count,
        0,
        table_ref,
        hits_ref,
        shares_ref,
        logits_refs,
        rows,
        (lse_ref, columns_ref, total_ref),
    )
    part = out_ref.shape[2]
    for j in range(lab_count):
        for b in range(total_ref.shape[0]):
            out_ref[j, b * BLK : (b + 1) * BLK, :] = total_ref[
                b, :, j * part : (j + 1) * part
            ].astype(jnp.bfloat16)


def smem():
    return pl.BlockSpec(memory_space=pltpu.SMEM)


def vmem():
    return pl.BlockSpec(memory_space=pltpu.VMEM)


def anywhere():
    return pl.BlockSpec(memory_space=pl.ANY)


def call(kernel, name, out_shape, in_specs, arrays, scratch=(), limit=VMEM_BYTES, out_specs=None):
    return pl.pallas_call(
        kernel,
        out_shape=out_shape,
        in_specs=in_specs,
        out_specs=out_specs or [vmem()] * len(out_shape),
        scratch_shapes=list(scratch),
        compiler_params=pltpu.CompilerParams(vmem_limit_bytes=limit),
        name=name,
    )(*arrays)


def shards(feats, weights, shortlist, slot_of, positives):
    dp_count = lax.axis_size("dp")
    lab_count = lax.axis_size("label")
    stored, cluster_size, width = weights.shape
    inst_count = feats.shape[0]
    pos_count = positives.shape[1]
    block_count = inst_count // BLK
    part = width // lab_count
    square = dp_count == 4 and lab_count == 8 and part % 128 == 0
    plan = Plan(square, dp_count, lab_count, stored, block_count, shortlist.shape[1])
    struct = jax.ShapeDtypeStruct
    row_type = struct((cluster_size, width), weights.dtype)
    stat_shape = (3, block_count, BLK)
    both = ("dp", "label")
    devices = [(dp, lab) for dp in range(dp_count) for lab in range(lab_count)]

    def move(x, target):
        pairs = []
        for dp, lab in devices:
            to_dp, to_lab = target(dp, lab)
            pairs.append((dp * lab_count + lab, to_dp * lab_count + to_lab))
        return lax.ppermute(x, both, pairs)

    feat_blocks = feats.reshape(block_count, BLK, width)
    pos_blocks = positives.reshape(block_count, BLK, pos_count).transpose(0, 2, 1)
    if square:
        other_feats = lax.ppermute(feat_blocks, "dp", [(i, i ^ 1) for i in range(dp_count)])
        other_pos = lax.ppermute(pos_blocks, "dp", [(i, i ^ 1) for i in range(dp_count)])
        feat_blocks, pos_blocks = call(
            home_kernel,
            "home",
            [struct(feat_blocks.shape, feats.dtype), struct(pos_blocks.shape, jnp.int32)],
            [vmem()] * 4,
            (feat_blocks, pos_blocks, other_feats, other_pos),
        )

    far = range(1, dp_count)
    far_rows = []
    for some in (far[:1], far[1:]) if square else (far,):
        far_rows += call(
            functools.partial(far_kernel, plan, some),
            "pick_far",
            [row_type] * len(some),
            [anywhere()] * 3,
            (shortlist, slot_of, weights),
            scratch=[
                pltpu.VMEM(weights.shape, weights.dtype),
                pltpu.SMEM(shortlist.shape, jnp.int32),
                pltpu.SMEM(slot_of.shape, jnp.int32),
                pltpu.SemaphoreType.DMA((3 + len(some),)),
            ],
            limit=VMEM_PICK,
            out_specs=[anywhere()] * len(some),
        )
    table, *rows = call(
        functools.partial(near_kernel, plan),
        "pick_near",
        [struct((dp_count, 4), jnp.int32), row_type],
        [smem(), smem(), anywhere()],
        (shortlist, slot_of, weights),
        scratch=[pltpu.SemaphoreType.DMA((1,))],
        out_specs=[smem(), vmem()],
    )
    for k, x in zip(far, far_rows):
        if square and k == 3:
            x, rows[1] = lax.optimization_barrier((x, rows[1]))
        rows.append(lax.ppermute(x, both, plan.pairs(k)))

    if square:
        groups = [(0,), (1,), (2,), (3,)]
    else:
        cuts = (0, dp_count // 2, dp_count * 3 // 4, dp_count)
        groups = [tuple(range(a, b)) for a, b in zip(cuts[:-1], cuts[1:])]
    early = [s for slots in groups[:-1] for s in slots]
    late = list(groups[-1])
    hits, shares, turned = call(
        functools.partial(target_kernel, early, late),
        "targets",
        [
            struct((dp_count, cluster_size, 2 * BLK), jnp.float32),
            struct((len(early), 2 * BLK, cluster_size), jnp.float32),
            struct((len(late), width, 2 * BLK), feats.dtype),
        ],
        [smem()] + [vmem()] * 2,
        (table, pos_blocks, feat_blocks),
    )
    kept = []
    stats = []
    for slots in groups:
        last = slots is groups[-1]
        copies = lab_count if last else 1
        shape = (cluster_size, 2 * BLK) if last else (2 * BLK, cluster_size)
        logits, stats_out = call(
            functools.partial(logit_kernel, slots, not last, copies),
            "logits",
            [
                struct((len(slots),) + shape, jnp.float32),
                struct((copies,) + stat_shape, jnp.float32),
            ],
            [smem()] + [vmem()] * (2 + len(slots) + len(stats)),
            (table, turned if last else feat_blocks, hits, *[rows[s] for s in slots], *stats),
            scratch=[pltpu.VMEM(stat_shape, jnp.float32)],
        )
        kept.append(logits)
        stats = [stats_out]

    in_specs = [smem()] + [vmem()] * (3 + len(groups) + dp_count)
    loss_type = struct((block_count, BLK), jnp.float32)
    lse_scratch = pltpu.VMEM((block_count, BLK), jnp.float32)
    if not square:
        all_stats = lax.all_to_all(stats[0], "label", split_axis=0, concat_axis=0, tiled=True)
        loss, parts = call(
            functools.partial(grad_kernel, groups, lab_count, pos_count),
            "grads",
            [loss_type, struct((lab_count, inst_count, part), jnp.bfloat16)],
            in_specs,
            (table, hits, shares, all_stats, *kept, *rows),
            scratch=[
                lse_scratch,
                pltpu.VMEM((block_count, BLK, BLK), jnp.float32),
                pltpu.VMEM((block_count, BLK, width), jnp.float32),
            ],
        )
        gathered = lax.all_to_all(parts, "label", split_axis=0, concat_axis=0, tiled=True)
        grads = jnp.sum(gathered.astype(jnp.float32), axis=0).astype(jnp.bfloat16)
        return loss.reshape(inst_count), grads

    owners = [
        [(2 * y + core) * lab_count + 2 * z + x for z in range(lab_count // 2) for core in range(2)]
        for y in range(dp_count // 2)
        for x in range(2)
    ]
    all_stats = lax.all_to_all(
        stats[0], both, split_axis=0, concat_axis=0, axis_index_groups=owners, tiled=True
    )
    pairs = lab_count // 2
    half_rows = inst_count // 2
    wide = struct((half_rows, part), jnp.float32)
    narrow = struct((half_rows, part), jnp.bfloat16)

    halves = []
    for side in range(2):
        loss, keep, send = call(
            functools.partial(half_kernel, side, groups, lab_count, pos_count),
            "grads",
            [
                loss_type,
                struct((pairs, half_rows, part), jnp.float32),
                struct((pairs, half_rows, part), jnp.bfloat16),
            ],
            in_specs,
            (table, hits, shares, all_stats, *kept, *rows),
            scratch=[
                lse_scratch,
                pltpu.VMEM((block_count // 2, BLK, BLK), jnp.float32),
                pltpu.VMEM((block_count // 2, BLK, width), jnp.float32),
            ],
        )
        halves.append((keep, lax.ppermute(send, "dp", [(i, i ^ 1) for i in range(dp_count)])))

    def hop(x, mask):
        return lax.ppermute(x, "label", [(i, i ^ mask) for i in range(lab_count)])

    keep, send = call(
        pair_kernel,
        "pair_sums",
        [struct((2, half_rows, part), jnp.float32), struct((2, half_rows, part), jnp.bfloat16)],
        [vmem()] * 2,
        halves[1],
    )
    got = hop(send, 2)
    spread = call(
        spread_kernel, "spread_sums", [wide] + [narrow] * (pairs - 1), [vmem()] * 2, halves[0]
    )
    low = [spread[0]] + [hop(spread[j], 2 * j) for j in range(pairs - 1, 0, -1)]
    got, *_ = lax.optimization_barrier((got, *spread))
    own, send = call(step_kernel, "step_sums", [wide, narrow], [vmem()] * 2, (keep, got))
    high = [own, hop(send, 4)]
    extra = -(-3 * block_count // 16) * 16

    def deliver(x):
        return move(x, lambda dp, lab: ((dp & ~1) | (lab & 1), (lab & ~1) | (1 - (dp & 1))))

    (low,) = call(
        line_and_loss_kernel,
        "line_sums_loss",
        [struct((half_rows + extra, part), jnp.bfloat16)],
        [vmem()] * (1 + len(low)),
        (loss, *low),
        scratch=[pltpu.VMEM((extra, part), jnp.float32)],
    )
    low_home = deliver(low)
    *high, low = lax.optimization_barrier((*high, low))
    (high,) = call(line_kernel, "line_sums", [narrow], [vmem()] * 2, high)
    loss, grads = call(
        home_again_kernel,
        "home_again",
        [loss_type, struct((inst_count, part), jnp.bfloat16)],
        [vmem()] * 2,
        (low_home, deliver(high)),
    )
    return loss.reshape(inst_count), grads


def solution(mesh):
    in_specs = (P("dp", None), P(("dp", "label"), None, None), P(), P(), P("dp", None))
    out_specs = (P("dp"), P("dp", "label"))
    return jax.shard_map(shards, mesh=mesh, in_specs=in_specs, out_specs=out_specs, check_vma=False)
```
